32 devices in a mesh: dp: 8 (over y, x, core), mp: 4 (over z).
Axes of the slice: x: 2, y: 2, z: 4, core: 2. Of those that a mesh axis runs over, the one named last changes fastest.
Arguments:
- tokens: bfloat16 [8, 2048, 1024], P(None, ('mp', 'dp')), may hold values from -6 to 6
- out_grad: bfloat16 [8, 2048, 1024], P(None, ('mp', 'dp')), may hold values from -6 to 6
- seq_lengths: int32 [8], replicated, may hold values from 1024 to 2048, as said below
- mix_gain: float32 [1024], replicated, may hold values from 0.1 to 1.9
- w_query: bfloat16 [1024, 1024], P('dp', 'mp'), may hold values from -0.1875 to 0.1875
- w_key: bfloat16 [1024, 1024], P('dp', 'mp'), may hold values from -0.1875 to 0.1875
- w_value: bfloat16 [1024, 2048], P('dp', 'mp'), may hold values from -0.1875 to 0.1875
- w_outgate: bfloat16 [1024, 2048], P('dp', 'mp'), may hold values from -0.1875 to 0.1875
- w_decay: bfloat16 [1024, 8], P('dp', 'mp'), may hold values from -0.1875 to 0.1875
- w_beta: bfloat16 [1024, 8], P('dp', 'mp'), may hold values from -0.1875 to 0.1875
- conv_weight: float32 [4, 4096], replicated, may hold values from -2.5 to 2.5
- rate_log: float32 [8], replicated, may hold values from 0 to 2.77
- step_bias: float32 [8], replicated, may hold values from -14 to -2.3
- head_gain: float32 [256], replicated, may hold values from 0.1 to 1.9
- w_out: bfloat16 [1024, 2048], P('dp', 'mp'), may hold values from -0.1875 to 0.1875
- ffn_gain: float32 [1024], replicated, may hold values from 0.1 to 1.9
- w_ffn_gate: bfloat16 [1024, 2816], P('dp', 'mp'), may hold values from -0.1875 to 0.1875
- w_ffn_up: bfloat16 [1024, 2816], P('dp', 'mp'), may hold values from -0.1875 to 0.1875
- w_ffn_down: bfloat16 [1024, 2816], P('dp', 'mp'), may hold values from -0.15625 to 0.15625
Outputs:
- block_out: bfloat16 [8, 2048, 1024], P(None, ('mp', 'dp'))
- input_grad: bfloat16 [8, 2048, 1024], P(None, ('mp', 'dp'))
- mix_gain_grad: float32 [1024], replicated
- w_query_grad: float32 [1024, 1024], P('dp', 'mp')
- w_key_grad: float32 [1024, 1024], P('dp', 'mp')
- w_value_grad: float32 [1024, 2048], P('dp', 'mp')
- w_outgate_grad: float32 [1024, 2048], P('dp', 'mp')
- w_decay_grad: float32 [1024, 8], P('dp', 'mp')
- w_beta_grad: float32 [1024, 8], P('dp', 'mp')
- conv_weight_grad: float32 [4, 4096], replicated
- rate_log_grad: float32 [8], replicated
- step_bias_grad: float32 [8], replicated
- head_gain_grad: float32 [256], replicated
- w_out_grad: float32 [1024, 2048], P('dp', 'mp')
- ffn_gain_grad: float32 [1024], replicated
- w_ffn_gate_grad: float32 [1024, 2816], P('dp', 'mp')
- w_ffn_up_grad: float32 [1024, 2816], P('dp', 'mp')
- w_ffn_down_grad: float32 [1024, 2816], P('dp', 'mp')
The draws below stay inside these ranges and needn't reach their ends.
Inputs may be any that keep to these rules, and one draw needn't show every extreme that they name: `seq_lengths`: one length per sequence; positions from the length on are padding; some sequence has length 2048 and some 1024.
All inputs are finite; a program needn't handle non-finite values.
Results may differ from the reference program's by a relative error of at most 0.015.
The reference program's roundings to bfloat16 on the way count: a program that leaves them out, or rounds other values in their place, can miss the bound.
Values may be sent and summed in bfloat16 or wider, within the bound.
A program may use at most 320 MiB of HBM per device.

```python
import jax
import jax.numpy as jnp
from jax import lax

D = 1024
H = 8
DK = 128
DV = 256
FF = 2816
CONV = 4
SPAN = 64
SHORTEST = 1024
MAXLEN = 2048
NSEQ = 8


def draw_seq_lengths(key, part):
    seq_total = NSEQ
    lengths_drawn = jax.random.randint(jax.random.fold_in(key, 11), (seq_total,), SHORTEST, MAXLEN + 1)
    longest = jax.random.randint(jax.random.fold_in(key, 12), (), 0, seq_total)
    skip_ahead = jax.random.randint(jax.random.fold_in(key, 13), (), 1, seq_total)
    shortest_at = (longest + skip_ahead) % seq_total
    lengths_drawn = lengths_drawn.at[longest].set(MAXLEN)
    lengths_drawn = lengths_drawn.at[shortest_at].set(SHORTEST)
    return lengths_drawn.astype(jnp.int32)


def draw_step_bias(key, part):
    head_order = jax.random.permutation(jax.random.fold_in(key, 21), H)
    fast_count = H // 2
    fast_heads = head_order < fast_count
    slow_values = jax.random.uniform(jax.random.fold_in(key, 22), (H,), jnp.float32, -14.0, -11.0)
    fast_values = jax.random.uniform(jax.random.fold_in(key, 23), (H,), jnp.float32, -4.6, -2.3)
    return jnp.where(fast_heads, fast_values, slow_values).astype(jnp.float32)


def steps_of(own_key, shape, pieces, low, high):
    level, own = 1.0, jax.random.fold_in(own_key, 6)
    for dim, shards_of in pieces:
        draws = jnp.exp(jax.random.uniform(jax.random.fold_in(own, dim), (shards_of,), jnp.float32, low / len(pieces), high / len(pieces)))
        level = level * jnp.repeat(draws, shape[dim] // shards_of).reshape([-1 if axis == dim else 1 for axis in range(len(shape))])
    return level


def noise(rng, extent, spread, limit, split=(), kind=jnp.bfloat16):
    entries = spread * jax.random.normal(rng, extent, jnp.float32)
    if split:
        entries = entries * steps_of(rng, extent, split, -0.22, 0.18)
    return jnp.clip(entries, -limit, limit).astype(kind)


def setup_inputs(seed: int = 0) -> dict:
    seeds = jax.random.split(jax.random.key(seed), 20)
    return {
        "tokens": noise(seeds[0], (NSEQ, MAXLEN, D), 1.0, 6.0, ((1, 32),)),
        "out_grad": noise(seeds[1], (NSEQ, MAXLEN, D), 1.0, 6.0, ((1, 32),)),
        "seq_lengths": draw_seq_lengths(jax.random.fold_in(seeds[19], 71), 0),
        "mix_gain": jnp.clip(1.0 + 0.18 * jax.random.normal(seeds[3], (D,), jnp.float32), 0.1, 1.9),
        "w_query": noise(seeds[4], (D, H * DK), D ** -0.5, 0.1875, ((0, 8), (1, 4))),
        "w_key": noise(seeds[5], (D, H * DK), D ** -0.5, 0.1875, ((0, 8), (1, 4))),
        "w_value": noise(seeds[6], (D, H * DV), D ** -0.5, 0.1875, ((0, 8), (1, 4))),
        "w_outgate": noise(seeds[7], (D, H * DV), D ** -0.5, 0.1875, ((0, 8), (1, 4))),
        "w_decay": noise(seeds[8], (D, H), D ** -0.5, 0.1875, ((0, 8), (1, 4))),
        "w_beta": noise(seeds[9], (D, H), D ** -0.5, 0.1875, ((0, 8), (1, 4))),
        "conv_weight": noise(seeds[10], (CONV, 2 * H * DK + H * DV), 0.5, 2.5, (), jnp.float32),
        "rate_log": jnp.clip(jax.random.uniform(seeds[11], (H,), jnp.float32, 0.0, 2.77), 0.0, 2.77),
        "step_bias": draw_step_bias(jax.random.fold_in(seeds[19], 71), 0),
        "head_gain": jnp.clip(1.0 + 0.18 * jax.random.normal(seeds[13], (DV,), jnp.float32), 0.1, 1.9),
        "w_out": noise(seeds[14], (D, H * DV), (H * DV // 2) ** -0.5, 0.1875, ((0, 8), (1, 4))),
        "ffn_gain": jnp.clip(1.0 + 0.18 * jax.random.normal(seeds[15], (D,), jnp.float32), 0.1, 1.9),
        "w_ffn_gate": noise(seeds[16], (D, FF), D ** -0.5, 0.1875, ((0, 8), (1, 4))),
        "w_ffn_up": noise(seeds[17], (D, FF), D ** -0.5, 0.1875, ((0, 8), (1, 4))),
        "w_ffn_down": noise(seeds[18], (D, FF), (FF // 2) ** -0.5, 0.15625, ((0, 8), (1, 4))),
    }


@jax.custom_vjp
def low(v):
    return lax.optimization_barrier(v.astype(jnp.bfloat16)).astype(jnp.float32)

@jax.custom_vjp
def low_back(v):
    return v

def low_keep(v):
    return (low(v), None)

def low_pass(kept, grad):
    return (grad,)

def back_keep(v):
    return (v, None)

def back_low(kept, grad):
    return (low(grad),)
low.defvjp(low_keep, low_pass)
low_back.defvjp(back_keep, back_low)

def product(left, right):
    return jnp.dot(left, right, precision=lax.Precision.HIGHEST, preferred_element_type=jnp.float32)

def rms_scale(value_vectors, gain):
    return value_vectors * lax.rsqrt(lax.optimization_barrier(jnp.mean(value_vectors * value_vectors, axis=-1, keepdims=True)) + 1e-05) * gain

def short_conv(raw_input, weights):
    tap_count = weights.shape[0]
    length = raw_input.shape[0]
    padded = jnp.pad(raw_input, ((tap_count - 1, 0), (0, 0)))
    summed = weights[0] * padded[0:length]
    for offset in range(1, tap_count):
        summed = summed + weights[offset] * padded[offset:offset + length]
    return summed

def delta_block(state, inputs):

    def advance(loop_carry_state, item):
        query_vectors, key_vectors, value_vectors, write_strength, log_decay = item
        loop_carry_state = jnp.exp(log_decay)[:, None, None] * loop_carry_state
        initial_estimate = jnp.einsum('djm,dj->dm', loop_carry_state, key_vectors, precision=lax.Precision.HIGHEST)
        loop_carry_state = loop_carry_state + jnp.einsum('me,mg->meg', key_vectors, write_strength[:, None] * (value_vectors - initial_estimate), precision=lax.Precision.HIGHEST)
        return (loop_carry_state, jnp.einsum('djm,dj->dm', loop_carry_state, query_vectors, precision=lax.Precision.HIGHEST))
    return lax.scan(advance, state, inputs)

def delta_rule(query_vectors, key_vectors, value_vectors, write_strength, log_decay):
    length, head_count, key_size = query_vectors.shape
    value_size = value_vectors.shape[-1]
    blocks = length // SPAN
    inputs = tuple((stacked.reshape((blocks, SPAN) + stacked.shape[1:]) for stacked in (query_vectors, key_vectors, value_vectors, write_strength, log_decay)))
    state = jnp.zeros((head_count, key_size, value_size), jnp.float32)
    final_state, outputs = lax.scan(jax.checkpoint(delta_block), state, inputs)
    return outputs.reshape(length, head_count, value_size)

def sequence_layer(params, tokens_seq, live):
    mix_gain, w_query, w_key, w_value, w_outgate, w_decay, w_beta, conv_weight, rate_log, step_bias, head_gain, w_out, ffn_gain, w_ffn_gate, w_ffn_up, w_ffn_down = params
    length = tokens_seq.shape[0]
    key_cols = H * DK
    normed_one = low(rms_scale(tokens_seq, mix_gain))
    query_raw = low_back(product(normed_one, w_query))
    keyed_raw = low_back(product(normed_one, w_key))
    value_raw = low_back(product(normed_one, w_value))
    gate_raw = low_back(product(normed_one, w_outgate))
    decay_raw = low_back(product(normed_one, w_decay))
    beta_raw = low_back(product(normed_one, w_beta))
    query_vectors = jax.nn.silu(short_conv(query_raw, conv_weight[:, :key_cols])).reshape(length, H, DK)
    key_vectors = jax.nn.silu(short_conv(keyed_raw, conv_weight[:, key_cols:2 * key_cols])).reshape(length, H, DK)
    value_vectors = jax.nn.silu(short_conv(value_raw, conv_weight[:, 2 * key_cols:])).reshape(length, H, DV)
    query_vectors = query_vectors * lax.rsqrt(lax.optimization_barrier(jnp.sum(query_vectors * query_vectors, axis=-1, keepdims=True)) + 1e-06) * DK ** (-0.5)
    key_vectors = key_vectors * lax.rsqrt(lax.optimization_barrier(jnp.sum(key_vectors * key_vectors, axis=-1, keepdims=True)) + 1e-06)
    write_strength = jax.nn.sigmoid(beta_raw)
    log_decay = -jnp.exp(rate_log) * jax.nn.softplus(decay_raw + step_bias)
    mixed = delta_rule(query_vectors, key_vectors, value_vectors, write_strength, log_decay)
    gated = rms_scale(mixed, head_gain) * jax.nn.silu(gate_raw.reshape(length, H, DV))
    head_out = low(gated.reshape(length, H * DV))
    after_mix = tokens_seq + low_back(product(head_out, w_out.T))
    normed_two = low(rms_scale(after_mix, ffn_gain))
    gate_activation = low_back(product(normed_two, w_ffn_gate))
    up_activation = low_back(product(normed_two, w_ffn_up))
    silu_activation = low(jax.nn.silu(gate_activation) * up_activation)
    return live[:, None] * (after_mix + low_back(product(silu_activation, w_ffn_down.T)))

def reference(tokens, out_grad, seq_lengths, mix_gain, w_query, w_key, w_value, w_outgate, w_decay, w_beta, conv_weight, rate_log, step_bias, head_gain, w_out, ffn_gain, w_ffn_gate, w_ffn_up, w_ffn_down):
    params = tuple((member.astype(jnp.float32) for member in (mix_gain, w_query, w_key, w_value, w_outgate, w_decay, w_beta, conv_weight, rate_log, step_bias, head_gain, w_out, ffn_gain, w_ffn_gate, w_ffn_up, w_ffn_down)))
    inputs = tokens.astype(jnp.float32)
    cotangent = out_grad.astype(jnp.float32)
    live = (jnp.arange(MAXLEN, dtype=jnp.int32)[None, :] < seq_lengths[:, None]).astype(jnp.float32)
    layer = jax.checkpoint(sequence_layer)

    def forward(weights, stream):
        return lax.map(lambda paired: layer(weights, paired[0], paired[1]), (stream, live))
    outputs, pullback = jax.vjp(forward, params, inputs)
    grad_params, grad_inputs = pullback(cotangent)
    g_mix_gain, g_query, g_key, g_value, g_outgate, g_decay, g_beta, g_conv, g_rate, g_bias, g_head_gain, output_weight_gradient, g_ffn_gain, gate_weight_gradient, up_weight_gradient, down_weight_gradient = grad_params
    return (outputs.astype(jnp.bfloat16), grad_inputs.astype(jnp.bfloat16), g_mix_gain, g_query, g_key, g_value, g_outgate, g_decay, g_beta, g_conv, g_rate, g_bias, g_head_gain, output_weight_gradient, g_ffn_gain, gate_weight_gradient, up_weight_gradient, down_weight_gradient)
```

```python
from functools import partial

import jax
import jax.numpy as jnp
from jax import lax
from jax.experimental import pallas as pl
from jax.experimental.pallas import tpu as pltpu
from jax.sharding import PartitionSpec as P

DK = 128
DV = 256
HEADW = 2 * DK + DV
TAPS = 4
CHUNK = 128
HALO = 8
WIDE = 256
F32 = jnp.float32
BF16 = jnp.bfloat16


def mm(a, b, ca=1, cb=0):
    return lax.dot_general(
        a, b, (((ca,), (cb,)), ((), ())), precision=lax.Precision.HIGHEST, preferred_element_type=F32
    )


def conv_chunk(raw_ref, convw, base, rows):
    total = None
    for i in range(TAPS):
        part = raw_ref[0, pl.ds(HALO - TAPS + 1 + i + base, rows), 0:HEADW] * convw[i : i + 1]
        total = part if total is None else total + part
    return total


def decays(ab_ref, base, rows, upper):
    ab = ab_ref[0, :, pl.ds(base, rows)]
    cum = mm(ab, upper)
    row_id = lax.broadcasted_iota(jnp.int32, ab.shape, 0)
    both = jnp.where(row_id == 0, cum, ab)
    cols = both.T
    return both[0:1], cols[:, 0:1], cols[:, 1:2]


def masks(size):
    rows = lax.broadcasted_iota(jnp.int32, (size, size), 0)
    cols = lax.broadcasted_iota(jnp.int32, (size, size), 1)
    return rows, cols


def fades(gamma_row, gamma_col, rows, cols):
    spread = jnp.minimum(gamma_col - gamma_row, 0.0)
    inclusive = jnp.where(rows >= cols, jnp.exp(spread), 0.0)
    strict = jnp.where(rows > cols, inclusive, 0.0)
    return inclusive, strict


def invert_many(lowers, rows, cols):
    size = lowers[0].shape[0]
    eye = (rows == cols).astype(F32)
    pair = ((rows // 2) == (cols // 2)) & (rows > cols)
    inverses = [eye - jnp.where(pair, low, 0.0) for low in lowers]
    width = 2
    while width < size:
        within = (rows // (2 * width)) == (cols // (2 * width))
        cross = within & ((rows // width) != (cols // width)) & (rows > cols)
        inner = [mm(jnp.where(cross, low, 0.0), inv) for low, inv in zip(lowers, inverses)]
        inverses = [inv - mm(inv, part) for inv, part in zip(inverses, inner)]
        width *= 2
    return inverses


def unit_parts(conv):
    sig = jax.nn.sigmoid(conv)
    silu = conv * sig
    q_silu = silu[:, :DK]
    k_silu = silu[:, DK : 2 * DK]
    value = silu[:, 2 * DK :]
    q_scale = lax.rsqrt(jnp.sum(q_silu * q_silu, axis=-1, keepdims=True) + 1e-06)
    k_scale = lax.rsqrt(jnp.sum(k_silu * k_silu, axis=-1, keepdims=True) + 1e-06)
    return sig, q_silu, k_silu, value, q_scale, k_scale


def greet(z, parts, first):
    @pl.when(first)
    def _():
        barrier = pltpu.get_barrier_semaphore()
        for delta in (1, parts - 1):
            pl.semaphore_signal(
                barrier, inc=1, device_id={"mp": lax.rem(z + delta, parts)},
                device_id_type=pl.DeviceIdType.MESH,
            )
        pl.semaphore_wait(barrier, 2)


def forward_kernel(
    heads, parts,
    raw_ref, gate_ref, convw_ref, ab_ref, gain_ref,
    head_ref, o_ref, s_ref, t_ref, qe_ref, phi_ref, phil_ref,
    qe_s, o0_s, phi_s, b_s, phil_s, bl_s, send_s, recv_s, send_sem, recv_sem,
):
    step = pl.program_id(0)
    z = lax.axis_index("mp")
    lag = parts - 1
    slots = lag + 1
    length = gate_ref.shape[1] - HALO
    size = min(CHUNK, length)
    chunks = length // size

    greet(z, parts, step == 0)

    def hop(h):
        return pltpu.make_async_remote_copy(
            src_ref=send_s.at[h], dst_ref=recv_s.at[h], send_sem=send_sem.at[h],
            recv_sem=recv_sem.at[h], device_id={"mp": lax.rem(z + 1, parts)},
            device_id_type=pl.DeviceIdType.MESH,
        )

    @pl.when((step == 0) & (z == 0))
    def _():
        recv_s[...] = jnp.zeros_like(recv_s)

    @pl.when(step < heads)
    def _():
        slot = lax.rem(step, slots)
        rows, cols = masks(size)
        upper = (rows <= cols).astype(F32)
        convw = convw_ref[0]
        kept = []
        lowers = []
        for c in range(chunks):
            conv = conv_chunk(raw_ref, convw, c * size, size)
            _, q_silu, k_silu, value, q_scale, k_scale = unit_parts(conv)
            query = q_silu * (q_scale * DK ** (-0.5))
            keyed = k_silu * k_scale
            gamma_row, gamma_col, beta = decays(ab_ref, c * size, size, upper)
            inclusive, strict = fades(gamma_row, gamma_col, rows, cols)
            gram = mm(jnp.concatenate([keyed, query], axis=0), keyed, 1, 1)
            lowers.append(beta * gram[:size] * strict)
            scores = gram[size:] * inclusive
            growth = jnp.exp(gamma_col)
            last = gamma_row[:, size - 1 :]
            rhs = jnp.concatenate([(beta * growth) * keyed, beta * value], axis=1)
            kept.append((scores, rhs, query * growth, keyed * jnp.exp(last - gamma_col), last))
        inverses = invert_many(lowers, rows, cols)
        eye = (masks(DK)[0] == masks(DK)[1]).astype(F32)
        phi_all = None
        b_all = None
        for c in range(chunks):
            scores, rhs, query_g, keyed_g, last = kept[c]
            t_ref[0, c] = inverses[c]
            solved = mm(inverses[c], rhs)
            mixed = mm(scores, solved)
            moved = mm(keyed_g, solved, 0, 0)
            query_e = query_g - mixed[:, :DK]
            phi = jnp.exp(last) * eye - moved[:, :DK]
            inflow = moved[:, DK:]
            qe_ref[0, c * size : (c + 1) * size] = query_e
            qe_s[slot, c * size : (c + 1) * size] = query_e
            o0_s[slot, c * size : (c + 1) * size] = mixed[:, DK:]
            phi_ref[0, c] = phi.T
            phi_s[slot, c] = phi
            b_s[slot, c] = inflow
            if c == 0:
                phi_all, b_all = phi, inflow
            else:
                moved_all = mm(phi, jnp.concatenate([phi_all, b_all], axis=1))
                phi_all = moved_all[:, :DK]
                b_all = moved_all[:, DK:] + inflow
        phil_ref[0] = phi_all.T
        phil_s[slot] = phi_all
        bl_s[slot] = b_all

    relay = step - z

    @pl.when((relay >= 0) & (relay < heads))
    def _():
        slot = lax.rem(relay, slots)

        @pl.when(z > 0)
        def _():
            hop(relay).wait_recv()

        @pl.when(z < parts - 1)
        def _():
            send_s[relay] = mm(phil_s[slot], recv_s[relay]) + bl_s[slot]
            hop(relay).start()

    @pl.when(step >= lag)
    def _():
        head = step - lag
        slot = lax.rem(head, slots)
        state = recv_s[head]
        for c in range(chunks):
            at = slice(c * size, (c + 1) * size)
            s_ref[0, c] = state
            result = mm(qe_s[slot, at], state) + o0_s[slot, at]
            if c + 1 < chunks:
                state = mm(phi_s[slot, c], state) + b_s[slot, c]
            o_ref[0, at] = result
            scale = lax.rsqrt(jnp.mean(result * result, axis=-1, keepdims=True) + 1e-05)
            gate = gate_ref[0, HALO + c * size : HALO + (c + 1) * size]
            gated = result * scale * gain_ref[...] * (gate * jax.nn.sigmoid(gate))
            head_ref[0, at] = gated.astype(BF16)

    @pl.when((step == pl.num_programs(0) - 1) & (z < parts - 1))
    def _():
        @pl.loop(0, heads)
        def _(h):
            hop(h).wait_send()


def backward_kernel(
    heads, parts,
    dhead_ref, o_ref, gate_ref, qe_ref, phi_ref, phil_ref,
    raw_ref, convw_ref, ab_ref, gain_ref, s_ref, t_ref, phi_late_ref,
    dproj_ref, dab_ref, dconv_ref, dgain_ref,
    do_s, d_s, dgate_s, dl_s, phil_s, g_s, dext_s, send_s, recv_s, halo_send, halo_recv,
    send_sem, recv_sem, halo_send_sem, halo_recv_sem,
):
    step = pl.program_id(0)
    z = lax.axis_index("mp")
    back = parts - 1 - z
    lag = parts - 1
    slots = lag + 1
    length = o_ref.shape[1]
    size = min(CHUNK, length)
    chunks = length // size

    greet(z, parts, step == 0)

    def hop(h):
        return pltpu.make_async_remote_copy(
            src_ref=send_s.at[h], dst_ref=recv_s.at[h], send_sem=send_sem.at[h],
            recv_sem=recv_sem.at[h], device_id={"mp": lax.rem(z + parts - 1, parts)},
            device_id_type=pl.DeviceIdType.MESH,
        )

    def halo_hop(h):
        return pltpu.make_async_remote_copy(
            src_ref=halo_send.at[h], dst_ref=halo_recv.at[h], send_sem=halo_send_sem.at[h],
            recv_sem=halo_recv_sem.at[h], device_id={"mp": lax.rem(z + parts - 1, parts)},
            device_id_type=pl.DeviceIdType.MESH,
        )

    @pl.when(step == 0)
    def _():
        dgain_ref[...] = jnp.zeros_like(dgain_ref)
        g_s[...] = jnp.zeros_like(g_s)

    @pl.when((step == 0) & (back == 0))
    def _():
        recv_s[...] = jnp.zeros_like(recv_s)
        halo_recv[...] = jnp.zeros_like(halo_recv)

    @pl.when(step < heads)
    def _():
        slot = lax.rem(step, slots)
        gslot = lax.rem(step, slots + 1)
        gain = gain_ref[...]
        d_gain = jnp.zeros((1, DV), F32)
        for c in range(chunks):
            at = slice(c * size, (c + 1) * size)
            out = o_ref[0, at]
            d_head = dhead_ref[0, at]
            gate = gate_ref[0, HALO + c * size : HALO + (c + 1) * size]
            scale = lax.rsqrt(jnp.mean(out * out, axis=-1, keepdims=True) + 1e-05)
            unit = out * scale
            sig = jax.nn.sigmoid(gate)
            gated = gate * sig
            both = d_head * unit
            d_gain = d_gain + jnp.sum(both * gated, axis=0, keepdims=True)
            e = d_head * gated * gain
            d_out = scale * (e - unit * jnp.mean(e * unit, axis=-1, keepdims=True))
            dgate_s[gslot, at] = (both * gain * sig * (1.0 + gate * (1.0 - sig))).astype(BF16)
            do_s[slot, at] = d_out
            d_s[slot, c] = mm(qe_ref[0, at], d_out, 0, 0)
        dgain_ref[...] += d_gain
        total = d_s[slot, chunks - 1]
        for c in range(chunks - 2, -1, -1):
            total = mm(phi_ref[0, c], total) + d_s[slot, c]
        dl_s[slot] = total
        phil_s[slot] = phil_ref[0]

    relay = step - back

    @pl.when((relay >= 0) & (relay < heads))
    def _():
        slot = lax.rem(relay, slots)

        @pl.when(back > 0)
        def _():
            hop(relay).wait_recv()

        @pl.when(z > 0)
        def _():
            send_s[relay] = mm(phil_s[slot], recv_s[relay]) + dl_s[slot]
            hop(relay).start()

    @pl.when((step >= lag) & (step < lag + heads))
    def _():
        head = step - lag
        slot = lax.rem(head, slots)
        eslot = lax.rem(head, 2)
        rows, cols = masks(size)
        upper = (rows <= cols).astype(F32)
        convw = convw_ref[0]
        d_state = recv_s[head]
        d_conv_rows = [jnp.zeros((1, HEADW), F32) for _ in range(TAPS)]
        for c in range(chunks - 1, -1, -1):
            at = slice(c * size, (c + 1) * size)
            conv = conv_chunk(raw_ref, convw, c * size, size)
            sig, q_silu, k_silu, value, q_scale, k_scale = unit_parts(conv)
            query = q_silu * (q_scale * DK ** (-0.5))
            keyed = k_silu * k_scale
            gamma_row, gamma_col, beta = decays(ab_ref, c * size, size, upper)
            inclusive, strict = fades(gamma_row, gamma_col, rows, cols)
            gram = mm(jnp.concatenate([keyed, query], axis=0), keyed, 1, 1)
            gram_f = gram[:size] * strict
            lower = beta * gram_f
            scores = gram[size:] * inclusive
            growth = jnp.exp(gamma_col)
            last = gamma_row[:, size - 1 :]
            tail = jnp.exp(last - gamma_col)
            query_g = query * growth
            grown = keyed * growth
            keyed_b = beta * grown
            keyed_g = keyed * tail
            state = s_ref[0, c]
            inverse = t_ref[0, c]
            d_out = do_s[slot, at]
            fresh = mm(inverse, beta * value - mm(keyed_b, state))
            d_fresh = mm(scores, d_out, 0, 0) + mm(keyed_g, d_state)
            d_rhs = mm(inverse, d_fresh, 0, 0)
            stacked = jnp.concatenate([d_out, d_rhs], axis=0)
            by_fresh = mm(stacked, fresh, 1, 1)
            by_state = mm(stacked, state, 1, 1)
            d_scores = by_fresh[:size] * inclusive
            d_lower = -by_fresh[size:]
            d_query_g = by_state[:size]
            d_keyed_b = -by_state[size:]
            d_keyed_g = mm(fresh, d_state, 1, 1)
            d_gram = d_lower * (beta * strict)
            by_keyed = mm(jnp.concatenate([d_scores, d_gram], axis=0), keyed)
            d_query = by_keyed[:size] + growth * d_query_g
            d_keyed = (
                by_keyed[size:]
                + mm(jnp.concatenate([d_scores, d_gram], axis=0),
                     jnp.concatenate([query, keyed], axis=0), 0, 0)
                + (beta * growth) * d_keyed_b
                + tail * d_keyed_g
            )
            d_value = beta * d_rhs
            d_beta = (
                jnp.sum(d_rhs * value, axis=-1, keepdims=True)
                + jnp.sum(d_lower * gram_f, axis=-1, keepdims=True)
                + jnp.sum(d_keyed_b * grown, axis=-1, keepdims=True)
            )
            moved = by_fresh[:size] * scores + d_lower * lower
            tail_part = jnp.sum(d_keyed_g * keyed_g, axis=-1, keepdims=True)
            d_gamma = (
                jnp.sum(moved, axis=-1, keepdims=True)
                + jnp.sum(d_query_g * query_g, axis=-1, keepdims=True)
                + jnp.sum(d_keyed_b * keyed_b, axis=-1, keepdims=True)
                - tail_part
            )
            at_end = jnp.sum(tail_part, axis=0, keepdims=True) + jnp.exp(last) * jnp.sum(
                jnp.sum(state * d_state, axis=-1, keepdims=True), axis=0, keepdims=True
            )
            lanes = lax.broadcasted_iota(jnp.int32, (size, DK), 1)
            packed = jnp.where(lanes == 0, d_gamma, jnp.where(lanes == 1, d_beta, 0.0)).T[:8]
            row_id = lax.broadcasted_iota(jnp.int32, packed.shape, 0)
            packed = packed - jnp.where(row_id == 0, jnp.sum(moved, axis=0, keepdims=True), 0.0)
            summed = mm(packed, upper, 1, 1) + at_end
            dab_ref[0, :, at] = jnp.where(row_id == 0, summed, packed)
            if c > 0:
                d_state = mm(phi_late_ref[0, c], d_state) + d_s[slot, c]
            d_q_silu = (DK ** (-0.5) * q_scale) * (
                d_query
                - q_silu * (q_scale * q_scale) * jnp.sum(q_silu * d_query, axis=-1, keepdims=True)
            )
            d_k_silu = k_scale * (
                d_keyed
                - k_silu * (k_scale * k_scale) * jnp.sum(k_silu * d_keyed, axis=-1, keepdims=True)
            )
            d_silu = jnp.concatenate([d_q_silu, d_k_silu, d_value], axis=1)
            d_conv = d_silu * sig * (1.0 + conv * (1.0 - sig))
            g_s[HALO + c * size : HALO + (c + 1) * size] = d_conv
            for i in range(TAPS):
                shifted = raw_ref[0, pl.ds(HALO - TAPS + 1 + i + c * size, size), 0:HEADW]
                d_conv_rows[i] = d_conv_rows[i] + jnp.sum(shifted * d_conv, axis=0, keepdims=True)
        for i in range(TAPS):
            dconv_ref[0, i : i + 1] = d_conv_rows[i]
        for base, count in [(0, HALO)] + [(HALO + c * size, size) for c in range(chunks)]:
            d_raw = None
            for i in range(TAPS):
                part = g_s[pl.ds(base + TAPS - 1 - i, count)] * convw[i : i + 1]
                d_raw = part if d_raw is None else d_raw + part
            if base == 0:
                halo_send[head] = d_raw
            else:
                dext_s[eslot, base - HALO : base - HALO + count] = d_raw

        @pl.when(z > 0)
        def _():
            halo_hop(head).start()

    @pl.when(step > lag)
    def _():
        head = step - lag - 1
        eslot = lax.rem(head, 2)
        gslot = lax.rem(head, slots + 1)

        @pl.when(back > 0)
        def _():
            halo_hop(head).wait_recv()

        dext_s[eslot, length - HALO : length] += halo_recv[head]
        dproj_ref[0, :, 0:HEADW] = dext_s[eslot].astype(BF16)
        dproj_ref[0, :, HEADW:] = dgate_s[gslot]

    @pl.when((step == pl.num_programs(0) - 1) & (z > 0))
    def _():
        @pl.loop(0, heads)
        def _(h):
            hop(h).wait_send()
            halo_hop(h).wait_send()


def forward_core(raw, convw, ab, gain, heads, parts):
    length = raw.shape[1] - HALO
    size = min(CHUNK, length)
    chunks = length // size
    per = heads // raw.shape[0]
    lag = parts - 1
    slots = lag + 1
    now = lambda s: jnp.minimum(s, heads - 1)
    late = lambda s: jnp.maximum(s - lag, 0)
    return pl.pallas_call(
        partial(forward_kernel, heads, parts),
        grid=(heads + lag,),
        out_shape=(
            jax.ShapeDtypeStruct((raw.shape[0], length, per * DV), BF16),
            jax.ShapeDtypeStruct((heads, length, DV), F32),
            jax.ShapeDtypeStruct((heads, chunks, DK, DV), F32),
            jax.ShapeDtypeStruct((heads, chunks, size, size), F32),
            jax.ShapeDtypeStruct((heads, length, DK), F32),
            jax.ShapeDtypeStruct((heads, chunks, DK, DK), F32),
            jax.ShapeDtypeStruct((heads, DK, DK), F32),
        ),
        in_specs=[
            pl.BlockSpec((1, length + HALO, HEADW + DV), lambda s: (now(s) // per, 0, now(s) % per)),
            pl.BlockSpec((1, length + HALO, DV), lambda s: (late(s) // per, 0, (late(s) % per) * 3 + 2)),
            pl.BlockSpec((1, TAPS, HEADW), lambda s: (now(s), 0, 0)),
            pl.BlockSpec((1, 8, length), lambda s: (now(s), 0, 0)),
            pl.BlockSpec((1, DV), lambda s: (0, 0)),
        ],
        out_specs=(
            pl.BlockSpec((1, length, DV), lambda s: (late(s) // per, 0, late(s) % per)),
            pl.BlockSpec((1, length, DV), lambda s: (late(s), 0, 0)),
            pl.BlockSpec((1, chunks, DK, DV), lambda s: (late(s), 0, 0, 0)),
            pl.BlockSpec((1, chunks, size, size), lambda s: (now(s), 0, 0, 0)),
            pl.BlockSpec((1, length, DK), lambda s: (now(s), 0, 0)),
            pl.BlockSpec((1, chunks, DK, DK), lambda s: (now(s), 0, 0, 0)),
            pl.BlockSpec((1, DK, DK), lambda s: (now(s), 0, 0)),
        ),
        scratch_shapes=[
            pltpu.VMEM((slots, length, DK), F32),
            pltpu.VMEM((slots, length, DV), F32),
            pltpu.VMEM((slots, chunks, DK, DK), F32),
            pltpu.VMEM((slots, chunks, DK, DV), F32),
            pltpu.VMEM((slots, DK, DK), F32),
            pltpu.VMEM((slots, DK, DV), F32),
            pltpu.VMEM((heads, DK, DV), F32),
            pltpu.VMEM((heads, DK, DV), F32),
            pltpu.SemaphoreType.DMA((heads,)),
            pltpu.SemaphoreType.DMA((heads,)),
        ],
        compiler_params=pltpu.CompilerParams(
            collective_id=0, has_side_effects=True, vmem_limit_bytes=56 * 2**20
        ),
        cost_estimate=pl.CostEstimate(flops=20 * 10**9, bytes_accessed=40 * 2**20, transcendentals=0),
        name="delta_forward",
    )(raw, raw, convw, ab, gain)


def backward_core(d_head, out, raw, query_e, phi, phi_all, convw, ab, gain, states, inverses, heads, parts):
    length = raw.shape[1] - HALO
    size = min(CHUNK, length)
    chunks = length // size
    per = heads // raw.shape[0]
    lag = parts - 1
    slots = lag + 1
    now = lambda s: jnp.minimum(s, heads - 1)
    late = lambda s: jnp.clip(s - lag, 0, heads - 1)
    later = lambda s: jnp.maximum(s - lag - 1, 0)
    return pl.pallas_call(
        partial(backward_kernel, heads, parts),
        grid=(heads + lag + 1,),
        out_shape=(
            jax.ShapeDtypeStruct((raw.shape[0], length, per * (HEADW + DV)), BF16),
            jax.ShapeDtypeStruct((heads, 8, length), F32),
            jax.ShapeDtypeStruct((heads, TAPS, HEADW), F32),
            jax.ShapeDtypeStruct((1, DV), F32),
        ),
        in_specs=[
            pl.BlockSpec((1, length, DV), lambda s: (now(s) // per, 0, now(s) % per)),
            pl.BlockSpec((1, length, DV), lambda s: (now(s), 0, 0)),
            pl.BlockSpec((1, length + HALO, DV), lambda s: (now(s) // per, 0, (now(s) % per) * 3 + 2)),
            pl.BlockSpec((1, length, DK), lambda s: (now(s), 0, 0)),
            pl.BlockSpec((1, chunks, DK, DK), lambda s: (now(s), 0, 0, 0)),
            pl.BlockSpec((1, DK, DK), lambda s: (now(s), 0, 0)),
            pl.BlockSpec((1, length + HALO, HEADW + DV), lambda s: (late(s) // per, 0, late(s) % per)),
            pl.BlockSpec((1, TAPS, HEADW), lambda s: (late(s), 0, 0)),
            pl.BlockSpec((1, 8, length), lambda s: (late(s), 0, 0)),
            pl.BlockSpec((1, DV), lambda s: (0, 0)),
            pl.BlockSpec((1, chunks, DK, DV), lambda s: (late(s), 0, 0, 0)),
            pl.BlockSpec((1, chunks, size, size), lambda s: (late(s), 0, 0, 0)),
            pl.BlockSpec((1, chunks, DK, DK), lambda s: (late(s), 0, 0, 0)),
        ],
        out_specs=(
            pl.BlockSpec((1, length, HEADW + DV), lambda s: (later(s) // per, 0, later(s) % per)),
            pl.BlockSpec((1, 8, length), lambda s: (late(s), 0, 0)),
            pl.BlockSpec((1, TAPS, HEADW), lambda s: (late(s), 0, 0)),
            pl.BlockSpec((1, DV), lambda s: (0, 0)),
        ),
        scratch_shapes=[
            pltpu.VMEM((slots, length, DV), F32),
            pltpu.VMEM((slots, chunks, DK, DV), F32),
            pltpu.VMEM((slots + 1, length, DV), BF16),
            pltpu.VMEM((slots, DK, DV), F32),
            pltpu.VMEM((slots, DK, DK), F32),
            pltpu.VMEM((length + 2 * HALO, HEADW), F32),
            pltpu.VMEM((2, length, HEADW), F32),
            pltpu.VMEM((heads, DK, DV), F32),
            pltpu.VMEM((heads, DK, DV), F32),
            pltpu.VMEM((heads, HALO, HEADW), F32),
            pltpu.VMEM((heads, HALO, HEADW), F32),
            pltpu.SemaphoreType.DMA((heads,)),
            pltpu.SemaphoreType.DMA((heads,)),
            pltpu.SemaphoreType.DMA((heads,)),
            pltpu.SemaphoreType.DMA((heads,)),
        ],
        compiler_params=pltpu.CompilerParams(
            collective_id=1, has_side_effects=True, vmem_limit_bytes=56 * 2**20
        ),
        cost_estimate=pl.CostEstimate(flops=40 * 10**9, bytes_accessed=60 * 2**20, transcendentals=0),
        name="delta_backward",
    )(d_head, out, raw, query_e, phi, phi_all, raw, convw, ab, gain, states, inverses, phi)


def scatter_kernel(bits, parts, plan, rows, length, lhs_ref, *refs):
    count = len(plan)
    sources = len({seg for seg, _, _ in plan})
    rhs_refs = refs[:sources]
    out_ref = refs[sources]
    rhs_s, grad_s, r1, *rest = refs[sources + 1 :]
    planes = bits - 1
    ra = rest[:planes]
    rb = rest[planes : 2 * planes]
    r4, load_sem, send1, recv1, send_a, recv_a, send_b, recv_b, send4, recv4 = rest[2 * planes :]
    d = lax.axis_index("dp")
    z = lax.axis_index("mp")
    half = 2 ** (bits - 1)
    mesh_id = pl.DeviceIdType.MESH

    def bit(b):
        return lax.rem(lax.div(d, 2**b), 2)

    def partner(b):
        return d + (1 - 2 * bit(b)) * 2**b

    barrier = pltpu.get_barrier_semaphore()
    for b in range(bits):
        pl.semaphore_signal(barrier, inc=1, device_id={"dp": partner(b)}, device_id_type=mesh_id)
    for delta in range(1, parts):
        pl.semaphore_signal(
            barrier, inc=1, device_id={"mp": lax.rem(z + delta, parts)}, device_id_type=mesh_id
        )
    pl.semaphore_wait(barrier, bits + parts - 1)

    def by_segment(t, act):
        for seg in range(sources):
            at = [k for k, item in enumerate(plan) if item[0] == seg]

            @pl.when((t >= at[0]) & (t <= at[-1]))
            def _():
                act(seg, plan[at[0]][1], t - at[0])

    def load(t):
        def act(seg, lhs_index, piece):
            pltpu.make_async_copy(
                rhs_refs[seg].at[:, :, pl.ds(pl.multiple_of(piece * WIDE, WIDE), WIDE)],
                rhs_s.at[lax.rem(t, 2)],
                load_sem.at[lax.rem(t, 2)],
            ).start()

        by_segment(t, act)

    def load_wait(t):
        slot = lax.rem(t, 2)
        pltpu.make_async_copy(
            rhs_refs[0].at[:, :, pl.ds(0, WIDE)], rhs_s.at[slot], load_sem.at[slot]
        ).wait()

    def first_hop(t):
        slot = lax.rem(t, 2)
        return pltpu.make_async_remote_copy(
            src_ref=grad_s.at[slot, :, :, 1 - bit(0)], dst_ref=r1.at[t], send_sem=send1.at[t],
            recv_sem=recv1.at[t], device_id={"dp": partner(0)}, device_id_type=mesh_id,
        )

    def a_hop(k, t):
        b = bits - 1 - k
        keep = half >> (k + 1)
        away = pl.ds((1 - bit(b)) * keep, keep)
        if k == 0:
            src = r1.at[t, :, away, :, 0 : WIDE // 2]
        else:
            src = ra[k - 1].at[t, :, away]
        return pltpu.make_async_remote_copy(
            src_ref=src, dst_ref=ra[k].at[t], send_sem=send_a.at[k, t], recv_sem=recv_a.at[k, t],
            device_id={"dp": partner(b)}, device_id_type=mesh_id,
        )

    def b_hops(k, t):
        b = 1 + k
        keep = half >> (k + 1)
        copies = []
        for hi in range(keep):
            away = 2 * hi + 1 - bit(b)
            if k == 0:
                src = r1.at[t, :, away, :, WIDE // 2 :]
            else:
                src = rb[k - 1].at[t, :, away]
            copies.append(
                pltpu.make_async_remote_copy(
                    src_ref=src, dst_ref=rb[k].at[t, :, hi], send_sem=send_b.at[k, t],
                    recv_sem=recv_b.at[k, t], device_id={"dp": partner(b)}, device_id_type=mesh_id,
                )
            )
        return copies

    def b_whole(k, t):
        return pltpu.make_async_remote_copy(
            src_ref=rb[k].at[t], dst_ref=rb[k].at[t], send_sem=send_b.at[k, t],
            recv_sem=recv_b.at[k, t], device_id={"dp": partner(1 + k)}, device_id_type=mesh_id,
        )

    def z_hops(t):
        copies = []
        for delta in range(1, parts):
            to = lax.rem(z + delta, parts)
            for side, buf in enumerate((ra[planes - 1], rb[planes - 1])):
                copies.append(
                    pltpu.make_async_remote_copy(
                        src_ref=buf.at[t, to, 0],
                        dst_ref=r4.at[t, parts - 1 - delta, :, side * (WIDE // 2) : (side + 1) * (WIDE // 2)],
                        send_sem=send4.at[t], recv_sem=recv4.at[t], device_id={"mp": to},
                        device_id_type=mesh_id,
                    )
                )
        return copies

    def z_whole(t):
        return pltpu.make_async_remote_copy(
            src_ref=r4.at[t], dst_ref=r4.at[t], send_sem=send4.at[t], recv_sem=recv4.at[t],
            device_id={"mp": lax.rem(z + 1, parts)}, device_id_type=mesh_id,
        )

    load(0)

    @pl.loop(0, count + planes + 2)
    def _(tick):
        t = tick - planes - 2

        @pl.when(t >= 0)
        def _():
            z_whole(t).wait_recv()
            side = WIDE // 2
            left = ra[planes - 1][t, z, 0].astype(F32)
            right = rb[planes - 1][t, z, 0].astype(F32)
            for s in range(parts - 1):
                left = left + r4[t, s, :, 0:side].astype(F32)
                right = right + r4[t, s, :, side:].astype(F32)
            out_ref[t, :, 0:side] = left
            out_ref[t, :, side:] = right

        for k in range(planes - 1, -1, -1):
            t_k = tick - k - 2

            @pl.when((t_k >= 0) & (t_k < count))
            def _():
                a_hop(k, t_k).wait_recv()
                b_whole(k, t_k).wait_recv()
                keep = half >> (k + 1)
                bit_a, bit_b = bit(bits - 1 - k), bit(1 + k)
                for m in range(keep):
                    own_a, own_b = bit_a * keep + m, 2 * m + bit_b
                    for j in range(parts):
                        if k == 0:
                            mine_a = r1[t_k, j, own_a, :, 0 : WIDE // 2]
                            mine_b = r1[t_k, j, own_b, :, WIDE // 2 :]
                        else:
                            mine_a = ra[k - 1][t_k, j, own_a]
                            mine_b = rb[k - 1][t_k, j, own_b]
                        ra[k][t_k, j, m] = (ra[k][t_k, j, m].astype(F32) + mine_a.astype(F32)).astype(BF16)
                        rb[k][t_k, j, m] = (rb[k][t_k, j, m].astype(F32) + mine_b.astype(F32)).astype(BF16)
                if k + 1 < planes:
                    a_hop(k + 1, t_k).start()
                    for copy in b_hops(k + 1, t_k):
                        copy.start()
                else:
                    for copy in z_hops(t_k):
                        copy.start()

        t_1 = tick - 1

        @pl.when((t_1 >= 0) & (t_1 < count))
        def _():
            first_hop(t_1).wait_recv()
            slot = lax.rem(t_1, 2)
            color = bit(0)

            @pl.loop(0, parts)
            def _(j):
                for m in range(half):
                    r1[t_1, j, m] = (
                        r1[t_1, j, m].astype(F32) + grad_s[slot, j, m, color].astype(F32)
                    ).astype(BF16)

            a_hop(0, t_1).start()
            for copy in b_hops(0, t_1):
                copy.start()

        @pl.when(tick < count)
        def _():
            slot = lax.rem(tick, 2)

            @pl.when(tick + 1 < count)
            def _():
                load(tick + 1)

            load_wait(tick)

            @pl.when(tick >= 2)
            def _():
                first_hop(tick - 2).wait_send()

            lhs_index = 0
            for k, item in enumerate(plan):
                lhs_index = jnp.where(tick == k, item[1], lhs_index)

            @pl.loop(0, parts)
            def _(j):
                full = jnp.dot(lhs_ref[lhs_index], rhs_s[slot, j], preferred_element_type=F32)
                grad_s[slot, j] = full.astype(BF16).reshape(half, 2, rows, WIDE)

            first_hop(tick).start()

    for t in range(max(count - 2, 0), count):
        first_hop(t).wait_send()

    @pl.loop(0, count)
    def _(t):
        for k in range(planes):
            a_hop(k, t).wait_send()
            b_whole(k, t).wait_send()
        z_whole(t).wait_send()


def scatter_sum(lefts, pairs, groups, parts, collective):
    kinds, width, length = lefts.shape
    bits = groups.bit_length() - 1
    rows = width // groups
    planes = bits - 1
    half = groups // 2
    plan = []
    for seg, (kind, right) in enumerate(pairs):
        plan += [(seg, kind, p) for p in range(right.shape[2] // WIDE)]
    count = len(plan)
    vmem = lambda *shape: pltpu.VMEM(shape, BF16)
    dma = lambda *shape: pltpu.SemaphoreType.DMA(shape)
    return pl.pallas_call(
        partial(scatter_kernel, bits, parts, plan, rows, length),
        out_shape=jax.ShapeDtypeStruct((count, rows, WIDE), F32),
        in_specs=[pl.BlockSpec(memory_space=pltpu.VMEM)] + [pl.BlockSpec(memory_space=pl.ANY)] * len(pairs),
        out_specs=pl.BlockSpec(memory_space=pltpu.VMEM),
        scratch_shapes=[
            vmem(2, parts, length, WIDE),
            vmem(2, parts, half, 2, rows, WIDE),
            vmem(count, parts, half, rows, WIDE),
            *[vmem(count, parts, half >> (k + 1), rows, WIDE // 2) for k in range(planes)],
            *[vmem(count, parts, half >> (k + 1), rows, WIDE // 2) for k in range(planes)],
            vmem(count, parts - 1, rows, WIDE),
            dma(2),
            dma(count), dma(count),
            dma(planes, count), dma(planes, count),
            dma(planes, count), dma(planes, count),
            dma(count), dma(count),
        ],
        compiler_params=pltpu.CompilerParams(
            collective_id=collective, has_side_effects=True, vmem_limit_bytes=60 * 2**20
        ),
        cost_estimate=pl.CostEstimate(
            flops=2 * count * WIDE * parts * length * width, bytes_accessed=count * parts * length * WIDE * 2,
            transcendentals=0,
        ),
        name="scatter_sum",
    )(lefts, *[right for _, right in pairs])


def dot(spec, a, b):
    return jnp.einsum(spec, a, b, preferred_element_type=F32)


def unit_rms(v):
    return lax.rsqrt(jnp.mean(v * v, axis=-1, keepdims=True) + 1e-05)


def per_device(
    tokens, out_grad, seq_lengths, mix_gain, w_query, w_key, w_value, w_outgate, w_decay, w_beta,
    conv_weight, rate_log, step_bias, head_gain, w_out, ffn_gain, w_ffn_gate, w_ffn_up, w_ffn_down,
):
    groups = lax.axis_size("dp")
    parts = lax.axis_size("mp")
    group = lax.axis_index("dp")
    share = lax.axis_index("mp")
    heads = rate_log.shape[0]
    per = heads // parts
    width = tokens.shape[2]
    local_rows = w_query.shape[0]

    x_bf = lax.all_to_all(tokens, "dp", split_axis=0, concat_axis=1, tiled=True)[0]
    dy_bf = lax.all_to_all(out_grad, "dp", split_axis=0, concat_axis=1, tiled=True)[0]
    length = x_bf.shape[0]
    before = lax.ppermute(x_bf[length - HALO :], "mp", [(i, i + 1) for i in range(parts - 1)])

    def by_head(w, size):
        return w.reshape(local_rows, per, size)

    joined = jnp.concatenate(
        [by_head(w_query, DK), by_head(w_key, DK), by_head(w_value, DV), by_head(w_outgate, DV)], axis=2
    ).reshape(local_rows, per * (HEADW + DV))
    main_cols = joined.shape[1]

    def gathered(w):
        whole = lax.all_gather(w, ("mp", "dp"), axis=0, tiled=True)
        return whole.reshape(parts, groups * local_rows, w.shape[1])

    g_proj = gathered(joined)
    g_small = gathered(jnp.concatenate([w_decay, w_beta], axis=1))
    g_out = gathered(w_out)
    g_gate = gathered(w_ffn_gate)
    g_up = gathered(w_ffn_up)
    g_down = gathered(w_ffn_down)

    my_length = lax.dynamic_slice_in_dim(seq_lengths, group, 1)
    positions = share * length + jnp.arange(length, dtype=jnp.int32)
    live = (positions < my_length).astype(F32)[:, None]

    x = x_bf.astype(F32)
    dy = live * dy_bf.astype(F32)
    d_ffo = dy.astype(BF16)
    ext = jnp.concatenate([before, x_bf], axis=0).astype(F32)
    h1_ext = (ext * unit_rms(ext) * mix_gain).astype(BF16)
    raw = dot("td,gdc->gtc", h1_ext, g_proj)
    h1 = h1_ext[HALO:]
    small = dot("td,gdc->gct", h1, g_small)
    decay_raw = small[:, :per].reshape(heads, length)
    beta_raw = small[:, per:].reshape(heads, length)
    rate = -jnp.exp(rate_log)[:, None]
    shifted = decay_raw + step_bias[:, None]
    decay = rate * jax.nn.softplus(shifted)
    beta = jax.nn.sigmoid(beta_raw)
    ab = jnp.concatenate(
        [decay[:, None], beta[:, None], jnp.zeros((heads, 6, length), F32)], axis=1
    )
    taps = conv_weight.shape[0]
    key_cols = heads * DK
    convw = jnp.concatenate(
        [
            conv_weight[:, :key_cols].reshape(taps, heads, DK),
            conv_weight[:, key_cols : 2 * key_cols].reshape(taps, heads, DK),
            conv_weight[:, 2 * key_cols :].reshape(taps, heads, DV),
        ],
        axis=2,
    ).transpose(1, 0, 2)
    gain_row = head_gain[None]
    head_out, mixed, states, inverses, query_e, phi, phi_all = forward_core(
        raw, convw, ab, gain_row, heads, parts
    )

    x1 = x + dot("gtc,gmc->tm", head_out, g_out)
    scale2 = unit_rms(x1)
    n2 = x1 * scale2
    h2 = (n2 * ffn_gain).astype(BF16)
    gate = dot("td,gdf->gtf", h2, g_gate)
    up = dot("td,gdf->gtf", h2, g_up)
    sig = jax.nn.sigmoid(gate)
    act = (gate * sig * up).astype(BF16)
    block_out = (live * (x1 + dot("gtf,gdf->td", act, g_down))).astype(BF16)
    d_act = dot("td,gdf->gtf", d_ffo, g_down)
    d_gate = (d_act * up * sig * (1.0 + gate * (1.0 - sig))).astype(BF16)
    d_up = (d_act * gate * sig).astype(BF16)
    d_h2 = dot("gtf,gdf->td", d_gate, g_gate) + dot("gtf,gdf->td", d_up, g_up)
    e2 = d_h2 * ffn_gain
    d_x1 = dy + scale2 * (e2 - n2 * jnp.mean(e2 * n2, axis=-1, keepdims=True))
    ffn_gain_grad = jnp.sum(d_h2 * n2, axis=0)
    d_mix = d_x1.astype(BF16)
    d_head = dot("tm,gmc->gtc", d_mix, g_out)

    d_proj, d_ab, d_convw, d_head_gain = backward_core(
        d_head, mixed, raw, query_e, phi, phi_all, convw, ab, gain_row, states, inverses, heads, parts
    )
    d_decay = d_ab[:, 0]
    d_beta_raw = d_ab[:, 1] * beta * (1.0 - beta)
    d_decay_raw = d_decay * rate * jax.nn.sigmoid(shifted)
    rate_grad = jnp.sum(d_decay * decay, axis=1)
    bias_grad = jnp.sum(d_decay_raw, axis=1)
    d_small = jnp.concatenate(
        [d_decay_raw.reshape(parts, per, length), d_beta_raw.reshape(parts, per, length)], axis=1
    ).astype(BF16)
    hidden = act.shape[2]
    wide = -(-hidden // WIDE) * WIDE
    padded = lambda v: jnp.pad(v, ((0, 0), (0, 0), (0, wide - hidden)))
    lefts = jnp.stack([h1.T, d_mix.T, h2.T, d_ffo.T])
    sums_w = scatter_sum(
        lefts,
        [(3, padded(act)), (2, padded(d_gate)), (2, padded(d_up)), (1, head_out), (0, d_proj)],
        groups, parts, 2,
    )

    def columns(start, size):
        pieces = -(-size // WIDE)
        return sums_w[start : start + pieces].transpose(1, 0, 2).reshape(local_rows, -1)[:, :size]

    step = wide // WIDE
    s_down = columns(0, hidden)
    s_gate = columns(step, hidden)
    s_up = columns(2 * step, hidden)
    s_out = columns(3 * step, per * DV)
    s_proj = columns(3 * step + per * DV // WIDE, main_cols)
    small_grad = dot("gct,td->gcd", d_small, h1)
    d_h1 = dot("gtc,gdc->td", d_proj, g_proj) + dot("gct,gdc->td", d_small, g_small)
    scale1 = unit_rms(x)
    n1 = x * scale1
    e1 = d_h1 * mix_gain
    d_x = d_x1 + scale1 * (e1 - n1 * jnp.mean(e1 * n1, axis=-1, keepdims=True))
    mix_gain_grad = jnp.sum(d_h1 * n1, axis=0)
    per_head = d_convw.transpose(1, 0, 2)
    d_conv = jnp.concatenate(
        [
            per_head[:, :, :DK].reshape(taps, key_cols),
            per_head[:, :, DK : 2 * DK].reshape(taps, key_cols),
            per_head[:, :, 2 * DK :].reshape(taps, heads * DV),
        ],
        axis=1,
    )
    sums = lax.psum(
        jnp.concatenate(
            [mix_gain_grad, ffn_gain_grad, d_head_gain[0], d_conv.reshape(-1), rate_grad, bias_grad,
             small_grad.reshape(-1)]
        ),
        ("dp", "mp"),
    )
    pieces = []
    start = 0
    for count in (width, width, DV, taps * conv_weight.shape[1], heads, heads):
        pieces.append(sums[start : start + count])
        start += count
    small_sum = sums[start:].reshape(parts, 2 * per, width)
    mine = lax.dynamic_slice(small_sum, (share, 0, group * local_rows), (1, 2 * per, local_rows))[0].T

    by = s_proj.reshape(local_rows, per, HEADW + DV)
    flat = lambda v: v.reshape(local_rows, -1)
    final_out = lax.all_to_all(block_out[None], "dp", split_axis=1, concat_axis=0, tiled=True)
    final_grad = lax.all_to_all(d_x.astype(BF16)[None], "dp", split_axis=1, concat_axis=0, tiled=True)
    return (
        final_out,
        final_grad,
        pieces[0],
        flat(by[:, :, :DK]),
        flat(by[:, :, DK : 2 * DK]),
        flat(by[:, :, 2 * DK : HEADW]),
        flat(by[:, :, HEADW:]),
        mine[:, :per],
        mine[:, per:],
        pieces[3].reshape(conv_weight.shape),
        pieces[4],
        pieces[5],
        pieces[2],
        s_out,
        pieces[1],
        s_gate,
        s_up,
        s_down,
    )


def solution(mesh):
    seq = P(None, ("mp", "dp"), None)
    shard = P("dp", "mp")
    rep = P()
    return jax.shard_map(
        per_device,
        mesh=mesh,
        in_specs=(
            seq, seq, rep, rep, shard, shard, shard, shard, shard, shard,
            rep, rep, rep, rep, shard, rep, shard, shard, shard,
        ),
        out_specs=(
            seq, seq, rep, shard, shard, shard, shard, shard, shard,
            rep, rep, rep, rep, shard, rep, shard, shard, shard,
        ),
        check_vma=False,
    )
```

```python
from functools import partial

import jax
import jax.numpy as jnp
from jax import lax
from jax.experimental import pallas as pl
from jax.experimental.pallas import tpu as pltpu
from jax.sharding import PartitionSpec as P

DK = 128
DV = 256
HEADW = 2 * DK + DV
TAPS = 4
CHUNK = 128
HALO = 8
WIDE = 256
STRIDE = 2
F32 = jnp.float32
BF16 = jnp.bfloat16


def halves(a):
    high = a.astype(BF16)
    return high, (a - high.astype(F32)).astype(BF16)


def mm(a, b, ca=1, cb=0):
    dims = (((ca,), (cb,)), ((), ()))
    a_high, a_low = halves(a)
    b_high, b_low = halves(b)
    one = lambda p, q: lax.dot_general(p, q, dims, preferred_element_type=F32)
    return one(a_high, b_high) + (one(a_high, b_low) + one(a_low, b_high))


def windows(raw_ref, ext_s, c, size):
    if c == 0:
        return [ext_s[pl.ds(HALO - TAPS + 1 + i, size)] for i in range(TAPS)]
    return [raw_ref[0, pl.ds(c * size - TAPS + 1 + i, size), 0:HEADW] for i in range(TAPS)]


def conv_of(shifted, convw):
    total = None
    for i in range(TAPS):
        part = shifted[i] * convw[i : i + 1]
        total = part if total is None else total + part
    return total


def decays(ab_ref, base, rows, upper):
    ab = ab_ref[0, :, pl.ds(base, rows)]
    cum = mm(ab, upper)
    row_id = lax.broadcasted_iota(jnp.int32, ab.shape, 0)
    both = jnp.where(row_id == 0, cum, ab)
    cols = both.T
    return both[0:1], cols[:, 0:1], cols[:, 1:2]


def masks(size):
    rows = lax.broadcasted_iota(jnp.int32, (size, size), 0)
    cols = lax.broadcasted_iota(jnp.int32, (size, size), 1)
    return rows, cols


def fades(gamma_row, gamma_col, rows, cols):
    spread = jnp.minimum(gamma_col - gamma_row, 0.0)
    inclusive = jnp.where(rows >= cols, jnp.exp(spread), 0.0)
    strict = jnp.where(rows > cols, inclusive, 0.0)
    return inclusive, strict


def invert_many(lowers, rows, cols):
    size = lowers[0].shape[0]
    eye = (rows == cols).astype(F32)
    pair = ((rows // 2) == (cols // 2)) & (rows > cols)
    inverses = [eye - jnp.where(pair, low, 0.0) for low in lowers]
    width = 2
    while width < size:
        within = (rows // (2 * width)) == (cols // (2 * width))
        cross = within & ((rows // width) != (cols // width)) & (rows > cols)
        inner = [mm(jnp.where(cross, low, 0.0), inv) for low, inv in zip(lowers, inverses)]
        inverses = [inv - mm(inv, part) for inv, part in zip(inverses, inner)]
        width *= 2
    return inverses


def unit_parts(conv):
    sig = jax.nn.sigmoid(conv)
    silu = conv * sig
    q_silu = silu[:, :DK]
    k_silu = silu[:, DK : 2 * DK]
    value = silu[:, 2 * DK :]
    q_scale = lax.rsqrt(jnp.sum(q_silu * q_silu, axis=-1, keepdims=True) + 1e-06)
    k_scale = lax.rsqrt(jnp.sum(k_silu * k_silu, axis=-1, keepdims=True) + 1e-06)
    return sig, q_silu, k_silu, value, q_scale, k_scale


class Gather:
    def __init__(self, bits, parts, sources, targets, pieces, sems):
        self.bits, self.parts, self.pieces = bits, parts, pieces
        self.sources, self.targets = sources, targets
        (self.own, self.z_send, self.z_recv, self.p_send, self.p_recv, self.s_send, self.s_recv) = sems
        self.d, self.z = lax.axis_index("dp"), lax.axis_index("mp")
        self.orders = (list(range(1, bits)), list(range(bits - 1, 0, -1)))
        self.ticks = bits + 1

    @staticmethod
    def scratch(bits, count):
        dma = lambda *shape: pltpu.SemaphoreType.DMA(shape)
        return [
            dma(count), dma(count), dma(count), dma(count, bits - 1, 2), dma(count, bits - 1, 2),
            dma(count), dma(count),
        ]

    def flip(self, index, b):
        return index + (1 - 2 * lax.rem(lax.div(self.d, 2**b), 2)) * 2**b

    def copy(self, src, dst, send, recv, to):
        return pltpu.make_async_remote_copy(
            src_ref=src, dst_ref=dst, send_sem=send, recv_sem=recv, device_id=to,
            device_id_type=pl.DeviceIdType.MESH,
        )

    def sides(self, p):
        _, start, mid, stop = self.pieces[p]
        return [(0, start, mid)] + ([(1, mid, stop)] if mid < stop else [])

    def held(self, side, k):
        out = [self.d]
        for b in self.orders[side][:k]:
            out = out + [self.flip(i, b) for i in out]
        return out

    def arrived(self, side, k):
        return [self.flip(i, self.orders[side][k]) for i in self.held(side, k)]

    def to_sibling(self, p, indices, start, stop):
        target = self.targets[self.pieces[p][0]]
        for i in indices:
            block = target.at[:, i, :, start:stop]
            self.copy(
                block, block, self.s_send.at[p], self.s_recv.at[p], {"dp": self.flip(self.d, 0)}
            ).start()

    def along(self, p, k, act):
        target = self.targets[self.pieces[p][0]]
        for side, start, stop in self.sides(p):
            b = self.orders[side][k]
            for i in self.held(side, k):
                block = target.at[:, i, :, start:stop]
                act(
                    self.copy(
                        block, block, self.p_send.at[p, k, side], self.p_recv.at[p, k, side],
                        {"dp": self.flip(self.d, b)},
                    )
                )

    def along_whole(self, p, k):
        target = self.targets[self.pieces[p][0]]
        out = []
        for side, start, stop in self.sides(p):
            block = target.at[:, pl.ds(0, 2**k), :, start:stop]
            out.append(
                self.copy(
                    block, block, self.p_send.at[p, k, side], self.p_recv.at[p, k, side],
                    {"dp": self.flip(self.d, self.orders[side][k])},
                )
            )
        return out

    def tick(self, p, stage):
        which, start, _, stop = self.pieces[p]
        source, target = self.sources[which], self.targets[which]
        if stage == 0:
            pltpu.make_async_copy(
                source.at[:, start:stop], target.at[self.z, self.d, :, start:stop], self.own.at[p]
            ).start()
            for delta in range(1, self.parts):
                self.copy(
                    source.at[:, start:stop], target.at[self.z, self.d, :, start:stop], self.z_send.at[p],
                    self.z_recv.at[p], {"mp": lax.rem(self.z + delta, self.parts)},
                ).start()
        elif stage == 1:
            pltpu.make_async_copy(
                source.at[:, start:stop], target.at[self.z, self.d, :, start:stop], self.own.at[p]
            ).wait()
            self.z_whole(p).wait_recv()
            self.along(p, 0, lambda copy: copy.start())
            self.to_sibling(p, [self.d], start, stop)
        elif stage <= self.bits:
            k = stage - 2
            for copy in self.along_whole(p, k):
                copy.wait_recv()
            if k + 1 < self.bits - 1:
                self.along(p, k + 1, lambda copy: copy.start())
            for side, low, high in self.sides(p):
                self.to_sibling(p, self.arrived(side, k), low, high)

    def moves(self):
        return len(self.pieces) + STRIDE * (self.ticks - 1)

    def move(self, now):
        for p in range(len(self.pieces)):
            if now >= p and (now - p) % STRIDE == 0 and (now - p) // STRIDE < self.ticks:
                self.tick(p, (now - p) // STRIDE)

    def z_whole(self, p):
        which, start, _, stop = self.pieces[p]
        block = self.targets[which].at[pl.ds(0, self.parts - 1), self.d, :, start:stop]
        return self.copy(
            block, block, self.z_send.at[p], self.z_recv.at[p],
            {"mp": lax.rem(self.z + 1, self.parts)},
        )

    def s_whole(self, p):
        which, start, _, stop = self.pieces[p]
        block = self.targets[which].at[:, pl.ds(0, 2 ** (self.bits - 1)), :, start:stop]
        return self.copy(
            block, block, self.s_send.at[p], self.s_recv.at[p], {"dp": self.flip(self.d, 0)}
        )

    def finish(self):
        for p in range(len(self.pieces)):
            self.s_whole(p).wait_recv()
            self.z_whole(p).wait_send()
            for k in range(self.bits - 1):
                for copy in self.along_whole(p, k):
                    copy.wait_send()
            self.s_whole(p).wait_send()


def greet_all(bits, parts, every):
    d, z = lax.axis_index("dp"), lax.axis_index("mp")
    barrier = pltpu.get_barrier_semaphore()
    if every:
        peers = [lax.rem(d + delta, 2**bits) for delta in range(1, 2**bits)]
    else:
        peers = [d + (1 - 2 * lax.rem(lax.div(d, 2**b), 2)) * 2**b for b in range(bits)]
    for peer in peers:
        pl.semaphore_signal(
            barrier, inc=1, device_id={"dp": peer}, device_id_type=pl.DeviceIdType.MESH
        )
    for delta in range(1, parts):
        pl.semaphore_signal(
            barrier, inc=1, device_id={"mp": lax.rem(z + delta, parts)},
            device_id_type=pl.DeviceIdType.MESH,
        )
    pl.semaphore_wait(barrier, len(peers) + parts - 1)


class Swap:
    def __init__(self, groups, source, target, own, send, recv):
        self.groups, self.source, self.target = groups, source, target
        self.own, self.send, self.recv = own, send, recv
        self.d = lax.axis_index("dp")

    def copy(self, src, dst, to):
        return pltpu.make_async_remote_copy(
            src_ref=src, dst_ref=dst, send_sem=self.send, recv_sem=self.recv, device_id={"dp": to},
            device_id_type=pl.DeviceIdType.MESH,
        )

    def local(self):
        return pltpu.make_async_copy(self.source.at[self.d], self.target.at[self.d], self.own)

    def start(self):
        self.local().start()
        for delta in range(1, self.groups):
            to = lax.rem(self.d + delta, self.groups)
            self.copy(self.source.at[to], self.target.at[self.d], to).start()

    def finish(self):
        self.local().wait()
        block = self.target.at[pl.ds(0, self.groups - 1)]
        whole = self.copy(block, block, lax.rem(self.d + 1, self.groups))
        whole.wait_recv()
        whole.wait_send()


def prologue_kernel(bits, parts, pieces, *refs):
    tokens, grads, joined, small, tokens_out, grads_out, joined_out, small_out = refs[:8]
    sems = refs[8:]
    gather = Gather(bits, parts, (joined, small), (joined_out, small_out), pieces, sems[:7])
    swaps = [
        Swap(2**bits, tokens, tokens_out, *[s.at[0] for s in sems[7:10]]),
        Swap(2**bits, grads, grads_out, *[s.at[1] for s in sems[7:10]]),
    ]
    greet_all(bits, parts, True)
    swaps[0].start()
    count = len(pieces)
    for now in range(gather.moves()):
        gather.move(now)
        if now == count - 1:
            swaps[1].start()
    gather.finish()
    for swap in swaps:
        swap.finish()


def prologue(tokens, grads, joined, small, groups, parts):
    bits = groups.bit_length() - 1
    rows, wide = joined.shape
    third = wide // 4
    pieces = [(1, 0, small.shape[1], small.shape[1])]
    pieces += [(0, 0, third, 2 * third), (0, 2 * third, 3 * third, wide)]
    swapped = jax.ShapeDtypeStruct(tokens.shape, BF16)
    any_spec = pl.BlockSpec(memory_space=pl.ANY)
    return pl.pallas_call(
        partial(prologue_kernel, bits, parts, pieces),
        out_shape=(
            swapped,
            swapped,
            jax.ShapeDtypeStruct((parts, groups, rows, wide), BF16),
            jax.ShapeDtypeStruct((parts, groups, rows, small.shape[1]), BF16),
        ),
        in_specs=[any_spec] * 4,
        out_specs=(any_spec,) * 4,
        scratch_shapes=Gather.scratch(bits, len(pieces)) + [pltpu.SemaphoreType.DMA((2,))] * 3,
        compiler_params=pltpu.CompilerParams(collective_id=3, has_side_effects=True),
        cost_estimate=pl.CostEstimate(flops=0, bytes_accessed=40 * 2**20, transcendentals=0),
        name="prologue",
    )(tokens, grads, joined, small)


def forward_kernel(
    heads, parts, bits, pieces,
    raw_ref, gate_ref, raw_any, convw_ref, ab_ref, gain_ref, *refs,
):
    weights = len({item[0] for item in pieces})
    sources, refs = refs[:weights], refs[weights:]
    head_ref, o_ref, s_ref, t_ref, qe_ref, phi_ref, phil_ref, halo_ref = refs[:8]
    targets, refs = refs[8 : 8 + weights], refs[8 + weights :]
    (qe_s, o0_s, phi_s, b_s, phil_s, bl_s, send_s, recv_s, halo_s, ext_s,
     send_sem, recv_sem, halo_send_sem, halo_recv_sem) = refs[:14]
    gather = Gather(bits, parts, sources, targets, pieces, refs[14:])
    step = pl.program_id(0)
    early = pl.program_id(1) == 0
    z = lax.axis_index("mp")
    lag = parts - 1
    slots = lag + 1
    length = gate_ref.shape[1]
    size = min(CHUNK, length)
    chunks = length // size
    per = heads // parts

    @pl.when((step == 0) & early)
    def _():
        greet_all(bits, parts, False)

    last = 2 * (heads + lag) - 1
    for now in range(min(gather.moves(), last)):
        @pl.when(step * 2 + pl.program_id(1) == now)
        def _():
            gather.move(now)

    @pl.when(step * 2 + pl.program_id(1) == last)
    def _():
        for now in range(last, gather.moves()):
            gather.move(now)

    def hop(h):
        return pltpu.make_async_remote_copy(
            src_ref=send_s.at[h], dst_ref=recv_s.at[h], send_sem=send_sem.at[h],
            recv_sem=recv_sem.at[h], device_id={"mp": lax.rem(z + 1, parts)},
            device_id_type=pl.DeviceIdType.MESH,
        )

    def halo_hop(g):
        return pltpu.make_async_remote_copy(
            src_ref=raw_any.at[g, length - HALO :], dst_ref=halo_s.at[g], send_sem=halo_send_sem.at[g],
            recv_sem=halo_recv_sem.at[g], device_id={"mp": lax.rem(z + 1, parts)},
            device_id_type=pl.DeviceIdType.MESH,
        )

    @pl.when((step == 0) & early & (z == 0))
    def _():
        recv_s[...] = jnp.zeros_like(recv_s)
        halo_s[...] = jnp.zeros_like(halo_s)

    @pl.when((step == 0) & early & (z < parts - 1))
    def _():
        for g in range(parts):
            halo_hop(g).start()

    @pl.when((step < heads) & early)
    def _():
        slot = lax.rem(step, slots)
        part, sub = lax.div(step, per), lax.rem(step, per)

        @pl.when((sub == 0) & (z > 0))
        def _():
            halo_hop(part).wait_recv()

        for k in range(per):
            @pl.when(sub == k)
            def _():
                ext_s[0:HALO] = halo_s[part, :, k * (HEADW + DV) : k * (HEADW + DV) + HEADW]

        ext_s[HALO:] = raw_ref[0, 0:size, 0:HEADW]
        rows, cols = masks(size)
        upper = (rows <= cols).astype(F32)
        convw = convw_ref[0]
        kept = []
        lowers = []
        for c in range(chunks):
            conv = conv_of(windows(raw_ref, ext_s, c, size), convw)
            _, q_silu, k_silu, value, q_scale, k_scale = unit_parts(conv)
            query = q_silu * (q_scale * DK ** (-0.5))
            keyed = k_silu * k_scale
            gamma_row, gamma_col, beta = decays(ab_ref, c * size, size, upper)
            inclusive, strict = fades(gamma_row, gamma_col, rows, cols)
            gram = mm(jnp.concatenate([keyed, query], axis=0), keyed, 1, 1)
            lowers.append(beta * gram[:size] * strict)
            scores = gram[size:] * inclusive
            growth = jnp.exp(gamma_col)
            last = gamma_row[:, size - 1 :]
            rhs = jnp.concatenate([(beta * growth) * keyed, beta * value], axis=1)
            kept.append((scores, rhs, query * growth, keyed * jnp.exp(last - gamma_col), last))
        inverses = invert_many(lowers, rows, cols)
        eye = (masks(DK)[0] == masks(DK)[1]).astype(F32)
        phi_all = None
        b_all = None
        for c in range(chunks):
            scores, rhs, query_g, keyed_g, last = kept[c]
            t_ref[0, c] = inverses[c]
            solved = mm(inverses[c], rhs)
            mixed = mm(scores, solved)
            moved = mm(keyed_g, solved, 0, 0)
            query_e = query_g - mixed[:, :DK]
            phi = jnp.exp(last) * eye - moved[:, :DK]
            inflow = moved[:, DK:]
            qe_ref[0, c * size : (c + 1) * size] = query_e
            qe_s[slot, c * size : (c + 1) * size] = query_e
            o0_s[slot, c * size : (c + 1) * size] = mixed[:, DK:]
            phi_ref[0, c] = phi.T
            phi_s[slot, c] = phi
            b_s[slot, c] = inflow
            if c == 0:
                phi_all, b_all = phi, inflow
            else:
                moved_all = mm(phi, jnp.concatenate([phi_all, b_all], axis=1))
                phi_all = moved_all[:, :DK]
                b_all = moved_all[:, DK:] + inflow
        phil_ref[0] = phi_all.T
        phil_s[slot] = phi_all
        bl_s[slot] = b_all

    relay = step - z

    @pl.when((relay >= 0) & (relay < heads) & ~early)
    def _():
        slot = lax.rem(relay, slots)

        @pl.when(z > 0)
        def _():
            hop(relay).wait_recv()

        @pl.when(z < parts - 1)
        def _():
            send_s[relay] = mm(phil_s[slot], recv_s[relay]) + bl_s[slot]
            hop(relay).start()

    @pl.when((step >= lag) & ~early)
    def _():
        head = step - lag
        slot = lax.rem(head, slots)
        state = recv_s[head]
        for c in range(chunks):
            at = slice(c * size, (c + 1) * size)
            s_ref[0, c] = state
            result = mm(qe_s[slot, at], state) + o0_s[slot, at]
            if c + 1 < chunks:
                state = mm(phi_s[slot, c], state) + b_s[slot, c]
            o_ref[0, at] = result
            scale = lax.rsqrt(jnp.mean(result * result, axis=-1, keepdims=True) + 1e-05)
            gate = gate_ref[0, c * size : (c + 1) * size]
            gated = result * scale * gain_ref[...] * (gate * jax.nn.sigmoid(gate))
            head_ref[0, at] = gated.astype(BF16)

    @pl.when((step == pl.num_programs(0) - 1) & ~early & (z < parts - 1))
    def _():
        @pl.loop(0, heads)
        def _(h):
            hop(h).wait_send()

        for g in range(parts):
            halo_hop(g).wait_send()

    @pl.when((step == pl.num_programs(0) - 1) & ~early)
    def _():
        halo_ref[...] = halo_s[...]
        gather.finish()


class Scatter:
    def __init__(self, bits, parts, plan, rows, lhs_ref, rhs_refs, out_ref, scratch):
        self.bits, self.parts, self.plan, self.rows = bits, parts, plan, rows
        self.lhs_ref, self.rhs_refs, self.out_ref = lhs_ref, rhs_refs, out_ref
        self.count = len(plan)
        self.planes = planes = bits - 1
        self.half = 2 ** (bits - 1)
        self.lhs_s, self.rhs_s, self.grad_s, self.r1, *rest = scratch
        self.ra, self.rb = rest[:planes], rest[planes : 2 * planes]
        (self.r4, self.load_sem, self.send1, self.recv1, self.send_a, self.recv_a, self.send_b,
         self.recv_b, self.send4, self.recv4) = rest[2 * planes :]
        self.d, self.z = lax.axis_index("dp"), lax.axis_index("mp")
        self.ticks = self.count + STRIDE * (planes + 2)

    @staticmethod
    def scratch(bits, parts, count, rows, length, width):
        planes, half = bits - 1, 2 ** (bits - 1)
        vmem = lambda *shape: pltpu.VMEM(shape, BF16)
        dma = lambda *shape: pltpu.SemaphoreType.DMA(shape)
        strips = [vmem(count, parts, half >> (k + 1), rows, WIDE // 2) for k in range(planes)]
        return [
            vmem(2, width, length),
            vmem(2, parts, length, WIDE),
            vmem(2, parts, half, 2, rows, WIDE),
            vmem(count, parts, half, rows, WIDE),
            *strips, *strips,
            vmem(count, parts - 1, rows, WIDE),
            dma(2, 2),
            dma(count), dma(count),
            dma(planes, count), dma(planes, count),
            dma(planes, count), dma(planes, count),
            dma(count), dma(count),
        ]

    def bit(self, b):
        return lax.rem(lax.div(self.d, 2**b), 2)

    def partner(self, b):
        return self.d + (1 - 2 * self.bit(b)) * 2**b

    def remote(self, src, dst, send, recv, to):
        return pltpu.make_async_remote_copy(
            src_ref=src, dst_ref=dst, send_sem=send, recv_sem=recv, device_id=to,
            device_id_type=pl.DeviceIdType.MESH,
        )

    def load(self, t):
        slot = lax.rem(t, 2)
        for seg in range(len(self.rhs_refs)):
            at = [k for k, item in enumerate(self.plan) if item[0] == seg]

            @pl.when((t >= at[0]) & (t <= at[-1]))
            def _():
                start = pl.multiple_of((t - at[0]) * WIDE, WIDE)
                pltpu.make_async_copy(
                    self.rhs_refs[seg].at[:, :, pl.ds(start, WIDE)], self.rhs_s.at[slot],
                    self.load_sem.at[0, slot],
                ).start()
                pltpu.make_async_copy(
                    self.lhs_ref.at[self.plan[at[0]][1]], self.lhs_s.at[slot], self.load_sem.at[1, slot]
                ).start()

    def load_wait(self, t):
        slot = lax.rem(t, 2)
        pltpu.make_async_copy(
            self.rhs_refs[0].at[:, :, pl.ds(0, WIDE)], self.rhs_s.at[slot], self.load_sem.at[0, slot]
        ).wait()
        pltpu.make_async_copy(
            self.lhs_ref.at[0], self.lhs_s.at[slot], self.load_sem.at[1, slot]
        ).wait()

    def first_hop(self, t):
        return self.remote(
            self.grad_s.at[lax.rem(t, 2), :, :, 1 - self.bit(0)], self.r1.at[t], self.send1.at[t],
            self.recv1.at[t], {"dp": self.partner(0)},
        )

    def a_hop(self, k, t):
        b = self.bits - 1 - k
        keep = self.half >> (k + 1)
        away = pl.ds((1 - self.bit(b)) * keep, keep)
        src = self.r1.at[t, :, away, :, 0 : WIDE // 2] if k == 0 else self.ra[k - 1].at[t, :, away]
        return self.remote(
            src, self.ra[k].at[t], self.send_a.at[k, t], self.recv_a.at[k, t], {"dp": self.partner(b)}
        )

    def b_hops(self, k, t):
        b = 1 + k
        copies = []
        for hi in range(self.half >> (k + 1)):
            away = 2 * hi + 1 - self.bit(b)
            src = self.r1.at[t, :, away, :, WIDE // 2 :] if k == 0 else self.rb[k - 1].at[t, :, away]
            copies.append(
                self.remote(
                    src, self.rb[k].at[t, :, hi], self.send_b.at[k, t], self.recv_b.at[k, t],
                    {"dp": self.partner(b)},
                )
            )
        return copies

    def b_whole(self, k, t):
        return self.remote(
            self.rb[k].at[t], self.rb[k].at[t], self.send_b.at[k, t], self.recv_b.at[k, t],
            {"dp": self.partner(1 + k)},
        )

    def z_hops(self, t):
        copies = []
        side = WIDE // 2
        for delta in range(1, self.parts):
            to = lax.rem(self.z + delta, self.parts)
            for i, buf in enumerate((self.ra[self.planes - 1], self.rb[self.planes - 1])):
                copies.append(
                    self.remote(
                        buf.at[t, to, 0],
                        self.r4.at[t, self.parts - 1 - delta, :, i * side : (i + 1) * side],
                        self.send4.at[t], self.recv4.at[t], {"mp": to},
                    )
                )
        return copies

    def z_whole(self, t):
        return self.remote(
            self.r4.at[t], self.r4.at[t], self.send4.at[t], self.recv4.at[t],
            {"mp": lax.rem(self.z + 1, self.parts)},
        )

    def tick(self, tick):
        count, planes, half, parts = self.count, self.planes, self.half, self.parts
        side = WIDE // 2

        @pl.when(tick == 0)
        def _():
            self.load(tick)

        t = tick - STRIDE * (planes + 2)

        @pl.when((t >= 0) & (t < count))
        def _():
            self.z_whole(t).wait_recv()
            left = self.ra[planes - 1][t, self.z, 0].astype(F32)
            right = self.rb[planes - 1][t, self.z, 0].astype(F32)
            for s in range(parts - 1):
                left = left + self.r4[t, s, :, 0:side].astype(F32)
                right = right + self.r4[t, s, :, side:].astype(F32)
            self.out_ref[t, :, 0:side] = left
            self.out_ref[t, :, side:] = right

        for k in range(planes - 1, -1, -1):
            t_k = tick - STRIDE * (k + 2)

            @pl.when((t_k >= 0) & (t_k < count))
            def _():
                self.a_hop(k, t_k).wait_recv()
                self.b_whole(k, t_k).wait_recv()
                keep = half >> (k + 1)
                bit_a, bit_b = self.bit(self.bits - 1 - k), self.bit(1 + k)
                for m in range(keep):
                    own_a, own_b = bit_a * keep + m, 2 * m + bit_b
                    for j in range(parts):
                        if k == 0:
                            mine_a = self.r1[t_k, j, own_a, :, 0:side]
                            mine_b = self.r1[t_k, j, own_b, :, side:]
                        else:
                            mine_a = self.ra[k - 1][t_k, j, own_a]
                            mine_b = self.rb[k - 1][t_k, j, own_b]
                        for buf, mine in ((self.ra[k], mine_a), (self.rb[k], mine_b)):
                            buf[t_k, j, m] = (buf[t_k, j, m].astype(F32) + mine.astype(F32)).astype(BF16)
                if k + 1 < planes:
                    self.a_hop(k + 1, t_k).start()
                    for copy in self.b_hops(k + 1, t_k):
                        copy.start()
                else:
                    for copy in self.z_hops(t_k):
                        copy.start()

        t_1 = tick - STRIDE

        @pl.when((t_1 >= 0) & (t_1 < count))
        def _():
            self.first_hop(t_1).wait_recv()
            slot = lax.rem(t_1, 2)
            color = self.bit(0)

            @pl.loop(0, parts)
            def _(j):
                for m in range(half):
                    self.r1[t_1, j, m] = (
                        self.r1[t_1, j, m].astype(F32) + self.grad_s[slot, j, m, color].astype(F32)
                    ).astype(BF16)

            self.a_hop(0, t_1).start()
            for copy in self.b_hops(0, t_1):
                copy.start()

        @pl.when(tick < count)
        def _():
            slot = lax.rem(tick, 2)

            @pl.when(tick + 1 < count)
            def _():
                self.load(tick + 1)

            self.load_wait(tick)

            @pl.when(tick >= 2)
            def _():
                self.first_hop(tick - 2).wait_send()

            @pl.loop(0, parts)
            def _(j):
                full = jnp.dot(self.lhs_s[slot], self.rhs_s[slot, j], preferred_element_type=F32)
                self.grad_s[slot, j] = full.astype(BF16).reshape(half, 2, self.rows, WIDE)

            self.first_hop(tick).start()

    def finish(self):
        for t in range(max(self.count - 2, 0), self.count):
            self.first_hop(t).wait_send()

        @pl.loop(0, self.count)
        def _(t):
            for k in range(self.planes):
                self.a_hop(k, t).wait_send()
                self.b_whole(k, t).wait_send()
            self.z_whole(t).wait_send()


def plan_of(pairs):
    plan = []
    for seg, (kind, right) in enumerate(pairs):
        plan += [(seg, kind)] * (right.shape[2] // WIDE)
    return plan


def scatter_kernel(bits, parts, plan, rows, lhs_ref, *refs):
    sources = len({item[0] for item in plan})
    rhs_refs, refs = refs[:sources], refs[sources:]
    vec_ref, y_ref, g_ref, out_ref, vec_out, y_out, g_out = refs[:7]
    v_acc, v_in, v_z, v_send, v_recv, v_z_send, v_z_recv = refs[7:14]
    swap_own, swap_send, swap_recv = refs[14:17]
    scatter = Scatter(bits, parts, plan, rows, lhs_ref, rhs_refs, out_ref, refs[17:])
    z = lax.axis_index("mp")
    mesh_id = pl.DeviceIdType.MESH
    greet_all(bits, parts, True)
    swaps = [
        Swap(2**bits, src, dst, swap_own.at[i], swap_send.at[i], swap_recv.at[i])
        for i, (src, dst) in enumerate(((y_ref, y_out), (g_ref, g_out)))
    ]

    def v_hop(b):
        return pltpu.make_async_remote_copy(
            src_ref=vec_ref if b == 0 else v_acc.at[b - 1], dst_ref=v_in.at[b], send_sem=v_send.at[b],
            recv_sem=v_recv.at[b], device_id={"dp": scatter.partner(b)}, device_id_type=mesh_id,
        )

    def v_z_hop(src, dst, delta):
        return pltpu.make_async_remote_copy(
            src_ref=src, dst_ref=dst, send_sem=v_z_send.at[0], recv_sem=v_z_recv.at[0],
            device_id={"mp": lax.rem(z + delta, parts)}, device_id_type=mesh_id,
        )

    def small_sum(stage):
        if stage == 0:
            v_hop(0).start()
        elif stage <= bits:
            b = stage - 1
            v_hop(b).wait_recv()
            total = (vec_ref[...] if b == 0 else v_acc[b - 1]) + v_in[b]
            if stage < bits:
                v_acc[b] = total
                v_hop(stage).start()
            else:
                v_z[z] = total
                for delta in range(1, parts):
                    v_z_hop(v_z.at[z], v_z.at[z], delta).start()
        else:
            whole = v_z.at[pl.ds(0, parts - 1)]
            v_z_hop(whole, whole, 1).wait_recv()
            total = v_z[0]
            for s in range(1, parts):
                total = total + v_z[s]
            vec_out[...] = total
            for b in range(bits):
                v_hop(b).wait_send()
            v_z_hop(whole, whole, 1).wait_send()
    for swap in swaps:
        swap.start()

    @pl.loop(0, scatter.ticks)
    def _(tick):
        for stage in range(bits + 2):
            @pl.when(tick == stage)
            def _():
                small_sum(stage)

        scatter.tick(tick)

    for swap in swaps:
        swap.finish()
    scatter.finish()


def scatter_sum(lefts, pairs, vector, block_out, d_x, groups, parts, collective):
    kinds, width, length = lefts.shape
    bits = groups.bit_length() - 1
    rows = width // groups
    plan = plan_of(pairs)
    count = len(plan)
    vmem_spec = pl.BlockSpec(memory_space=pltpu.VMEM)
    any_spec = pl.BlockSpec(memory_space=pl.ANY)
    dma = lambda *shape: pltpu.SemaphoreType.DMA(shape)
    return pl.pallas_call(
        partial(scatter_kernel, bits, parts, plan, rows),
        out_shape=(
            jax.ShapeDtypeStruct((count, rows, WIDE), F32),
            jax.ShapeDtypeStruct(vector.shape, F32),
            jax.ShapeDtypeStruct(block_out.shape, BF16),
            jax.ShapeDtypeStruct(d_x.shape, BF16),
        ),
        in_specs=[any_spec] * (1 + len(pairs)) + [vmem_spec, any_spec, any_spec],
        out_specs=(vmem_spec, vmem_spec, any_spec, any_spec),
        scratch_shapes=[
            pltpu.VMEM((bits - 1,) + vector.shape, F32),
            pltpu.VMEM((bits,) + vector.shape, F32),
            pltpu.VMEM((parts,) + vector.shape, F32),
            dma(bits), dma(bits), dma(1), dma(1),
            dma(2), dma(2), dma(2),
            *Scatter.scratch(bits, parts, count, rows, length, width),
        ],
        compiler_params=pltpu.CompilerParams(
            collective_id=collective, has_side_effects=True, vmem_limit_bytes=60 * 2**20
        ),
        cost_estimate=pl.CostEstimate(
            flops=2 * count * WIDE * parts * length * width, bytes_accessed=count * parts * length * WIDE * 2,
            transcendentals=0,
        ),
        name="scatter_sum",
    )(lefts, *[right for _, right in pairs], vector, block_out, d_x)


def backward_kernel(
    heads, parts, bits, plan, rows_held,
    dhead_ref, o_ref, gate_ref, qe_ref, phi_ref, phil_ref,
    raw_ref, halo_ref, convw_ref, ab_ref, gain_ref, s_ref, t_ref, phi_late_ref, lhs_ref, *refs,
):
    sources = len({item[0] for item in plan})
    rhs_refs, refs = refs[:sources], refs[sources:]
    dproj_ref, dab_ref, dconv_ref, dgain_ref, sums_ref = refs[:5]
    (do_s, d_s, dgate_s, dl_s, phil_s, g_s, dext_s, ext_s, send_s, recv_s, halo_send, halo_recv,
     send_sem, recv_sem, halo_send_sem, halo_recv_sem) = refs[5:21]
    scatter = Scatter(bits, parts, plan, rows_held, lhs_ref, rhs_refs, sums_ref, refs[21:])
    step = pl.program_id(0)
    early = pl.program_id(1) == 0
    z = lax.axis_index("mp")
    back = parts - 1 - z
    lag = parts - 1
    slots = lag + 1
    length = o_ref.shape[1]
    size = min(CHUNK, length)
    chunks = length // size

    @pl.when((step == 0) & early)
    def _():
        greet_all(bits, parts, False)

    now = step * 2 + pl.program_id(1)
    last = 2 * (heads + lag + 1) - 1
    stop = jnp.where(now == last, max(scatter.ticks, last + 1), now + 1)

    @pl.loop(now, stop)
    def _(tick):
        scatter.tick(tick)


    def hop(h):
        return pltpu.make_async_remote_copy(
            src_ref=send_s.at[h], dst_ref=recv_s.at[h], send_sem=send_sem.at[h],
            recv_sem=recv_sem.at[h], device_id={"mp": lax.rem(z + parts - 1, parts)},
            device_id_type=pl.DeviceIdType.MESH,
        )

    def halo_hop(h):
        return pltpu.make_async_remote_copy(
            src_ref=halo_send.at[h], dst_ref=halo_recv.at[h], send_sem=halo_send_sem.at[h],
            recv_sem=halo_recv_sem.at[h], device_id={"mp": lax.rem(z + parts - 1, parts)},
            device_id_type=pl.DeviceIdType.MESH,
        )

    @pl.when((step == 0) & early)
    def _():
        dgain_ref[...] = jnp.zeros_like(dgain_ref)
        g_s[...] = jnp.zeros_like(g_s)

    @pl.when((step == 0) & early & (back == 0))
    def _():
        recv_s[...] = jnp.zeros_like(recv_s)
        halo_recv[...] = jnp.zeros_like(halo_recv)

    @pl.when((step < heads) & early)
    def _():
        slot = lax.rem(step, slots)
        gslot = lax.rem(step, slots + 1)
        gain = gain_ref[...]
        d_gain = jnp.zeros((1, DV), F32)
        for c in range(chunks):
            at = slice(c * size, (c + 1) * size)
            out = o_ref[0, at]
            d_head = dhead_ref[0, at]
            gate = gate_ref[0, c * size : (c + 1) * size]
            scale = lax.rsqrt(jnp.mean(out * out, axis=-1, keepdims=True) + 1e-05)
            unit = out * scale
            sig = jax.nn.sigmoid(gate)
            gated = gate * sig
            both = d_head * unit
            d_gain = d_gain + jnp.sum(both * gated, axis=0, keepdims=True)
            e = d_head * gated * gain
            d_out = scale * (e - unit * jnp.mean(e * unit, axis=-1, keepdims=True))
            dgate_s[gslot, at] = (both * gain * sig * (1.0 + gate * (1.0 - sig))).astype(BF16)
            do_s[slot, at] = d_out
            d_s[slot, c] = mm(qe_ref[0, at], d_out, 0, 0)
        dgain_ref[...] += d_gain
        total = d_s[slot, chunks - 1]
        for c in range(chunks - 2, -1, -1):
            total = mm(phi_ref[0, c], total) + d_s[slot, c]
        dl_s[slot] = total
        phil_s[slot] = phil_ref[0]

    relay = step - back

    @pl.when((relay >= 0) & (relay < heads) & early)
    def _():
        slot = lax.rem(relay, slots)

        @pl.when(back > 0)
        def _():
            hop(relay).wait_recv()

        @pl.when(z > 0)
        def _():
            send_s[relay] = mm(phil_s[slot], recv_s[relay]) + dl_s[slot]
            hop(relay).start()

    @pl.when((step >= lag) & (step < lag + heads) & ~early)
    def _():
        head = step - lag
        slot = lax.rem(head, slots)
        eslot = lax.rem(head, 2)
        rows, cols = masks(size)
        upper = (rows <= cols).astype(F32)
        convw = convw_ref[0]
        d_state = recv_s[head]
        ext_s[0:HALO] = halo_ref[0, :, 0:HEADW]
        ext_s[HALO:] = raw_ref[0, 0:size, 0:HEADW]
        d_conv_rows = [jnp.zeros((1, HEADW), F32) for _ in range(TAPS)]
        for c in range(chunks - 1, -1, -1):
            at = slice(c * size, (c + 1) * size)
            shifted = windows(raw_ref, ext_s, c, size)
            conv = conv_of(shifted, convw)
            sig, q_silu, k_silu, value, q_scale, k_scale = unit_parts(conv)
            query = q_silu * (q_scale * DK ** (-0.5))
            keyed = k_silu * k_scale
            gamma_row, gamma_col, beta = decays(ab_ref, c * size, size, upper)
            inclusive, strict = fades(gamma_row, gamma_col, rows, cols)
            gram = mm(jnp.concatenate([keyed, query], axis=0), keyed, 1, 1)
            gram_f = gram[:size] * strict
            lower = beta * gram_f
            scores = gram[size:] * inclusive
            growth = jnp.exp(gamma_col)
            last = gamma_row[:, size - 1 :]
            tail = jnp.exp(last - gamma_col)
            query_g = query * growth
            grown = keyed * growth
            keyed_b = beta * grown
            keyed_g = keyed * tail
            state = s_ref[0, c]
            inverse = t_ref[0, c]
            d_out = do_s[slot, at]
            fresh = mm(inverse, beta * value - mm(keyed_b, state))
            d_fresh = mm(scores, d_out, 0, 0) + mm(keyed_g, d_state)
            d_rhs = mm(inverse, d_fresh, 0, 0)
            stacked = jnp.concatenate([d_out, d_rhs], axis=0)
            by_fresh = mm(stacked, fresh, 1, 1)
            by_state = mm(stacked, state, 1, 1)
            d_scores = by_fresh[:size] * inclusive
            d_lower = -by_fresh[size:]
            d_query_g = by_state[:size]
            d_keyed_b = -by_state[size:]
            d_keyed_g = mm(fresh, d_state, 1, 1)
            d_gram = d_lower * (beta * strict)
            by_keyed = mm(jnp.concatenate([d_scores, d_gram], axis=0), keyed)
            d_query = by_keyed[:size] + growth * d_query_g
            d_keyed = (
                by_keyed[size:]
                + mm(jnp.concatenate([d_scores, d_gram], axis=0),
                     jnp.concatenate([query, keyed], axis=0), 0, 0)
                + (beta * growth) * d_keyed_b
                + tail * d_keyed_g
            )
            d_value = beta * d_rhs
            d_beta = (
                jnp.sum(d_rhs * value, axis=-1, keepdims=True)
                + jnp.sum(d_lower * gram_f, axis=-1, keepdims=True)
                + jnp.sum(d_keyed_b * grown, axis=-1, keepdims=True)
            )
            moved = by_fresh[:size] * scores + d_lower * lower
            tail_part = jnp.sum(d_keyed_g * keyed_g, axis=-1, keepdims=True)
            d_gamma = (
                jnp.sum(moved, axis=-1, keepdims=True)
                + jnp.sum(d_query_g * query_g, axis=-1, keepdims=True)
                + jnp.sum(d_keyed_b * keyed_b, axis=-1, keepdims=True)
                - tail_part
            )
            at_end = jnp.sum(tail_part, axis=0, keepdims=True) + jnp.exp(last) * jnp.sum(
                jnp.sum(state * d_state, axis=-1, keepdims=True), axis=0, keepdims=True
            )
            lanes = lax.broadcasted_iota(jnp.int32, (size, DK), 1)
            packed = jnp.where(lanes == 0, d_gamma, jnp.where(lanes == 1, d_beta, 0.0)).T[:8]
            row_id = lax.broadcasted_iota(jnp.int32, packed.shape, 0)
            packed = packed - jnp.where(row_id == 0, jnp.sum(moved, axis=0, keepdims=True), 0.0)
            summed = mm(packed, upper, 1, 1) + at_end
            dab_ref[0, :, at] = jnp.where(row_id == 0, summed, packed)
            if c > 0:
                d_state = mm(phi_late_ref[0, c], d_state) + d_s[slot, c]
            d_q_silu = (DK ** (-0.5) * q_scale) * (
                d_query
                - q_silu * (q_scale * q_scale) * jnp.sum(q_silu * d_query, axis=-1, keepdims=True)
            )
            d_k_silu = k_scale * (
                d_keyed
                - k_silu * (k_scale * k_scale) * jnp.sum(k_silu * d_keyed, axis=-1, keepdims=True)
            )
            d_silu = jnp.concatenate([d_q_silu, d_k_silu, d_value], axis=1)
            d_conv = d_silu * sig * (1.0 + conv * (1.0 - sig))
            g_s[HALO + c * size : HALO + (c + 1) * size] = d_conv
            for i in range(TAPS):
                d_conv_rows[i] = d_conv_rows[i] + jnp.sum(shifted[i] * d_conv, axis=0, keepdims=True)
        for i in range(TAPS):
            dconv_ref[0, i : i + 1] = d_conv_rows[i]
        for base, count in [(0, HALO)] + [(HALO + c * size, size) for c in range(chunks)]:
            d_raw = None
            for i in range(TAPS):
                part = g_s[pl.ds(base + TAPS - 1 - i, count)] * convw[i : i + 1]
                d_raw = part if d_raw is None else d_raw + part
            if base == 0:
                halo_send[head] = d_raw
            else:
                dext_s[eslot, base - HALO : base - HALO + count] = d_raw

        @pl.when(z > 0)
        def _():
            halo_hop(head).start()

    @pl.when((step > lag) & ~early)
    def _():
        head = step - lag - 1
        eslot = lax.rem(head, 2)
        gslot = lax.rem(head, slots + 1)

        @pl.when(back > 0)
        def _():
            halo_hop(head).wait_recv()

        dext_s[eslot, length - HALO : length] += halo_recv[head]
        dproj_ref[0, :, 0:HEADW] = dext_s[eslot].astype(BF16)
        dproj_ref[0, :, HEADW:] = dgate_s[gslot]

    @pl.when((step == pl.num_programs(0) - 1) & ~early)
    def _():
        scatter.finish()

    @pl.when((step == pl.num_programs(0) - 1) & ~early & (z > 0))
    def _():
        @pl.loop(0, heads)
        def _(h):
            hop(h).wait_send()
            halo_hop(h).wait_send()


def forward_core(raw, convw, ab, gain, weights, heads, parts, groups):
    bits = groups.bit_length() - 1
    pieces = []
    for w, weight in enumerate(weights):
        wide = weight.shape[1]
        pieces += [(w, at, at + WIDE // 2, at + WIDE) for at in range(0, wide, WIDE)]
    rows = weights[0].shape[0]
    any_spec = pl.BlockSpec(memory_space=pl.ANY)
    length = raw.shape[1]
    size = min(CHUNK, length)
    chunks = length // size
    per = heads // raw.shape[0]
    lag = parts - 1
    slots = lag + 1
    now = lambda s: jnp.minimum(s, heads - 1)
    late = lambda s: jnp.maximum(s - lag, 0)
    return pl.pallas_call(
        partial(forward_kernel, heads, parts, bits, pieces),
        grid=(heads + lag, 2),
        out_shape=(
            jax.ShapeDtypeStruct((raw.shape[0], length, per * DV), BF16),
            jax.ShapeDtypeStruct((heads, length, DV), F32),
            jax.ShapeDtypeStruct((heads, chunks, DK, DV), F32),
            jax.ShapeDtypeStruct((heads, chunks, size, size), F32),
            jax.ShapeDtypeStruct((heads, length, DK), F32),
            jax.ShapeDtypeStruct((heads, chunks, DK, DK), F32),
            jax.ShapeDtypeStruct((heads, DK, DK), F32),
            jax.ShapeDtypeStruct((parts, HALO, per * (HEADW + DV)), F32),
            *[jax.ShapeDtypeStruct((parts, groups) + w.shape, BF16) for w in weights],
        ),
        in_specs=[
            pl.BlockSpec((1, length, HEADW + DV), lambda s, _: (now(s) // per, 0, now(s) % per)),
            pl.BlockSpec((1, length, DV), lambda s, _: (late(s) // per, 0, (late(s) % per) * 3 + 2)),
            any_spec,
            pl.BlockSpec((1, TAPS, HEADW), lambda s, _: (now(s), 0, 0)),
            pl.BlockSpec((1, 8, length), lambda s, _: (now(s), 0, 0)),
            pl.BlockSpec((1, DV), lambda s, _: (0, 0)),
            *[any_spec] * len(weights),
        ],
        out_specs=(
            pl.BlockSpec((1, length, DV), lambda s, _: (late(s) // per, 0, late(s) % per)),
            pl.BlockSpec((1, length, DV), lambda s, _: (late(s), 0, 0)),
            pl.BlockSpec((1, chunks, DK, DV), lambda s, _: (late(s), 0, 0, 0)),
            pl.BlockSpec((1, chunks, size, size), lambda s, _: (now(s), 0, 0, 0)),
            pl.BlockSpec((1, length, DK), lambda s, _: (now(s), 0, 0)),
            pl.BlockSpec((1, chunks, DK, DK), lambda s, _: (now(s), 0, 0, 0)),
            pl.BlockSpec((1, DK, DK), lambda s, _: (now(s), 0, 0)),
            pl.BlockSpec((parts, HALO, per * (HEADW + DV)), lambda s, _: (0, 0, 0)),
            *[any_spec] * len(weights),
        ),
        scratch_shapes=[
            pltpu.VMEM((slots, length, DK), F32),
            pltpu.VMEM((slots, length, DV), F32),
            pltpu.VMEM((slots, chunks, DK, DK), F32),
            pltpu.VMEM((slots, chunks, DK, DV), F32),
            pltpu.VMEM((slots, DK, DK), F32),
            pltpu.VMEM((slots, DK, DV), F32),
            pltpu.VMEM((heads, DK, DV), F32),
            pltpu.VMEM((heads, DK, DV), F32),
            pltpu.VMEM((parts, HALO, per * (HEADW + DV)), F32),
            pltpu.VMEM((HALO + size, HEADW), F32),
            pltpu.SemaphoreType.DMA((heads,)),
            pltpu.SemaphoreType.DMA((heads,)),
            pltpu.SemaphoreType.DMA((parts,)),
            pltpu.SemaphoreType.DMA((parts,)),
            *Gather.scratch(bits, len(pieces)),
        ],
        compiler_params=pltpu.CompilerParams(
            collective_id=0, has_side_effects=True, vmem_limit_bytes=56 * 2**20
        ),
        cost_estimate=pl.CostEstimate(flops=20 * 10**9, bytes_accessed=40 * 2**20, transcendentals=0),
        name="delta_forward",
    )(raw, raw, raw, convw, ab, gain, *weights)


def backward_core(d_head, out, raw, halo, query_e, phi, phi_all, convw, ab, gain, states, inverses, lefts, pairs,
                  heads, parts, groups):
    length = raw.shape[1]
    size = min(CHUNK, length)
    chunks = length // size
    per = heads // raw.shape[0]
    lag = parts - 1
    slots = lag + 1
    bits = groups.bit_length() - 1
    plan = plan_of(pairs)
    rows = lefts.shape[1] // groups
    any_spec = pl.BlockSpec(memory_space=pl.ANY)
    now = lambda s: jnp.minimum(s, heads - 1)
    late = lambda s: jnp.clip(s - lag, 0, heads - 1)
    later = lambda s: jnp.maximum(s - lag - 1, 0)
    return pl.pallas_call(
        partial(backward_kernel, heads, parts, bits, plan, rows),
        grid=(heads + lag + 1, 2),
        out_shape=(
            jax.ShapeDtypeStruct((raw.shape[0], length, per * (HEADW + DV)), BF16),
            jax.ShapeDtypeStruct((heads, 8, length), F32),
            jax.ShapeDtypeStruct((heads, TAPS, HEADW), F32),
            jax.ShapeDtypeStruct((1, DV), F32),
            jax.ShapeDtypeStruct((len(plan), rows, WIDE), F32),
        ),
        in_specs=[
            pl.BlockSpec((1, length, DV), lambda s, _: (now(s) // per, 0, now(s) % per)),
            pl.BlockSpec((1, length, DV), lambda s, _: (now(s), 0, 0)),
            pl.BlockSpec((1, length, DV), lambda s, _: (now(s) // per, 0, (now(s) % per) * 3 + 2)),
            pl.BlockSpec((1, length, DK), lambda s, _: (now(s), 0, 0)),
            pl.BlockSpec((1, chunks, DK, DK), lambda s, _: (now(s), 0, 0, 0)),
            pl.BlockSpec((1, DK, DK), lambda s, _: (now(s), 0, 0)),
            pl.BlockSpec((1, length, HEADW + DV), lambda s, _: (late(s) // per, 0, late(s) % per)),
            pl.BlockSpec((1, HALO, HEADW + DV), lambda s, _: (late(s) // per, 0, late(s) % per)),
            pl.BlockSpec((1, TAPS, HEADW), lambda s, _: (late(s), 0, 0)),
            pl.BlockSpec((1, 8, length), lambda s, _: (late(s), 0, 0)),
            pl.BlockSpec((1, DV), lambda s, _: (0, 0)),
            pl.BlockSpec((1, chunks, DK, DV), lambda s, _: (late(s), 0, 0, 0)),
            pl.BlockSpec((1, chunks, size, size), lambda s, _: (late(s), 0, 0, 0)),
            pl.BlockSpec((1, chunks, DK, DK), lambda s, _: (late(s), 0, 0, 0)),
            *[any_spec] * (1 + len(pairs)),
        ],
        out_specs=(
            pl.BlockSpec((1, length, HEADW + DV), lambda s, _: (later(s) // per, 0, later(s) % per)),
            pl.BlockSpec((1, 8, length), lambda s, _: (late(s), 0, 0)),
            pl.BlockSpec((1, TAPS, HEADW), lambda s, _: (late(s), 0, 0)),
            pl.BlockSpec((1, DV), lambda s, _: (0, 0)),
            pl.BlockSpec((len(plan), rows, WIDE), lambda s, _: (0, 0, 0)),
        ),
        scratch_shapes=[
            pltpu.VMEM((slots, length, DV), F32),
            pltpu.VMEM((slots, chunks, DK, DV), F32),
            pltpu.VMEM((slots + 1, length, DV), BF16),
            pltpu.VMEM((slots, DK, DV), F32),
            pltpu.VMEM((slots, DK, DK), F32),
            pltpu.VMEM((length + 2 * HALO, HEADW), F32),
            pltpu.VMEM((2, length, HEADW), F32),
            pltpu.VMEM((HALO + size, HEADW), F32),
            pltpu.VMEM((heads, DK, DV), F32),
            pltpu.VMEM((heads, DK, DV), F32),
            pltpu.VMEM((heads, HALO, HEADW), F32),
            pltpu.VMEM((heads, HALO, HEADW), F32),
            pltpu.SemaphoreType.DMA((heads,)),
            pltpu.SemaphoreType.DMA((heads,)),
            pltpu.SemaphoreType.DMA((heads,)),
            pltpu.SemaphoreType.DMA((heads,)),
            *Scatter.scratch(bits, parts, len(plan), rows, length, lefts.shape[1]),
        ],
        compiler_params=pltpu.CompilerParams(
            collective_id=1, has_side_effects=True, vmem_limit_bytes=62 * 2**20
        ),
        cost_estimate=pl.CostEstimate(flops=40 * 10**9, bytes_accessed=60 * 2**20, transcendentals=0),
        name="delta_backward",
    )(d_head, out, raw, query_e, phi, phi_all, raw, halo, convw, ab, gain, states, inverses, phi,
      lefts, *[right for _, right in pairs])


def dot(spec, a, b):
    return jnp.einsum(spec, a, b, preferred_element_type=F32)


def unit_rms(v):
    return lax.rsqrt(jnp.mean(v * v, axis=-1, keepdims=True) + 1e-05)


def per_device(
    tokens, out_grad, seq_lengths, mix_gain, w_query, w_key, w_value, w_outgate, w_decay, w_beta,
    conv_weight, rate_log, step_bias, head_gain, w_out, ffn_gain, w_ffn_gate, w_ffn_up, w_ffn_down,
):
    groups = lax.axis_size("dp")
    parts = lax.axis_size("mp")
    group = lax.axis_index("dp")
    share = lax.axis_index("mp")
    heads = rate_log.shape[0]
    per = heads // parts
    width = tokens.shape[2]
    local_rows = w_query.shape[0]

    def by_head(w, size):
        return w.reshape(local_rows, per, size)

    joined = jnp.concatenate(
        [by_head(w_query, DK), by_head(w_key, DK), by_head(w_value, DV), by_head(w_outgate, DV)], axis=2
    ).reshape(local_rows, per * (HEADW + DV))
    main_cols = joined.shape[1]

    hidden = w_ffn_gate.shape[1]
    wide = -(-hidden // WIDE) * WIDE
    small_w = jnp.concatenate([w_decay, w_beta], axis=1)
    lanes = -(-small_w.shape[1] // 128) * 128
    widen = lambda w, size: jnp.pad(w, ((0, 0), (0, size - w.shape[1])))
    x_bf, dy_bf, g_proj, g_small = prologue(
        tokens, out_grad, joined, widen(small_w, lanes), groups, parts
    )
    whole = lambda g: g.reshape(parts, width, g.shape[3])
    g_proj = whole(g_proj)
    g_small = whole(g_small)
    x_bf = x_bf.reshape(-1, width)
    dy_bf = dy_bf.reshape(-1, width)
    length = x_bf.shape[0]

    my_length = lax.dynamic_slice_in_dim(seq_lengths, group, 1)
    positions = share * length + jnp.arange(length, dtype=jnp.int32)
    live = (positions < my_length).astype(F32)[:, None]

    x = x_bf.astype(F32)
    dy = live * dy_bf.astype(F32)
    d_ffo = dy.astype(BF16)
    scale1 = unit_rms(x)
    n1 = x * scale1
    h1 = (n1 * mix_gain).astype(BF16)
    raw = dot("td,gdc->gtc", h1, g_proj)
    small = dot("td,gdc->gct", h1, g_small)[:, : 2 * per]
    decay_raw = small[:, :per].reshape(heads, length)
    beta_raw = small[:, per:].reshape(heads, length)
    rate = -jnp.exp(rate_log)[:, None]
    shifted = decay_raw + step_bias[:, None]
    decay = rate * jax.nn.softplus(shifted)
    beta = jax.nn.sigmoid(beta_raw)
    ab = jnp.concatenate(
        [decay[:, None], beta[:, None], jnp.zeros((heads, 6, length), F32)], axis=1
    )
    taps = conv_weight.shape[0]
    key_cols = heads * DK
    convw = jnp.concatenate(
        [
            conv_weight[:, :key_cols].reshape(taps, heads, DK),
            conv_weight[:, key_cols : 2 * key_cols].reshape(taps, heads, DK),
            conv_weight[:, 2 * key_cols :].reshape(taps, heads, DV),
        ],
        axis=2,
    ).transpose(1, 0, 2)
    gain_row = head_gain[None]
    head_out, mixed, states, inverses, query_e, phi, phi_all, halo, *rest = forward_core(
        raw, convw, ab, gain_row,
        [w_out] + [widen(w, wide) for w in (w_ffn_gate, w_ffn_up, w_ffn_down)],
        heads, parts, groups,
    )
    g_out, g_gate, g_up, g_down = [whole(w) for w in rest]

    x1 = x + dot("gtc,gmc->tm", head_out, g_out)
    scale2 = unit_rms(x1)
    n2 = x1 * scale2
    h2 = (n2 * ffn_gain).astype(BF16)
    gate = dot("td,gdf->gtf", h2, g_gate)
    up = dot("td,gdf->gtf", h2, g_up)
    sig = jax.nn.sigmoid(gate)
    act = (gate * sig * up).astype(BF16)
    block_out = (live * (x1 + dot("gtf,gdf->td", act, g_down))).astype(BF16)
    d_act = dot("td,gdf->gtf", d_ffo, g_down)
    d_gate = (d_act * up * sig * (1.0 + gate * (1.0 - sig))).astype(BF16)
    d_up = (d_act * gate * sig).astype(BF16)
    d_h2 = dot("gtf,gdf->td", d_gate, g_gate) + dot("gtf,gdf->td", d_up, g_up)
    e2 = d_h2 * ffn_gain
    d_x1 = dy + scale2 * (e2 - n2 * jnp.mean(e2 * n2, axis=-1, keepdims=True))
    ffn_gain_grad = jnp.sum(d_h2 * n2, axis=0)
    d_mix = d_x1.astype(BF16)
    d_head = dot("tm,gmc->gtc", d_mix, g_out)

    d_proj, d_ab, d_convw, d_head_gain, sums_ffn = backward_core(
        d_head, mixed, raw, halo, query_e, phi, phi_all, convw, ab, gain_row, states, inverses,
        jnp.stack([d_mix.T, h2.T, d_ffo.T]), [(2, act), (1, d_gate), (1, d_up), (0, head_out)],
        heads, parts, groups,
    )
    d_decay = d_ab[:, 0]
    d_beta_raw = d_ab[:, 1] * beta * (1.0 - beta)
    d_decay_raw = d_decay * rate * jax.nn.sigmoid(shifted)
    rate_grad = jnp.sum(d_decay * decay, axis=1)
    bias_grad = jnp.sum(d_decay_raw, axis=1)
    d_small = jnp.concatenate(
        [d_decay_raw.reshape(parts, per, length), d_beta_raw.reshape(parts, per, length)], axis=1
    ).astype(BF16)
    small_grad = dot("gct,td->gcd", d_small, h1)
    d_h1 = dot("gtc,gdc->td", d_proj, g_proj) + dot("gct,gdc->td", d_small, g_small[:, :, : 2 * per])
    e1 = d_h1 * mix_gain
    d_x = d_x1 + scale1 * (e1 - n1 * jnp.mean(e1 * n1, axis=-1, keepdims=True))
    mix_gain_grad = jnp.sum(d_h1 * n1, axis=0)
    per_head = d_convw.transpose(1, 0, 2)
    d_conv = jnp.concatenate(
        [
            per_head[:, :, :DK].reshape(taps, key_cols),
            per_head[:, :, DK : 2 * DK].reshape(taps, key_cols),
            per_head[:, :, 2 * DK :].reshape(taps, heads * DV),
        ],
        axis=1,
    )
    vector = jnp.concatenate(
        [mix_gain_grad, ffn_gain_grad, d_head_gain[0], d_conv.reshape(-1), rate_grad, bias_grad,
         small_grad.reshape(-1)]
    )
    used = vector.shape[0]
    vector = jnp.pad(vector, (0, -used % 1024)).reshape(-1, 128)
    sums_proj, sums, final_out, final_grad = scatter_sum(
        h1.T[None], [(0, d_proj)],
        vector, block_out.reshape(tokens.shape), d_x.astype(BF16).reshape(tokens.shape),
        groups, parts, 2,
    )
    sums = sums.reshape(-1)

    sums_w = jnp.concatenate([sums_ffn, sums_proj], axis=0)

    def columns(start, size):
        pieces = -(-size // WIDE)
        return sums_w[start : start + pieces].transpose(1, 0, 2).reshape(local_rows, -1)[:, :size]

    step = wide // WIDE
    s_down = columns(0, hidden)
    s_gate = columns(step, hidden)
    s_up = columns(2 * step, hidden)
    s_out = columns(3 * step, per * DV)
    s_proj = columns(3 * step + per * DV // WIDE, main_cols)
    pieces = []
    start = 0
    for count in (width, width, DV, taps * conv_weight.shape[1], heads, heads):
        pieces.append(sums[start : start + count])
        start += count
    small_sum = sums[start:used].reshape(parts, 2 * per, width)
    mine = lax.dynamic_slice(small_sum, (share, 0, group * local_rows), (1, 2 * per, local_rows))[0].T

    by = s_proj.reshape(local_rows, per, HEADW + DV)
    flat = lambda v: v.reshape(local_rows, -1)
    return (
        final_out,
        final_grad,
        pieces[0],
        flat(by[:, :, :DK]),
        flat(by[:, :, DK : 2 * DK]),
        flat(by[:, :, 2 * DK : HEADW]),
        flat(by[:, :, HEADW:]),
        mine[:, :per],
        mine[:, per:],
        pieces[3].reshape(conv_weight.shape),
        pieces[4],
        pieces[5],
        pieces[2],
        s_out,
        pieces[1],
        s_gate,
        s_up,
        s_down,
    )


def solution(mesh):
    seq = P(None, ("mp", "dp"), None)
    shard = P("dp", "mp")
    rep = P()
    return jax.shard_map(
        per_device,
        mesh=mesh,
        in_specs=(
            seq, seq, rep, rep, shard, shard, shard, shard, shard, shard,
            rep, rep, rep, rep, shard, rep, shard, shard, shard,
        ),
        out_specs=(
            seq, seq, rep, shard, shard, shard, shard, shard, shard,
            rep, rep, rep, rep, shard, rep, shard, shard, shard,
        ),
        check_vma=False,
    )
```

```python
from functools import partial

import jax
import jax.numpy as jnp
from jax import lax
from jax.experimental import pallas as pl
from jax.experimental.pallas import tpu as pltpu
from jax.sharding import PartitionSpec as P

DK = 128
DV = 256
HEADW = 2 * DK + DV
TAPS = 4
CHUNK = 128
HALO = 8
WIDE = 256
STRIDE = 2
F32 = jnp.float32
BF16 = jnp.bfloat16


def halves(a):
    high = a.astype(BF16)
    return high, (a - high.astype(F32)).astype(BF16)


def mm(a, b, ca=1, cb=0):
    dims = (((ca,), (cb,)), ((), ()))
    a_high, a_low = halves(a)
    b_high, b_low = halves(b)
    one = lambda p, q: lax.dot_general(p, q, dims, preferred_element_type=F32)
    if a.shape[ca] <= 128:
        return one(
            jnp.concatenate([a_high, a_low], axis=ca), jnp.concatenate([b_high, b_high], axis=cb)
        ) + one(a_high, b_low)
    return one(a_high, b_high) + (one(a_high, b_low) + one(a_low, b_high))


def windows(raw_ref, ext_s, c, size):
    if c == 0:
        return [ext_s[pl.ds(HALO - TAPS + 1 + i, size)] for i in range(TAPS)]
    return [raw_ref[0, pl.ds(c * size - TAPS + 1 + i, size), 0:HEADW] for i in range(TAPS)]


def conv_of(shifted, convw):
    total = None
    for i in range(TAPS):
        part = shifted[i] * convw[i : i + 1]
        total = part if total is None else total + part
    return total


def decays(ab_ref, base, rows, upper):
    ab = ab_ref[0, :, pl.ds(base, rows)]
    cum = mm(ab, upper)
    row_id = lax.broadcasted_iota(jnp.int32, ab.shape, 0)
    both = jnp.where(row_id == 0, cum, ab)
    cols = both.T
    return both[0:1], cols[:, 0:1], cols[:, 1:2]


def masks(size):
    rows = lax.broadcasted_iota(jnp.int32, (size, size), 0)
    cols = lax.broadcasted_iota(jnp.int32, (size, size), 1)
    return rows, cols


def fades(gamma_row, gamma_col, rows, cols):
    spread = jnp.minimum(gamma_col - gamma_row, 0.0)
    inclusive = jnp.where(rows >= cols, jnp.exp(spread), 0.0)
    strict = jnp.where(rows > cols, inclusive, 0.0)
    return inclusive, strict


def invert_many(lowers, rows, cols):
    size = lowers[0].shape[0]
    eye = (rows == cols).astype(F32)
    pair = ((rows // 2) == (cols // 2)) & (rows > cols)
    inverses = [eye - jnp.where(pair, low, 0.0) for low in lowers]
    width = 2
    while width < size:
        within = (rows // (2 * width)) == (cols // (2 * width))
        cross = within & ((rows // width) != (cols // width)) & (rows > cols)
        inner = [mm(jnp.where(cross, low, 0.0), inv) for low, inv in zip(lowers, inverses)]
        inverses = [inv - mm(inv, part) for inv, part in zip(inverses, inner)]
        width *= 2
    return inverses


def unit_parts(conv):
    sig = jax.nn.sigmoid(conv)
    silu = conv * sig
    q_silu = silu[:, :DK]
    k_silu = silu[:, DK : 2 * DK]
    value = silu[:, 2 * DK :]
    q_scale = lax.rsqrt(jnp.sum(q_silu * q_silu, axis=-1, keepdims=True) + 1e-06)
    k_scale = lax.rsqrt(jnp.sum(k_silu * k_silu, axis=-1, keepdims=True) + 1e-06)
    return sig, q_silu, k_silu, value, q_scale, k_scale


class Gather:
    def __init__(self, bits, parts, sources, targets, pieces, sems):
        self.bits, self.parts, self.pieces = bits, parts, pieces
        self.sources, self.targets = sources, targets
        (self.own, self.z_send, self.z_recv, self.p_send, self.p_recv, self.s_send, self.s_recv) = sems
        self.d, self.z = lax.axis_index("dp"), lax.axis_index("mp")
        self.orders = (list(range(1, bits)), list(range(bits - 1, 0, -1)))
        self.ticks = bits + 1

    @staticmethod
    def scratch(bits, count):
        dma = lambda *shape: pltpu.SemaphoreType.DMA(shape)
        return [
            dma(count), dma(count), dma(count), dma(count, bits - 1, 2), dma(count, bits - 1, 2),
            dma(count), dma(count),
        ]

    def flip(self, index, b):
        return index + (1 - 2 * lax.rem(lax.div(self.d, 2**b), 2)) * 2**b

    def copy(self, src, dst, send, recv, to):
        return pltpu.make_async_remote_copy(
            src_ref=src, dst_ref=dst, send_sem=send, recv_sem=recv, device_id=to,
            device_id_type=pl.DeviceIdType.MESH,
        )

    def sides(self, p):
        _, start, mid, stop = self.pieces[p]
        return [(0, start, mid)] + ([(1, mid, stop)] if mid < stop else [])

    def held(self, side, k):
        out = [self.d]
        for b in self.orders[side][:k]:
            out = out + [self.flip(i, b) for i in out]
        return out

    def arrived(self, side, k):
        return [self.flip(i, self.orders[side][k]) for i in self.held(side, k)]

    def to_sibling(self, p, indices, start, stop):
        target = self.targets[self.pieces[p][0]]
        for i in indices:
            block = target.at[:, i, :, start:stop]
            self.copy(
                block, block, self.s_send.at[p], self.s_recv.at[p], {"dp": self.flip(self.d, 0)}
            ).start()

    def along(self, p, k, act):
        target = self.targets[self.pieces[p][0]]
        for side, start, stop in self.sides(p):
            b = self.orders[side][k]
            for i in self.held(side, k):
                block = target.at[:, i, :, start:stop]
                act(
                    self.copy(
                        block, block, self.p_send.at[p, k, side], self.p_recv.at[p, k, side],
                        {"dp": self.flip(self.d, b)},
                    )
                )

    def along_whole(self, p, k):
        target = self.targets[self.pieces[p][0]]
        out = []
        for side, start, stop in self.sides(p):
            block = target.at[:, pl.ds(0, 2**k), :, start:stop]
            out.append(
                self.copy(
                    block, block, self.p_send.at[p, k, side], self.p_recv.at[p, k, side],
                    {"dp": self.flip(self.d, self.orders[side][k])},
                )
            )
        return out

    def tick(self, p, stage):
        which, start, _, stop = self.pieces[p]
        source, target = self.sources[which], self.targets[which]
        if stage == 0:
            pltpu.make_async_copy(
                source.at[:, start:stop], target.at[self.z, self.d, :, start:stop], self.own.at[p]
            ).start()
            for delta in range(1, self.parts):
                self.copy(
                    source.at[:, start:stop], target.at[self.z, self.d, :, start:stop], self.z_send.at[p],
                    self.z_recv.at[p], {"mp": lax.rem(self.z + delta, self.parts)},
                ).start()
        elif stage == 1:
            pltpu.make_async_copy(
                source.at[:, start:stop], target.at[self.z, self.d, :, start:stop], self.own.at[p]
            ).wait()
            self.z_whole(p).wait_recv()
            self.along(p, 0, lambda copy: copy.start())
            self.to_sibling(p, [self.d], start, stop)
        elif stage <= self.bits:
            k = stage - 2
            for copy in self.along_whole(p, k):
                copy.wait_recv()
            if k + 1 < self.bits - 1:
                self.along(p, k + 1, lambda copy: copy.start())
            for side, low, high in self.sides(p):
                self.to_sibling(p, self.arrived(side, k), low, high)

    def moves(self):
        return len(self.pieces) + STRIDE * (self.ticks - 1)

    def move(self, now):
        for p in range(len(self.pieces)):
            if now >= p and (now - p) % STRIDE == 0 and (now - p) // STRIDE < self.ticks:
                self.tick(p, (now - p) // STRIDE)

    def z_whole(self, p):
        which, start, _, stop = self.pieces[p]
        block = self.targets[which].at[pl.ds(0, self.parts - 1), self.d, :, start:stop]
        return self.copy(
            block, block, self.z_send.at[p], self.z_recv.at[p],
            {"mp": lax.rem(self.z + 1, self.parts)},
        )

    def s_whole(self, p):
        which, start, _, stop = self.pieces[p]
        block = self.targets[which].at[:, pl.ds(0, 2 ** (self.bits - 1)), :, start:stop]
        return self.copy(
            block, block, self.s_send.at[p], self.s_recv.at[p], {"dp": self.flip(self.d, 0)}
        )

    def finish(self, waited=()):
        for p in range(len(self.pieces)):
            if p not in waited:
                self.s_whole(p).wait_recv()
            self.z_whole(p).wait_send()
            for k in range(self.bits - 1):
                for copy in self.along_whole(p, k):
                    copy.wait_send()
            self.s_whole(p).wait_send()


def greet_all(bits, parts, every):
    d, z = lax.axis_index("dp"), lax.axis_index("mp")
    barrier = pltpu.get_barrier_semaphore()
    if every:
        peers = [lax.rem(d + delta, 2**bits) for delta in range(1, 2**bits)]
    else:
        peers = [d + (1 - 2 * lax.rem(lax.div(d, 2**b), 2)) * 2**b for b in range(bits)]
    for peer in peers:
        pl.semaphore_signal(
            barrier, inc=1, device_id={"dp": peer}, device_id_type=pl.DeviceIdType.MESH
        )
    for delta in range(1, parts):
        pl.semaphore_signal(
            barrier, inc=1, device_id={"mp": lax.rem(z + delta, parts)},
            device_id_type=pl.DeviceIdType.MESH,
        )
    pl.semaphore_wait(barrier, len(peers) + parts - 1)


class Swap:
    def __init__(self, groups, source, target, own, send, recv):
        self.groups, self.source, self.target = groups, source, target
        self.own, self.send, self.recv = own, send, recv
        self.d = lax.axis_index("dp")

    def copy(self, src, dst, to):
        return pltpu.make_async_remote_copy(
            src_ref=src, dst_ref=dst, send_sem=self.send, recv_sem=self.recv, device_id={"dp": to},
            device_id_type=pl.DeviceIdType.MESH,
        )

    def local(self):
        return pltpu.make_async_copy(self.source.at[self.d], self.target.at[self.d], self.own)

    def start(self):
        self.local().start()
        for delta in range(1, self.groups):
            to = lax.rem(self.d + delta, self.groups)
            self.copy(self.source.at[to], self.target.at[self.d], to).start()

    def finish(self):
        self.local().wait()
        block = self.target.at[pl.ds(0, self.groups - 1)]
        whole = self.copy(block, block, lax.rem(self.d + 1, self.groups))
        whole.wait_recv()
        whole.wait_send()


def prologue_kernel(bits, parts, pieces, *refs):
    tokens, small, gain, *refs = refs
    members, narrow, refs = refs[:4], refs[4:7], refs[7:]
    tokens_out, joined_out, small_out, raw_out, h1_out, h1t_out = refs[:6]
    padded, refs = refs[6:9], refs[9:]
    member_s, narrow_s, padded_s, refs = refs[:4], refs[4:7], refs[7:10], refs[10:]
    in_sem, out_sem, joined, x_s, w_s, raw_s, x_sem, w_sem, raw_sem, *sems = refs
    loads = [
        pltpu.make_async_copy(src, dst, in_sem.at[i])
        for i, (src, dst) in enumerate(zip((*members, *narrow), (*member_s, *narrow_s)))
    ]
    for load in loads:
        load.start()
    gather = Gather(bits, parts, (joined, small), (joined_out, small_out), pieces, sems[:7])
    swap = Swap(2**bits, tokens, tokens_out, *[s.at[0] for s in sems[7:10]])
    greet_all(bits, parts, True)
    swap.start()
    blocks, rows, width = x_s.shape
    at = 0
    for load in loads[:4]:
        load.wait()
    for h in range(joined.shape[1] // (HEADW + DV)):
        for member, size in zip(member_s, (DK, DK, DV, DV)):
            joined[:, at : at + size] = member[:, h * size : (h + 1) * size]
            at += size

    def put(i):
        return pltpu.make_async_copy(padded_s[i], padded[i], out_sem.at[i])

    def widen():
        for i, (source, target) in enumerate(zip(narrow_s, padded_s)):
            loads[4 + i].wait()
            have, wide = source.shape[0], target.shape[1]
            edge = have // 128 * 128
            target[:, edge:] = jnp.zeros((target.shape[0], wide - edge), BF16)
            target[:, 0:have] = source[...].T
            put(i).start()

    def normalize():
        swap.finish()
        copy = pltpu.make_async_copy(tokens_out, x_s, x_sem.at[0])
        copy.start()
        copy.wait()

        @pl.loop(0, blocks)
        def _(i):
            x = x_s[i].astype(F32)
            scale = lax.rsqrt(jnp.mean(x * x, axis=-1, keepdims=True) + 1e-05)
            h1_out[i] = (x * scale * gain[...]).astype(BF16)

        h1t_out[...] = h1_out[...].reshape(blocks * rows, width).T

    def fetch(p):
        _, start, _, stop = pieces[p]
        return pltpu.make_async_copy(
            joined_out.at[:, :, :, start:stop], w_s.at[p % 2], w_sem.at[p % 2]
        )

    def store(p):
        _, start, _, stop = pieces[p]
        return pltpu.make_async_copy(raw_s.at[p % 2], raw_out.at[:, :, start:stop], raw_sem.at[p % 2])

    main = [p for p, item in enumerate(pieces) if item[0] == 0]

    def project(p):
        if p - 2 in main:
            store(p - 2).wait()
        fetch(p).wait()
        h1 = h1_out[...].reshape(blocks * rows, width)

        @pl.loop(0, parts)
        def _(g):
            raw_s[p % 2, g] = jnp.dot(
                h1, w_s[p % 2, g].reshape(width, WIDE), preferred_element_type=F32
            )

        store(p).start()

    ready = {p + STRIDE * gather.ticks: p for p in main}
    for now in range(max(ready) + 2):
        if now < gather.moves():
            gather.move(now)
        if now == 1:
            widen()
        if now == min(ready):
            normalize()
        if now - 1 in ready:
            project(ready[now - 1])
        if now in ready:
            gather.s_whole(ready[now]).wait_recv()
            fetch(ready[now]).start()
    gather.finish(main)
    for p in main[-2:]:
        store(p).wait()
    for i in range(3):
        put(i).wait()


def prologue(tokens, small, gain, members, narrow, groups, parts):
    bits = groups.bit_length() - 1
    rows = members[0].shape[0]
    wide = sum(w.shape[1] for w in members)
    padded = -(-narrow[0].shape[0] // WIDE) * WIDE
    blocks, token_rows, width = tokens.shape
    pieces = [(1, 0, small.shape[1], small.shape[1])]
    pieces += [(0, at, at + WIDE // 2, at + WIDE) for at in range(0, wide, WIDE)]
    length = blocks * token_rows
    any_spec = pl.BlockSpec(memory_space=pl.ANY)
    vmem_spec = pl.BlockSpec(memory_space=pltpu.VMEM)
    dma = lambda *shape: pltpu.SemaphoreType.DMA(shape)
    return pl.pallas_call(
        partial(prologue_kernel, bits, parts, pieces),
        out_shape=(
            jax.ShapeDtypeStruct(tokens.shape, BF16),
            jax.ShapeDtypeStruct((parts, groups, rows, wide), BF16),
            jax.ShapeDtypeStruct((parts, groups) + small.shape, BF16),
            jax.ShapeDtypeStruct((parts, length, wide), F32),
            jax.ShapeDtypeStruct(tokens.shape, BF16),
            jax.ShapeDtypeStruct((width, length), BF16),
            *[jax.ShapeDtypeStruct((rows, padded), BF16)] * 3,
        ),
        in_specs=[any_spec] * 2 + [vmem_spec] + [any_spec] * 7,
        out_specs=(any_spec,) * 4 + (vmem_spec,) * 2 + (any_spec,) * 3,
        scratch_shapes=[
            *[pltpu.VMEM(w.shape, BF16) for w in (*members, *narrow)],
            *[pltpu.VMEM((rows, padded), BF16)] * 3,
            dma(7), dma(3),
            pltpu.VMEM((rows, wide), BF16),
            pltpu.VMEM(tokens.shape, BF16),
            pltpu.VMEM((2, parts, groups, rows, WIDE), BF16),
            pltpu.VMEM((2, parts, length, WIDE), F32),
            dma(1), dma(2), dma(2),
            *Gather.scratch(bits, len(pieces)),
            dma(1), dma(1), dma(1),
        ],
        compiler_params=pltpu.CompilerParams(
            collective_id=3, has_side_effects=True, vmem_limit_bytes=62 * 2**20
        ),
        cost_estimate=pl.CostEstimate(
            flops=2 * length * width * wide * parts, bytes_accessed=40 * 2**20, transcendentals=0
        ),
        name="prologue",
    )(tokens, small, gain, *members, *narrow)


def forward_kernel(
    heads, parts, bits, pieces,
    raw_ref, gate_ref, raw_any, convw_ref, ab_ref, gain_ref, *refs,
):
    weights = len({item[0] for item in pieces})
    swap_in, sources, refs = refs[0], refs[1 : 1 + weights], refs[1 + weights :]
    head_ref, o_ref, s_ref, t_ref, qe_ref, phi_ref, phil_ref, halo_ref = refs[:8]
    swap_out, targets, refs = refs[8], refs[9 : 9 + weights], refs[9 + weights :]
    (qe_s, o0_s, phi_s, b_s, phil_s, bl_s, send_s, recv_s, halo_s, ext_s,
     send_sem, recv_sem, halo_send_sem, halo_recv_sem) = refs[:14]
    swap = Swap(2**bits, swap_in, swap_out, *[s.at[0] for s in refs[14:17]])
    gather = Gather(bits, parts, sources, targets, pieces, refs[17:])
    step = pl.program_id(0)
    early = pl.program_id(1) == 0
    z = lax.axis_index("mp")
    lag = parts - 1
    slots = lag + 1
    length = gate_ref.shape[1]
    size = min(CHUNK, length)
    chunks = length // size
    per = heads // parts

    @pl.when((step == 0) & early)
    def _():
        greet_all(bits, parts, True)
        swap.start()

    last = 2 * (heads + lag) - 1
    for now in range(min(gather.moves(), last)):
        @pl.when(step * 2 + pl.program_id(1) == now)
        def _():
            gather.move(now)

    @pl.when(step * 2 + pl.program_id(1) == last)
    def _():
        for now in range(last, gather.moves()):
            gather.move(now)

    def hop(h):
        return pltpu.make_async_remote_copy(
            src_ref=send_s.at[h], dst_ref=recv_s.at[h], send_sem=send_sem.at[h],
            recv_sem=recv_sem.at[h], device_id={"mp": lax.rem(z + 1, parts)},
            device_id_type=pl.DeviceIdType.MESH,
        )

    def halo_hop(g):
        return pltpu.make_async_remote_copy(
            src_ref=raw_any.at[g, length - HALO :], dst_ref=halo_s.at[g], send_sem=halo_send_sem.at[g],
            recv_sem=halo_recv_sem.at[g], device_id={"mp": lax.rem(z + 1, parts)},
            device_id_type=pl.DeviceIdType.MESH,
        )

    @pl.when((step == 0) & early & (z == 0))
    def _():
        recv_s[...] = jnp.zeros_like(recv_s)
        halo_s[...] = jnp.zeros_like(halo_s)

    @pl.when((step == 0) & early & (z < parts - 1))
    def _():
        for g in range(parts):
            halo_hop(g).start()

    @pl.when((step < heads) & early)
    def _():
        slot = lax.rem(step, slots)
        part, sub = lax.div(step, per), lax.rem(step, per)

        @pl.when((sub == 0) & (z > 0))
        def _():
            halo_hop(part).wait_recv()

        for k in range(per):
            @pl.when(sub == k)
            def _():
                ext_s[0:HALO] = halo_s[part, :, k * (HEADW + DV) : k * (HEADW + DV) + HEADW]

        ext_s[HALO:] = raw_ref[0, 0:size, 0:HEADW]
        rows, cols = masks(size)
        upper = (rows <= cols).astype(F32)
        convw = convw_ref[0]
        kept = []
        lowers = []
        for c in range(chunks):
            conv = conv_of(windows(raw_ref, ext_s, c, size), convw)
            _, q_silu, k_silu, value, q_scale, k_scale = unit_parts(conv)
            query = q_silu * (q_scale * DK ** (-0.5))
            keyed = k_silu * k_scale
            gamma_row, gamma_col, beta = decays(ab_ref, c * size, size, upper)
            inclusive, strict = fades(gamma_row, gamma_col, rows, cols)
            gram = mm(jnp.concatenate([keyed, query], axis=0), keyed, 1, 1)
            lowers.append(beta * gram[:size] * strict)
            scores = gram[size:] * inclusive
            growth = jnp.exp(gamma_col)
            last = gamma_row[:, size - 1 :]
            rhs = jnp.concatenate([(beta * growth) * keyed, beta * value], axis=1)
            kept.append((scores, rhs, query * growth, keyed * jnp.exp(last - gamma_col), last))
        inverses = invert_many(lowers, rows, cols)
        eye = (masks(DK)[0] == masks(DK)[1]).astype(F32)
        phi_all = None
        b_all = None
        for c in range(chunks):
            scores, rhs, query_g, keyed_g, last = kept[c]
            t_ref[0, c] = inverses[c]
            solved = mm(inverses[c], rhs)
            mixed = mm(scores, solved)
            moved = mm(keyed_g, solved, 0, 0)
            query_e = query_g - mixed[:, :DK]
            phi = jnp.exp(last) * eye - moved[:, :DK]
            inflow = moved[:, DK:]
            qe_ref[0, c * size : (c + 1) * size] = query_e
            qe_s[slot, c * size : (c + 1) * size] = query_e
            o0_s[slot, c * size : (c + 1) * size] = mixed[:, DK:]
            phi_ref[0, c] = phi.T
            phi_s[slot, c] = phi
            b_s[slot, c] = inflow
            if c == 0:
                phi_all, b_all = phi, inflow
            else:
                moved_all = mm(phi, jnp.concatenate([phi_all, b_all], axis=1))
                phi_all = moved_all[:, :DK]
                b_all = moved_all[:, DK:] + inflow
        phil_ref[0] = phi_all.T
        phil_s[slot] = phi_all
        bl_s[slot] = b_all

    relay = step - z

    @pl.when((relay >= 0) & (relay < heads) & ~early)
    def _():
        slot = lax.rem(relay, slots)

        @pl.when(z > 0)
        def _():
            hop(relay).wait_recv()

        @pl.when(z < parts - 1)
        def _():
            send_s[relay] = mm(phil_s[slot], recv_s[relay]) + bl_s[slot]
            hop(relay).start()

    @pl.when((step >= lag) & ~early)
    def _():
        head = step - lag
        slot = lax.rem(head, slots)
        state = recv_s[head]
        for c in range(chunks):
            at = slice(c * size, (c + 1) * size)
            s_ref[0, c] = state
            result = mm(qe_s[slot, at], state) + o0_s[slot, at]
            if c + 1 < chunks:
                state = mm(phi_s[slot, c], state) + b_s[slot, c]
            o_ref[0, at] = result
            scale = lax.rsqrt(jnp.mean(result * result, axis=-1, keepdims=True) + 1e-05)
            gate = gate_ref[0, c * size : (c + 1) * size]
            gated = result * scale * gain_ref[...] * (gate * jax.nn.sigmoid(gate))
            head_ref[0, at] = gated.astype(BF16)

    @pl.when((step == pl.num_programs(0) - 1) & ~early & (z < parts - 1))
    def _():
        @pl.loop(0, heads)
        def _(h):
            hop(h).wait_send()

        for g in range(parts):
            halo_hop(g).wait_send()

    @pl.when((step == pl.num_programs(0) - 1) & ~early)
    def _():
        halo_ref[...] = halo_s[...]
        gather.finish()
        swap.finish()


class Scatter:
    def __init__(self, bits, parts, plan, rows, lhs_refs, rhs_refs, out_ref, scratch, stride):
        self.stride = stride
        self.bits, self.parts, self.plan, self.rows = bits, parts, plan, rows
        self.lhs_refs, self.rhs_refs, self.out_ref = lhs_refs, rhs_refs, out_ref
        self.count = len(plan)
        self.planes = planes = bits - 1
        self.half = 2 ** (bits - 1)
        self.lhs_s, self.rhs_s, self.grad_s, self.r1, *rest = scratch
        self.ra, self.rb = rest[:planes], rest[planes : 2 * planes]
        (self.r4, self.load_sem, self.send1, self.recv1, self.send_a, self.recv_a, self.send_b,
         self.recv_b, self.send4, self.recv4) = rest[2 * planes :]
        self.d, self.z = lax.axis_index("dp"), lax.axis_index("mp")
        self.ticks = self.count + 1 + self.stride * (planes + 1)

    @staticmethod
    def scratch(bits, parts, count, rows, length, width):
        planes, half = bits - 1, 2 ** (bits - 1)
        vmem = lambda *shape: pltpu.VMEM(shape, BF16)
        dma = lambda *shape: pltpu.SemaphoreType.DMA(shape)
        strips = [vmem(count, parts, half >> (k + 1), rows, WIDE // 2) for k in range(planes)]
        return [
            vmem(2, width, length),
            vmem(2, parts, length, WIDE),
            vmem(2, parts, half, 2, rows, WIDE),
            vmem(count, parts, half, rows, WIDE),
            *strips, *strips,
            vmem(count, parts - 1, rows, WIDE),
            dma(2, 2),
            dma(count), dma(count),
            dma(planes, count), dma(planes, count),
            dma(planes, count), dma(planes, count),
            dma(count), dma(count),
        ]

    def bit(self, b):
        return lax.rem(lax.div(self.d, 2**b), 2)

    def partner(self, b):
        return self.d + (1 - 2 * self.bit(b)) * 2**b

    def remote(self, src, dst, send, recv, to):
        return pltpu.make_async_remote_copy(
            src_ref=src, dst_ref=dst, send_sem=send, recv_sem=recv, device_id=to,
            device_id_type=pl.DeviceIdType.MESH,
        )

    def load(self, t):
        slot = lax.rem(t, 2)
        for seg in range(len(self.rhs_refs)):
            at = [k for k, item in enumerate(self.plan) if item[0] == seg]

            @pl.when((t >= at[0]) & (t <= at[-1]))
            def _():
                start = pl.multiple_of((t - at[0]) * WIDE, WIDE)
                pltpu.make_async_copy(
                    self.rhs_refs[seg].at[:, :, pl.ds(start, WIDE)], self.rhs_s.at[slot],
                    self.load_sem.at[0, slot],
                ).start()
                pltpu.make_async_copy(
                    self.lhs_refs[self.plan[at[0]][1]], self.lhs_s.at[slot], self.load_sem.at[1, slot]
                ).start()

    def load_wait(self, t):
        slot = lax.rem(t, 2)
        pltpu.make_async_copy(
            self.rhs_refs[0].at[:, :, pl.ds(0, WIDE)], self.rhs_s.at[slot], self.load_sem.at[0, slot]
        ).wait()
        pltpu.make_async_copy(
            self.lhs_refs[0], self.lhs_s.at[slot], self.load_sem.at[1, slot]
        ).wait()

    def first_hop(self, t):
        return self.remote(
            self.grad_s.at[lax.rem(t, 2), :, :, 1 - self.bit(0)], self.r1.at[t], self.send1.at[t],
            self.recv1.at[t], {"dp": self.partner(0)},
        )

    def a_hop(self, k, t):
        b = self.bits - 1 - k
        keep = self.half >> (k + 1)
        away = pl.ds((1 - self.bit(b)) * keep, keep)
        src = self.r1.at[t, :, away, :, 0 : WIDE // 2] if k == 0 else self.ra[k - 1].at[t, :, away]
        return self.remote(
            src, self.ra[k].at[t], self.send_a.at[k, t], self.recv_a.at[k, t], {"dp": self.partner(b)}
        )

    def b_hops(self, k, t):
        b = 1 + k
        copies = []
        for hi in range(self.half >> (k + 1)):
            away = 2 * hi + 1 - self.bit(b)
            src = self.r1.at[t, :, away, :, WIDE // 2 :] if k == 0 else self.rb[k - 1].at[t, :, away]
            copies.append(
                self.remote(
                    src, self.rb[k].at[t, :, hi], self.send_b.at[k, t], self.recv_b.at[k, t],
                    {"dp": self.partner(b)},
                )
            )
        return copies

    def b_whole(self, k, t):
        return self.remote(
            self.rb[k].at[t], self.rb[k].at[t], self.send_b.at[k, t], self.recv_b.at[k, t],
            {"dp": self.partner(1 + k)},
        )

    def z_hops(self, t):
        copies = []
        side = WIDE // 2
        for delta in range(1, self.parts):
            to = lax.rem(self.z + delta, self.parts)
            for i, buf in enumerate((self.ra[self.planes - 1], self.rb[self.planes - 1])):
                copies.append(
                    self.remote(
                        buf.at[t, to, 0],
                        self.r4.at[t, self.parts - 1 - delta, :, i * side : (i + 1) * side],
                        self.send4.at[t], self.recv4.at[t], {"mp": to},
                    )
                )
        return copies

    def z_whole(self, t):
        return self.remote(
            self.r4.at[t], self.r4.at[t], self.send4.at[t], self.recv4.at[t],
            {"mp": lax.rem(self.z + 1, self.parts)},
        )

    def tick(self, tick):
        count, planes, half, parts = self.count, self.planes, self.half, self.parts
        side = WIDE // 2

        @pl.when(tick == 0)
        def _():
            self.load(tick)

        t = tick - 1 - self.stride * (planes + 1)

        @pl.when((t >= 0) & (t < count))
        def _():
            self.z_whole(t).wait_recv()
            left = self.ra[planes - 1][t, self.z, 0].astype(F32)
            right = self.rb[planes - 1][t, self.z, 0].astype(F32)
            for s in range(parts - 1):
                left = left + self.r4[t, s, :, 0:side].astype(F32)
                right = right + self.r4[t, s, :, side:].astype(F32)
            self.out_ref[t, :, 0:side] = left
            self.out_ref[t, :, side:] = right

        for k in range(planes - 1, -1, -1):
            t_k = tick - 1 - self.stride * (k + 1)

            @pl.when((t_k >= 0) & (t_k < count))
            def _():
                self.a_hop(k, t_k).wait_recv()
                self.b_whole(k, t_k).wait_recv()
                keep = half >> (k + 1)
                bit_a, bit_b = self.bit(self.bits - 1 - k), self.bit(1 + k)
                for m in range(keep):
                    own_a, own_b = bit_a * keep + m, 2 * m + bit_b
                    for j in range(parts):
                        if k == 0:
                            mine_a = self.r1[t_k, j, own_a, :, 0:side]
                            mine_b = self.r1[t_k, j, own_b, :, side:]
                        else:
                            mine_a = self.ra[k - 1][t_k, j, own_a]
                            mine_b = self.rb[k - 1][t_k, j, own_b]
                        for buf, mine in ((self.ra[k], mine_a), (self.rb[k], mine_b)):
                            buf[t_k, j, m] = (buf[t_k, j, m].astype(F32) + mine.astype(F32)).astype(BF16)
                if k + 1 < planes:
                    self.a_hop(k + 1, t_k).start()
                    for copy in self.b_hops(k + 1, t_k):
                        copy.start()
                else:
                    for copy in self.z_hops(t_k):
                        copy.start()

        t_1 = tick - 1

        @pl.when((t_1 >= 0) & (t_1 < count))
        def _():
            self.first_hop(t_1).wait_recv()
            slot = lax.rem(t_1, 2)
            color = self.bit(0)

            @pl.loop(0, parts)
            def _(j):
                for m in range(half):
                    self.r1[t_1, j, m] = (
                        self.r1[t_1, j, m].astype(F32) + self.grad_s[slot, j, m, color].astype(F32)
                    ).astype(BF16)

            self.a_hop(0, t_1).start()
            for copy in self.b_hops(0, t_1):
                copy.start()

        @pl.when(tick < count)
        def _():
            slot = lax.rem(tick, 2)

            @pl.when(tick + 1 < count)
            def _():
                self.load(tick + 1)

            self.load_wait(tick)

            @pl.when(tick >= 2)
            def _():
                self.first_hop(tick - 2).wait_send()

            @pl.loop(0, parts)
            def _(j):
                full = jnp.dot(self.lhs_s[slot], self.rhs_s[slot, j], preferred_element_type=F32)
                self.grad_s[slot, j] = full.astype(BF16).reshape(half, 2, self.rows, WIDE)

            self.first_hop(tick).start()

    def finish(self):
        for t in range(max(self.count - 2, 0), self.count):
            self.first_hop(t).wait_send()

        @pl.loop(0, self.count)
        def _(t):
            for k in range(self.planes):
                self.a_hop(k, t).wait_send()
                self.b_whole(k, t).wait_send()
            self.z_whole(t).wait_send()


def plan_of(pairs):
    plan = []
    for seg, (kind, right) in enumerate(pairs):
        plan += [(seg, kind)] * (right.shape[2] // WIDE)
    return plan


def small_rows(heads, width, smalls):
    starts = [0]
    for count in (width // 128, width // 128, DV // 128, heads * TAPS * HEADW // 128, 1, smalls * width // 128):
        starts.append(starts[-1] + count)
    return starts, -(-starts[-1] // 8) * 8


def scatter_kernel(bits, parts, plan, rows, lhs_ref, *refs):
    sources = len({item[0] for item in plan})
    rhs_refs, refs = refs[:sources], refs[sources:]
    (ffn_ref, hgain_ref, conv_ref, line_ref, w_ref, d_small, w_small, x_ref, dx1_ref, gain_ref, out_ref, vec_out,
     g_out) = refs[:13]
    refs = refs[3:]
    v_own, v_acc, v_in, v_z, v_send, v_recv, v_z_send, v_z_recv = refs[10:18]
    swap_own, swap_send, swap_recv = refs[18:21]
    dp_s, w_s, acc_s, dx_s, in_sem = refs[21:26]
    scatter = Scatter(bits, parts, plan, rows, [lhs_ref], rhs_refs, out_ref, refs[26:], STRIDE)
    z = lax.axis_index("mp")
    mesh_id = pl.DeviceIdType.MESH
    greet_all(bits, parts, True)
    swap = Swap(2**bits, dx_s, g_out, swap_own.at[0], swap_send.at[0], swap_recv.at[0])

    def v_hop(b):
        return pltpu.make_async_remote_copy(
            src_ref=v_own if b == 0 else v_acc.at[b - 1], dst_ref=v_in.at[b], send_sem=v_send.at[b],
            recv_sem=v_recv.at[b], device_id={"dp": scatter.partner(b)}, device_id_type=mesh_id,
        )

    def v_z_hop(src, dst, delta):
        return pltpu.make_async_remote_copy(
            src_ref=src, dst_ref=dst, send_sem=v_z_send.at[0], recv_sem=v_z_recv.at[0],
            device_id={"mp": lax.rem(z + delta, parts)}, device_id_type=mesh_id,
        )

    def small_sum(stage):
        if stage == 0:
            v_hop(0).start()
        elif stage <= bits:
            b = stage - 1
            v_hop(b).wait_recv()
            total = (v_own[...] if b == 0 else v_acc[b - 1]) + v_in[b]
            if stage < bits:
                v_acc[b] = total
                v_hop(stage).start()
            else:
                v_z[z] = total
                for delta in range(1, parts):
                    v_z_hop(v_z.at[z], v_z.at[z], delta).start()
        else:
            whole = v_z.at[pl.ds(0, parts - 1)]
            v_z_hop(whole, whole, 1).wait_recv()
            total = v_z[0]
            for s in range(1, parts):
                total = total + v_z[s]
            vec_out[...] = total
            for b in range(bits):
                v_hop(b).wait_send()
            v_z_hop(whole, whole, 1).wait_send()

    def fetch(g, slot):
        return (
            pltpu.make_async_copy(rhs_refs[0].at[g], dp_s.at[slot], in_sem.at[0, slot]),
            pltpu.make_async_copy(w_ref.at[g], w_s.at[slot], in_sem.at[1, slot]),
        )

    def input_grad():
        acc_s[...] += lax.dot_general(
            d_small[...], w_small[...], (((0,), (0,)), ((), ())), preferred_element_type=F32
        )
        blocks, token_rows, width = x_ref.shape

        def body(i, gain_sum):
            x = x_ref[i].astype(F32)
            scale = lax.rsqrt(jnp.mean(x * x, axis=-1, keepdims=True) + 1e-05)
            unit = x * scale
            at = pl.ds(pl.multiple_of(i * token_rows, token_rows), token_rows)
            d_h1 = acc_s[at]
            e = d_h1 * gain_ref[...]
            d_x = dx1_ref[at] + scale * (e - unit * jnp.mean(e * unit, axis=-1, keepdims=True))
            dx_s[i] = d_x.astype(BF16)
            return gain_sum + jnp.sum(d_h1 * unit, axis=0, keepdims=True)

        gain_sum = lax.fori_loop(0, blocks, body, jnp.zeros((1, width), F32))
        starts, _ = small_rows(conv_ref.shape[0], width, d_small.shape[0])

        def put(start, row):
            for i in range(row.shape[1] // 128):
                v_own[start + i : start + i + 1] = row[:, i * 128 : (i + 1) * 128]

        put(starts[0], gain_sum)
        put(starts[1], ffn_ref[...])
        put(starts[2], hgain_ref[...])
        for h in range(conv_ref.shape[0]):
            for tap in range(TAPS):
                put(starts[3] + (h * TAPS + tap) * HEADW // 128, conv_ref[h, tap : tap + 1])
        put(starts[4], line_ref[...])
        small_grad = lax.dot_general(
            d_small[...], scatter.lhs_s[0], (((1,), (1,)), ((), ())), preferred_element_type=F32
        )
        for i in range(d_small.shape[0]):
            put(starts[5] + i * width // 128, small_grad[i : i + 1])
        if starts[6] < v_own.shape[0]:
            v_own[starts[6] :] = jnp.zeros((v_own.shape[0] - starts[6], 128), F32)

    for copy in fetch(0, 0):
        copy.start()

    @pl.loop(0, max(scatter.ticks, 2 + parts + bits + 2))
    def _(now):
        scatter.tick(now)
        tick = now - 2

        @pl.when((tick >= 0) & (tick < parts))
        def _():
            slot = lax.rem(tick, 2)

            @pl.when(tick + 1 < parts)
            def _():
                for copy in fetch(tick + 1, 1 - slot):
                    copy.start()

            for copy in fetch(tick, slot):
                copy.wait()
            part = lax.dot_general(
                dp_s[slot], w_s[slot], (((1,), (1,)), ((), ())), preferred_element_type=F32
            )

            @pl.when(tick == 0)
            def _():
                acc_s[...] = part

            @pl.when(tick > 0)
            def _():
                acc_s[...] += part

        @pl.when(tick == parts)
        def _():
            input_grad()
            swap.start()

        for stage in range(bits + 2):
            @pl.when(tick == parts + stage)
            def _():
                small_sum(stage)

    swap.finish()
    scatter.finish()


def scatter_sum(left, pairs, smalls, weight, d_small, w_small, x, d_x1, gain, groups, parts, collective):
    width, length = left.shape
    vector = jax.ShapeDtypeStruct((small_rows(smalls[2].shape[0], width, d_small.shape[0])[1], 128), F32)
    bits = groups.bit_length() - 1
    rows = width // groups
    plan = plan_of(pairs)
    count = len(plan)
    vmem_spec = pl.BlockSpec(memory_space=pltpu.VMEM)
    any_spec = pl.BlockSpec(memory_space=pl.ANY)
    dma = lambda *shape: pltpu.SemaphoreType.DMA(shape)
    return pl.pallas_call(
        partial(scatter_kernel, bits, parts, plan, rows),
        out_shape=(
            jax.ShapeDtypeStruct((count, rows, WIDE), F32),
            jax.ShapeDtypeStruct(vector.shape, F32),
            jax.ShapeDtypeStruct(x.shape, BF16),
        ),
        in_specs=[any_spec] * (1 + len(pairs)) + [vmem_spec] * 4 + [any_spec] + [vmem_spec] * 5,
        out_specs=(vmem_spec, vmem_spec, any_spec),
        scratch_shapes=[
            pltpu.VMEM(vector.shape, F32),
            pltpu.VMEM((bits - 1,) + vector.shape, F32),
            pltpu.VMEM((bits,) + vector.shape, F32),
            pltpu.VMEM((parts,) + vector.shape, F32),
            dma(bits), dma(bits), dma(1), dma(1),
            dma(1), dma(1), dma(1),
            pltpu.VMEM((2,) + pairs[0][1].shape[1:], BF16),
            pltpu.VMEM((2,) + weight.shape[1:], BF16),
            pltpu.VMEM((length, width), F32),
            pltpu.VMEM(x.shape, BF16),
            dma(2, 2),
            *Scatter.scratch(bits, parts, count, rows, length, width),
        ],
        compiler_params=pltpu.CompilerParams(
            collective_id=collective, has_side_effects=True, vmem_limit_bytes=60 * 2**20
        ),
        cost_estimate=pl.CostEstimate(
            flops=4 * count * WIDE * parts * length * width, bytes_accessed=count * parts * length * WIDE * 4,
            transcendentals=0,
        ),
        name="scatter_sum",
    )(left, *[right for _, right in pairs], *smalls, weight, d_small, w_small, x, d_x1, gain)


def backward_kernel(
    heads, parts, bits, plan, rows_held,
    dhead_ref, o_ref, gate_ref, qe_ref, phi_ref, phil_ref,
    raw_ref, halo_ref, convw_ref, ab_ref, gain_ref, s_ref, t_ref, phi_late_ref, *refs,
):
    sources = len({item[0] for item in plan})
    kinds = len({item[1] for item in plan})
    lhs_refs, refs = refs[:kinds], refs[kinds:]
    rhs_refs, swap_in, refs = refs[:sources], refs[sources], refs[sources + 1 :]
    dproj_ref, dab_ref, dconv_ref, dgain_ref, sums_ref, swap_out = refs[:6]
    (do_s, d_s, dgate_s, dl_s, phil_s, g_s, dext_s, ext_s, send_s, recv_s, halo_send, halo_recv,
     send_sem, recv_sem, halo_send_sem, halo_recv_sem) = refs[6:22]
    scatter = Scatter(bits, parts, plan, rows_held, lhs_refs, rhs_refs, sums_ref, refs[25:], 3)
    swap = Swap(2**bits, swap_in, swap_out, *[s.at[0] for s in refs[22:25]])
    step = pl.program_id(0)
    early = pl.program_id(1) == 0
    z = lax.axis_index("mp")
    back = parts - 1 - z
    lag = parts - 1
    slots = lag + 1
    length = o_ref.shape[1]
    size = min(CHUNK, length)
    chunks = length // size

    @pl.when((step == 0) & early)
    def _():
        greet_all(bits, parts, True)
        swap.start()

    sub = pl.program_id(1)
    now = jnp.where(step < lag, step, lag + 2 * (step - lag) + sub)
    last = lag + 2 * (heads + 1) - 1
    stop = jnp.where(now == last, max(scatter.ticks, last + 1), now + 1)
    stop = jnp.where((step < lag) & early, now, stop)

    @pl.loop(now, stop)
    def _(tick):
        scatter.tick(tick)


    def hop(h):
        return pltpu.make_async_remote_copy(
            src_ref=send_s.at[h], dst_ref=recv_s.at[h], send_sem=send_sem.at[h],
            recv_sem=recv_sem.at[h], device_id={"mp": lax.rem(z + parts - 1, parts)},
            device_id_type=pl.DeviceIdType.MESH,
        )

    def halo_hop(h):
        return pltpu.make_async_remote_copy(
            src_ref=halo_send.at[h], dst_ref=halo_recv.at[h], send_sem=halo_send_sem.at[h],
            recv_sem=halo_recv_sem.at[h], device_id={"mp": lax.rem(z + parts - 1, parts)},
            device_id_type=pl.DeviceIdType.MESH,
        )

    @pl.when((step == 0) & early)
    def _():
        dgain_ref[...] = jnp.zeros_like(dgain_ref)
        g_s[...] = jnp.zeros_like(g_s)

    @pl.when((step == 0) & early & (back == 0))
    def _():
        recv_s[...] = jnp.zeros_like(recv_s)
        halo_recv[...] = jnp.zeros_like(halo_recv)

    @pl.when((step < heads) & early)
    def _():
        slot = lax.rem(step, slots)
        gslot = lax.rem(step, slots + 1)
        gain = gain_ref[...]
        d_gain = jnp.zeros((1, DV), F32)
        for c in range(chunks):
            at = slice(c * size, (c + 1) * size)
            out = o_ref[0, at]
            d_head = dhead_ref[0, at]
            gate = gate_ref[0, c * size : (c + 1) * size]
            scale = lax.rsqrt(jnp.mean(out * out, axis=-1, keepdims=True) + 1e-05)
            unit = out * scale
            sig = jax.nn.sigmoid(gate)
            gated = gate * sig
            both = d_head * unit
            d_gain = d_gain + jnp.sum(both * gated, axis=0, keepdims=True)
            e = d_head * gated * gain
            d_out = scale * (e - unit * jnp.mean(e * unit, axis=-1, keepdims=True))
            dgate_s[gslot, at] = (both * gain * sig * (1.0 + gate * (1.0 - sig))).astype(BF16)
            do_s[slot, at] = d_out
            d_s[slot, c] = mm(qe_ref[0, at], d_out, 0, 0)
        dgain_ref[...] += d_gain
        total = d_s[slot, chunks - 1]
        for c in range(chunks - 2, -1, -1):
            total = mm(phi_ref[0, c], total) + d_s[slot, c]
        dl_s[slot] = total
        phil_s[slot] = phil_ref[0]

    relay = step - back

    @pl.when((relay >= 0) & (relay < heads) & early)
    def _():
        slot = lax.rem(relay, slots)

        @pl.when(back > 0)
        def _():
            hop(relay).wait_recv()

        @pl.when(z > 0)
        def _():
            send_s[relay] = mm(phil_s[slot], recv_s[relay]) + dl_s[slot]
            hop(relay).start()

    @pl.when((step >= lag) & (step < lag + heads) & ~early)
    def _():
        head = step - lag
        slot = lax.rem(head, slots)
        eslot = lax.rem(head, 2)
        rows, cols = masks(size)
        upper = (rows <= cols).astype(F32)
        convw = convw_ref[0]
        d_state = recv_s[head]
        ext_s[0:HALO] = halo_ref[0, :, 0:HEADW]
        ext_s[HALO:] = raw_ref[0, 0:size, 0:HEADW]
        d_conv_rows = [jnp.zeros((1, HEADW), F32) for _ in range(TAPS)]
        for c in range(chunks - 1, -1, -1):
            at = slice(c * size, (c + 1) * size)
            shifted = windows(raw_ref, ext_s, c, size)
            conv = conv_of(shifted, convw)
            sig, q_silu, k_silu, value, q_scale, k_scale = unit_parts(conv)
            query = q_silu * (q_scale * DK ** (-0.5))
            keyed = k_silu * k_scale
            gamma_row, gamma_col, beta = decays(ab_ref, c * size, size, upper)
            inclusive, strict = fades(gamma_row, gamma_col, rows, cols)
            gram = mm(jnp.concatenate([keyed, query], axis=0), keyed, 1, 1)
            gram_f = gram[:size] * strict
            lower = beta * gram_f
            scores = gram[size:] * inclusive
            growth = jnp.exp(gamma_col)
            last = gamma_row[:, size - 1 :]
            tail = jnp.exp(last - gamma_col)
            query_g = query * growth
            grown = keyed * growth
            keyed_b = beta * grown
            keyed_g = keyed * tail
            state = s_ref[0, c]
            inverse = t_ref[0, c]
            d_out = do_s[slot, at]
            fresh = mm(inverse, beta * value - mm(keyed_b, state))
            d_fresh = mm(scores, d_out, 0, 0) + mm(keyed_g, d_state)
            d_rhs = mm(inverse, d_fresh, 0, 0)
            stacked = jnp.concatenate([d_out, d_rhs], axis=0)
            by_fresh = mm(stacked, fresh, 1, 1)
            by_state = mm(stacked, state, 1, 1)
            d_scores = by_fresh[:size] * inclusive
            d_lower = -by_fresh[size:]
            d_query_g = by_state[:size]
            d_keyed_b = -by_state[size:]
            d_keyed_g = mm(fresh, d_state, 1, 1)
            d_gram = d_lower * (beta * strict)
            by_keyed = mm(jnp.concatenate([d_scores, d_gram], axis=0), keyed)
            d_query = by_keyed[:size] + growth * d_query_g
            d_keyed = (
                by_keyed[size:]
                + mm(jnp.concatenate([d_scores, d_gram], axis=0),
                     jnp.concatenate([query, keyed], axis=0), 0, 0)
                + (beta * growth) * d_keyed_b
                + tail * d_keyed_g
            )
            d_value = beta * d_rhs
            d_beta = (
                jnp.sum(d_rhs * value, axis=-1, keepdims=True)
                + jnp.sum(d_lower * gram_f, axis=-1, keepdims=True)
                + jnp.sum(d_keyed_b * grown, axis=-1, keepdims=True)
            )
            moved = by_fresh[:size] * scores + d_lower * lower
            tail_part = jnp.sum(d_keyed_g * keyed_g, axis=-1, keepdims=True)
            d_gamma = (
                jnp.sum(moved, axis=-1, keepdims=True)
                + jnp.sum(d_query_g * query_g, axis=-1, keepdims=True)
                + jnp.sum(d_keyed_b * keyed_b, axis=-1, keepdims=True)
                - tail_part
            )
            at_end = jnp.sum(tail_part, axis=0, keepdims=True) + jnp.exp(last) * jnp.sum(
                jnp.sum(state * d_state, axis=-1, keepdims=True), axis=0, keepdims=True
            )
            lanes = lax.broadcasted_iota(jnp.int32, (size, DK), 1)
            packed = jnp.where(lanes == 0, d_gamma, jnp.where(lanes == 1, d_beta, 0.0)).T[:8]
            row_id = lax.broadcasted_iota(jnp.int32, packed.shape, 0)
            packed = packed - jnp.where(row_id == 0, jnp.sum(moved, axis=0, keepdims=True), 0.0)
            summed = mm(packed, upper, 1, 1) + at_end
            dab_ref[0, :, at] = jnp.where(row_id == 0, summed, packed)
            if c > 0:
                d_state = mm(phi_late_ref[0, c], d_state) + d_s[slot, c]
            d_q_silu = (DK ** (-0.5) * q_scale) * (
                d_query
                - q_silu * (q_scale * q_scale) * jnp.sum(q_silu * d_query, axis=-1, keepdims=True)
            )
            d_k_silu = k_scale * (
                d_keyed
                - k_silu * (k_scale * k_scale) * jnp.sum(k_silu * d_keyed, axis=-1, keepdims=True)
            )
            d_silu = jnp.concatenate([d_q_silu, d_k_silu, d_value], axis=1)
            d_conv = d_silu * sig * (1.0 + conv * (1.0 - sig))
            g_s[HALO + c * size : HALO + (c + 1) * size] = d_conv
            for i in range(TAPS):
                d_conv_rows[i] = d_conv_rows[i] + jnp.sum(shifted[i] * d_conv, axis=0, keepdims=True)
        for i in range(TAPS):
            dconv_ref[0, i : i + 1] = d_conv_rows[i]
        for base, count in [(0, HALO)] + [(HALO + c * size, size) for c in range(chunks)]:
            d_raw = None
            for i in range(TAPS):
                part = g_s[pl.ds(base + TAPS - 1 - i, count)] * convw[i : i + 1]
                d_raw = part if d_raw is None else d_raw + part
            if base == 0:
                halo_send[head] = d_raw
            else:
                dext_s[eslot, base - HALO : base - HALO + count] = d_raw

        @pl.when(z > 0)
        def _():
            halo_hop(head).start()

    @pl.when((step > lag) & ~early)
    def _():
        head = step - lag - 1
        eslot = lax.rem(head, 2)
        gslot = lax.rem(head, slots + 1)

        @pl.when(back > 0)
        def _():
            halo_hop(head).wait_recv()

        dext_s[eslot, length - HALO : length] += halo_recv[head]
        dproj_ref[0, :, 0:HEADW] = dext_s[eslot].astype(BF16)
        dproj_ref[0, :, HEADW:] = dgate_s[gslot]

    @pl.when((step == pl.num_programs(0) - 1) & ~early)
    def _():
        scatter.finish()
        swap.finish()

    @pl.when((step == pl.num_programs(0) - 1) & ~early & (z > 0))
    def _():
        @pl.loop(0, heads)
        def _(h):
            hop(h).wait_send()
            halo_hop(h).wait_send()


def assemble_kernel(
    per, base, ffn_ref, proj_ref, vec_ref, y_ref, g_ref,
    query_ref, key_ref, value_ref, outgate_ref, out_ref, gate_ref, up_ref, down_ref, conv_ref, y_out, g_out,
):
    y_out[...] = y_ref[...]
    g_out[...] = g_ref[...]
    for h in range(per):
        query_ref[:, h * DK : (h + 1) * DK] = proj_ref[3 * h, :, 0:DK]
        key_ref[:, h * DK : (h + 1) * DK] = proj_ref[3 * h, :, DK:]
        value_ref[:, h * DV : (h + 1) * DV] = proj_ref[3 * h + 1]
        outgate_ref[:, h * DV : (h + 1) * DV] = proj_ref[3 * h + 2]
    piece = 0
    for target in (down_ref, gate_ref, up_ref):
        total = target.shape[0]
        for start in range(0, total, WIDE):
            size = min(WIDE, total - start)
            target[start : start + size] = ffn_ref[piece].T[0:size]
            piece += 1
    for start in range(0, out_ref.shape[1], WIDE):
        out_ref[:, start : start + WIDE] = ffn_ref[piece]
        piece += 1
    width = conv_ref.shape[1]
    heads = width // HEADW
    for h in range(heads):
        for tap in range(TAPS):
            row = base + (h * TAPS + tap) * HEADW // 128
            spots = [h * DK, (heads + h) * DK, 2 * heads * DK + h * DV, 2 * heads * DK + h * DV + 128]
            for i, spot in enumerate(spots):
                conv_ref[tap : tap + 1, spot : spot + 128] = vec_ref[row + i : row + i + 1]


def assemble(ffn, proj, vec, y, g, per, hidden, base, conv_shape):
    rows = ffn.shape[1]
    f32 = lambda *shape: jax.ShapeDtypeStruct(shape, F32)
    vmem_spec = pl.BlockSpec(memory_space=pltpu.VMEM)
    return pl.pallas_call(
        partial(assemble_kernel, per, base),
        out_shape=(
            f32(rows, per * DK), f32(rows, per * DK), f32(rows, per * DV), f32(rows, per * DV), f32(rows, per * DV),
            f32(hidden, rows), f32(hidden, rows), f32(hidden, rows), f32(*conv_shape),
            jax.ShapeDtypeStruct(y.shape, BF16), jax.ShapeDtypeStruct(g.shape, BF16),
        ),
        in_specs=[vmem_spec] * 5,
        out_specs=(vmem_spec,) * 11,
        compiler_params=pltpu.CompilerParams(vmem_limit_bytes=40 * 2**20),
        cost_estimate=pl.CostEstimate(flops=0, bytes_accessed=10 * 2**20, transcendentals=0),
        name="assemble",
    )(ffn, proj, vec, y, g)


def forward_core(raw, convw, ab, gain, swapped, weights, heads, parts, groups):
    bits = groups.bit_length() - 1
    pieces = []
    for w, weight in enumerate(weights):
        wide = weight.shape[1]
        pieces += [(w, at, at + WIDE // 2, at + WIDE) for at in range(0, wide, WIDE)]
    rows = weights[0].shape[0]
    any_spec = pl.BlockSpec(memory_space=pl.ANY)
    length = raw.shape[1]
    size = min(CHUNK, length)
    chunks = length // size
    per = heads // raw.shape[0]
    lag = parts - 1
    slots = lag + 1
    now = lambda s: jnp.minimum(s, heads - 1)
    late = lambda s: jnp.maximum(s - lag, 0)
    return pl.pallas_call(
        partial(forward_kernel, heads, parts, bits, pieces),
        grid=(heads + lag, 2),
        out_shape=(
            jax.ShapeDtypeStruct((raw.shape[0], length, per * DV), BF16),
            jax.ShapeDtypeStruct((heads, length, DV), F32),
            jax.ShapeDtypeStruct((heads, chunks, DK, DV), F32),
            jax.ShapeDtypeStruct((heads, chunks, size, size), F32),
            jax.ShapeDtypeStruct((heads, length, DK), F32),
            jax.ShapeDtypeStruct((heads, chunks, DK, DK), F32),
            jax.ShapeDtypeStruct((heads, DK, DK), F32),
            jax.ShapeDtypeStruct((parts, HALO, per * (HEADW + DV)), F32),
            jax.ShapeDtypeStruct(swapped.shape, BF16),
            *[jax.ShapeDtypeStruct((parts, groups) + w.shape, BF16) for w in weights],
        ),
        in_specs=[
            pl.BlockSpec((1, length, HEADW + DV), lambda s, _: (now(s) // per, 0, now(s) % per)),
            pl.BlockSpec((1, length, DV), lambda s, _: (late(s) // per, 0, (late(s) % per) * 3 + 2)),
            any_spec,
            pl.BlockSpec((1, TAPS, HEADW), lambda s, _: (now(s), 0, 0)),
            pl.BlockSpec((1, 8, length), lambda s, _: (now(s), 0, 0)),
            pl.BlockSpec((1, DV), lambda s, _: (0, 0)),
            *[any_spec] * (1 + len(weights)),
        ],
        out_specs=(
            pl.BlockSpec((1, length, DV), lambda s, _: (late(s) // per, 0, late(s) % per)),
            pl.BlockSpec((1, length, DV), lambda s, _: (late(s), 0, 0)),
            pl.BlockSpec((1, chunks, DK, DV), lambda s, _: (late(s), 0, 0, 0)),
            pl.BlockSpec((1, chunks, size, size), lambda s, _: (now(s), 0, 0, 0)),
            pl.BlockSpec((1, length, DK), lambda s, _: (now(s), 0, 0)),
            pl.BlockSpec((1, chunks, DK, DK), lambda s, _: (now(s), 0, 0, 0)),
            pl.BlockSpec((1, DK, DK), lambda s, _: (now(s), 0, 0)),
            pl.BlockSpec((parts, HALO, per * (HEADW + DV)), lambda s, _: (0, 0, 0)),
            *[any_spec] * (1 + len(weights)),
        ),
        scratch_shapes=[
            pltpu.VMEM((slots, length, DK), F32),
            pltpu.VMEM((slots, length, DV), F32),
            pltpu.VMEM((slots, chunks, DK, DK), F32),
            pltpu.VMEM((slots, chunks, DK, DV), F32),
            pltpu.VMEM((slots, DK, DK), F32),
            pltpu.VMEM((slots, DK, DV), F32),
            pltpu.VMEM((heads, DK, DV), F32),
            pltpu.VMEM((heads, DK, DV), F32),
            pltpu.VMEM((parts, HALO, per * (HEADW + DV)), F32),
            pltpu.VMEM((HALO + size, HEADW), F32),
            pltpu.SemaphoreType.DMA((heads,)),
            pltpu.SemaphoreType.DMA((heads,)),
            pltpu.SemaphoreType.DMA((parts,)),
            pltpu.SemaphoreType.DMA((parts,)),
            *[pltpu.SemaphoreType.DMA((1,))] * 3,
            *Gather.scratch(bits, len(pieces)),
        ],
        compiler_params=pltpu.CompilerParams(
            collective_id=0, has_side_effects=True, vmem_limit_bytes=56 * 2**20
        ),
        cost_estimate=pl.CostEstimate(flops=20 * 10**9, bytes_accessed=40 * 2**20, transcendentals=0),
        name="delta_forward",
    )(raw, raw, raw, convw, ab, gain, swapped, *weights)


def backward_core(d_head, out, raw, halo, query_e, phi, phi_all, convw, ab, gain, states, inverses, lefts, pairs, swapped,
                  heads, parts, groups):
    length = raw.shape[1]
    size = min(CHUNK, length)
    chunks = length // size
    per = heads // raw.shape[0]
    lag = parts - 1
    slots = lag + 1
    bits = groups.bit_length() - 1
    plan = plan_of(pairs)
    rows = lefts[0].shape[0] // groups
    any_spec = pl.BlockSpec(memory_space=pl.ANY)
    now = lambda s: jnp.minimum(s, heads - 1)
    late = lambda s: jnp.clip(s - lag, 0, heads - 1)
    later = lambda s: jnp.maximum(s - lag - 1, 0)
    return pl.pallas_call(
        partial(backward_kernel, heads, parts, bits, plan, rows),
        grid=(heads + lag + 1, 2),
        out_shape=(
            jax.ShapeDtypeStruct((raw.shape[0], length, per * (HEADW + DV)), BF16),
            jax.ShapeDtypeStruct((heads, 8, length), F32),
            jax.ShapeDtypeStruct((heads, TAPS, HEADW), F32),
            jax.ShapeDtypeStruct((1, DV), F32),
            jax.ShapeDtypeStruct((len(plan), rows, WIDE), F32),
            jax.ShapeDtypeStruct(swapped.shape, BF16),
        ),
        in_specs=[
            pl.BlockSpec((1, length, DV), lambda s, _: (now(s) // per, 0, now(s) % per)),
            pl.BlockSpec((1, length, DV), lambda s, _: (now(s), 0, 0)),
            pl.BlockSpec((1, length, DV), lambda s, _: (now(s) // per, 0, (now(s) % per) * 3 + 2)),
            pl.BlockSpec((1, length, DK), lambda s, _: (now(s), 0, 0)),
            pl.BlockSpec((1, chunks, DK, DK), lambda s, _: (now(s), 0, 0, 0)),
            pl.BlockSpec((1, DK, DK), lambda s, _: (now(s), 0, 0)),
            pl.BlockSpec((1, length, HEADW + DV), lambda s, _: (late(s) // per, 0, late(s) % per)),
            pl.BlockSpec((1, HALO, HEADW + DV), lambda s, _: (late(s) // per, 0, late(s) % per)),
            pl.BlockSpec((1, TAPS, HEADW), lambda s, _: (late(s), 0, 0)),
            pl.BlockSpec((1, 8, length), lambda s, _: (late(s), 0, 0)),
            pl.BlockSpec((1, DV), lambda s, _: (0, 0)),
            pl.BlockSpec((1, chunks, DK, DV), lambda s, _: (late(s), 0, 0, 0)),
            pl.BlockSpec((1, chunks, size, size), lambda s, _: (late(s), 0, 0, 0)),
            pl.BlockSpec((1, chunks, DK, DK), lambda s, _: (late(s), 0, 0, 0)),
            *[any_spec] * (1 + len(lefts) + len(pairs)),
        ],
        out_specs=(
            pl.BlockSpec((1, length, HEADW + DV), lambda s, _: (later(s) // per, 0, later(s) % per)),
            pl.BlockSpec((1, 8, length), lambda s, _: (late(s), 0, 0)),
            pl.BlockSpec((1, TAPS, HEADW), lambda s, _: (late(s), 0, 0)),
            pl.BlockSpec((1, DV), lambda s, _: (0, 0)),
            pl.BlockSpec((len(plan), rows, WIDE), lambda s, _: (0, 0, 0)),
            any_spec,
        ),
        scratch_shapes=[
            pltpu.VMEM((slots, length, DV), F32),
            pltpu.VMEM((slots, chunks, DK, DV), F32),
            pltpu.VMEM((slots + 1, length, DV), BF16),
            pltpu.VMEM((slots, DK, DV), F32),
            pltpu.VMEM((slots, DK, DK), F32),
            pltpu.VMEM((length + 2 * HALO, HEADW), F32),
            pltpu.VMEM((2, length, HEADW), F32),
            pltpu.VMEM((HALO + size, HEADW), F32),
            pltpu.VMEM((heads, DK, DV), F32),
            pltpu.VMEM((heads, DK, DV), F32),
            pltpu.VMEM((heads, HALO, HEADW), F32),
            pltpu.VMEM((heads, HALO, HEADW), F32),
            pltpu.SemaphoreType.DMA((heads,)),
            pltpu.SemaphoreType.DMA((heads,)),
            pltpu.SemaphoreType.DMA((heads,)),
            pltpu.SemaphoreType.DMA((heads,)),
            *[pltpu.SemaphoreType.DMA((1,))] * 3,
            *Scatter.scratch(bits, parts, len(plan), rows, length, lefts[0].shape[0]),
        ],
        compiler_params=pltpu.CompilerParams(
            collective_id=1, has_side_effects=True, vmem_limit_bytes=62 * 2**20
        ),
        cost_estimate=pl.CostEstimate(flops=40 * 10**9, bytes_accessed=60 * 2**20, transcendentals=0),
        name="delta_backward",
    )(d_head, out, raw, query_e, phi, phi_all, raw, halo, convw, ab, gain, states, inverses, phi,
      *lefts, *[right for _, right in pairs], swapped)


def dot(spec, a, b):
    return jnp.einsum(spec, a, b, preferred_element_type=F32)


def unit_rms(v):
    return lax.rsqrt(jnp.mean(v * v, axis=-1, keepdims=True) + 1e-05)


def per_device(
    tokens, out_grad, seq_lengths, mix_gain, w_query, w_key, w_value, w_outgate, w_decay, w_beta,
    conv_weight, rate_log, step_bias, head_gain, w_out, ffn_gain, w_ffn_gate, w_ffn_up, w_ffn_down,
):
    groups = lax.axis_size("dp")
    parts = lax.axis_size("mp")
    group = lax.axis_index("dp")
    share = lax.axis_index("mp")
    heads = rate_log.shape[0]
    per = heads // parts
    width = tokens.shape[2]
    local_rows = w_query.shape[0]

    hidden = w_ffn_gate.shape[1]
    wide = -(-hidden // WIDE) * WIDE
    small_w = jnp.concatenate([w_decay, w_beta], axis=1).T
    small_w = jnp.pad(small_w, ((0, -small_w.shape[0] % 16), (0, 0)))
    x_bf, g_proj, g_small, raw, h1, h1_t, *padded = prologue(
        tokens, small_w, mix_gain[None], (w_query, w_key, w_value, w_outgate),
        (w_ffn_gate.T, w_ffn_up.T, w_ffn_down.T), groups, parts,
    )
    h1 = h1.reshape(-1, width)
    whole = lambda g: g.reshape(parts, width, g.shape[3])
    g_proj = whole(g_proj)
    g_small = g_small[:, :, : 2 * per].transpose(0, 2, 1, 3).reshape(parts, 2 * per, width)
    x_swapped = x_bf
    x_bf = x_bf.reshape(-1, width)
    length = x_bf.shape[0]

    my_length = lax.dynamic_slice_in_dim(seq_lengths, group, 1)
    positions = share * length + jnp.arange(length, dtype=jnp.int32)
    live = (positions < my_length).astype(F32)[:, None]

    x = x_bf.astype(F32)
    small = dot("td,gcd->gct", h1, g_small)
    decay_raw = small[:, :per].reshape(heads, length)
    beta_raw = small[:, per:].reshape(heads, length)
    rate = -jnp.exp(rate_log)[:, None]
    shifted = decay_raw + step_bias[:, None]
    decay = rate * jax.nn.softplus(shifted)
    beta = jax.nn.sigmoid(beta_raw)
    ab = jnp.concatenate(
        [decay[:, None], beta[:, None], jnp.zeros((heads, 6, length), F32)], axis=1
    )
    taps = conv_weight.shape[0]
    key_cols = heads * DK
    convw = jnp.concatenate(
        [
            conv_weight[:, :key_cols].reshape(taps, heads, DK),
            conv_weight[:, key_cols : 2 * key_cols].reshape(taps, heads, DK),
            conv_weight[:, 2 * key_cols :].reshape(taps, heads, DV),
        ],
        axis=2,
    ).transpose(1, 0, 2)
    gain_row = head_gain[None]
    head_out, mixed, states, inverses, query_e, phi, phi_all, halo, dy_bf, *rest = forward_core(
        raw, convw, ab, gain_row, out_grad,
        [w_out] + padded,
        heads, parts, groups,
    )
    g_out, g_gate, g_up, g_down = [whole(w) for w in rest]

    dy = live * dy_bf.reshape(-1, width).astype(F32)
    d_ffo = dy.astype(BF16)
    x1 = x + dot("gtc,gmc->tm", head_out, g_out)
    scale2 = unit_rms(x1)
    n2 = x1 * scale2
    h2 = (n2 * ffn_gain).astype(BF16)
    gate = dot("td,gdf->gtf", h2, g_gate)
    up = dot("td,gdf->gtf", h2, g_up)
    sig = jax.nn.sigmoid(gate)
    act = (gate * sig * up).astype(BF16)
    block_out = (live * (x1 + dot("gtf,gdf->td", act, g_down))).astype(BF16)
    d_act = dot("td,gdf->gtf", d_ffo, g_down)
    d_gate = (d_act * up * sig * (1.0 + gate * (1.0 - sig))).astype(BF16)
    d_up = (d_act * gate * sig).astype(BF16)
    d_h2 = dot("gtf,gdf->td", d_gate, g_gate) + dot("gtf,gdf->td", d_up, g_up)
    e2 = d_h2 * ffn_gain
    d_x1 = dy + scale2 * (e2 - n2 * jnp.mean(e2 * n2, axis=-1, keepdims=True))
    ffn_gain_grad = jnp.sum(d_h2 * n2, axis=0)
    d_mix = d_x1.astype(BF16)
    d_head = dot("tm,gmc->gtc", d_mix, g_out)

    d_proj, d_ab, d_convw, d_head_gain, sums_ffn, final_out = backward_core(
        d_head, mixed, raw, halo, query_e, phi, phi_all, convw, ab, gain_row, states, inverses,
        [d_mix.T, h2.T, d_ffo.T], [(2, act), (1, d_gate), (1, d_up), (0, head_out)],
        block_out.reshape(tokens.shape), heads, parts, groups,
    )
    d_decay = d_ab[:, 0]
    d_beta_raw = d_ab[:, 1] * beta * (1.0 - beta)
    d_decay_raw = d_decay * rate * jax.nn.sigmoid(shifted)
    rate_grad = jnp.sum(d_decay * decay, axis=1)
    bias_grad = jnp.sum(d_decay_raw, axis=1)
    d_small = jnp.concatenate(
        [d_decay_raw.reshape(parts, per, length), d_beta_raw.reshape(parts, per, length)], axis=1
    ).astype(BF16)
    line = jnp.pad(jnp.concatenate([rate_grad, bias_grad])[None], ((0, 0), (0, 128 - 2 * heads)))
    sums_proj, sums, final_grad = scatter_sum(
        h1_t, [(0, d_proj)],
        (ffn_gain_grad[None], d_head_gain, d_convw, line), g_proj, d_small.reshape(-1, length),
        g_small.reshape(-1, width), x_swapped, d_x1, mix_gain[None], groups, parts, 2,
    )
    starts, _ = small_rows(heads, width, 2 * heads)
    part = lambda i: sums[starts[i] : starts[i + 1]].reshape(-1)
    (s_query, s_key, s_value, s_outgate, s_out, s_gate, s_up, s_down, s_conv, final_out, final_grad) = assemble(
        sums_ffn, sums_proj, sums, final_out, final_grad, per, hidden, starts[3], conv_weight.shape
    )
    small_sum = part(5).reshape(parts, 2 * per, width)
    mine = lax.dynamic_slice(small_sum, (share, 0, group * local_rows), (1, 2 * per, local_rows))[0].T

    return (
        final_out,
        final_grad,
        part(0),
        s_query,
        s_key,
        s_value,
        s_outgate,
        mine[:, :per],
        mine[:, per:],
        s_conv,
        part(4)[:heads],
        part(4)[heads : 2 * heads],
        part(2),
        s_out,
        part(1),
        s_gate.T,
        s_up.T,
        s_down.T,
    )


def solution(mesh):
    seq = P(None, ("mp", "dp"), None)
    shard = P("dp", "mp")
    rep = P()
    return jax.shard_map(
        per_device,
        mesh=mesh,
        in_specs=(
            seq, seq, rep, rep, shard, shard, shard, shard, shard, shard,
            rep, rep, rep, rep, shard, rep, shard, shard, shard,
        ),
        out_specs=(
            seq, seq, rep, shard, shard, shard, shard, shard, shard,
            rep, rep, rep, rep, shard, rep, shard, shard, shard,
        ),
        check_vma=False,
    )
```

```python
from functools import partial

import jax
import jax.numpy as jnp
from jax import lax
from jax.experimental import pallas as pl
from jax.experimental.pallas import tpu as pltpu
from jax.sharding import PartitionSpec as P

DK = 128
DV = 256
HEADW = 2 * DK + DV
TAPS = 4
CHUNK = 128
HALO = 8
WIDE = 256
STRIDE = 2
F32 = jnp.float32
BF16 = jnp.bfloat16


def halves(a):
    high = a.astype(BF16)
    return high, (a - high.astype(F32)).astype(BF16)


def mm(a, b, ca=1, cb=0):
    dims = (((ca,), (cb,)), ((), ()))
    a_high, a_low = halves(a)
    b_high, b_low = halves(b)
    one = lambda p, q: lax.dot_general(p, q, dims, preferred_element_type=F32)
    if a.shape[ca] <= 128:
        return one(
            jnp.concatenate([a_high, a_low], axis=ca), jnp.concatenate([b_high, b_high], axis=cb)
        ) + one(a_high, b_low)
    return one(a_high, b_high) + (one(a_high, b_low) + one(a_low, b_high))


def windows(raw_ref, ext_s, c, size):
    if c == 0:
        return [ext_s[pl.ds(HALO - TAPS + 1 + i, size)] for i in range(TAPS)]
    return [raw_ref[0, pl.ds(c * size - TAPS + 1 + i, size), 0:HEADW] for i in range(TAPS)]


def conv_of(shifted, convw):
    total = None
    for i in range(TAPS):
        part = shifted[i] * convw[i : i + 1]
        total = part if total is None else total + part
    return total


def decays(ab_ref, base, rows, upper):
    ab = ab_ref[0, :, pl.ds(base, rows)]
    cum = mm(ab, upper)
    row_id = lax.broadcasted_iota(jnp.int32, ab.shape, 0)
    both = jnp.where(row_id == 0, cum, ab)
    cols = both.T
    return both[0:1], cols[:, 0:1], cols[:, 1:2]


def masks(size):
    rows = lax.broadcasted_iota(jnp.int32, (size, size), 0)
    cols = lax.broadcasted_iota(jnp.int32, (size, size), 1)
    return rows, cols


def fades(gamma_row, gamma_col, rows, cols):
    spread = jnp.minimum(gamma_col - gamma_row, 0.0)
    inclusive = jnp.where(rows >= cols, jnp.exp(spread), 0.0)
    strict = jnp.where(rows > cols, inclusive, 0.0)
    return inclusive, strict


def invert_many(lowers, rows, cols):
    size = lowers[0].shape[0]
    eye = (rows == cols).astype(F32)
    pair = ((rows // 2) == (cols // 2)) & (rows > cols)
    inverses = [eye - jnp.where(pair, low, 0.0) for low in lowers]
    width = 2
    while width < size:
        within = (rows // (2 * width)) == (cols // (2 * width))
        cross = within & ((rows // width) != (cols // width)) & (rows > cols)
        inner = [mm(jnp.where(cross, low, 0.0), inv) for low, inv in zip(lowers, inverses)]
        inverses = [inv - mm(inv, part) for inv, part in zip(inverses, inner)]
        width *= 2
    return inverses


def in_step(works):
    while works:
        works = [work for work in works if next(work, True) is None]


def unit_parts(conv):
    sig = jax.nn.sigmoid(conv)
    silu = conv * sig
    q_silu = silu[:, :DK]
    k_silu = silu[:, DK : 2 * DK]
    value = silu[:, 2 * DK :]
    q_scale = lax.rsqrt(jnp.sum(q_silu * q_silu, axis=-1, keepdims=True) + 1e-06)
    k_scale = lax.rsqrt(jnp.sum(k_silu * k_silu, axis=-1, keepdims=True) + 1e-06)
    return sig, q_silu, k_silu, value, q_scale, k_scale


class Gather:
    def __init__(self, bits, parts, sources, targets, pieces, sems):
        self.bits, self.parts, self.pieces = bits, parts, pieces
        self.sources, self.targets = sources, targets
        (self.own, self.z_send, self.z_recv, self.p_send, self.p_recv, self.s_send, self.s_recv) = sems
        self.d, self.z = lax.axis_index("dp"), lax.axis_index("mp")
        self.orders = (list(range(1, bits)), list(range(bits - 1, 0, -1)))
        self.ticks = bits + 1

    @staticmethod
    def scratch(bits, count):
        dma = lambda *shape: pltpu.SemaphoreType.DMA(shape)
        return [
            dma(count), dma(count), dma(count), dma(count, bits - 1, 2), dma(count, bits - 1, 2),
            dma(count), dma(count),
        ]

    def flip(self, index, b):
        return index + (1 - 2 * lax.rem(lax.div(self.d, 2**b), 2)) * 2**b

    def copy(self, src, dst, send, recv, to):
        return pltpu.make_async_remote_copy(
            src_ref=src, dst_ref=dst, send_sem=send, recv_sem=recv, device_id=to,
            device_id_type=pl.DeviceIdType.MESH,
        )

    def sides(self, p):
        _, start, mid, stop = self.pieces[p]
        return [(0, start, mid)] + ([(1, mid, stop)] if mid < stop else [])

    def held(self, side, k):
        out = [self.d]
        for b in self.orders[side][:k]:
            out = out + [self.flip(i, b) for i in out]
        return out

    def arrived(self, side, k):
        return [self.flip(i, self.orders[side][k]) for i in self.held(side, k)]

    def to_sibling(self, p, indices, start, stop):
        target = self.targets[self.pieces[p][0]]
        for i in indices:
            block = target.at[:, i, :, start:stop]
            self.copy(
                block, block, self.s_send.at[p], self.s_recv.at[p], {"dp": self.flip(self.d, 0)}
            ).start()

    def along(self, p, k, act):
        target = self.targets[self.pieces[p][0]]
        for side, start, stop in self.sides(p):
            b = self.orders[side][k]
            for i in self.held(side, k):
                block = target.at[:, i, :, start:stop]
                act(
                    self.copy(
                        block, block, self.p_send.at[p, k, side], self.p_recv.at[p, k, side],
                        {"dp": self.flip(self.d, b)},
                    )
                )

    def along_whole(self, p, k):
        target = self.targets[self.pieces[p][0]]
        out = []
        for side, start, stop in self.sides(p):
            block = target.at[:, pl.ds(0, 2**k), :, start:stop]
            out.append(
                self.copy(
                    block, block, self.p_send.at[p, k, side], self.p_recv.at[p, k, side],
                    {"dp": self.flip(self.d, self.orders[side][k])},
                )
            )
        return out

    def tick(self, p, stage):
        which, start, _, stop = self.pieces[p]
        source, target = self.sources[which], self.targets[which]
        if stage == 0:
            pltpu.make_async_copy(
                source.at[:, start:stop], target.at[self.z, self.d, :, start:stop], self.own.at[p]
            ).start()
            for delta in range(1, self.parts):
                self.copy(
                    source.at[:, start:stop], target.at[self.z, self.d, :, start:stop], self.z_send.at[p],
                    self.z_recv.at[p], {"mp": lax.rem(self.z + delta, self.parts)},
                ).start()
        elif stage == 1:
            pltpu.make_async_copy(
                source.at[:, start:stop], target.at[self.z, self.d, :, start:stop], self.own.at[p]
            ).wait()
            self.z_whole(p).wait_recv()
            self.along(p, 0, lambda copy: copy.start())
            self.to_sibling(p, [self.d], start, stop)
        elif stage <= self.bits:
            k = stage - 2
            for copy in self.along_whole(p, k):
                copy.wait_recv()
            if k + 1 < self.bits - 1:
                self.along(p, k + 1, lambda copy: copy.start())
            for side, low, high in self.sides(p):
                self.to_sibling(p, self.arrived(side, k), low, high)

    def moves(self):
        return len(self.pieces) + STRIDE * (self.ticks - 1)

    def move(self, now):
        for p in range(len(self.pieces)):
            if now >= p and (now - p) % STRIDE == 0 and (now - p) // STRIDE < self.ticks:
                self.tick(p, (now - p) // STRIDE)

    def z_whole(self, p):
        which, start, _, stop = self.pieces[p]
        block = self.targets[which].at[pl.ds(0, self.parts - 1), self.d, :, start:stop]
        return self.copy(
            block, block, self.z_send.at[p], self.z_recv.at[p],
            {"mp": lax.rem(self.z + 1, self.parts)},
        )

    def s_whole(self, p):
        which, start, _, stop = self.pieces[p]
        block = self.targets[which].at[:, pl.ds(0, 2 ** (self.bits - 1)), :, start:stop]
        return self.copy(
            block, block, self.s_send.at[p], self.s_recv.at[p], {"dp": self.flip(self.d, 0)}
        )

    def finish(self, waited=()):
        for p in range(len(self.pieces)):
            if p not in waited:
                self.s_whole(p).wait_recv()
            self.z_whole(p).wait_send()
            for k in range(self.bits - 1):
                for copy in self.along_whole(p, k):
                    copy.wait_send()
            self.s_whole(p).wait_send()


def greet_all(bits, parts, every):
    d, z = lax.axis_index("dp"), lax.axis_index("mp")
    barrier = pltpu.get_barrier_semaphore()
    if every:
        peers = [lax.rem(d + delta, 2**bits) for delta in range(1, 2**bits)]
    else:
        peers = [d + (1 - 2 * lax.rem(lax.div(d, 2**b), 2)) * 2**b for b in range(bits)]
    for peer in peers:
        pl.semaphore_signal(
            barrier, inc=1, device_id={"dp": peer}, device_id_type=pl.DeviceIdType.MESH
        )
    for delta in range(1, parts):
        pl.semaphore_signal(
            barrier, inc=1, device_id={"mp": lax.rem(z + delta, parts)},
            device_id_type=pl.DeviceIdType.MESH,
        )
    pl.semaphore_wait(barrier, len(peers) + parts - 1)


class Swap:
    def __init__(self, groups, source, target, own, send, recv):
        self.groups, self.source, self.target = groups, source, target
        self.own, self.send, self.recv = own, send, recv
        self.d = lax.axis_index("dp")

    def copy(self, src, dst, to):
        return pltpu.make_async_remote_copy(
            src_ref=src, dst_ref=dst, send_sem=self.send, recv_sem=self.recv, device_id={"dp": to},
            device_id_type=pl.DeviceIdType.MESH,
        )

    def local(self):
        return pltpu.make_async_copy(self.source.at[self.d], self.target.at[self.d], self.own)

    def start(self):
        self.local().start()
        for delta in range(1, self.groups):
            to = lax.rem(self.d + delta, self.groups)
            self.copy(self.source.at[to], self.target.at[self.d], to).start()

    def finish(self):
        self.local().wait()
        block = self.target.at[pl.ds(0, self.groups - 1)]
        whole = self.copy(block, block, lax.rem(self.d + 1, self.groups))
        whole.wait_recv()
        whole.wait_send()


def prologue_kernel(bits, parts, pieces, *refs):
    tokens, small, gain, *refs = refs
    members, narrow, refs = refs[:4], refs[4:7], refs[7:]
    tokens_out, joined_out, small_out, raw_out, h1_out, h1t_out = refs[:6]
    padded, refs = refs[6:9], refs[9:]
    member_s, narrow_s, padded_s, refs = refs[:4], refs[4:7], refs[7:10], refs[10:]
    in_sem, out_sem, joined, x_s, w_s, raw_s, x_sem, w_sem, raw_sem, *sems = refs
    loads = [
        pltpu.make_async_copy(src, dst, in_sem.at[i])
        for i, (src, dst) in enumerate(zip((*members, *narrow), (*member_s, *narrow_s)))
    ]
    for load in loads:
        load.start()
    gather = Gather(bits, parts, (joined, small), (joined_out, small_out), pieces, sems[:7])
    swap = Swap(2**bits, tokens, tokens_out, *[s.at[0] for s in sems[7:10]])
    greet_all(bits, parts, True)
    swap.start()
    blocks, rows, width = x_s.shape
    at = 0
    for load in loads[:4]:
        load.wait()
    for h in range(joined.shape[1] // (HEADW + DV)):
        for member, size in zip(member_s, (DK, DK, DV, DV)):
            joined[:, at : at + size] = member[:, h * size : (h + 1) * size]
            at += size

    def put(i):
        return pltpu.make_async_copy(padded_s[i], padded[i], out_sem.at[i])

    def widen():
        for i, (source, target) in enumerate(zip(narrow_s, padded_s)):
            loads[4 + i].wait()
            have, wide = source.shape[0], target.shape[1]
            edge = have // 128 * 128
            target[:, edge:] = jnp.zeros((target.shape[0], wide - edge), BF16)
            target[:, 0:have] = source[...].T
            put(i).start()

    def normalize():
        swap.finish()
        copy = pltpu.make_async_copy(tokens_out, x_s, x_sem.at[0])
        copy.start()
        copy.wait()

        @pl.loop(0, blocks)
        def _(i):
            x = x_s[i].astype(F32)
            scale = lax.rsqrt(jnp.mean(x * x, axis=-1, keepdims=True) + 1e-05)
            h1_out[i] = (x * scale * gain[...]).astype(BF16)

        h1t_out[...] = h1_out[...].reshape(blocks * rows, width).T

    def fetch(p):
        _, start, _, stop = pieces[p]
        return pltpu.make_async_copy(
            joined_out.at[:, :, :, start:stop], w_s.at[p % 2], w_sem.at[p % 2]
        )

    def store(p):
        _, start, _, stop = pieces[p]
        return pltpu.make_async_copy(raw_s.at[p % 2], raw_out.at[:, :, start:stop], raw_sem.at[p % 2])

    main = [p for p, item in enumerate(pieces) if item[0] == 0]

    def project(p):
        if p - 2 in main:
            store(p - 2).wait()
        fetch(p).wait()
        h1 = h1_out[...].reshape(blocks * rows, width)

        @pl.loop(0, parts)
        def _(g):
            raw_s[p % 2, g] = jnp.dot(
                h1, w_s[p % 2, g].reshape(width, WIDE), preferred_element_type=F32
            )

        store(p).start()

    ready = {p + STRIDE * gather.ticks: p for p in main}
    for now in range(max(ready) + 2):
        if now < gather.moves():
            gather.move(now)
        if now == 1:
            widen()
        if now == min(ready):
            normalize()
        if now - 1 in ready:
            project(ready[now - 1])
        if now in ready:
            gather.s_whole(ready[now]).wait_recv()
            fetch(ready[now]).start()
    gather.finish(main)
    for p in main[-2:]:
        store(p).wait()
    for i in range(3):
        put(i).wait()


def prologue(tokens, small, gain, members, narrow, groups, parts):
    bits = groups.bit_length() - 1
    rows = members[0].shape[0]
    wide = sum(w.shape[1] for w in members)
    padded = -(-narrow[0].shape[0] // WIDE) * WIDE
    blocks, token_rows, width = tokens.shape
    pieces = [(1, 0, small.shape[1], small.shape[1])]
    pieces += [(0, at, at + WIDE // 2, at + WIDE) for at in range(0, wide, WIDE)]
    length = blocks * token_rows
    any_spec = pl.BlockSpec(memory_space=pl.ANY)
    vmem_spec = pl.BlockSpec(memory_space=pltpu.VMEM)
    dma = lambda *shape: pltpu.SemaphoreType.DMA(shape)
    return pl.pallas_call(
        partial(prologue_kernel, bits, parts, pieces),
        out_shape=(
            jax.ShapeDtypeStruct(tokens.shape, BF16),
            jax.ShapeDtypeStruct((parts, groups, rows, wide), BF16),
            jax.ShapeDtypeStruct((parts, groups) + small.shape, BF16),
            jax.ShapeDtypeStruct((parts, length, wide), F32),
            jax.ShapeDtypeStruct(tokens.shape, BF16),
            jax.ShapeDtypeStruct((width, length), BF16),
            *[jax.ShapeDtypeStruct((rows, padded), BF16)] * 3,
        ),
        in_specs=[any_spec] * 2 + [vmem_spec] + [any_spec] * 7,
        out_specs=(any_spec,) * 4 + (vmem_spec,) * 2 + (any_spec,) * 3,
        scratch_shapes=[
            *[pltpu.VMEM(w.shape, BF16) for w in (*members, *narrow)],
            *[pltpu.VMEM((rows, padded), BF16)] * 3,
            dma(7), dma(3),
            pltpu.VMEM((rows, wide), BF16),
            pltpu.VMEM(tokens.shape, BF16),
            pltpu.VMEM((2, parts, groups, rows, WIDE), BF16),
            pltpu.VMEM((2, parts, length, WIDE), F32),
            dma(1), dma(2), dma(2),
            *Gather.scratch(bits, len(pieces)),
            dma(1), dma(1), dma(1),
        ],
        compiler_params=pltpu.CompilerParams(
            collective_id=3, has_side_effects=True, vmem_limit_bytes=62 * 2**20
        ),
        cost_estimate=pl.CostEstimate(
            flops=2 * length * width * wide * parts, bytes_accessed=40 * 2**20, transcendentals=0
        ),
        name="prologue",
    )(tokens, small, gain, *members, *narrow)


def forward_kernel(
    heads, parts, bits, pieces,
    raw_ref, gate_ref, raw_any, convw_ref, ab_ref, gain_ref, *refs,
):
    weights = len({item[0] for item in pieces})
    swap_in, sources, refs = refs[0], refs[1 : 1 + weights], refs[1 + weights :]
    head_ref, o_ref, s_ref, t_ref, qe_ref, phi_ref, phil_ref, halo_ref = refs[:8]
    swap_out, targets, refs = refs[8], refs[9 : 9 + weights], refs[9 + weights :]
    (qe_s, o0_s, phi_s, b_s, phil_s, bl_s, send_s, recv_s, halo_s, ext_s,
     send_sem, recv_sem, halo_send_sem, halo_recv_sem) = refs[:14]
    swap = Swap(2**bits, swap_in, swap_out, *[s.at[0] for s in refs[14:17]])
    gather = Gather(bits, parts, sources, targets, pieces, refs[17:])
    step = pl.program_id(0)
    early = pl.program_id(1) == 0
    z = lax.axis_index("mp")
    lag = parts - 1
    slots = lag + 1
    length = gate_ref.shape[1]
    size = min(CHUNK, length)
    chunks = length // size
    per = heads // parts

    @pl.when((step == 0) & early)
    def _():
        greet_all(bits, parts, True)
        swap.start()

    last = 2 * (heads + lag) - 1
    for now in range(min(gather.moves(), last)):
        @pl.when(step * 2 + pl.program_id(1) == now)
        def _():
            gather.move(now)

    @pl.when(step * 2 + pl.program_id(1) == last)
    def _():
        for now in range(last, gather.moves()):
            gather.move(now)

    def hop(h):
        return pltpu.make_async_remote_copy(
            src_ref=send_s.at[h], dst_ref=recv_s.at[h], send_sem=send_sem.at[h],
            recv_sem=recv_sem.at[h], device_id={"mp": lax.rem(z + 1, parts)},
            device_id_type=pl.DeviceIdType.MESH,
        )

    def halo_hop(g):
        return pltpu.make_async_remote_copy(
            src_ref=raw_any.at[g, length - HALO :], dst_ref=halo_s.at[g], send_sem=halo_send_sem.at[g],
            recv_sem=halo_recv_sem.at[g], device_id={"mp": lax.rem(z + 1, parts)},
            device_id_type=pl.DeviceIdType.MESH,
        )

    @pl.when((step == 0) & early & (z == 0))
    def _():
        recv_s[...] = jnp.zeros_like(recv_s)
        halo_s[...] = jnp.zeros_like(halo_s)

    @pl.when((step == 0) & early & (z < parts - 1))
    def _():
        for g in range(parts):
            halo_hop(g).start()

    @pl.when((step < heads) & early)
    def _():
        slot = lax.rem(step, slots)
        part, sub = lax.div(step, per), lax.rem(step, per)

        @pl.when((sub == 0) & (z > 0))
        def _():
            halo_hop(part).wait_recv()

        for k in range(per):
            @pl.when(sub == k)
            def _():
                ext_s[0:HALO] = halo_s[part, :, k * (HEADW + DV) : k * (HEADW + DV) + HEADW]

        ext_s[HALO:] = raw_ref[0, 0:size, 0:HEADW]
        rows, cols = masks(size)
        upper = (rows <= cols).astype(F32)
        convw = convw_ref[0]
        kept = [None] * chunks
        lowers = [None] * chunks

        def open_chunk(c):
            conv = conv_of(windows(raw_ref, ext_s, c, size), convw)
            _, q_silu, k_silu, value, q_scale, k_scale = unit_parts(conv)
            query = q_silu * (q_scale * DK ** (-0.5))
            keyed = k_silu * k_scale
            yield
            gamma_row, gamma_col, beta = decays(ab_ref, c * size, size, upper)
            inclusive, strict = fades(gamma_row, gamma_col, rows, cols)
            gram = mm(jnp.concatenate([keyed, query], axis=0), keyed, 1, 1)
            yield
            lowers[c] = beta * gram[:size] * strict
            scores = gram[size:] * inclusive
            growth = jnp.exp(gamma_col)
            last = gamma_row[:, size - 1 :]
            rhs = jnp.concatenate([(beta * growth) * keyed, beta * value], axis=1)
            kept[c] = (scores, rhs, query * growth, keyed * jnp.exp(last - gamma_col), last)

        in_step([open_chunk(c) for c in range(chunks)])
        inverses = invert_many(lowers, rows, cols)
        eye = (masks(DK)[0] == masks(DK)[1]).astype(F32)
        flows = [None] * chunks

        def close_chunk(c):
            scores, rhs, query_g, keyed_g, last = kept[c]
            t_ref[0, c] = inverses[c]
            solved = mm(inverses[c], rhs)
            yield
            mixed = mm(scores, solved)
            yield
            moved = mm(keyed_g, solved, 0, 0)
            yield
            query_e = query_g - mixed[:, :DK]
            phi = jnp.exp(last) * eye - moved[:, :DK]
            qe_ref[0, c * size : (c + 1) * size] = query_e
            qe_s[slot, c * size : (c + 1) * size] = query_e
            o0_s[slot, c * size : (c + 1) * size] = mixed[:, DK:]
            phi_ref[0, c] = phi.T
            phi_s[slot, c] = phi
            b_s[slot, c] = moved[:, DK:]
            flows[c] = phi

        in_step([close_chunk(c) for c in range(chunks)])
        phi_all, b_all = flows[0], b_s[slot, 0]
        for c in range(1, chunks):
            moved_all = mm(flows[c], jnp.concatenate([phi_all, b_all], axis=1))
            phi_all = moved_all[:, :DK]
            b_all = moved_all[:, DK:] + b_s[slot, c]
        phil_ref[0] = phi_all.T
        phil_s[slot] = phi_all
        bl_s[slot] = b_all

    relay = step - z

    @pl.when((relay >= 0) & (relay < heads) & ~early)
    def _():
        slot = lax.rem(relay, slots)

        @pl.when(z > 0)
        def _():
            hop(relay).wait_recv()

        @pl.when(z < parts - 1)
        def _():
            send_s[relay] = mm(phil_s[slot], recv_s[relay]) + bl_s[slot]
            hop(relay).start()

    @pl.when((step >= lag) & ~early)
    def _():
        head = step - lag
        slot = lax.rem(head, slots)
        state = recv_s[head]
        for c in range(chunks):
            at = slice(c * size, (c + 1) * size)
            s_ref[0, c] = state
            result = mm(qe_s[slot, at], state) + o0_s[slot, at]
            if c + 1 < chunks:
                state = mm(phi_s[slot, c], state) + b_s[slot, c]
            o_ref[0, at] = result
            scale = lax.rsqrt(jnp.mean(result * result, axis=-1, keepdims=True) + 1e-05)
            gate = gate_ref[0, c * size : (c + 1) * size]
            gated = result * scale * gain_ref[...] * (gate * jax.nn.sigmoid(gate))
            head_ref[0, at] = gated.astype(BF16)

    @pl.when((step == pl.num_programs(0) - 1) & ~early & (z < parts - 1))
    def _():
        @pl.loop(0, heads)
        def _(h):
            hop(h).wait_send()

        for g in range(parts):
            halo_hop(g).wait_send()

    @pl.when((step == pl.num_programs(0) - 1) & ~early)
    def _():
        halo_ref[...] = halo_s[...]
        gather.finish()
        swap.finish()


class Scatter:
    def __init__(self, bits, parts, plan, rows, lhs_refs, rhs_refs, out_ref, scratch, stride):
        self.stride = stride
        self.bits, self.parts, self.plan, self.rows = bits, parts, plan, rows
        self.lhs_refs, self.rhs_refs, self.out_ref = lhs_refs, rhs_refs, out_ref
        self.count = len(plan)
        self.planes = planes = bits - 1
        self.half = 2 ** (bits - 1)
        self.lhs_s, self.rhs_s, self.grad_s, self.r1, *rest = scratch
        self.ra, self.rb = rest[:planes], rest[planes : 2 * planes]
        (self.r4, self.load_sem, self.send1, self.recv1, self.send_a, self.recv_a, self.send_b,
         self.recv_b, self.send4, self.recv4) = rest[2 * planes :]
        self.d, self.z = lax.axis_index("dp"), lax.axis_index("mp")
        self.ticks = self.count + 1 + self.stride * (planes + 1)

    @staticmethod
    def scratch(bits, parts, count, rows, length, width):
        planes, half = bits - 1, 2 ** (bits - 1)
        vmem = lambda *shape: pltpu.VMEM(shape, BF16)
        dma = lambda *shape: pltpu.SemaphoreType.DMA(shape)
        strips = [vmem(count, parts, half >> (k + 1), rows, WIDE // 2) for k in range(planes)]
        return [
            vmem(2, width, length),
            vmem(2, parts, length, WIDE),
            vmem(2, parts, half, 2, rows, WIDE),
            vmem(count, parts, half, rows, WIDE),
            *strips, *strips,
            vmem(count, parts - 1, rows, WIDE),
            dma(2, 2),
            dma(count), dma(count),
            dma(planes, count), dma(planes, count),
            dma(planes, count), dma(planes, count),
            dma(count), dma(count),
        ]

    def bit(self, b):
        return lax.rem(lax.div(self.d, 2**b), 2)

    def partner(self, b):
        return self.d + (1 - 2 * self.bit(b)) * 2**b

    def remote(self, src, dst, send, recv, to):
        return pltpu.make_async_remote_copy(
            src_ref=src, dst_ref=dst, send_sem=send, recv_sem=recv, device_id=to,
            device_id_type=pl.DeviceIdType.MESH,
        )

    def load(self, t):
        slot = lax.rem(t, 2)
        for seg in range(len(self.rhs_refs)):
            at = [k for k, item in enumerate(self.plan) if item[0] == seg]

            @pl.when((t >= at[0]) & (t <= at[-1]))
            def _():
                start = pl.multiple_of((t - at[0]) * WIDE, WIDE)
                pltpu.make_async_copy(
                    self.rhs_refs[seg].at[:, :, pl.ds(start, WIDE)], self.rhs_s.at[slot],
                    self.load_sem.at[0, slot],
                ).start()
                pltpu.make_async_copy(
                    self.lhs_refs[self.plan[at[0]][1]], self.lhs_s.at[slot], self.load_sem.at[1, slot]
                ).start()

    def load_wait(self, t):
        slot = lax.rem(t, 2)
        pltpu.make_async_copy(
            self.rhs_refs[0].at[:, :, pl.ds(0, WIDE)], self.rhs_s.at[slot], self.load_sem.at[0, slot]
        ).wait()
        pltpu.make_async_copy(
            self.lhs_refs[0], self.lhs_s.at[slot], self.load_sem.at[1, slot]
        ).wait()

    def first_hop(self, t):
        return self.remote(
            self.grad_s.at[lax.rem(t, 2), :, :, 1 - self.bit(0)], self.r1.at[t], self.send1.at[t],
            self.recv1.at[t], {"dp": self.partner(0)},
        )

    def a_hop(self, k, t):
        b = self.bits - 1 - k
        keep = self.half >> (k + 1)
        away = pl.ds((1 - self.bit(b)) * keep, keep)
        src = self.r1.at[t, :, away, :, 0 : WIDE // 2] if k == 0 else self.ra[k - 1].at[t, :, away]
        return self.remote(
            src, self.ra[k].at[t], self.send_a.at[k, t], self.recv_a.at[k, t], {"dp": self.partner(b)}
        )

    def b_hops(self, k, t):
        b = 1 + k
        copies = []
        for hi in range(self.half >> (k + 1)):
            away = 2 * hi + 1 - self.bit(b)
            src = self.r1.at[t, :, away, :, WIDE // 2 :] if k == 0 else self.rb[k - 1].at[t, :, away]
            copies.append(
                self.remote(
                    src, self.rb[k].at[t, :, hi], self.send_b.at[k, t], self.recv_b.at[k, t],
                    {"dp": self.partner(b)},
                )
            )
        return copies

    def b_whole(self, k, t):
        return self.remote(
            self.rb[k].at[t], self.rb[k].at[t], self.send_b.at[k, t], self.recv_b.at[k, t],
            {"dp": self.partner(1 + k)},
        )

    def z_hops(self, t):
        copies = []
        side = WIDE // 2
        for delta in range(1, self.parts):
            to = lax.rem(self.z + delta, self.parts)
            for i, buf in enumerate((self.ra[self.planes - 1], self.rb[self.planes - 1])):
                copies.append(
                    self.remote(
                        buf.at[t, to, 0],
                        self.r4.at[t, self.parts - 1 - delta, :, i * side : (i + 1) * side],
                        self.send4.at[t], self.recv4.at[t], {"mp": to},
                    )
                )
        return copies

    def z_whole(self, t):
        return self.remote(
            self.r4.at[t], self.r4.at[t], self.send4.at[t], self.recv4.at[t],
            {"mp": lax.rem(self.z + 1, self.parts)},
        )

    def tick(self, tick):
        count, planes, half, parts = self.count, self.planes, self.half, self.parts
        side = WIDE // 2

        @pl.when(tick == 0)
        def _():
            self.load(tick)

        t = tick - 1 - self.stride * (planes + 1)

        @pl.when((t >= 0) & (t < count))
        def _():
            self.z_whole(t).wait_recv()
            left = self.ra[planes - 1][t, self.z, 0].astype(F32)
            right = self.rb[planes - 1][t, self.z, 0].astype(F32)
            for s in range(parts - 1):
                left = left + self.r4[t, s, :, 0:side].astype(F32)
                right = right + self.r4[t, s, :, side:].astype(F32)
            self.out_ref[t, :, 0:side] = left
            self.out_ref[t, :, side:] = right

        for k in range(planes - 1, -1, -1):
            t_k = tick - 1 - self.stride * (k + 1)

            @pl.when((t_k >= 0) & (t_k < count))
            def _():
                self.a_hop(k, t_k).wait_recv()
                self.b_whole(k, t_k).wait_recv()
                keep = half >> (k + 1)
                bit_a, bit_b = self.bit(self.bits - 1 - k), self.bit(1 + k)
                for m in range(keep):
                    own_a, own_b = bit_a * keep + m, 2 * m + bit_b
                    for j in range(parts):
                        if k == 0:
                            mine_a = self.r1[t_k, j, own_a, :, 0:side]
                            mine_b = self.r1[t_k, j, own_b, :, side:]
                        else:
                            mine_a = self.ra[k - 1][t_k, j, own_a]
                            mine_b = self.rb[k - 1][t_k, j, own_b]
                        for buf, mine in ((self.ra[k], mine_a), (self.rb[k], mine_b)):
                            buf[t_k, j, m] = (buf[t_k, j, m].astype(F32) + mine.astype(F32)).astype(BF16)
                if k + 1 < planes:
                    self.a_hop(k + 1, t_k).start()
                    for copy in self.b_hops(k + 1, t_k):
                        copy.start()
                else:
                    for copy in self.z_hops(t_k):
                        copy.start()

        t_1 = tick - 1

        @pl.when((t_1 >= 0) & (t_1 < count))
        def _():
            self.first_hop(t_1).wait_recv()
            slot = lax.rem(t_1, 2)
            color = self.bit(0)

            @pl.loop(0, parts)
            def _(j):
                for m in range(half):
                    self.r1[t_1, j, m] = (
                        self.r1[t_1, j, m].astype(F32) + self.grad_s[slot, j, m, color].astype(F32)
                    ).astype(BF16)

            self.a_hop(0, t_1).start()
            for copy in self.b_hops(0, t_1):
                copy.start()

        @pl.when(tick < count)
        def _():
            slot = lax.rem(tick, 2)

            @pl.when(tick + 1 < count)
            def _():
                self.load(tick + 1)

            self.load_wait(tick)

            @pl.when(tick >= 2)
            def _():
                self.first_hop(tick - 2).wait_send()

            @pl.loop(0, parts)
            def _(j):
                full = jnp.dot(self.lhs_s[slot], self.rhs_s[slot, j], preferred_element_type=F32)
                self.grad_s[slot, j] = full.astype(BF16).reshape(half, 2, self.rows, WIDE)

            self.first_hop(tick).start()

    def finish(self):
        for t in range(max(self.count - 2, 0), self.count):
            self.first_hop(t).wait_send()

        @pl.loop(0, self.count)
        def _(t):
            for k in range(self.planes):
                self.a_hop(k, t).wait_send()
                self.b_whole(k, t).wait_send()
            self.z_whole(t).wait_send()


def plan_of(pairs):
    plan = []
    for seg, (kind, right) in enumerate(pairs):
        plan += [(seg, kind)] * (right.shape[2] // WIDE)
    return plan


def small_rows(heads, width, smalls):
    starts = [0]
    for count in (width // 128, width // 128, DV // 128, heads * TAPS * HEADW // 128, 1, smalls * width // 128):
        starts.append(starts[-1] + count)
    return starts, -(-starts[-1] // 8) * 8


def scatter_kernel(bits, parts, plan, rows, lhs_ref, *refs):
    sources = len({item[0] for item in plan})
    rhs_refs, refs = refs[:sources], refs[sources:]
    (ffn_ref, hgain_ref, conv_ref, line_ref, w_ref, d_small, w_small, x_ref, dx1_ref, gain_ref, out_ref, vec_out,
     g_out) = refs[:13]
    refs = refs[3:]
    v_own, v_acc, v_in, v_z, v_send, v_recv, v_z_send, v_z_recv = refs[10:18]
    swap_own, swap_send, swap_recv = refs[18:21]
    dp_s, w_s, acc_s, dx_s, in_sem = refs[21:26]
    scatter = Scatter(bits, parts, plan, rows, [lhs_ref], rhs_refs, out_ref, refs[26:], STRIDE)
    z = lax.axis_index("mp")
    mesh_id = pl.DeviceIdType.MESH
    greet_all(bits, parts, True)
    swap = Swap(2**bits, dx_s, g_out, swap_own.at[0], swap_send.at[0], swap_recv.at[0])

    def v_hop(b):
        return pltpu.make_async_remote_copy(
            src_ref=v_own if b == 0 else v_acc.at[b - 1], dst_ref=v_in.at[b], send_sem=v_send.at[b],
            recv_sem=v_recv.at[b], device_id={"dp": scatter.partner(b)}, device_id_type=mesh_id,
        )

    def v_z_hop(src, dst, delta):
        return pltpu.make_async_remote_copy(
            src_ref=src, dst_ref=dst, send_sem=v_z_send.at[0], recv_sem=v_z_recv.at[0],
            device_id={"mp": lax.rem(z + delta, parts)}, device_id_type=mesh_id,
        )

    def small_sum(stage):
        if stage == 0:
            v_hop(0).start()
        elif stage <= bits:
            b = stage - 1
            v_hop(b).wait_recv()
            total = (v_own[...] if b == 0 else v_acc[b - 1]) + v_in[b]
            if stage < bits:
                v_acc[b] = total
                v_hop(stage).start()
            else:
                v_z[z] = total
                for delta in range(1, parts):
                    v_z_hop(v_z.at[z], v_z.at[z], delta).start()
        else:
            whole = v_z.at[pl.ds(0, parts - 1)]
            v_z_hop(whole, whole, 1).wait_recv()
            total = v_z[0]
            for s in range(1, parts):
                total = total + v_z[s]
            vec_out[...] = total
            for b in range(bits):
                v_hop(b).wait_send()
            v_z_hop(whole, whole, 1).wait_send()

    def fetch(g, slot):
        return (
            pltpu.make_async_copy(rhs_refs[0].at[g], dp_s.at[slot], in_sem.at[0, slot]),
            pltpu.make_async_copy(w_ref.at[g], w_s.at[slot], in_sem.at[1, slot]),
        )

    def input_grad():
        acc_s[...] += lax.dot_general(
            d_small[...], w_small[...], (((0,), (0,)), ((), ())), preferred_element_type=F32
        )
        blocks, token_rows, width = x_ref.shape

        def body(i, gain_sum):
            x = x_ref[i].astype(F32)
            scale = lax.rsqrt(jnp.mean(x * x, axis=-1, keepdims=True) + 1e-05)
            unit = x * scale
            at = pl.ds(pl.multiple_of(i * token_rows, token_rows), token_rows)
            d_h1 = acc_s[at]
            e = d_h1 * gain_ref[...]
            d_x = dx1_ref[at] + scale * (e - unit * jnp.mean(e * unit, axis=-1, keepdims=True))
            dx_s[i] = d_x.astype(BF16)
            return gain_sum + jnp.sum(d_h1 * unit, axis=0, keepdims=True)

        gain_sum = lax.fori_loop(0, blocks, body, jnp.zeros((1, width), F32))
        starts, _ = small_rows(conv_ref.shape[0], width, d_small.shape[0])

        def put(start, row):
            for i in range(row.shape[1] // 128):
                v_own[start + i : start + i + 1] = row[:, i * 128 : (i + 1) * 128]

        put(starts[0], gain_sum)
        put(starts[1], ffn_ref[...])
        put(starts[2], hgain_ref[...])
        for h in range(conv_ref.shape[0]):
            for tap in range(TAPS):
                put(starts[3] + (h * TAPS + tap) * HEADW // 128, conv_ref[h, tap : tap + 1])
        put(starts[4], line_ref[...])
        small_grad = lax.dot_general(
            d_small[...], scatter.lhs_s[0], (((1,), (1,)), ((), ())), preferred_element_type=F32
        )
        for i in range(d_small.shape[0]):
            put(starts[5] + i * width // 128, small_grad[i : i + 1])
        if starts[6] < v_own.shape[0]:
            v_own[starts[6] :] = jnp.zeros((v_own.shape[0] - starts[6], 128), F32)

    for copy in fetch(0, 0):
        copy.start()

    @pl.loop(0, max(scatter.ticks, 2 + parts + bits + 2))
    def _(now):
        scatter.tick(now)
        tick = now - 2

        @pl.when((tick >= 0) & (tick < parts))
        def _():
            slot = lax.rem(tick, 2)

            @pl.when(tick + 1 < parts)
            def _():
                for copy in fetch(tick + 1, 1 - slot):
                    copy.start()

            for copy in fetch(tick, slot):
                copy.wait()
            part = lax.dot_general(
                dp_s[slot], w_s[slot], (((1,), (1,)), ((), ())), preferred_element_type=F32
            )

            @pl.when(tick == 0)
            def _():
                acc_s[...] = part

            @pl.when(tick > 0)
            def _():
                acc_s[...] += part

        @pl.when(tick == parts)
        def _():
            input_grad()
            swap.start()

        for stage in range(bits + 2):
            @pl.when(tick == parts + stage)
            def _():
                small_sum(stage)

    swap.finish()
    scatter.finish()


def scatter_sum(left, pairs, smalls, weight, d_small, w_small, x, d_x1, gain, groups, parts, collective):
    width, length = left.shape
    vector = jax.ShapeDtypeStruct((small_rows(smalls[2].shape[0], width, d_small.shape[0])[1], 128), F32)
    bits = groups.bit_length() - 1
    rows = width // groups
    plan = plan_of(pairs)
    count = len(plan)
    vmem_spec = pl.BlockSpec(memory_space=pltpu.VMEM)
    any_spec = pl.BlockSpec(memory_space=pl.ANY)
    dma = lambda *shape: pltpu.SemaphoreType.DMA(shape)
    return pl.pallas_call(
        partial(scatter_kernel, bits, parts, plan, rows),
        out_shape=(
            jax.ShapeDtypeStruct((count, rows, WIDE), F32),
            jax.ShapeDtypeStruct(vector.shape, F32),
            jax.ShapeDtypeStruct(x.shape, BF16),
        ),
        in_specs=[any_spec] * (1 + len(pairs)) + [vmem_spec] * 4 + [any_spec] + [vmem_spec] * 5,
        out_specs=(vmem_spec, vmem_spec, any_spec),
        scratch_shapes=[
            pltpu.VMEM(vector.shape, F32),
            pltpu.VMEM((bits - 1,) + vector.shape, F32),
            pltpu.VMEM((bits,) + vector.shape, F32),
            pltpu.VMEM((parts,) + vector.shape, F32),
            dma(bits), dma(bits), dma(1), dma(1),
            dma(1), dma(1), dma(1),
            pltpu.VMEM((2,) + pairs[0][1].shape[1:], BF16),
            pltpu.VMEM((2,) + weight.shape[1:], BF16),
            pltpu.VMEM((length, width), F32),
            pltpu.VMEM(x.shape, BF16),
            dma(2, 2),
            *Scatter.scratch(bits, parts, count, rows, length, width),
        ],
        compiler_params=pltpu.CompilerParams(
            collective_id=collective, has_side_effects=True, vmem_limit_bytes=60 * 2**20
        ),
        cost_estimate=pl.CostEstimate(
            flops=4 * count * WIDE * parts * length * width, bytes_accessed=count * parts * length * WIDE * 4,
            transcendentals=0,
        ),
        name="scatter_sum",
    )(left, *[right for _, right in pairs], *smalls, weight, d_small, w_small, x, d_x1, gain)


def backward_kernel(
    heads, parts, bits, plan, rows_held,
    dhead_ref, o_ref, gate_ref, qe_ref, phi_ref, phil_ref,
    raw_ref, halo_ref, convw_ref, ab_ref, gain_ref, s_ref, t_ref, phi_late_ref, *refs,
):
    sources = len({item[0] for item in plan})
    kinds = len({item[1] for item in plan})
    lhs_refs, refs = refs[:kinds], refs[kinds:]
    rhs_refs, swap_in, refs = refs[:sources], refs[sources], refs[sources + 1 :]
    dproj_ref, dab_ref, dconv_ref, dgain_ref, sums_ref, swap_out = refs[:6]
    (do_s, d_s, dgate_s, dl_s, phil_s, g_s, dext_s, ext_s, send_s, recv_s, halo_send, halo_recv,
     send_sem, recv_sem, halo_send_sem, halo_recv_sem) = refs[6:22]
    scatter = Scatter(bits, parts, plan, rows_held, lhs_refs, rhs_refs, sums_ref, refs[25:], 3)
    swap = Swap(2**bits, swap_in, swap_out, *[s.at[0] for s in refs[22:25]])
    step = pl.program_id(0)
    early = pl.program_id(1) == 0
    z = lax.axis_index("mp")
    back = parts - 1 - z
    lag = parts - 1
    slots = lag + 1
    length = o_ref.shape[1]
    size = min(CHUNK, length)
    chunks = length // size

    @pl.when((step == 0) & early)
    def _():
        greet_all(bits, parts, True)
        swap.start()

    sub = pl.program_id(1)
    now = jnp.where(step < lag, step, lag + 2 * (step - lag) + sub)
    last = lag + 2 * (heads + 1) - 1
    stop = jnp.where(now == last, max(scatter.ticks, last + 1), now + 1)
    stop = jnp.where((step < lag) & early, now, stop)

    @pl.loop(now, stop)
    def _(tick):
        scatter.tick(tick)


    def hop(h):
        return pltpu.make_async_remote_copy(
            src_ref=send_s.at[h], dst_ref=recv_s.at[h], send_sem=send_sem.at[h],
            recv_sem=recv_sem.at[h], device_id={"mp": lax.rem(z + parts - 1, parts)},
            device_id_type=pl.DeviceIdType.MESH,
        )

    def halo_hop(h):
        return pltpu.make_async_remote_copy(
            src_ref=halo_send.at[h], dst_ref=halo_recv.at[h], send_sem=halo_send_sem.at[h],
            recv_sem=halo_recv_sem.at[h], device_id={"mp": lax.rem(z + parts - 1, parts)},
            device_id_type=pl.DeviceIdType.MESH,
        )

    @pl.when((step == 0) & early)
    def _():
        dgain_ref[...] = jnp.zeros_like(dgain_ref)
        g_s[...] = jnp.zeros_like(g_s)

    @pl.when((step == 0) & early & (back == 0))
    def _():
        recv_s[...] = jnp.zeros_like(recv_s)
        halo_recv[...] = jnp.zeros_like(halo_recv)

    @pl.when((step < heads) & early)
    def _():
        slot = lax.rem(step, slots)
        gslot = lax.rem(step, slots + 1)
        gain = gain_ref[...]
        d_gain = jnp.zeros((1, DV), F32)
        for c in range(chunks):
            at = slice(c * size, (c + 1) * size)
            out = o_ref[0, at]
            d_head = dhead_ref[0, at]
            gate = gate_ref[0, c * size : (c + 1) * size]
            scale = lax.rsqrt(jnp.mean(out * out, axis=-1, keepdims=True) + 1e-05)
            unit = out * scale
            sig = jax.nn.sigmoid(gate)
            gated = gate * sig
            both = d_head * unit
            d_gain = d_gain + jnp.sum(both * gated, axis=0, keepdims=True)
            e = d_head * gated * gain
            d_out = scale * (e - unit * jnp.mean(e * unit, axis=-1, keepdims=True))
            dgate_s[gslot, at] = (both * gain * sig * (1.0 + gate * (1.0 - sig))).astype(BF16)
            do_s[slot, at] = d_out
            d_s[slot, c] = mm(qe_ref[0, at], d_out, 0, 0)
        dgain_ref[...] += d_gain
        total = d_s[slot, chunks - 1]
        for c in range(chunks - 2, -1, -1):
            total = mm(phi_ref[0, c], total) + d_s[slot, c]
        dl_s[slot] = total
        phil_s[slot] = phil_ref[0]

    relay = step - back

    @pl.when((relay >= 0) & (relay < heads) & early)
    def _():
        slot = lax.rem(relay, slots)

        @pl.when(back > 0)
        def _():
            hop(relay).wait_recv()

        @pl.when(z > 0)
        def _():
            send_s[relay] = mm(phil_s[slot], recv_s[relay]) + dl_s[slot]
            hop(relay).start()

    @pl.when((step >= lag) & (step < lag + heads) & ~early)
    def _():
        head = step - lag
        slot = lax.rem(head, slots)
        eslot = lax.rem(head, 2)
        rows, cols = masks(size)
        upper = (rows <= cols).astype(F32)
        convw = convw_ref[0]
        d_state = recv_s[head]
        ext_s[0:HALO] = halo_ref[0, :, 0:HEADW]
        ext_s[HALO:] = raw_ref[0, 0:size, 0:HEADW]
        d_states = [None] * chunks
        d_states[chunks - 1] = d_state
        for c in range(chunks - 1, 0, -1):
            d_states[c - 1] = mm(phi_late_ref[0, c], d_states[c]) + d_s[slot, c]
        taps_grad = [None] * chunks

        def work(c):
            at = slice(c * size, (c + 1) * size)
            shifted = windows(raw_ref, ext_s, c, size)
            conv = conv_of(shifted, convw)
            sig, q_silu, k_silu, value, q_scale, k_scale = unit_parts(conv)
            query = q_silu * (q_scale * DK ** (-0.5))
            keyed = k_silu * k_scale
            yield
            gamma_row, gamma_col, beta = decays(ab_ref, c * size, size, upper)
            inclusive, strict = fades(gamma_row, gamma_col, rows, cols)
            gram = mm(jnp.concatenate([keyed, query], axis=0), keyed, 1, 1)
            yield
            gram_f = gram[:size] * strict
            lower = beta * gram_f
            scores = gram[size:] * inclusive
            growth = jnp.exp(gamma_col)
            last = gamma_row[:, size - 1 :]
            tail = jnp.exp(last - gamma_col)
            query_g = query * growth
            grown = keyed * growth
            keyed_b = beta * grown
            keyed_g = keyed * tail
            state = s_ref[0, c]
            d_state = d_states[c]
            inverse = t_ref[0, c]
            d_out = do_s[slot, at]
            held = mm(keyed_b, state)
            yield
            fresh = mm(inverse, beta * value - held)
            yield
            d_fresh = mm(scores, d_out, 0, 0) + mm(keyed_g, d_state)
            yield
            d_rhs = mm(inverse, d_fresh, 0, 0)
            yield
            stacked = jnp.concatenate([d_out, d_rhs], axis=0)
            by_fresh = mm(stacked, fresh, 1, 1)
            yield
            by_state = mm(stacked, state, 1, 1)
            yield
            d_scores = by_fresh[:size] * inclusive
            d_lower = -by_fresh[size:]
            d_query_g = by_state[:size]
            d_keyed_b = -by_state[size:]
            d_keyed_g = mm(fresh, d_state, 1, 1)
            yield
            d_gram = d_lower * (beta * strict)
            by_keyed = mm(jnp.concatenate([d_scores, d_gram], axis=0), keyed)
            yield
            d_query = by_keyed[:size] + growth * d_query_g
            d_keyed = (
                by_keyed[size:]
                + mm(jnp.concatenate([d_scores, d_gram], axis=0),
                     jnp.concatenate([query, keyed], axis=0), 0, 0)
                + (beta * growth) * d_keyed_b
                + tail * d_keyed_g
            )
            yield
            d_value = beta * d_rhs
            d_beta = (
                jnp.sum(d_rhs * value, axis=-1, keepdims=True)
                + jnp.sum(d_lower * gram_f, axis=-1, keepdims=True)
                + jnp.sum(d_keyed_b * grown, axis=-1, keepdims=True)
            )
            moved = by_fresh[:size] * scores + d_lower * lower
            tail_part = jnp.sum(d_keyed_g * keyed_g, axis=-1, keepdims=True)
            d_gamma = (
                jnp.sum(moved, axis=-1, keepdims=True)
                + jnp.sum(d_query_g * query_g, axis=-1, keepdims=True)
                + jnp.sum(d_keyed_b * keyed_b, axis=-1, keepdims=True)
                - tail_part
            )
            at_end = jnp.sum(tail_part, axis=0, keepdims=True) + jnp.exp(last) * jnp.sum(
                jnp.sum(state * d_state, axis=-1, keepdims=True), axis=0, keepdims=True
            )
            lanes = lax.broadcasted_iota(jnp.int32, (size, DK), 1)
            packed = jnp.where(lanes == 0, d_gamma, jnp.where(lanes == 1, d_beta, 0.0)).T[:8]
            row_id = lax.broadcasted_iota(jnp.int32, packed.shape, 0)
            packed = packed - jnp.where(row_id == 0, jnp.sum(moved, axis=0, keepdims=True), 0.0)
            yield
            summed = mm(packed, upper, 1, 1) + at_end
            dab_ref[0, :, at] = jnp.where(row_id == 0, summed, packed)
            d_q_silu = (DK ** (-0.5) * q_scale) * (
                d_query
                - q_silu * (q_scale * q_scale) * jnp.sum(q_silu * d_query, axis=-1, keepdims=True)
            )
            d_k_silu = k_scale * (
                d_keyed
                - k_silu * (k_scale * k_scale) * jnp.sum(k_silu * d_keyed, axis=-1, keepdims=True)
            )
            d_silu = jnp.concatenate([d_q_silu, d_k_silu, d_value], axis=1)
            d_conv = d_silu * sig * (1.0 + conv * (1.0 - sig))
            g_s[HALO + c * size : HALO + (c + 1) * size] = d_conv
            taps_grad[c] = [jnp.sum(shifted[i] * d_conv, axis=0, keepdims=True) for i in range(TAPS)]

        for first in range(0, chunks, 2):
            in_step([work(c) for c in range(first, min(first + 2, chunks))])
        d_conv_rows = [sum(row[i] for row in taps_grad[1:]) + taps_grad[0][i] for i in range(TAPS)]
        for i in range(TAPS):
            dconv_ref[0, i : i + 1] = d_conv_rows[i]
        for base, count in [(0, HALO)] + [(HALO + c * size, size) for c in range(chunks)]:
            d_raw = None
            for i in range(TAPS):
                part = g_s[pl.ds(base + TAPS - 1 - i, count)] * convw[i : i + 1]
                d_raw = part if d_raw is None else d_raw + part
            if base == 0:
                halo_send[head] = d_raw
            else:
                dext_s[eslot, base - HALO : base - HALO + count] = d_raw

        @pl.when(z > 0)
        def _():
            halo_hop(head).start()

    @pl.when((step > lag) & ~early)
    def _():
        head = step - lag - 1
        eslot = lax.rem(head, 2)
        gslot = lax.rem(head, slots + 1)

        @pl.when(back > 0)
        def _():
            halo_hop(head).wait_recv()

        dext_s[eslot, length - HALO : length] += halo_recv[head]
        dproj_ref[0, :, 0:HEADW] = dext_s[eslot].astype(BF16)
        dproj_ref[0, :, HEADW:] = dgate_s[gslot]

    @pl.when((step == pl.num_programs(0) - 1) & ~early)
    def _():
        scatter.finish()
        swap.finish()

    @pl.when((step == pl.num_programs(0) - 1) & ~early & (z > 0))
    def _():
        @pl.loop(0, heads)
        def _(h):
            hop(h).wait_send()
            halo_hop(h).wait_send()


def assemble_kernel(
    per, base, ffn_ref, proj_ref, vec_ref, y_ref, g_ref,
    query_ref, key_ref, value_ref, outgate_ref, out_ref, gate_ref, up_ref, down_ref, conv_ref, y_out, g_out,
):
    y_out[...] = y_ref[...]
    g_out[...] = g_ref[...]
    for h in range(per):
        query_ref[:, h * DK : (h + 1) * DK] = proj_ref[3 * h, :, 0:DK]
        key_ref[:, h * DK : (h + 1) * DK] = proj_ref[3 * h, :, DK:]
        value_ref[:, h * DV : (h + 1) * DV] = proj_ref[3 * h + 1]
        outgate_ref[:, h * DV : (h + 1) * DV] = proj_ref[3 * h + 2]
    piece = 0
    for target in (down_ref, gate_ref, up_ref):
        total = target.shape[0]
        for start in range(0, total, WIDE):
            size = min(WIDE, total - start)
            target[start : start + size] = ffn_ref[piece].T[0:size]
            piece += 1
    for start in range(0, out_ref.shape[1], WIDE):
        out_ref[:, start : start + WIDE] = ffn_ref[piece]
        piece += 1
    width = conv_ref.shape[1]
    heads = width // HEADW
    for h in range(heads):
        for tap in range(TAPS):
            row = base + (h * TAPS + tap) * HEADW // 128
            spots = [h * DK, (heads + h) * DK, 2 * heads * DK + h * DV, 2 * heads * DK + h * DV + 128]
            for i, spot in enumerate(spots):
                conv_ref[tap : tap + 1, spot : spot + 128] = vec_ref[row + i : row + i + 1]


def assemble(ffn, proj, vec, y, g, per, hidden, base, conv_shape):
    rows = ffn.shape[1]
    f32 = lambda *shape: jax.ShapeDtypeStruct(shape, F32)
    vmem_spec = pl.BlockSpec(memory_space=pltpu.VMEM)
    return pl.pallas_call(
        partial(assemble_kernel, per, base),
        out_shape=(
            f32(rows, per * DK), f32(rows, per * DK), f32(rows, per * DV), f32(rows, per * DV), f32(rows, per * DV),
            f32(hidden, rows), f32(hidden, rows), f32(hidden, rows), f32(*conv_shape),
            jax.ShapeDtypeStruct(y.shape, BF16), jax.ShapeDtypeStruct(g.shape, BF16),
        ),
        in_specs=[vmem_spec] * 5,
        out_specs=(vmem_spec,) * 11,
        compiler_params=pltpu.CompilerParams(vmem_limit_bytes=40 * 2**20),
        cost_estimate=pl.CostEstimate(flops=0, bytes_accessed=10 * 2**20, transcendentals=0),
        name="assemble",
    )(ffn, proj, vec, y, g)


def forward_core(raw, convw, ab, gain, swapped, weights, heads, parts, groups):
    bits = groups.bit_length() - 1
    pieces = []
    for w, weight in enumerate(weights):
        wide = weight.shape[1]
        pieces += [(w, at, at + WIDE // 2, at + WIDE) for at in range(0, wide, WIDE)]
    rows = weights[0].shape[0]
    any_spec = pl.BlockSpec(memory_space=pl.ANY)
    length = raw.shape[1]
    size = min(CHUNK, length)
    chunks = length // size
    per = heads // raw.shape[0]
    lag = parts - 1
    slots = lag + 1
    now = lambda s: jnp.minimum(s, heads - 1)
    late = lambda s: jnp.maximum(s - lag, 0)
    return pl.pallas_call(
        partial(forward_kernel, heads, parts, bits, pieces),
        grid=(heads + lag, 2),
        out_shape=(
            jax.ShapeDtypeStruct((raw.shape[0], length, per * DV), BF16),
            jax.ShapeDtypeStruct((heads, length, DV), F32),
            jax.ShapeDtypeStruct((heads, chunks, DK, DV), F32),
            jax.ShapeDtypeStruct((heads, chunks, size, size), F32),
            jax.ShapeDtypeStruct((heads, length, DK), F32),
            jax.ShapeDtypeStruct((heads, chunks, DK, DK), F32),
            jax.ShapeDtypeStruct((heads, DK, DK), F32),
            jax.ShapeDtypeStruct((parts, HALO, per * (HEADW + DV)), F32),
            jax.ShapeDtypeStruct(swapped.shape, BF16),
            *[jax.ShapeDtypeStruct((parts, groups) + w.shape, BF16) for w in weights],
        ),
        in_specs=[
            pl.BlockSpec((1, length, HEADW + DV), lambda s, _: (now(s) // per, 0, now(s) % per)),
            pl.BlockSpec((1, length, DV), lambda s, _: (late(s) // per, 0, (late(s) % per) * 3 + 2)),
            any_spec,
            pl.BlockSpec((1, TAPS, HEADW), lambda s, _: (now(s), 0, 0)),
            pl.BlockSpec((1, 8, length), lambda s, _: (now(s), 0, 0)),
            pl.BlockSpec((1, DV), lambda s, _: (0, 0)),
            *[any_spec] * (1 + len(weights)),
        ],
        out_specs=(
            pl.BlockSpec((1, length, DV), lambda s, _: (late(s) // per, 0, late(s) % per)),
            pl.BlockSpec((1, length, DV), lambda s, _: (late(s), 0, 0)),
            pl.BlockSpec((1, chunks, DK, DV), lambda s, _: (late(s), 0, 0, 0)),
            pl.BlockSpec((1, chunks, size, size), lambda s, _: (now(s), 0, 0, 0)),
            pl.BlockSpec((1, length, DK), lambda s, _: (now(s), 0, 0)),
            pl.BlockSpec((1, chunks, DK, DK), lambda s, _: (now(s), 0, 0, 0)),
            pl.BlockSpec((1, DK, DK), lambda s, _: (now(s), 0, 0)),
            pl.BlockSpec((parts, HALO, per * (HEADW + DV)), lambda s, _: (0, 0, 0)),
            *[any_spec] * (1 + len(weights)),
        ),
        scratch_shapes=[
            pltpu.VMEM((slots, length, DK), F32),
            pltpu.VMEM((slots, length, DV), F32),
            pltpu.VMEM((slots, chunks, DK, DK), F32),
            pltpu.VMEM((slots, chunks, DK, DV), F32),
            pltpu.VMEM((slots, DK, DK), F32),
            pltpu.VMEM((slots, DK, DV), F32),
            pltpu.VMEM((heads, DK, DV), F32),
            pltpu.VMEM((heads, DK, DV), F32),
            pltpu.VMEM((parts, HALO, per * (HEADW + DV)), F32),
            pltpu.VMEM((HALO + size, HEADW), F32),
            pltpu.SemaphoreType.DMA((heads,)),
            pltpu.SemaphoreType.DMA((heads,)),
            pltpu.SemaphoreType.DMA((parts,)),
            pltpu.SemaphoreType.DMA((parts,)),
            *[pltpu.SemaphoreType.DMA((1,))] * 3,
            *Gather.scratch(bits, len(pieces)),
        ],
        compiler_params=pltpu.CompilerParams(
            collective_id=0, has_side_effects=True, vmem_limit_bytes=56 * 2**20
        ),
        cost_estimate=pl.CostEstimate(flops=20 * 10**9, bytes_accessed=40 * 2**20, transcendentals=0),
        name="delta_forward",
    )(raw, raw, raw, convw, ab, gain, swapped, *weights)


def backward_core(d_head, out, raw, halo, query_e, phi, phi_all, convw, ab, gain, states, inverses, lefts, pairs, swapped,
                  heads, parts, groups):
    length = raw.shape[1]
    size = min(CHUNK, length)
    chunks = length // size
    per = heads // raw.shape[0]
    lag = parts - 1
    slots = lag + 1
    bits = groups.bit_length() - 1
    plan = plan_of(pairs)
    rows = lefts[0].shape[0] // groups
    any_spec = pl.BlockSpec(memory_space=pl.ANY)
    now = lambda s: jnp.minimum(s, heads - 1)
    late = lambda s: jnp.clip(s - lag, 0, heads - 1)
    later = lambda s: jnp.maximum(s - lag - 1, 0)
    return pl.pallas_call(
        partial(backward_kernel, heads, parts, bits, plan, rows),
        grid=(heads + lag + 1, 2),
        out_shape=(
            jax.ShapeDtypeStruct((raw.shape[0], length, per * (HEADW + DV)), BF16),
            jax.ShapeDtypeStruct((heads, 8, length), F32),
            jax.ShapeDtypeStruct((heads, TAPS, HEADW), F32),
            jax.ShapeDtypeStruct((1, DV), F32),
            jax.ShapeDtypeStruct((len(plan), rows, WIDE), F32),
            jax.ShapeDtypeStruct(swapped.shape, BF16),
        ),
        in_specs=[
            pl.BlockSpec((1, length, DV), lambda s, _: (now(s) // per, 0, now(s) % per)),
            pl.BlockSpec((1, length, DV), lambda s, _: (now(s), 0, 0)),
            pl.BlockSpec((1, length, DV), lambda s, _: (now(s) // per, 0, (now(s) % per) * 3 + 2)),
            pl.BlockSpec((1, length, DK), lambda s, _: (now(s), 0, 0)),
            pl.BlockSpec((1, chunks, DK, DK), lambda s, _: (now(s), 0, 0, 0)),
            pl.BlockSpec((1, DK, DK), lambda s, _: (now(s), 0, 0)),
            pl.BlockSpec((1, length, HEADW + DV), lambda s, _: (late(s) // per, 0, late(s) % per)),
            pl.BlockSpec((1, HALO, HEADW + DV), lambda s, _: (late(s) // per, 0, late(s) % per)),
            pl.BlockSpec((1, TAPS, HEADW), lambda s, _: (late(s), 0, 0)),
            pl.BlockSpec((1, 8, length), lambda s, _: (late(s), 0, 0)),
            pl.BlockSpec((1, DV), lambda s, _: (0, 0)),
            pl.BlockSpec((1, chunks, DK, DV), lambda s, _: (late(s), 0, 0, 0)),
            pl.BlockSpec((1, chunks, size, size), lambda s, _: (late(s), 0, 0, 0)),
            pl.BlockSpec((1, chunks, DK, DK), lambda s, _: (late(s), 0, 0, 0)),
            *[any_spec] * (1 + len(lefts) + len(pairs)),
        ],
        out_specs=(
            pl.BlockSpec((1, length, HEADW + DV), lambda s, _: (later(s) // per, 0, later(s) % per)),
            pl.BlockSpec((1, 8, length), lambda s, _: (late(s), 0, 0)),
            pl.BlockSpec((1, TAPS, HEADW), lambda s, _: (late(s), 0, 0)),
            pl.BlockSpec((1, DV), lambda s, _: (0, 0)),
            pl.BlockSpec((len(plan), rows, WIDE), lambda s, _: (0, 0, 0)),
            any_spec,
        ),
        scratch_shapes=[
            pltpu.VMEM((slots, length, DV), F32),
            pltpu.VMEM((slots, chunks, DK, DV), F32),
            pltpu.VMEM((slots + 1, length, DV), BF16),
            pltpu.VMEM((slots, DK, DV), F32),
            pltpu.VMEM((slots, DK, DK), F32),
            pltpu.VMEM((length + 2 * HALO, HEADW), F32),
            pltpu.VMEM((2, length, HEADW), F32),
            pltpu.VMEM((HALO + size, HEADW), F32),
            pltpu.VMEM((heads, DK, DV), F32),
            pltpu.VMEM((heads, DK, DV), F32),
            pltpu.VMEM((heads, HALO, HEADW), F32),
            pltpu.VMEM((heads, HALO, HEADW), F32),
            pltpu.SemaphoreType.DMA((heads,)),
            pltpu.SemaphoreType.DMA((heads,)),
            pltpu.SemaphoreType.DMA((heads,)),
            pltpu.SemaphoreType.DMA((heads,)),
            *[pltpu.SemaphoreType.DMA((1,))] * 3,
            *Scatter.scratch(bits, parts, len(plan), rows, length, lefts[0].shape[0]),
        ],
        compiler_params=pltpu.CompilerParams(
            collective_id=1, has_side_effects=True, vmem_limit_bytes=62 * 2**20
        ),
        cost_estimate=pl.CostEstimate(flops=40 * 10**9, bytes_accessed=60 * 2**20, transcendentals=0),
        name="delta_backward",
    )(d_head, out, raw, query_e, phi, phi_all, raw, halo, convw, ab, gain, states, inverses, phi,
      *lefts, *[right for _, right in pairs], swapped)


def dot(spec, a, b):
    return jnp.einsum(spec, a, b, preferred_element_type=F32)


def unit_rms(v):
    return lax.rsqrt(jnp.mean(v * v, axis=-1, keepdims=True) + 1e-05)


def per_device(
    tokens, out_grad, seq_lengths, mix_gain, w_query, w_key, w_value, w_outgate, w_decay, w_beta,
    conv_weight, rate_log, step_bias, head_gain, w_out, ffn_gain, w_ffn_gate, w_ffn_up, w_ffn_down,
):
    groups = lax.axis_size("dp")
    parts = lax.axis_size("mp")
    group = lax.axis_index("dp")
    share = lax.axis_index("mp")
    heads = rate_log.shape[0]
    per = heads // parts
    width = tokens.shape[2]
    local_rows = w_query.shape[0]

    hidden = w_ffn_gate.shape[1]
    wide = -(-hidden // WIDE) * WIDE
    small_w = jnp.concatenate([w_decay, w_beta], axis=1).T
    small_w = jnp.pad(small_w, ((0, -small_w.shape[0] % 16), (0, 0)))
    x_bf, g_proj, g_small, raw, h1, h1_t, *padded = prologue(
        tokens, small_w, mix_gain[None], (w_query, w_key, w_value, w_outgate),
        (w_ffn_gate.T, w_ffn_up.T, w_ffn_down.T), groups, parts,
    )
    h1 = h1.reshape(-1, width)
    whole = lambda g: g.reshape(parts, width, g.shape[3])
    g_proj = whole(g_proj)
    g_small = g_small[:, :, : 2 * per].transpose(0, 2, 1, 3).reshape(parts, 2 * per, width)
    x_swapped = x_bf
    x_bf = x_bf.reshape(-1, width)
    length = x_bf.shape[0]

    my_length = lax.dynamic_slice_in_dim(seq_lengths, group, 1)
    positions = share * length + jnp.arange(length, dtype=jnp.int32)
    live = (positions < my_length).astype(F32)[:, None]

    x = x_bf.astype(F32)
    small = dot("td,gcd->gct", h1, g_small)
    decay_raw = small[:, :per].reshape(heads, length)
    beta_raw = small[:, per:].reshape(heads, length)
    rate = -jnp.exp(rate_log)[:, None]
    shifted = decay_raw + step_bias[:, None]
    decay = rate * jax.nn.softplus(shifted)
    beta = jax.nn.sigmoid(beta_raw)
    ab = jnp.concatenate(
        [decay[:, None], beta[:, None], jnp.zeros((heads, 6, length), F32)], axis=1
    )
    taps = conv_weight.shape[0]
    key_cols = heads * DK
    convw = jnp.concatenate(
        [
            conv_weight[:, :key_cols].reshape(taps, heads, DK),
            conv_weight[:, key_cols : 2 * key_cols].reshape(taps, heads, DK),
            conv_weight[:, 2 * key_cols :].reshape(taps, heads, DV),
        ],
        axis=2,
    ).transpose(1, 0, 2)
    gain_row = head_gain[None]
    head_out, mixed, states, inverses, query_e, phi, phi_all, halo, dy_bf, *rest = forward_core(
        raw, convw, ab, gain_row, out_grad,
        [w_out] + padded,
        heads, parts, groups,
    )
    g_out, g_gate, g_up, g_down = [whole(w) for w in rest]

    dy = live * dy_bf.reshape(-1, width).astype(F32)
    d_ffo = dy.astype(BF16)
    x1 = x + dot("gtc,gmc->tm", head_out, g_out)
    scale2 = unit_rms(x1)
    n2 = x1 * scale2
    h2 = (n2 * ffn_gain).astype(BF16)
    gate = dot("td,gdf->gtf", h2, g_gate)
    up = dot("td,gdf->gtf", h2, g_up)
    sig = jax.nn.sigmoid(gate)
    act = (gate * sig * up).astype(BF16)
    block_out = (live * (x1 + dot("gtf,gdf->td", act, g_down))).astype(BF16)
    d_act = dot("td,gdf->gtf", d_ffo, g_down)
    d_gate = (d_act * up * sig * (1.0 + gate * (1.0 - sig))).astype(BF16)
    d_up = (d_act * gate * sig).astype(BF16)
    d_h2 = dot("gtf,gdf->td", d_gate, g_gate) + dot("gtf,gdf->td", d_up, g_up)
    e2 = d_h2 * ffn_gain
    d_x1 = dy + scale2 * (e2 - n2 * jnp.mean(e2 * n2, axis=-1, keepdims=True))
    ffn_gain_grad = jnp.sum(d_h2 * n2, axis=0)
    d_mix = d_x1.astype(BF16)
    d_head = dot("tm,gmc->gtc", d_mix, g_out)

    d_proj, d_ab, d_convw, d_head_gain, sums_ffn, final_out = backward_core(
        d_head, mixed, raw, halo, query_e, phi, phi_all, convw, ab, gain_row, states, inverses,
        [d_mix.T, h2.T, d_ffo.T], [(2, act), (1, d_gate), (1, d_up), (0, head_out)],
        block_out.reshape(tokens.shape), heads, parts, groups,
    )
    d_decay = d_ab[:, 0]
    d_beta_raw = d_ab[:, 1] * beta * (1.0 - beta)
    d_decay_raw = d_decay * rate * jax.nn.sigmoid(shifted)
    rate_grad = jnp.sum(d_decay * decay, axis=1)
    bias_grad = jnp.sum(d_decay_raw, axis=1)
    d_small = jnp.concatenate(
        [d_decay_raw.reshape(parts, per, length), d_beta_raw.reshape(parts, per, length)], axis=1
    ).astype(BF16)
    line = jnp.pad(jnp.concatenate([rate_grad, bias_grad])[None], ((0, 0), (0, 128 - 2 * heads)))
    sums_proj, sums, final_grad = scatter_sum(
        h1_t, [(0, d_proj)],
        (ffn_gain_grad[None], d_head_gain, d_convw, line), g_proj, d_small.reshape(-1, length),
        g_small.reshape(-1, width), x_swapped, d_x1, mix_gain[None], groups, parts, 2,
    )
    starts, _ = small_rows(heads, width, 2 * heads)
    part = lambda i: sums[starts[i] : starts[i + 1]].reshape(-1)
    (s_query, s_key, s_value, s_outgate, s_out, s_gate, s_up, s_down, s_conv, final_out, final_grad) = assemble(
        sums_ffn, sums_proj, sums, final_out, final_grad, per, hidden, starts[3], conv_weight.shape
    )
    small_sum = part(5).reshape(parts, 2 * per, width)
    mine = lax.dynamic_slice(small_sum, (share, 0, group * local_rows), (1, 2 * per, local_rows))[0].T

    return (
        final_out,
        final_grad,
        part(0),
        s_query,
        s_key,
        s_value,
        s_outgate,
        mine[:, :per],
        mine[:, per:],
        s_conv,
        part(4)[:heads],
        part(4)[heads : 2 * heads],
        part(2),
        s_out,
        part(1),
        s_gate.T,
        s_up.T,
        s_down.T,
    )


def solution(mesh):
    seq = P(None, ("mp", "dp"), None)
    shard = P("dp", "mp")
    rep = P()
    return jax.shard_map(
        per_device,
        mesh=mesh,
        in_specs=(
            seq, seq, rep, rep, shard, shard, shard, shard, shard, shard,
            rep, rep, rep, rep, shard, rep, shard, shard, shard,
        ),
        out_specs=(
            seq, seq, rep, shard, shard, shard, shard, shard, shard,
            rep, rep, rep, rep, shard, rep, shard, shard, shard,
        ),
        check_vma=False,
    )
```

```python
from functools import partial

import jax
import jax.numpy as jnp
from jax import lax
from jax.experimental import pallas as pl
from jax.experimental.pallas import tpu as pltpu
from jax.sharding import PartitionSpec as P

DK = 128
DV = 256
HEADW = 2 * DK + DV
TAPS = 4
CHUNK = 128
HALO = 8
WIDE = 256
STRIDE = 2
F32 = jnp.float32
BF16 = jnp.bfloat16


def halves(a):
    high = a.astype(BF16)
    return high, (a - high.astype(F32)).astype(BF16)


def mm(a, b, ca=1, cb=0):
    dims = (((ca,), (cb,)), ((), ()))
    a_high, a_low = halves(a)
    b_high, b_low = halves(b)
    one = lambda p, q: lax.dot_general(p, q, dims, preferred_element_type=F32)
    if a.shape[ca] <= 128:
        return one(
            jnp.concatenate([a_high, a_low], axis=ca), jnp.concatenate([b_high, b_high], axis=cb)
        ) + one(a_high, b_low)
    return one(a_high, b_high) + (one(a_high, b_low) + one(a_low, b_high))


def windows(raw_ref, ext_s, c, size):
    if c == 0:
        return [ext_s[pl.ds(HALO - TAPS + 1 + i, size)] for i in range(TAPS)]
    return [raw_ref[0, pl.ds(c * size - TAPS + 1 + i, size), 0:HEADW] for i in range(TAPS)]


def conv_of(shifted, convw):
    total = None
    for i in range(TAPS):
        part = shifted[i] * convw[i : i + 1]
        total = part if total is None else total + part
    return total


def decays(ab_ref, base, rows, upper):
    ab = ab_ref[0, :, pl.ds(base, rows)]
    cum = mm(ab, upper)
    row_id = lax.broadcasted_iota(jnp.int32, ab.shape, 0)
    both = jnp.where(row_id == 0, cum, ab)
    cols = both.T
    return both[0:1], cols[:, 0:1], cols[:, 1:2]


def masks(size):
    rows = lax.broadcasted_iota(jnp.int32, (size, size), 0)
    cols = lax.broadcasted_iota(jnp.int32, (size, size), 1)
    return rows, cols


def fades(gamma_row, gamma_col, rows, cols):
    spread = jnp.minimum(gamma_col - gamma_row, 0.0)
    inclusive = jnp.where(rows >= cols, jnp.exp(spread), 0.0)
    strict = jnp.where(rows > cols, inclusive, 0.0)
    return inclusive, strict


def invert_many(lowers, rows, cols):
    size = lowers[0].shape[0]
    eye = (rows == cols).astype(F32)
    pair = ((rows // 2) == (cols // 2)) & (rows > cols)
    inverses = [eye - jnp.where(pair, low, 0.0) for low in lowers]
    width = 2
    while width < size:
        within = (rows // (2 * width)) == (cols // (2 * width))
        cross = within & ((rows // width) != (cols // width)) & (rows > cols)
        inner = [mm(jnp.where(cross, low, 0.0), inv) for low, inv in zip(lowers, inverses)]
        inverses = [inv - mm(inv, part) for inv, part in zip(inverses, inner)]
        width *= 2
    return inverses


def in_step(works):
    while works:
        works = [work for work in works if next(work, True) is None]


def unit_parts(conv):
    sig = jax.nn.sigmoid(conv)
    silu = conv * sig
    q_silu = silu[:, :DK]
    k_silu = silu[:, DK : 2 * DK]
    value = silu[:, 2 * DK :]
    q_scale = lax.rsqrt(jnp.sum(q_silu * q_silu, axis=-1, keepdims=True) + 1e-06)
    k_scale = lax.rsqrt(jnp.sum(k_silu * k_silu, axis=-1, keepdims=True) + 1e-06)
    return sig, q_silu, k_silu, value, q_scale, k_scale


class Gather:
    def __init__(self, bits, parts, sources, targets, pieces, sems):
        self.bits, self.parts, self.pieces = bits, parts, pieces
        self.sources, self.targets = sources, targets
        (self.own, self.z_send, self.z_recv, self.p_send, self.p_recv, self.s_send, self.s_recv) = sems
        self.d, self.z = lax.axis_index("dp"), lax.axis_index("mp")
        self.orders = (list(range(1, bits)), list(range(bits - 1, 0, -1)))
        self.ticks = bits + 1

    @staticmethod
    def scratch(bits, count):
        dma = lambda *shape: pltpu.SemaphoreType.DMA(shape)
        return [
            dma(count), dma(count), dma(count), dma(count, bits - 1, 2), dma(count, bits - 1, 2),
            dma(count), dma(count),
        ]

    def flip(self, index, b):
        return index + (1 - 2 * lax.rem(lax.div(self.d, 2**b), 2)) * 2**b

    def copy(self, src, dst, send, recv, to):
        return pltpu.make_async_remote_copy(
            src_ref=src, dst_ref=dst, send_sem=send, recv_sem=recv, device_id=to,
            device_id_type=pl.DeviceIdType.MESH,
        )

    def sides(self, p):
        _, start, mid, stop = self.pieces[p]
        return [(0, start, mid)] + ([(1, mid, stop)] if mid < stop else [])

    def held(self, side, k):
        out = [self.d]
        for b in self.orders[side][:k]:
            out = out + [self.flip(i, b) for i in out]
        return out

    def arrived(self, side, k):
        return [self.flip(i, self.orders[side][k]) for i in self.held(side, k)]

    def to_sibling(self, p, indices, start, stop):
        target = self.targets[self.pieces[p][0]]
        for i in indices:
            block = target.at[:, i, :, start:stop]
            self.copy(
                block, block, self.s_send.at[p], self.s_recv.at[p], {"dp": self.flip(self.d, 0)}
            ).start()

    def along(self, p, k, act):
        target = self.targets[self.pieces[p][0]]
        for side, start, stop in self.sides(p):
            b = self.orders[side][k]
            for i in self.held(side, k):
                block = target.at[:, i, :, start:stop]
                act(
                    self.copy(
                        block, block, self.p_send.at[p, k, side], self.p_recv.at[p, k, side],
                        {"dp": self.flip(self.d, b)},
                    )
                )

    def along_whole(self, p, k):
        target = self.targets[self.pieces[p][0]]
        out = []
        for side, start, stop in self.sides(p):
            block = target.at[:, pl.ds(0, 2**k), :, start:stop]
            out.append(
                self.copy(
                    block, block, self.p_send.at[p, k, side], self.p_recv.at[p, k, side],
                    {"dp": self.flip(self.d, self.orders[side][k])},
                )
            )
        return out

    def tick(self, p, stage):
        which, start, _, stop = self.pieces[p]
        source, target = self.sources[which], self.targets[which]
        if stage == 0:
            pltpu.make_async_copy(
                source.at[:, start:stop], target.at[self.z, self.d, :, start:stop], self.own.at[p]
            ).start()
            for delta in range(1, self.parts):
                self.copy(
                    source.at[:, start:stop], target.at[self.z, self.d, :, start:stop], self.z_send.at[p],
                    self.z_recv.at[p], {"mp": lax.rem(self.z + delta, self.parts)},
                ).start()
        elif stage == 1:
            pltpu.make_async_copy(
                source.at[:, start:stop], target.at[self.z, self.d, :, start:stop], self.own.at[p]
            ).wait()
            self.z_whole(p).wait_recv()
            self.along(p, 0, lambda copy: copy.start())
            self.to_sibling(p, [self.d], start, stop)
        elif stage <= self.bits:
            k = stage - 2
            for copy in self.along_whole(p, k):
                copy.wait_recv()
            if k + 1 < self.bits - 1:
                self.along(p, k + 1, lambda copy: copy.start())
            for side, low, high in self.sides(p):
                self.to_sibling(p, self.arrived(side, k), low, high)

    def moves(self):
        return len(self.pieces) + STRIDE * (self.ticks - 1)

    def move(self, now):
        for p in range(len(self.pieces)):
            if now >= p and (now - p) % STRIDE == 0 and (now - p) // STRIDE < self.ticks:
                self.tick(p, (now - p) // STRIDE)

    def z_whole(self, p):
        which, start, _, stop = self.pieces[p]
        block = self.targets[which].at[pl.ds(0, self.parts - 1), self.d, :, start:stop]
        return self.copy(
            block, block, self.z_send.at[p], self.z_recv.at[p],
            {"mp": lax.rem(self.z + 1, self.parts)},
        )

    def s_whole(self, p):
        which, start, _, stop = self.pieces[p]
        block = self.targets[which].at[:, pl.ds(0, 2 ** (self.bits - 1)), :, start:stop]
        return self.copy(
            block, block, self.s_send.at[p], self.s_recv.at[p], {"dp": self.flip(self.d, 0)}
        )

    def finish(self, waited=()):
        for p in range(len(self.pieces)):
            if p not in waited:
                self.s_whole(p).wait_recv()
            self.z_whole(p).wait_send()
            for k in range(self.bits - 1):
                for copy in self.along_whole(p, k):
                    copy.wait_send()
            self.s_whole(p).wait_send()


def greet_all(bits, parts, every):
    d, z = lax.axis_index("dp"), lax.axis_index("mp")
    barrier = pltpu.get_barrier_semaphore()
    if every:
        peers = [lax.rem(d + delta, 2**bits) for delta in range(1, 2**bits)]
    else:
        peers = [d + (1 - 2 * lax.rem(lax.div(d, 2**b), 2)) * 2**b for b in range(bits)]
    for peer in peers:
        pl.semaphore_signal(
            barrier, inc=1, device_id={"dp": peer}, device_id_type=pl.DeviceIdType.MESH
        )
    for delta in range(1, parts):
        pl.semaphore_signal(
            barrier, inc=1, device_id={"mp": lax.rem(z + delta, parts)},
            device_id_type=pl.DeviceIdType.MESH,
        )
    pl.semaphore_wait(barrier, len(peers) + parts - 1)


class Swap:
    def __init__(self, groups, source, target, own, send, recv):
        self.groups, self.source, self.target = groups, source, target
        self.own, self.send, self.recv = own, send, recv
        self.d = lax.axis_index("dp")

    def copy(self, src, dst, to):
        return pltpu.make_async_remote_copy(
            src_ref=src, dst_ref=dst, send_sem=self.send, recv_sem=self.recv, device_id={"dp": to},
            device_id_type=pl.DeviceIdType.MESH,
        )

    def local(self):
        return pltpu.make_async_copy(self.source.at[self.d], self.target.at[self.d], self.own)

    def start(self):
        self.local().start()
        for delta in range(1, self.groups):
            to = lax.rem(self.d + delta, self.groups)
            self.copy(self.source.at[to], self.target.at[self.d], to).start()

    def finish(self):
        self.local().wait()
        block = self.target.at[pl.ds(0, self.groups - 1)]
        whole = self.copy(block, block, lax.rem(self.d + 1, self.groups))
        whole.wait_recv()
        whole.wait_send()


def prologue_kernel(bits, parts, pieces, *refs):
    tokens, small, gain, *refs = refs
    members, narrow, refs = refs[:4], refs[4:7], refs[7:]
    tokens_out, joined_out, small_out, raw_out, h1_out, h1t_out = refs[:6]
    padded, refs = refs[6:9], refs[9:]
    member_s, narrow_s, padded_s, refs = refs[:4], refs[4:7], refs[7:10], refs[10:]
    in_sem, out_sem, joined, x_s, w_s, raw_s, x_sem, w_sem, raw_sem, *sems = refs
    loads = [
        pltpu.make_async_copy(src, dst, in_sem.at[i])
        for i, (src, dst) in enumerate(zip((*members, *narrow), (*member_s, *narrow_s)))
    ]
    for load in loads:
        load.start()
    gather = Gather(bits, parts, (joined, small), (joined_out, small_out), pieces, sems[:7])
    swap = Swap(2**bits, tokens, tokens_out, *[s.at[0] for s in sems[7:10]])
    greet_all(bits, parts, True)
    swap.start()
    blocks, rows, width = x_s.shape
    at = 0
    for load in loads[:4]:
        load.wait()
    for h in range(joined.shape[1] // (HEADW + DV)):
        for member, size in zip(member_s, (DK, DK, DV, DV)):
            joined[:, at : at + size] = member[:, h * size : (h + 1) * size]
            at += size

    def put(i):
        return pltpu.make_async_copy(padded_s[i], padded[i], out_sem.at[i])

    def widen():
        for i, (source, target) in enumerate(zip(narrow_s, padded_s)):
            loads[4 + i].wait()
            have, wide = source.shape[0], target.shape[1]
            edge = have // 128 * 128
            target[:, edge:] = jnp.zeros((target.shape[0], wide - edge), BF16)
            target[:, 0:have] = source[...].T
            put(i).start()

    def normalize():
        swap.finish()
        copy = pltpu.make_async_copy(tokens_out, x_s, x_sem.at[0])
        copy.start()
        copy.wait()

        @pl.loop(0, blocks)
        def _(i):
            x = x_s[i].astype(F32)
            scale = lax.rsqrt(jnp.mean(x * x, axis=-1, keepdims=True) + 1e-05)
            h1_out[i] = (x * scale * gain[...]).astype(BF16)

        h1t_out[...] = h1_out[...].reshape(blocks * rows, width).T

    def fetch(p):
        _, start, _, stop = pieces[p]
        return pltpu.make_async_copy(
            joined_out.at[:, :, :, start:stop], w_s.at[p % 2], w_sem.at[p % 2]
        )

    def store(p):
        _, start, _, stop = pieces[p]
        return pltpu.make_async_copy(raw_s.at[p % 2], raw_out.at[:, :, start:stop], raw_sem.at[p % 2])

    main = [p for p, item in enumerate(pieces) if item[0] == 0]

    def project(p):
        if p - 2 in main:
            store(p - 2).wait()
        fetch(p).wait()
        h1 = h1_out[...].reshape(blocks * rows, width)

        @pl.loop(0, parts)
        def _(g):
            raw_s[p % 2, g] = jnp.dot(
                h1, w_s[p % 2, g].reshape(width, WIDE), preferred_element_type=F32
            )

        store(p).start()

    ready = {p + STRIDE * gather.ticks: p for p in main}
    for now in range(max(ready) + 2):
        if now < gather.moves():
            gather.move(now)
        if now == 1:
            widen()
        if now == min(ready):
            normalize()
        if now - 1 in ready:
            project(ready[now - 1])
        if now in ready:
            gather.s_whole(ready[now]).wait_recv()
            fetch(ready[now]).start()
    gather.finish(main)
    for p in main[-2:]:
        store(p).wait()
    for i in range(3):
        put(i).wait()


def prologue(tokens, small, gain, members, narrow, groups, parts):
    bits = groups.bit_length() - 1
    rows = members[0].shape[0]
    wide = sum(w.shape[1] for w in members)
    padded = -(-narrow[0].shape[0] // WIDE) * WIDE
    blocks, token_rows, width = tokens.shape
    pieces = [(1, 0, small.shape[1], small.shape[1])]
    pieces += [(0, at, at + WIDE // 2, at + WIDE) for at in range(0, wide, WIDE)]
    length = blocks * token_rows
    any_spec = pl.BlockSpec(memory_space=pl.ANY)
    vmem_spec = pl.BlockSpec(memory_space=pltpu.VMEM)
    dma = lambda *shape: pltpu.SemaphoreType.DMA(shape)
    return pl.pallas_call(
        partial(prologue_kernel, bits, parts, pieces),
        out_shape=(
            jax.ShapeDtypeStruct(tokens.shape, BF16),
            jax.ShapeDtypeStruct((parts, groups, rows, wide), BF16),
            jax.ShapeDtypeStruct((parts, groups) + small.shape, BF16),
            jax.ShapeDtypeStruct((parts, length, wide), F32),
            jax.ShapeDtypeStruct(tokens.shape, BF16),
            jax.ShapeDtypeStruct((width, length), BF16),
            *[jax.ShapeDtypeStruct((rows, padded), BF16)] * 3,
        ),
        in_specs=[any_spec] * 2 + [vmem_spec] + [any_spec] * 7,
        out_specs=(any_spec,) * 4 + (vmem_spec,) * 2 + (any_spec,) * 3,
        scratch_shapes=[
            *[pltpu.VMEM(w.shape, BF16) for w in (*members, *narrow)],
            *[pltpu.VMEM((rows, padded), BF16)] * 3,
            dma(7), dma(3),
            pltpu.VMEM((rows, wide), BF16),
            pltpu.VMEM(tokens.shape, BF16),
            pltpu.VMEM((2, parts, groups, rows, WIDE), BF16),
            pltpu.VMEM((2, parts, length, WIDE), F32),
            dma(1), dma(2), dma(2),
            *Gather.scratch(bits, len(pieces)),
            dma(1), dma(1), dma(1),
        ],
        compiler_params=pltpu.CompilerParams(
            collective_id=3, has_side_effects=True, vmem_limit_bytes=62 * 2**20
        ),
        cost_estimate=pl.CostEstimate(
            flops=2 * length * width * wide * parts, bytes_accessed=40 * 2**20, transcendentals=0
        ),
        name="prologue",
    )(tokens, small, gain, *members, *narrow)


def forward_kernel(
    heads, parts, bits, pieces,
    raw_ref, gate_ref, raw_any, convw_ref, ab_ref, gain_ref, *refs,
):
    weights = len({item[0] for item in pieces})
    swap_in, sources, refs = refs[0], refs[1 : 1 + weights], refs[1 + weights :]
    head_ref, o_ref, s_ref, t_ref, qe_ref, phi_ref, phil_ref, halo_ref = refs[:8]
    swap_out, targets, refs = refs[8], refs[9 : 9 + weights], refs[9 + weights :]
    (qe_s, o0_s, phi_s, b_s, phil_s, bl_s, send_s, recv_s, halo_s, ext_s,
     send_sem, recv_sem, halo_send_sem, halo_recv_sem) = refs[:14]
    swap = Swap(2**bits, swap_in, swap_out, *[s.at[0] for s in refs[14:17]])
    gather = Gather(bits, parts, sources, targets, pieces, refs[17:])
    step = pl.program_id(0)
    early = pl.program_id(1) == 0
    z = lax.axis_index("mp")
    lag = parts - 1
    slots = lag + 1
    length = gate_ref.shape[1]
    size = min(CHUNK, length)
    chunks = length // size
    per = heads // parts

    @pl.when((step == 0) & early)
    def _():
        greet_all(bits, parts, True)
        swap.start()

    last = 2 * (heads + lag) - 1
    for spot in range(last + 1):
        moves = [m for m in range(gather.moves()) if m * last // (gather.moves() - 1) == spot]
        if moves:
            @pl.when(step * 2 + pl.program_id(1) == spot)
            def _():
                for m in moves:
                    gather.move(m)

    def hop(h):
        return pltpu.make_async_remote_copy(
            src_ref=send_s.at[h], dst_ref=recv_s.at[h], send_sem=send_sem.at[h],
            recv_sem=recv_sem.at[h], device_id={"mp": lax.rem(z + 1, parts)},
            device_id_type=pl.DeviceIdType.MESH,
        )

    def halo_hop(g):
        return pltpu.make_async_remote_copy(
            src_ref=raw_any.at[g, length - HALO :], dst_ref=halo_s.at[g], send_sem=halo_send_sem.at[g],
            recv_sem=halo_recv_sem.at[g], device_id={"mp": lax.rem(z + 1, parts)},
            device_id_type=pl.DeviceIdType.MESH,
        )

    @pl.when((step == 0) & early & (z == 0))
    def _():
        recv_s[...] = jnp.zeros_like(recv_s)
        halo_s[...] = jnp.zeros_like(halo_s)

    @pl.when((step == 0) & early & (z < parts - 1))
    def _():
        for g in range(parts):
            halo_hop(g).start()

    @pl.when((step < heads) & early)
    def _():
        slot = lax.rem(step, slots)
        part, sub = lax.div(step, per), lax.rem(step, per)

        @pl.when((sub == 0) & (z > 0))
        def _():
            halo_hop(part).wait_recv()

        for k in range(per):
            @pl.when(sub == k)
            def _():
                ext_s[0:HALO] = halo_s[part, :, k * (HEADW + DV) : k * (HEADW + DV) + HEADW]

        ext_s[HALO:] = raw_ref[0, 0:size, 0:HEADW]
        rows, cols = masks(size)
        upper = (rows <= cols).astype(F32)
        convw = convw_ref[0]
        kept = [None] * chunks
        lowers = [None] * chunks

        def open_chunk(c):
            conv = conv_of(windows(raw_ref, ext_s, c, size), convw)
            _, q_silu, k_silu, value, q_scale, k_scale = unit_parts(conv)
            query = q_silu * (q_scale * DK ** (-0.5))
            keyed = k_silu * k_scale
            yield
            gamma_row, gamma_col, beta = decays(ab_ref, c * size, size, upper)
            inclusive, strict = fades(gamma_row, gamma_col, rows, cols)
            gram = mm(jnp.concatenate([keyed, query], axis=0), keyed, 1, 1)
            yield
            lowers[c] = beta * gram[:size] * strict
            scores = gram[size:] * inclusive
            growth = jnp.exp(gamma_col)
            last = gamma_row[:, size - 1 :]
            rhs = jnp.concatenate([(beta * growth) * keyed, beta * value], axis=1)
            kept[c] = (scores, rhs, query * growth, keyed * jnp.exp(last - gamma_col), last)

        in_step([open_chunk(c) for c in range(chunks)])
        inverses = invert_many(lowers, rows, cols)
        eye = (masks(DK)[0] == masks(DK)[1]).astype(F32)
        flows = [None] * chunks

        def close_chunk(c):
            scores, rhs, query_g, keyed_g, last = kept[c]
            t_ref[0, c] = inverses[c]
            solved = mm(inverses[c], rhs)
            yield
            mixed = mm(scores, solved)
            yield
            moved = mm(keyed_g, solved, 0, 0)
            yield
            query_e = query_g - mixed[:, :DK]
            phi = jnp.exp(last) * eye - moved[:, :DK]
            qe_ref[0, c * size : (c + 1) * size] = query_e
            qe_s[slot, c * size : (c + 1) * size] = query_e
            o0_s[slot, c * size : (c + 1) * size] = mixed[:, DK:]
            phi_ref[0, c] = phi.T
            phi_s[slot, c] = phi
            b_s[slot, c] = moved[:, DK:]
            flows[c] = phi

        in_step([close_chunk(c) for c in range(chunks)])
        phi_all, b_all = flows[0], b_s[slot, 0]
        for c in range(1, chunks):
            moved_all = mm(flows[c], jnp.concatenate([phi_all, b_all], axis=1))
            phi_all = moved_all[:, :DK]
            b_all = moved_all[:, DK:] + b_s[slot, c]
        phil_ref[0] = phi_all.T
        phil_s[slot] = phi_all
        bl_s[slot] = b_all

    relay = step - z

    @pl.when((relay >= 0) & (relay < heads) & ~early)
    def _():
        slot = lax.rem(relay, slots)

        @pl.when(z > 0)
        def _():
            hop(relay).wait_recv()

        @pl.when(z < parts - 1)
        def _():
            send_s[relay] = mm(phil_s[slot], recv_s[relay]) + bl_s[slot]
            hop(relay).start()

    @pl.when((step >= lag) & ~early)
    def _():
        head = step - lag
        slot = lax.rem(head, slots)
        state = recv_s[head]
        for c in range(chunks):
            at = slice(c * size, (c + 1) * size)
            s_ref[0, c] = state
            result = mm(qe_s[slot, at], state) + o0_s[slot, at]
            if c + 1 < chunks:
                state = mm(phi_s[slot, c], state) + b_s[slot, c]
            o_ref[0, at] = result
            scale = lax.rsqrt(jnp.mean(result * result, axis=-1, keepdims=True) + 1e-05)
            gate = gate_ref[0, c * size : (c + 1) * size]
            gated = result * scale * gain_ref[...] * (gate * jax.nn.sigmoid(gate))
            head_ref[0, at] = gated.astype(BF16)

    @pl.when((step == pl.num_programs(0) - 1) & ~early & (z < parts - 1))
    def _():
        @pl.loop(0, heads)
        def _(h):
            hop(h).wait_send()

        for g in range(parts):
            halo_hop(g).wait_send()

    @pl.when((step == pl.num_programs(0) - 1) & ~early)
    def _():
        halo_ref[...] = halo_s[...]
        gather.finish()
        swap.finish()


class Scatter:
    def __init__(self, bits, parts, plan, rows, lhs_refs, rhs_refs, out_ref, scratch, stride):
        self.stride = stride
        self.bits, self.parts, self.plan, self.rows = bits, parts, plan, rows
        self.lhs_refs, self.rhs_refs, self.out_ref = lhs_refs, rhs_refs, out_ref
        self.count = len(plan)
        self.planes = planes = bits - 1
        self.half = 2 ** (bits - 1)
        self.lhs_s, self.rhs_s, self.grad_s, self.r1, *rest = scratch
        self.ra, self.rb = rest[:planes], rest[planes : 2 * planes]
        (self.r4, self.load_sem, self.send1, self.recv1, self.send_a, self.recv_a, self.send_b,
         self.recv_b, self.send4, self.recv4) = rest[2 * planes :]
        self.d, self.z = lax.axis_index("dp"), lax.axis_index("mp")
        self.ticks = self.count + 1 + self.stride * (planes + 1)

    @staticmethod
    def scratch(bits, parts, count, rows, length, width):
        planes, half = bits - 1, 2 ** (bits - 1)
        vmem = lambda *shape: pltpu.VMEM(shape, BF16)
        dma = lambda *shape: pltpu.SemaphoreType.DMA(shape)
        strips = [vmem(count, parts, half >> (k + 1), rows, WIDE // 2) for k in range(planes)]
        return [
            vmem(2, width, length),
            vmem(2, parts, length, WIDE),
            vmem(2, parts, half, 2, rows, WIDE),
            vmem(count, parts, half, rows, WIDE),
            *strips, *strips,
            vmem(count, parts - 1, rows, WIDE),
            dma(2, 2),
            dma(count), dma(count),
            dma(planes, count), dma(planes, count),
            dma(planes, count), dma(planes, count),
            dma(count), dma(count),
        ]

    def bit(self, b):
        return lax.rem(lax.div(self.d, 2**b), 2)

    def partner(self, b):
        return self.d + (1 - 2 * self.bit(b)) * 2**b

    def remote(self, src, dst, send, recv, to):
        return pltpu.make_async_remote_copy(
            src_ref=src, dst_ref=dst, send_sem=send, recv_sem=recv, device_id=to,
            device_id_type=pl.DeviceIdType.MESH,
        )

    def load(self, t):
        slot = lax.rem(t, 2)
        for seg in range(len(self.rhs_refs)):
            at = [k for k, item in enumerate(self.plan) if item[0] == seg]

            @pl.when((t >= at[0]) & (t <= at[-1]))
            def _():
                start = pl.multiple_of((t - at[0]) * WIDE, WIDE)
                pltpu.make_async_copy(
                    self.rhs_refs[seg].at[:, :, pl.ds(start, WIDE)], self.rhs_s.at[slot],
                    self.load_sem.at[0, slot],
                ).start()
                pltpu.make_async_copy(
                    self.lhs_refs[self.plan[at[0]][1]], self.lhs_s.at[slot], self.load_sem.at[1, slot]
                ).start()

    def load_wait(self, t):
        slot = lax.rem(t, 2)
        pltpu.make_async_copy(
            self.rhs_refs[0].at[:, :, pl.ds(0, WIDE)], self.rhs_s.at[slot], self.load_sem.at[0, slot]
        ).wait()
        pltpu.make_async_copy(
            self.lhs_refs[0], self.lhs_s.at[slot], self.load_sem.at[1, slot]
        ).wait()

    def first_hop(self, t):
        return self.remote(
            self.grad_s.at[lax.rem(t, 2), :, :, 1 - self.bit(0)], self.r1.at[t], self.send1.at[t],
            self.recv1.at[t], {"dp": self.partner(0)},
        )

    def a_hop(self, k, t):
        b = self.bits - 1 - k
        keep = self.half >> (k + 1)
        away = pl.ds((1 - self.bit(b)) * keep, keep)
        src = self.r1.at[t, :, away, :, 0 : WIDE // 2] if k == 0 else self.ra[k - 1].at[t, :, away]
        return self.remote(
            src, self.ra[k].at[t], self.send_a.at[k, t], self.recv_a.at[k, t], {"dp": self.partner(b)}
        )

    def b_hops(self, k, t):
        b = 1 + k
        copies = []
        for hi in range(self.half >> (k + 1)):
            away = 2 * hi + 1 - self.bit(b)
            src = self.r1.at[t, :, away, :, WIDE // 2 :] if k == 0 else self.rb[k - 1].at[t, :, away]
            copies.append(
                self.remote(
                    src, self.rb[k].at[t, :, hi], self.send_b.at[k, t], self.recv_b.at[k, t],
                    {"dp": self.partner(b)},
                )
            )
        return copies

    def b_whole(self, k, t):
        return self.remote(
            self.rb[k].at[t], self.rb[k].at[t], self.send_b.at[k, t], self.recv_b.at[k, t],
            {"dp": self.partner(1 + k)},
        )

    def z_hops(self, t):
        copies = []
        side = WIDE // 2
        for delta in range(1, self.parts):
            to = lax.rem(self.z + delta, self.parts)
            for i, buf in enumerate((self.ra[self.planes - 1], self.rb[self.planes - 1])):
                copies.append(
                    self.remote(
                        buf.at[t, to, 0],
                        self.r4.at[t, self.parts - 1 - delta, :, i * side : (i + 1) * side],
                        self.send4.at[t], self.recv4.at[t], {"mp": to},
                    )
                )
        return copies

    def z_whole(self, t):
        return self.remote(
            self.r4.at[t], self.r4.at[t], self.send4.at[t], self.recv4.at[t],
            {"mp": lax.rem(self.z + 1, self.parts)},
        )

    def tick(self, tick):
        count, planes, half, parts = self.count, self.planes, self.half, self.parts
        side = WIDE // 2

        @pl.when(tick == 0)
        def _():
            self.load(tick)

        t = tick - 1 - self.stride * (planes + 1)

        @pl.when((t >= 0) & (t < count))
        def _():
            self.z_whole(t).wait_recv()
            left = self.ra[planes - 1][t, self.z, 0].astype(F32)
            right = self.rb[planes - 1][t, self.z, 0].astype(F32)
            for s in range(parts - 1):
                left = left + self.r4[t, s, :, 0:side].astype(F32)
                right = right + self.r4[t, s, :, side:].astype(F32)
            self.out_ref[t, :, 0:side] = left
            self.out_ref[t, :, side:] = right

        for k in range(planes - 1, -1, -1):
            t_k = tick - 1 - self.stride * (k + 1)

            @pl.when((t_k >= 0) & (t_k < count))
            def _():
                self.a_hop(k, t_k).wait_recv()
                self.b_whole(k, t_k).wait_recv()
                keep = half >> (k + 1)
                bit_a, bit_b = self.bit(self.bits - 1 - k), self.bit(1 + k)
                for m in range(keep):
                    own_a, own_b = bit_a * keep + m, 2 * m + bit_b
                    for j in range(parts):
                        if k == 0:
                            mine_a = self.r1[t_k, j, own_a, :, 0:side]
                            mine_b = self.r1[t_k, j, own_b, :, side:]
                        else:
                            mine_a = self.ra[k - 1][t_k, j, own_a]
                            mine_b = self.rb[k - 1][t_k, j, own_b]
                        for buf, mine in ((self.ra[k], mine_a), (self.rb[k], mine_b)):
                            buf[t_k, j, m] = buf[t_k, j, m] + mine
                if k + 1 < planes:
                    self.a_hop(k + 1, t_k).start()
                    for copy in self.b_hops(k + 1, t_k):
                        copy.start()
                else:
                    for copy in self.z_hops(t_k):
                        copy.start()

        t_1 = tick - 1

        @pl.when((t_1 >= 0) & (t_1 < count))
        def _():
            self.first_hop(t_1).wait_recv()
            slot = lax.rem(t_1, 2)
            color = self.bit(0)

            @pl.loop(0, parts)
            def _(j):
                for m in range(half):
                    self.r1[t_1, j, m] = self.r1[t_1, j, m] + self.grad_s[slot, j, m, color]

            self.a_hop(0, t_1).start()
            for copy in self.b_hops(0, t_1):
                copy.start()

        @pl.when(tick < count)
        def _():
            slot = lax.rem(tick, 2)

            @pl.when(tick + 1 < count)
            def _():
                self.load(tick + 1)

            self.load_wait(tick)

            @pl.when(tick >= 2)
            def _():
                self.first_hop(tick - 2).wait_send()

            @pl.loop(0, parts)
            def _(j):
                full = jnp.dot(self.lhs_s[slot], self.rhs_s[slot, j], preferred_element_type=F32)
                self.grad_s[slot, j] = full.astype(BF16).reshape(half, 2, self.rows, WIDE)

            self.first_hop(tick).start()

    def finish(self):
        for t in range(max(self.count - 2, 0), self.count):
            self.first_hop(t).wait_send()

        @pl.loop(0, self.count)
        def _(t):
            for k in range(self.planes):
                self.a_hop(k, t).wait_send()
                self.b_whole(k, t).wait_send()
            self.z_whole(t).wait_send()


def plan_of(pairs):
    plan = []
    for seg, (kind, right) in enumerate(pairs):
        plan += [(seg, kind)] * (right.shape[2] // WIDE)
    return plan


def small_rows(heads, width, smalls):
    starts = [0]
    for count in (width // 128, width // 128, DV // 128, heads * TAPS * HEADW // 128, 1, smalls * width // 128):
        starts.append(starts[-1] + count)
    return starts, -(-starts[-1] // 8) * 8


def scatter_kernel(bits, parts, plan, rows, lhs_ref, *refs):
    sources = len({item[0] for item in plan})
    rhs_refs, refs = refs[:sources], refs[sources:]
    (ffn_ref, hgain_ref, conv_ref, line_ref, w_ref, d_small, w_small, x_ref, dx1_ref, gain_ref, out_ref, vec_out,
     g_out) = refs[:13]
    refs = refs[3:]
    v_own, v_acc, v_in, v_z, v_send, v_recv, v_z_send, v_z_recv = refs[10:18]
    swap_own, swap_send, swap_recv = refs[18:21]
    dp_s, w_s, acc_s, dx_s, in_sem = refs[21:26]
    scatter = Scatter(bits, parts, plan, rows, [lhs_ref], rhs_refs, out_ref, refs[26:], STRIDE)
    z = lax.axis_index("mp")
    mesh_id = pl.DeviceIdType.MESH
    greet_all(bits, parts, True)
    swap = Swap(2**bits, dx_s, g_out, swap_own.at[0], swap_send.at[0], swap_recv.at[0])

    def v_hop(b):
        return pltpu.make_async_remote_copy(
            src_ref=v_own if b == 0 else v_acc.at[b - 1], dst_ref=v_in.at[b], send_sem=v_send.at[b],
            recv_sem=v_recv.at[b], device_id={"dp": scatter.partner(b)}, device_id_type=mesh_id,
        )

    def v_z_hop(src, dst, delta):
        return pltpu.make_async_remote_copy(
            src_ref=src, dst_ref=dst, send_sem=v_z_send.at[0], recv_sem=v_z_recv.at[0],
            device_id={"mp": lax.rem(z + delta, parts)}, device_id_type=mesh_id,
        )

    def small_sum(stage):
        if stage == 0:
            v_hop(0).start()
        elif stage <= bits:
            b = stage - 1
            v_hop(b).wait_recv()
            total = (v_own[...] if b == 0 else v_acc[b - 1]) + v_in[b]
            if stage < bits:
                v_acc[b] = total
                v_hop(stage).start()
            else:
                v_z[z] = total
                for delta in range(1, parts):
                    v_z_hop(v_z.at[z], v_z.at[z], delta).start()
        else:
            whole = v_z.at[pl.ds(0, parts - 1)]
            v_z_hop(whole, whole, 1).wait_recv()
            total = v_z[0]
            for s in range(1, parts):
                total = total + v_z[s]
            vec_out[...] = total
            for b in range(bits):
                v_hop(b).wait_send()
            v_z_hop(whole, whole, 1).wait_send()

    def fetch(g, slot):
        return (
            pltpu.make_async_copy(rhs_refs[0].at[g], dp_s.at[slot], in_sem.at[0, slot]),
            pltpu.make_async_copy(w_ref.at[g], w_s.at[slot], in_sem.at[1, slot]),
        )

    def input_grad():
        acc_s[...] += lax.dot_general(
            d_small[...], w_small[...], (((0,), (0,)), ((), ())), preferred_element_type=F32
        )
        blocks, token_rows, width = x_ref.shape

        def body(i, gain_sum):
            x = x_ref[i].astype(F32)
            scale = lax.rsqrt(jnp.mean(x * x, axis=-1, keepdims=True) + 1e-05)
            unit = x * scale
            at = pl.ds(pl.multiple_of(i * token_rows, token_rows), token_rows)
            d_h1 = acc_s[at]
            e = d_h1 * gain_ref[...]
            d_x = dx1_ref[at] + scale * (e - unit * jnp.mean(e * unit, axis=-1, keepdims=True))
            dx_s[i] = d_x.astype(BF16)
            return gain_sum + jnp.sum(d_h1 * unit, axis=0, keepdims=True)

        gain_sum = lax.fori_loop(0, blocks, body, jnp.zeros((1, width), F32))
        starts, _ = small_rows(conv_ref.shape[0], width, d_small.shape[0])

        def put(start, row):
            for i in range(row.shape[1] // 128):
                v_own[start + i : start + i + 1] = row[:, i * 128 : (i + 1) * 128]

        put(starts[0], gain_sum)
        put(starts[1], ffn_ref[...])
        put(starts[2], hgain_ref[...])
        for h in range(conv_ref.shape[0]):
            for tap in range(TAPS):
                put(starts[3] + (h * TAPS + tap) * HEADW // 128, conv_ref[h, tap : tap + 1])
        put(starts[4], line_ref[...])
        small_grad = lax.dot_general(
            d_small[...], scatter.lhs_s[0], (((1,), (1,)), ((), ())), preferred_element_type=F32
        )
        for i in range(d_small.shape[0]):
            put(starts[5] + i * width // 128, small_grad[i : i + 1])
        if starts[6] < v_own.shape[0]:
            v_own[starts[6] :] = jnp.zeros((v_own.shape[0] - starts[6], 128), F32)

    for copy in fetch(0, 0):
        copy.start()

    @pl.loop(0, max(scatter.ticks, 2 + parts + bits + 2))
    def _(now):
        scatter.tick(now)
        tick = now - 2

        @pl.when((tick >= 0) & (tick < parts))
        def _():
            slot = lax.rem(tick, 2)

            @pl.when(tick + 1 < parts)
            def _():
                for copy in fetch(tick + 1, 1 - slot):
                    copy.start()

            for copy in fetch(tick, slot):
                copy.wait()
            part = lax.dot_general(
                dp_s[slot], w_s[slot], (((1,), (1,)), ((), ())), preferred_element_type=F32
            )

            @pl.when(tick == 0)
            def _():
                acc_s[...] = part

            @pl.when(tick > 0)
            def _():
                acc_s[...] += part

        @pl.when(tick == parts)
        def _():
            input_grad()
            swap.start()

        for stage in range(bits + 2):
            @pl.when(tick == parts + stage)
            def _():
                small_sum(stage)

    swap.finish()
    scatter.finish()


def scatter_sum(left, pairs, smalls, weight, d_small, w_small, x, d_x1, gain, groups, parts, collective):
    width, length = left.shape
    vector = jax.ShapeDtypeStruct((small_rows(smalls[2].shape[0], width, d_small.shape[0])[1], 128), F32)
    bits = groups.bit_length() - 1
    rows = width // groups
    plan = plan_of(pairs)
    count = len(plan)
    vmem_spec = pl.BlockSpec(memory_space=pltpu.VMEM)
    any_spec = pl.BlockSpec(memory_space=pl.ANY)
    dma = lambda *shape: pltpu.SemaphoreType.DMA(shape)
    return pl.pallas_call(
        partial(scatter_kernel, bits, parts, plan, rows),
        out_shape=(
            jax.ShapeDtypeStruct((count, rows, WIDE), F32),
            jax.ShapeDtypeStruct(vector.shape, F32),
            jax.ShapeDtypeStruct(x.shape, BF16),
        ),
        in_specs=[any_spec] * (1 + len(pairs)) + [vmem_spec] * 4 + [any_spec] + [vmem_spec] * 5,
        out_specs=(vmem_spec, vmem_spec, any_spec),
        scratch_shapes=[
            pltpu.VMEM(vector.shape, F32),
            pltpu.VMEM((bits - 1,) + vector.shape, F32),
            pltpu.VMEM((bits,) + vector.shape, F32),
            pltpu.VMEM((parts,) + vector.shape, F32),
            dma(bits), dma(bits), dma(1), dma(1),
            dma(1), dma(1), dma(1),
            pltpu.VMEM((2,) + pairs[0][1].shape[1:], BF16),
            pltpu.VMEM((2,) + weight.shape[1:], BF16),
            pltpu.VMEM((length, width), F32),
            pltpu.VMEM(x.shape, BF16),
            dma(2, 2),
            *Scatter.scratch(bits, parts, count, rows, length, width),
        ],
        compiler_params=pltpu.CompilerParams(
            collective_id=collective, has_side_effects=True, vmem_limit_bytes=60 * 2**20
        ),
        cost_estimate=pl.CostEstimate(
            flops=4 * count * WIDE * parts * length * width, bytes_accessed=count * parts * length * WIDE * 4,
            transcendentals=0,
        ),
        name="scatter_sum",
    )(left, *[right for _, right in pairs], *smalls, weight, d_small, w_small, x, d_x1, gain)


def backward_kernel(
    heads, parts, bits, plan, rows_held,
    dhead_ref, o_ref, gate_ref, qe_ref, phi_ref, phil_ref,
    raw_ref, halo_ref, convw_ref, ab_ref, gain_ref, s_ref, t_ref, phi_late_ref, *refs,
):
    sources = len({item[0] for item in plan})
    kinds = len({item[1] for item in plan})
    lhs_refs, refs = refs[:kinds], refs[kinds:]
    rhs_refs, swap_in, refs = refs[:sources], refs[sources], refs[sources + 1 :]
    dproj_ref, dab_ref, dconv_ref, dgain_ref, sums_ref, swap_out = refs[:6]
    (do_s, d_s, dgate_s, dl_s, phil_s, g_s, dext_s, ext_s, send_s, recv_s, halo_send, halo_recv,
     send_sem, recv_sem, halo_send_sem, halo_recv_sem) = refs[6:22]
    scatter = Scatter(bits, parts, plan, rows_held, lhs_refs, rhs_refs, sums_ref, refs[25:], 3)
    swap = Swap(2**bits, swap_in, swap_out, *[s.at[0] for s in refs[22:25]])
    step = pl.program_id(0)
    early = pl.program_id(1) == 0
    z = lax.axis_index("mp")
    back = parts - 1 - z
    lag = parts - 1
    slots = lag + 1
    length = o_ref.shape[1]
    size = min(CHUNK, length)
    chunks = length // size

    @pl.when((step == 0) & early)
    def _():
        greet_all(bits, parts, True)
        swap.start()

    sub = pl.program_id(1)
    now = jnp.where(step < lag, step, lag + 2 * (step - lag) + sub)
    last = lag + 2 * (heads + 1) - 1
    stop = jnp.where(now == last, max(scatter.ticks, last + 1), now + 1)
    stop = jnp.where((step < lag) & early, now, stop)

    @pl.loop(now, stop)
    def _(tick):
        scatter.tick(tick)


    def hop(h):
        return pltpu.make_async_remote_copy(
            src_ref=send_s.at[h], dst_ref=recv_s.at[h], send_sem=send_sem.at[h],
            recv_sem=recv_sem.at[h], device_id={"mp": lax.rem(z + parts - 1, parts)},
            device_id_type=pl.DeviceIdType.MESH,
        )

    def halo_hop(h):
        return pltpu.make_async_remote_copy(
            src_ref=halo_send.at[h], dst_ref=halo_recv.at[h], send_sem=halo_send_sem.at[h],
            recv_sem=halo_recv_sem.at[h], device_id={"mp": lax.rem(z + parts - 1, parts)},
            device_id_type=pl.DeviceIdType.MESH,
        )

    @pl.when((step == 0) & early)
    def _():
        dgain_ref[...] = jnp.zeros_like(dgain_ref)
        g_s[...] = jnp.zeros_like(g_s)

    @pl.when((step == 0) & early & (back == 0))
    def _():
        recv_s[...] = jnp.zeros_like(recv_s)
        halo_recv[...] = jnp.zeros_like(halo_recv)

    @pl.when((step < heads) & early)
    def _():
        slot = lax.rem(step, slots)
        gslot = lax.rem(step, slots + 1)
        gain = gain_ref[...]
        d_gain = jnp.zeros((1, DV), F32)
        for c in range(chunks):
            at = slice(c * size, (c + 1) * size)
            out = o_ref[0, at]
            d_head = dhead_ref[0, at]
            gate = gate_ref[0, c * size : (c + 1) * size]
            scale = lax.rsqrt(jnp.mean(out * out, axis=-1, keepdims=True) + 1e-05)
            unit = out * scale
            sig = jax.nn.sigmoid(gate)
            gated = gate * sig
            both = d_head * unit
            d_gain = d_gain + jnp.sum(both * gated, axis=0, keepdims=True)
            e = d_head * gated * gain
            d_out = scale * (e - unit * jnp.mean(e * unit, axis=-1, keepdims=True))
            dgate_s[gslot, at] = (both * gain * sig * (1.0 + gate * (1.0 - sig))).astype(BF16)
            do_s[slot, at] = d_out
            d_s[slot, c] = mm(qe_ref[0, at], d_out, 0, 0)
        dgain_ref[...] += d_gain
        total = d_s[slot, chunks - 1]
        for c in range(chunks - 2, -1, -1):
            total = mm(phi_ref[0, c], total) + d_s[slot, c]
        dl_s[slot] = total
        phil_s[slot] = phil_ref[0]

    relay = step - back

    @pl.when((relay >= 0) & (relay < heads) & early)
    def _():
        slot = lax.rem(relay, slots)

        @pl.when(back > 0)
        def _():
            hop(relay).wait_recv()

        @pl.when(z > 0)
        def _():
            send_s[relay] = mm(phil_s[slot], recv_s[relay]) + dl_s[slot]
            hop(relay).start()

    @pl.when((step >= lag) & (step < lag + heads) & ~early)
    def _():
        head = step - lag
        slot = lax.rem(head, slots)
        eslot = lax.rem(head, 2)
        rows, cols = masks(size)
        upper = (rows <= cols).astype(F32)
        convw = convw_ref[0]
        d_state = recv_s[head]
        ext_s[0:HALO] = halo_ref[0, :, 0:HEADW]
        ext_s[HALO:] = raw_ref[0, 0:size, 0:HEADW]
        d_states = [None] * chunks
        d_states[chunks - 1] = d_state
        for c in range(chunks - 1, 0, -1):
            d_states[c - 1] = mm(phi_late_ref[0, c], d_states[c]) + d_s[slot, c]
        taps_grad = [None] * chunks

        def work(c):
            at = slice(c * size, (c + 1) * size)
            shifted = windows(raw_ref, ext_s, c, size)
            conv = conv_of(shifted, convw)
            sig, q_silu, k_silu, value, q_scale, k_scale = unit_parts(conv)
            query = q_silu * (q_scale * DK ** (-0.5))
            keyed = k_silu * k_scale
            yield
            gamma_row, gamma_col, beta = decays(ab_ref, c * size, size, upper)
            inclusive, strict = fades(gamma_row, gamma_col, rows, cols)
            gram = mm(jnp.concatenate([keyed, query], axis=0), keyed, 1, 1)
            yield
            gram_f = gram[:size] * strict
            lower = beta * gram_f
            scores = gram[size:] * inclusive
            growth = jnp.exp(gamma_col)
            last = gamma_row[:, size - 1 :]
            tail = jnp.exp(last - gamma_col)
            query_g = query * growth
            grown = keyed * growth
            keyed_b = beta * grown
            keyed_g = keyed * tail
            state = s_ref[0, c]
            d_state = d_states[c]
            inverse = t_ref[0, c]
            d_out = do_s[slot, at]
            held = mm(keyed_b, state)
            yield
            fresh = mm(inverse, beta * value - held)
            yield
            d_fresh = mm(scores, d_out, 0, 0) + mm(keyed_g, d_state)
            yield
            d_rhs = mm(inverse, d_fresh, 0, 0)
            yield
            stacked = jnp.concatenate([d_out, d_rhs], axis=0)
            by_fresh = mm(stacked, fresh, 1, 1)
            yield
            by_state = mm(stacked, state, 1, 1)
            yield
            d_scores = by_fresh[:size] * inclusive
            d_lower = -by_fresh[size:]
            d_query_g = by_state[:size]
            d_keyed_b = -by_state[size:]
            d_keyed_g = mm(fresh, d_state, 1, 1)
            yield
            d_gram = d_lower * (beta * strict)
            by_keyed = mm(jnp.concatenate([d_scores, d_gram], axis=0), keyed)
            yield
            d_query = by_keyed[:size] + growth * d_query_g
            d_keyed = (
                by_keyed[size:]
                + mm(jnp.concatenate([d_scores, d_gram], axis=0),
                     jnp.concatenate([query, keyed], axis=0), 0, 0)
                + (beta * growth) * d_keyed_b
                + tail * d_keyed_g
            )
            yield
            d_value = beta * d_rhs
            d_beta = (
                jnp.sum(d_rhs * value, axis=-1, keepdims=True)
                + jnp.sum(d_lower * gram_f, axis=-1, keepdims=True)
                + jnp.sum(d_keyed_b * grown, axis=-1, keepdims=True)
            )
            moved = by_fresh[:size] * scores + d_lower * lower
            tail_part = jnp.sum(d_keyed_g * keyed_g, axis=-1, keepdims=True)
            d_gamma = (
                jnp.sum(moved, axis=-1, keepdims=True)
                + jnp.sum(d_query_g * query_g, axis=-1, keepdims=True)
                + jnp.sum(d_keyed_b * keyed_b, axis=-1, keepdims=True)
                - tail_part
            )
            at_end = jnp.sum(tail_part, axis=0, keepdims=True) + jnp.exp(last) * jnp.sum(
                jnp.sum(state * d_state, axis=-1, keepdims=True), axis=0, keepdims=True
            )
            lanes = lax.broadcasted_iota(jnp.int32, (size, DK), 1)
            packed = jnp.where(lanes == 0, d_gamma, jnp.where(lanes == 1, d_beta, 0.0)).T[:8]
            row_id = lax.broadcasted_iota(jnp.int32, packed.shape, 0)
            packed = packed - jnp.where(row_id == 0, jnp.sum(moved, axis=0, keepdims=True), 0.0)
            yield
            summed = mm(packed, upper, 1, 1) + at_end
            dab_ref[0, :, at] = jnp.where(row_id == 0, summed, packed)
            d_q_silu = (DK ** (-0.5) * q_scale) * (
                d_query
                - q_silu * (q_scale * q_scale) * jnp.sum(q_silu * d_query, axis=-1, keepdims=True)
            )
            d_k_silu = k_scale * (
                d_keyed
                - k_silu * (k_scale * k_scale) * jnp.sum(k_silu * d_keyed, axis=-1, keepdims=True)
            )
            d_silu = jnp.concatenate([d_q_silu, d_k_silu, d_value], axis=1)
            d_conv = d_silu * sig * (1.0 + conv * (1.0 - sig))
            g_s[HALO + c * size : HALO + (c + 1) * size] = d_conv
            taps_grad[c] = [jnp.sum(shifted[i] * d_conv, axis=0, keepdims=True) for i in range(TAPS)]

        for first in range(0, chunks, 2):
            in_step([work(c) for c in range(first, min(first + 2, chunks))])
        d_conv_rows = [sum(row[i] for row in taps_grad[1:]) + taps_grad[0][i] for i in range(TAPS)]
        for i in range(TAPS):
            dconv_ref[0, i : i + 1] = d_conv_rows[i]
        for base, count in [(0, HALO)] + [(HALO + c * size, size) for c in range(chunks)]:
            d_raw = None
            for i in range(TAPS):
                part = g_s[pl.ds(base + TAPS - 1 - i, count)] * convw[i : i + 1]
                d_raw = part if d_raw is None else d_raw + part
            if base == 0:
                halo_send[head] = d_raw
            else:
                dext_s[eslot, base - HALO : base - HALO + count] = d_raw

        @pl.when(z > 0)
        def _():
            halo_hop(head).start()

    @pl.when((step > lag) & ~early)
    def _():
        head = step - lag - 1
        eslot = lax.rem(head, 2)
        gslot = lax.rem(head, slots + 1)

        @pl.when(back > 0)
        def _():
            halo_hop(head).wait_recv()

        dext_s[eslot, length - HALO : length] += halo_recv[head]
        dproj_ref[0, :, 0:HEADW] = dext_s[eslot].astype(BF16)
        dproj_ref[0, :, HEADW:] = dgate_s[gslot]

    @pl.when((step == pl.num_programs(0) - 1) & ~early)
    def _():
        scatter.finish()
        swap.finish()

    @pl.when((step == pl.num_programs(0) - 1) & ~early & (z > 0))
    def _():
        @pl.loop(0, heads)
        def _(h):
            hop(h).wait_send()
            halo_hop(h).wait_send()


def assemble_kernel(
    per, starts, ffn_ref, proj_ref, vec_ref, y_ref, g_ref,
    query_ref, key_ref, value_ref, outgate_ref, out_ref, gate_ref, up_ref, down_ref, conv_ref, y_out, g_out,
    mix_ref, gain_ref, hgain_ref, small_ref,
):
    y_out[...] = y_ref[...]
    g_out[...] = g_ref[...]
    for h in range(per):
        query_ref[:, h * DK : (h + 1) * DK] = proj_ref[3 * h, :, 0:DK]
        key_ref[:, h * DK : (h + 1) * DK] = proj_ref[3 * h, :, DK:]
        value_ref[:, h * DV : (h + 1) * DV] = proj_ref[3 * h + 1]
        outgate_ref[:, h * DV : (h + 1) * DV] = proj_ref[3 * h + 2]
    piece = 0
    for target in (down_ref, gate_ref, up_ref):
        total = target.shape[0]
        for start in range(0, total, WIDE):
            size = min(WIDE, total - start)
            target[start : start + size] = ffn_ref[piece].T[0:size]
            piece += 1
    for start in range(0, out_ref.shape[1], WIDE):
        out_ref[:, start : start + WIDE] = ffn_ref[piece]
        piece += 1
    width = conv_ref.shape[1]
    heads = width // HEADW
    for h in range(heads):
        for tap in range(TAPS):
            row = starts[3] + (h * TAPS + tap) * HEADW // 128
            spots = [h * DK, (heads + h) * DK, 2 * heads * DK + h * DV, 2 * heads * DK + h * DV + 128]
            for i, spot in enumerate(spots):
                conv_ref[tap : tap + 1, spot : spot + 128] = vec_ref[row + i : row + i + 1]
    mix_ref[...] = vec_ref[starts[0] : starts[1]]
    gain_ref[...] = vec_ref[starts[1] : starts[2]]
    hgain_ref[...] = vec_ref[starts[2] : starts[3]]
    smalls, rows = small_ref.shape
    lines = starts[1] - starts[0]
    first = lax.axis_index("dp") * rows
    share = lax.axis_index("mp")
    shift = lax.rem(first, 128)
    pick = lax.broadcasted_iota(jnp.int32, (128, rows), 0) == lax.broadcasted_iota(jnp.int32, (128, rows), 1) + shift
    for c in range(smalls):
        row = vec_ref[pl.ds(starts[5] + (share * smalls + c) * lines + lax.div(first, 128), 1)]
        if rows != 128:
            row = jnp.sum(jnp.where(pick, row.T, 0.0), axis=0, keepdims=True)
        small_ref[c : c + 1] = row


def assemble(ffn, proj, vec, y, g, per, hidden, starts, conv_shape):
    rows = ffn.shape[1]
    f32 = lambda *shape: jax.ShapeDtypeStruct(shape, F32)
    vmem_spec = pl.BlockSpec(memory_space=pltpu.VMEM)
    return pl.pallas_call(
        partial(assemble_kernel, per, starts),
        out_shape=(
            f32(rows, per * DK), f32(rows, per * DK), f32(rows, per * DV), f32(rows, per * DV), f32(rows, per * DV),
            f32(hidden, rows), f32(hidden, rows), f32(hidden, rows), f32(*conv_shape),
            jax.ShapeDtypeStruct(y.shape, BF16), jax.ShapeDtypeStruct(g.shape, BF16),
            *[f32(starts[i + 1] - starts[i], 128) for i in range(3)], f32(2 * per, rows),
        ),
        in_specs=[vmem_spec] * 5,
        out_specs=(vmem_spec,) * 15,
        compiler_params=pltpu.CompilerParams(vmem_limit_bytes=40 * 2**20),
        cost_estimate=pl.CostEstimate(flops=0, bytes_accessed=10 * 2**20, transcendentals=0),
        name="assemble",
    )(ffn, proj, vec, y, g)


def forward_core(raw, convw, ab, gain, swapped, weights, heads, parts, groups):
    bits = groups.bit_length() - 1
    pieces = []
    for w, weight in enumerate(weights):
        wide = weight.shape[1]
        pieces += [(w, at, at + WIDE // 2, at + WIDE) for at in range(0, wide, WIDE)]
    rows = weights[0].shape[0]
    any_spec = pl.BlockSpec(memory_space=pl.ANY)
    length = raw.shape[1]
    size = min(CHUNK, length)
    chunks = length // size
    per = heads // raw.shape[0]
    lag = parts - 1
    slots = lag + 1
    now = lambda s: jnp.minimum(s, heads - 1)
    late = lambda s: jnp.maximum(s - lag, 0)
    return pl.pallas_call(
        partial(forward_kernel, heads, parts, bits, pieces),
        grid=(heads + lag, 2),
        out_shape=(
            jax.ShapeDtypeStruct((raw.shape[0], length, per * DV), BF16),
            jax.ShapeDtypeStruct((heads, length, DV), F32),
            jax.ShapeDtypeStruct((heads, chunks, DK, DV), F32),
            jax.ShapeDtypeStruct((heads, chunks, size, size), F32),
            jax.ShapeDtypeStruct((heads, length, DK), F32),
            jax.ShapeDtypeStruct((heads, chunks, DK, DK), F32),
            jax.ShapeDtypeStruct((heads, DK, DK), F32),
            jax.ShapeDtypeStruct((parts, HALO, per * (HEADW + DV)), F32),
            jax.ShapeDtypeStruct(swapped.shape, BF16),
            *[jax.ShapeDtypeStruct((parts, groups) + w.shape, BF16) for w in weights],
        ),
        in_specs=[
            pl.BlockSpec((1, length, HEADW + DV), lambda s, _: (now(s) // per, 0, now(s) % per)),
            pl.BlockSpec((1, length, DV), lambda s, _: (late(s) // per, 0, (late(s) % per) * 3 + 2)),
            any_spec,
            pl.BlockSpec((1, TAPS, HEADW), lambda s, _: (now(s), 0, 0)),
            pl.BlockSpec((1, 8, length), lambda s, _: (now(s), 0, 0)),
            pl.BlockSpec((1, DV), lambda s, _: (0, 0)),
            *[any_spec] * (1 + len(weights)),
        ],
        out_specs=(
            pl.BlockSpec((1, length, DV), lambda s, _: (late(s) // per, 0, late(s) % per)),
            pl.BlockSpec((1, length, DV), lambda s, _: (late(s), 0, 0)),
            pl.BlockSpec((1, chunks, DK, DV), lambda s, _: (late(s), 0, 0, 0)),
            pl.BlockSpec((1, chunks, size, size), lambda s, _: (now(s), 0, 0, 0)),
            pl.BlockSpec((1, length, DK), lambda s, _: (now(s), 0, 0)),
            pl.BlockSpec((1, chunks, DK, DK), lambda s, _: (now(s), 0, 0, 0)),
            pl.BlockSpec((1, DK, DK), lambda s, _: (now(s), 0, 0)),
            pl.BlockSpec((parts, HALO, per * (HEADW + DV)), lambda s, _: (0, 0, 0)),
            *[any_spec] * (1 + len(weights)),
        ),
        scratch_shapes=[
            pltpu.VMEM((slots, length, DK), F32),
            pltpu.VMEM((slots, length, DV), F32),
            pltpu.VMEM((slots, chunks, DK, DK), F32),
            pltpu.VMEM((slots, chunks, DK, DV), F32),
            pltpu.VMEM((slots, DK, DK), F32),
            pltpu.VMEM((slots, DK, DV), F32),
            pltpu.VMEM((heads, DK, DV), F32),
            pltpu.VMEM((heads, DK, DV), F32),
            pltpu.VMEM((parts, HALO, per * (HEADW + DV)), F32),
            pltpu.VMEM((HALO + size, HEADW), F32),
            pltpu.SemaphoreType.DMA((heads,)),
            pltpu.SemaphoreType.DMA((heads,)),
            pltpu.SemaphoreType.DMA((parts,)),
            pltpu.SemaphoreType.DMA((parts,)),
            *[pltpu.SemaphoreType.DMA((1,))] * 3,
            *Gather.scratch(bits, len(pieces)),
        ],
        compiler_params=pltpu.CompilerParams(
            collective_id=0, has_side_effects=True, vmem_limit_bytes=56 * 2**20
        ),
        cost_estimate=pl.CostEstimate(flops=20 * 10**9, bytes_accessed=40 * 2**20, transcendentals=0),
        name="delta_forward",
    )(raw, raw, raw, convw, ab, gain, swapped, *weights)


def backward_core(d_head, out, raw, halo, query_e, phi, phi_all, convw, ab, gain, states, inverses, lefts, pairs, swapped,
                  heads, parts, groups):
    length = raw.shape[1]
    size = min(CHUNK, length)
    chunks = length // size
    per = heads // raw.shape[0]
    lag = parts - 1
    slots = lag + 1
    bits = groups.bit_length() - 1
    plan = plan_of(pairs)
    rows = lefts[0].shape[0] // groups
    any_spec = pl.BlockSpec(memory_space=pl.ANY)
    now = lambda s: jnp.minimum(s, heads - 1)
    late = lambda s: jnp.clip(s - lag, 0, heads - 1)
    later = lambda s: jnp.maximum(s - lag - 1, 0)
    return pl.pallas_call(
        partial(backward_kernel, heads, parts, bits, plan, rows),
        grid=(heads + lag + 1, 2),
        out_shape=(
            jax.ShapeDtypeStruct((raw.shape[0], length, per * (HEADW + DV)), BF16),
            jax.ShapeDtypeStruct((heads, 8, length), F32),
            jax.ShapeDtypeStruct((heads, TAPS, HEADW), F32),
            jax.ShapeDtypeStruct((1, DV), F32),
            jax.ShapeDtypeStruct((len(plan), rows, WIDE), F32),
            jax.ShapeDtypeStruct(swapped.shape, BF16),
        ),
        in_specs=[
            pl.BlockSpec((1, length, DV), lambda s, _: (now(s) // per, 0, now(s) % per)),
            pl.BlockSpec((1, length, DV), lambda s, _: (now(s), 0, 0)),
            pl.BlockSpec((1, length, DV), lambda s, _: (now(s) // per, 0, (now(s) % per) * 3 + 2)),
            pl.BlockSpec((1, length, DK), lambda s, _: (now(s), 0, 0)),
            pl.BlockSpec((1, chunks, DK, DK), lambda s, _: (now(s), 0, 0, 0)),
            pl.BlockSpec((1, DK, DK), lambda s, _: (now(s), 0, 0)),
            pl.BlockSpec((1, length, HEADW + DV), lambda s, _: (late(s) // per, 0, late(s) % per)),
            pl.BlockSpec((1, HALO, HEADW + DV), lambda s, _: (late(s) // per, 0, late(s) % per)),
            pl.BlockSpec((1, TAPS, HEADW), lambda s, _: (late(s), 0, 0)),
            pl.BlockSpec((1, 8, length), lambda s, _: (late(s), 0, 0)),
            pl.BlockSpec((1, DV), lambda s, _: (0, 0)),
            pl.BlockSpec((1, chunks, DK, DV), lambda s, _: (late(s), 0, 0, 0)),
            pl.BlockSpec((1, chunks, size, size), lambda s, _: (late(s), 0, 0, 0)),
            pl.BlockSpec((1, chunks, DK, DK), lambda s, _: (late(s), 0, 0, 0)),
            *[any_spec] * (1 + len(lefts) + len(pairs)),
        ],
        out_specs=(
            pl.BlockSpec((1, length, HEADW + DV), lambda s, _: (later(s) // per, 0, later(s) % per)),
            pl.BlockSpec((1, 8, length), lambda s, _: (late(s), 0, 0)),
            pl.BlockSpec((1, TAPS, HEADW), lambda s, _: (late(s), 0, 0)),
            pl.BlockSpec((1, DV), lambda s, _: (0, 0)),
            pl.BlockSpec((len(plan), rows, WIDE), lambda s, _: (0, 0, 0)),
            any_spec,
        ),
        scratch_shapes=[
            pltpu.VMEM((slots, length, DV), F32),
            pltpu.VMEM((slots, chunks, DK, DV), F32),
            pltpu.VMEM((slots + 1, length, DV), BF16),
            pltpu.VMEM((slots, DK, DV), F32),
            pltpu.VMEM((slots, DK, DK), F32),
            pltpu.VMEM((length + 2 * HALO, HEADW), F32),
            pltpu.VMEM((2, length, HEADW), F32),
            pltpu.VMEM((HALO + size, HEADW), F32),
            pltpu.VMEM((heads, DK, DV), F32),
            pltpu.VMEM((heads, DK, DV), F32),
            pltpu.VMEM((heads, HALO, HEADW), F32),
            pltpu.VMEM((heads, HALO, HEADW), F32),
            pltpu.SemaphoreType.DMA((heads,)),
            pltpu.SemaphoreType.DMA((heads,)),
            pltpu.SemaphoreType.DMA((heads,)),
            pltpu.SemaphoreType.DMA((heads,)),
            *[pltpu.SemaphoreType.DMA((1,))] * 3,
            *Scatter.scratch(bits, parts, len(plan), rows, length, lefts[0].shape[0]),
        ],
        compiler_params=pltpu.CompilerParams(
            collective_id=1, has_side_effects=True, vmem_limit_bytes=62 * 2**20
        ),
        cost_estimate=pl.CostEstimate(flops=40 * 10**9, bytes_accessed=60 * 2**20, transcendentals=0),
        name="delta_backward",
    )(d_head, out, raw, query_e, phi, phi_all, raw, halo, convw, ab, gain, states, inverses, phi,
      *lefts, *[right for _, right in pairs], swapped)


def dot(spec, a, b):
    return jnp.einsum(spec, a, b, preferred_element_type=F32)


def unit_rms(v):
    return lax.rsqrt(jnp.mean(v * v, axis=-1, keepdims=True) + 1e-05)


def per_device(
    tokens, out_grad, seq_lengths, mix_gain, w_query, w_key, w_value, w_outgate, w_decay, w_beta,
    conv_weight, rate_log, step_bias, head_gain, w_out, ffn_gain, w_ffn_gate, w_ffn_up, w_ffn_down,
):
    groups = lax.axis_size("dp")
    parts = lax.axis_size("mp")
    group = lax.axis_index("dp")
    share = lax.axis_index("mp")
    heads = rate_log.shape[0]
    per = heads // parts
    width = tokens.shape[2]
    local_rows = w_query.shape[0]

    hidden = w_ffn_gate.shape[1]
    wide = -(-hidden // WIDE) * WIDE
    small_w = jnp.concatenate([w_decay, w_beta], axis=1).T
    small_w = jnp.pad(small_w, ((0, -small_w.shape[0] % 16), (0, 0)))
    x_bf, g_proj, g_small, raw, h1, h1_t, *padded = prologue(
        tokens, small_w, mix_gain[None], (w_query, w_key, w_value, w_outgate),
        (w_ffn_gate.T, w_ffn_up.T, w_ffn_down.T), groups, parts,
    )
    h1 = h1.reshape(-1, width)
    whole = lambda g: g.reshape(parts, width, g.shape[3])
    g_proj = whole(g_proj)
    g_small = g_small[:, :, : 2 * per].transpose(0, 2, 1, 3).reshape(parts, 2 * per, width)
    x_swapped = x_bf
    x_bf = x_bf.reshape(-1, width)
    length = x_bf.shape[0]

    my_length = lax.dynamic_slice_in_dim(seq_lengths, group, 1)
    positions = share * length + jnp.arange(length, dtype=jnp.int32)
    live = (positions < my_length).astype(F32)[:, None]

    x = x_bf.astype(F32)
    small = dot("td,gcd->gct", h1, g_small)
    decay_raw = small[:, :per].reshape(heads, length)
    beta_raw = small[:, per:].reshape(heads, length)
    rate = -jnp.exp(rate_log)[:, None]
    shifted = decay_raw + step_bias[:, None]
    decay = rate * jax.nn.softplus(shifted)
    beta = jax.nn.sigmoid(beta_raw)
    ab = jnp.concatenate(
        [decay[:, None], beta[:, None], jnp.zeros((heads, 6, length), F32)], axis=1
    )
    taps = conv_weight.shape[0]
    key_cols = heads * DK
    convw = jnp.concatenate(
        [
            conv_weight[:, :key_cols].reshape(taps, heads, DK),
            conv_weight[:, key_cols : 2 * key_cols].reshape(taps, heads, DK),
            conv_weight[:, 2 * key_cols :].reshape(taps, heads, DV),
        ],
        axis=2,
    ).transpose(1, 0, 2)
    gain_row = head_gain[None]
    head_out, mixed, states, inverses, query_e, phi, phi_all, halo, dy_bf, *rest = forward_core(
        raw, convw, ab, gain_row, out_grad,
        [w_out] + padded,
        heads, parts, groups,
    )
    g_out, g_gate, g_up, g_down = [whole(w) for w in rest]

    dy = live * dy_bf.reshape(-1, width).astype(F32)
    d_ffo = dy.astype(BF16)
    x1 = x + dot("gtc,gmc->tm", head_out, g_out)
    scale2 = unit_rms(x1)
    n2 = x1 * scale2
    h2 = (n2 * ffn_gain).astype(BF16)
    gate = dot("td,gdf->gtf", h2, g_gate)
    up = dot("td,gdf->gtf", h2, g_up)
    sig = jax.nn.sigmoid(gate)
    act = (gate * sig * up).astype(BF16)
    block_out = (live * (x1 + dot("gtf,gdf->td", act, g_down))).astype(BF16)
    d_act = dot("td,gdf->gtf", d_ffo, g_down)
    d_gate = (d_act * up * sig * (1.0 + gate * (1.0 - sig))).astype(BF16)
    d_up = (d_act * gate * sig).astype(BF16)
    d_h2 = dot("gtf,gdf->td", d_gate, g_gate) + dot("gtf,gdf->td", d_up, g_up)
    e2 = d_h2 * ffn_gain
    d_x1 = dy + scale2 * (e2 - n2 * jnp.mean(e2 * n2, axis=-1, keepdims=True))
    ffn_gain_grad = jnp.sum(d_h2 * n2, axis=0)
    d_mix = d_x1.astype(BF16)
    d_head = dot("tm,gmc->gtc", d_mix, g_out)

    d_proj, d_ab, d_convw, d_head_gain, sums_ffn, final_out = backward_core(
        d_head, mixed, raw, halo, query_e, phi, phi_all, convw, ab, gain_row, states, inverses,
        [d_mix.T, h2.T, d_ffo.T], [(2, act), (1, d_gate), (1, d_up), (0, head_out)],
        block_out.reshape(tokens.shape), heads, parts, groups,
    )
    d_decay = d_ab[:, 0]
    d_beta_raw = d_ab[:, 1] * beta * (1.0 - beta)
    d_decay_raw = d_decay * rate * jax.nn.sigmoid(shifted)
    rate_grad = jnp.sum(d_decay * decay, axis=1)
    bias_grad = jnp.sum(d_decay_raw, axis=1)
    d_small = jnp.concatenate(
        [d_decay_raw.reshape(parts, per, length), d_beta_raw.reshape(parts, per, length)], axis=1
    ).astype(BF16)
    line = jnp.pad(jnp.concatenate([rate_grad, bias_grad])[None], ((0, 0), (0, 128 - 2 * heads)))
    sums_proj, sums, final_grad = scatter_sum(
        h1_t, [(0, d_proj)],
        (ffn_gain_grad[None], d_head_gain, d_convw, line), g_proj, d_small.reshape(-1, length),
        g_small.reshape(-1, width), x_swapped, d_x1, mix_gain[None], groups, parts, 2,
    )
    starts, _ = small_rows(heads, width, 2 * heads)
    part = lambda i: sums[starts[i] : starts[i + 1]].reshape(-1)
    (s_query, s_key, s_value, s_outgate, s_out, s_gate, s_up, s_down, s_conv, final_out, final_grad,
     s_mix, s_gain, s_hgain, s_small) = assemble(
        sums_ffn, sums_proj, sums, final_out, final_grad, per, hidden, starts, conv_weight.shape
    )
    return (
        final_out,
        final_grad,
        s_mix.reshape(-1),
        s_query,
        s_key,
        s_value,
        s_outgate,
        s_small[:per].T,
        s_small[per:].T,
        s_conv,
        part(4)[:heads],
        part(4)[heads : 2 * heads],
        s_hgain.reshape(-1),
        s_out,
        s_gain.reshape(-1),
        s_gate.T,
        s_up.T,
        s_down.T,
    )


def solution(mesh):
    seq = P(None, ("mp", "dp"), None)
    shard = P("dp", "mp")
    rep = P()
    return jax.shard_map(
        per_device,
        mesh=mesh,
        in_specs=(
            seq, seq, rep, rep, shard, shard, shard, shard, shard, shard,
            rep, rep, rep, rep, shard, rep, shard, shard, shard,
        ),
        out_specs=(
            seq, seq, rep, shard, shard, shard, shard, shard, shard,
            rep, rep, rep, rep, shard, rep, shard, shard, shard,
        ),
        check_vma=False,
    )
```

```python
from functools import partial

import jax
import jax.numpy as jnp
from jax import lax
from jax.experimental import pallas as pl
from jax.experimental.pallas import tpu as pltpu
from jax.sharding import PartitionSpec as P

DK = 128
DV = 256
HEADW = 2 * DK + DV
TAPS = 4
CHUNK = 128
HALO = 8
WIDE = 256
STRIDE = 2
F32 = jnp.float32
BF16 = jnp.bfloat16


def halves(a):
    high = a.astype(BF16)
    return high, (a - high.astype(F32)).astype(BF16)


def mm(a, b, ca=1, cb=0):
    dims = (((ca,), (cb,)), ((), ()))
    a_high, a_low = halves(a)
    b_high, b_low = halves(b)
    one = lambda p, q: lax.dot_general(p, q, dims, preferred_element_type=F32)
    if a.shape[ca] <= 128:
        return one(
            jnp.concatenate([a_high, a_low], axis=ca), jnp.concatenate([b_high, b_high], axis=cb)
        ) + one(a_high, b_low)
    return one(a_high, b_high) + (one(a_high, b_low) + one(a_low, b_high))


def windows(raw_ref, ext_s, c, size):
    if c == 0:
        return [ext_s[pl.ds(HALO - TAPS + 1 + i, size)] for i in range(TAPS)]
    return [raw_ref[0, pl.ds(c * size - TAPS + 1 + i, size), 0:HEADW] for i in range(TAPS)]


def conv_of(shifted, convw):
    total = None
    for i in range(TAPS):
        part = shifted[i] * convw[i : i + 1]
        total = part if total is None else total + part
    return total


def decays(ab_ref, base, rows, upper):
    ab = ab_ref[0, :, pl.ds(base, rows)]
    cum = mm(ab, upper)
    row_id = lax.broadcasted_iota(jnp.int32, ab.shape, 0)
    both = jnp.where(row_id == 0, cum, ab)
    cols = both.T
    return both[0:1], cols[:, 0:1], cols[:, 1:2]


def masks(size):
    rows = lax.broadcasted_iota(jnp.int32, (size, size), 0)
    cols = lax.broadcasted_iota(jnp.int32, (size, size), 1)
    return rows, cols


def fades(gamma_row, gamma_col, rows, cols):
    spread = jnp.minimum(gamma_col - gamma_row, 0.0)
    inclusive = jnp.where(rows >= cols, jnp.exp(spread), 0.0)
    strict = jnp.where(rows > cols, inclusive, 0.0)
    return inclusive, strict


def invert_many(lowers, rows, cols):
    size = lowers[0].shape[0]
    eye = (rows == cols).astype(F32)
    pair = ((rows // 2) == (cols // 2)) & (rows > cols)
    inverses = [eye - jnp.where(pair, low, 0.0) for low in lowers]
    width = 2
    while width < size:
        within = (rows // (2 * width)) == (cols // (2 * width))
        cross = within & ((rows // width) != (cols // width)) & (rows > cols)
        inner = [mm(jnp.where(cross, low, 0.0), inv) for low, inv in zip(lowers, inverses)]
        inverses = [inv - mm(inv, part) for inv, part in zip(inverses, inner)]
        width *= 2
    return inverses


def in_step(works):
    while works:
        works = [work for work in works if next(work, True) is None]


def unit_parts(conv):
    sig = jax.nn.sigmoid(conv)
    silu = conv * sig
    q_silu = silu[:, :DK]
    k_silu = silu[:, DK : 2 * DK]
    value = silu[:, 2 * DK :]
    q_scale = lax.rsqrt(jnp.sum(q_silu * q_silu, axis=-1, keepdims=True) + 1e-06)
    k_scale = lax.rsqrt(jnp.sum(k_silu * k_silu, axis=-1, keepdims=True) + 1e-06)
    return sig, q_silu, k_silu, value, q_scale, k_scale


class Gather:
    def __init__(self, bits, parts, sources, targets, pieces, sems):
        self.bits, self.parts, self.pieces = bits, parts, pieces
        self.sources, self.targets = sources, targets
        (self.own, self.z_send, self.z_recv, self.p_send, self.p_recv, self.s_send, self.s_recv) = sems
        self.d, self.z = lax.axis_index("dp"), lax.axis_index("mp")
        self.orders = (list(range(1, bits)), list(range(bits - 1, 0, -1)))
        self.ticks = bits + 1

    @staticmethod
    def scratch(bits, count):
        dma = lambda *shape: pltpu.SemaphoreType.DMA(shape)
        return [
            dma(count), dma(count), dma(count), dma(count, bits - 1, 2), dma(count, bits - 1, 2),
            dma(count), dma(count),
        ]

    def flip(self, index, b):
        return index + (1 - 2 * lax.rem(lax.div(self.d, 2**b), 2)) * 2**b

    def copy(self, src, dst, send, recv, to):
        return pltpu.make_async_remote_copy(
            src_ref=src, dst_ref=dst, send_sem=send, recv_sem=recv, device_id=to,
            device_id_type=pl.DeviceIdType.MESH,
        )

    def sides(self, p):
        _, start, mid, stop = self.pieces[p]
        return [(0, start, mid)] + ([(1, mid, stop)] if mid < stop else [])

    def held(self, side, k):
        out = [self.d]
        for b in self.orders[side][:k]:
            out = out + [self.flip(i, b) for i in out]
        return out

    def arrived(self, side, k):
        return [self.flip(i, self.orders[side][k]) for i in self.held(side, k)]

    def to_sibling(self, p, indices, start, stop):
        target = self.targets[self.pieces[p][0]]
        for i in indices:
            block = target.at[:, i, :, start:stop]
            self.copy(
                block, block, self.s_send.at[p], self.s_recv.at[p], {"dp": self.flip(self.d, 0)}
            ).start()

    def along(self, p, k, act):
        target = self.targets[self.pieces[p][0]]
        for side, start, stop in self.sides(p):
            b = self.orders[side][k]
            for i in self.held(side, k):
                block = target.at[:, i, :, start:stop]
                act(
                    self.copy(
                        block, block, self.p_send.at[p, k, side], self.p_recv.at[p, k, side],
                        {"dp": self.flip(self.d, b)},
                    )
                )

    def along_whole(self, p, k):
        target = self.targets[self.pieces[p][0]]
        out = []
        for side, start, stop in self.sides(p):
            block = target.at[:, pl.ds(0, 2**k), :, start:stop]
            out.append(
                self.copy(
                    block, block, self.p_send.at[p, k, side], self.p_recv.at[p, k, side],
                    {"dp": self.flip(self.d, self.orders[side][k])},
                )
            )
        return out

    def tick(self, p, stage):
        which, start, _, stop = self.pieces[p]
        source, target = self.sources[which], self.targets[which]
        if stage == 0:
            pltpu.make_async_copy(
                source.at[:, start:stop], target.at[self.z, self.d, :, start:stop], self.own.at[p]
            ).start()
            for delta in range(1, self.parts):
                self.copy(
                    source.at[:, start:stop], target.at[self.z, self.d, :, start:stop], self.z_send.at[p],
                    self.z_recv.at[p], {"mp": lax.rem(self.z + delta, self.parts)},
                ).start()
        elif stage == 1:
            pltpu.make_async_copy(
                source.at[:, start:stop], target.at[self.z, self.d, :, start:stop], self.own.at[p]
            ).wait()
            self.z_whole(p).wait_recv()
            self.along(p, 0, lambda copy: copy.start())
            self.to_sibling(p, [self.d], start, stop)
        elif stage <= self.bits:
            k = stage - 2
            for copy in self.along_whole(p, k):
                copy.wait_recv()
            if k + 1 < self.bits - 1:
                self.along(p, k + 1, lambda copy: copy.start())
            for side, low, high in self.sides(p):
                self.to_sibling(p, self.arrived(side, k), low, high)

    def moves(self):
        return len(self.pieces) + STRIDE * (self.ticks - 1)

    def move(self, now):
        for p in range(len(self.pieces)):
            if now >= p and (now - p) % STRIDE == 0 and (now - p) // STRIDE < self.ticks:
                self.tick(p, (now - p) // STRIDE)

    def z_whole(self, p):
        which, start, _, stop = self.pieces[p]
        block = self.targets[which].at[pl.ds(0, self.parts - 1), self.d, :, start:stop]
        return self.copy(
            block, block, self.z_send.at[p], self.z_recv.at[p],
            {"mp": lax.rem(self.z + 1, self.parts)},
        )

    def s_whole(self, p):
        which, start, _, stop = self.pieces[p]
        block = self.targets[which].at[:, pl.ds(0, 2 ** (self.bits - 1)), :, start:stop]
        return self.copy(
            block, block, self.s_send.at[p], self.s_recv.at[p], {"dp": self.flip(self.d, 0)}
        )

    def finish(self, waited=()):
        for p in range(len(self.pieces)):
            if p not in waited:
                self.s_whole(p).wait_recv()
            self.z_whole(p).wait_send()
            for k in range(self.bits - 1):
                for copy in self.along_whole(p, k):
                    copy.wait_send()
            self.s_whole(p).wait_send()


def greet_all(bits, parts, every):
    d, z = lax.axis_index("dp"), lax.axis_index("mp")
    barrier = pltpu.get_barrier_semaphore()
    if every:
        peers = [lax.rem(d + delta, 2**bits) for delta in range(1, 2**bits)]
    else:
        peers = [d + (1 - 2 * lax.rem(lax.div(d, 2**b), 2)) * 2**b for b in range(bits)]
    for peer in peers:
        pl.semaphore_signal(
            barrier, inc=1, device_id={"dp": peer}, device_id_type=pl.DeviceIdType.MESH
        )
    for delta in range(1, parts):
        pl.semaphore_signal(
            barrier, inc=1, device_id={"mp": lax.rem(z + delta, parts)},
            device_id_type=pl.DeviceIdType.MESH,
        )
    pl.semaphore_wait(barrier, len(peers) + parts - 1)


class Swap:
    def __init__(self, groups, source, target, own, send, recv):
        self.groups, self.source, self.target = groups, source, target
        self.own, self.send, self.recv = own, send, recv
        self.d = lax.axis_index("dp")

    def copy(self, src, dst, to):
        return pltpu.make_async_remote_copy(
            src_ref=src, dst_ref=dst, send_sem=self.send, recv_sem=self.recv, device_id={"dp": to},
            device_id_type=pl.DeviceIdType.MESH,
        )

    def local(self):
        return pltpu.make_async_copy(self.source.at[self.d], self.target.at[self.d], self.own)

    def start(self):
        self.local().start()
        for delta in range(1, self.groups):
            to = lax.rem(self.d + delta, self.groups)
            self.copy(self.source.at[to], self.target.at[self.d], to).start()

    def finish(self):
        self.local().wait()
        block = self.target.at[pl.ds(0, self.groups - 1)]
        whole = self.copy(block, block, lax.rem(self.d + 1, self.groups))
        whole.wait_recv()
        whole.wait_send()


def prologue_kernel(bits, parts, pieces, *refs):
    tokens, small, gain, *refs = refs
    members, narrow, refs = refs[:4], refs[4:7], refs[7:]
    tokens_out, joined_out, small_out, raw_out, h1_out, h1t_out = refs[:6]
    padded, refs = refs[6:9], refs[9:]
    member_s, narrow_s, padded_s, refs = refs[:4], refs[4:7], refs[7:10], refs[10:]
    in_sem, out_sem, joined, x_s, w_s, raw_s, x_sem, w_sem, raw_sem, *sems = refs
    loads = [
        pltpu.make_async_copy(src, dst, in_sem.at[i])
        for i, (src, dst) in enumerate(zip((*members, *narrow), (*member_s, *narrow_s)))
    ]
    for load in loads:
        load.start()
    gather = Gather(bits, parts, (joined, small), (joined_out, small_out), pieces, sems[:7])
    swap = Swap(2**bits, tokens, tokens_out, *[s.at[0] for s in sems[7:10]])
    greet_all(bits, parts, True)
    swap.start()
    blocks, rows, width = x_s.shape
    at = 0
    for load in loads[:4]:
        load.wait()
    for h in range(joined.shape[1] // (HEADW + DV)):
        for member, size in zip(member_s, (DK, DK, DV, DV)):
            joined[:, at : at + size] = member[:, h * size : (h + 1) * size]
            at += size

    def put(i):
        return pltpu.make_async_copy(padded_s[i], padded[i], out_sem.at[i])

    def widen():
        for i, (source, target) in enumerate(zip(narrow_s, padded_s)):
            loads[4 + i].wait()
            have, wide = source.shape[0], target.shape[1]
            edge = have // 128 * 128
            target[:, edge:] = jnp.zeros((target.shape[0], wide - edge), BF16)
            target[:, 0:have] = source[...].T
            put(i).start()

    def normalize():
        swap.finish()
        copy = pltpu.make_async_copy(tokens_out, x_s, x_sem.at[0])
        copy.start()
        copy.wait()

        @pl.loop(0, blocks)
        def _(i):
            x = x_s[i].astype(F32)
            scale = lax.rsqrt(jnp.mean(x * x, axis=-1, keepdims=True) + 1e-05)
            h1_out[i] = (x * scale * gain[...]).astype(BF16)

        h1t_out[...] = h1_out[...].reshape(blocks * rows, width).T

    def fetch(p):
        _, start, _, stop = pieces[p]
        return pltpu.make_async_copy(
            joined_out.at[:, :, :, start:stop], w_s.at[p % 2], w_sem.at[p % 2]
        )

    def store(p):
        _, start, _, stop = pieces[p]
        return pltpu.make_async_copy(raw_s.at[p % 2], raw_out.at[:, :, start:stop], raw_sem.at[p % 2])

    main = [p for p, item in enumerate(pieces) if item[0] == 0]

    def project(p):
        if p - 2 in main:
            store(p - 2).wait()
        fetch(p).wait()
        h1 = h1_out[...].reshape(blocks * rows, width)

        @pl.loop(0, parts)
        def _(g):
            raw_s[p % 2, g] = jnp.dot(
                h1, w_s[p % 2, g].reshape(width, WIDE), preferred_element_type=F32
            )

        store(p).start()

    ready = {p + STRIDE * gather.ticks: p for p in main}
    for now in range(max(ready) + 2):
        if now < gather.moves():
            gather.move(now)
        if now == 1:
            widen()
        if now == min(ready):
            normalize()
        if now - 1 in ready:
            project(ready[now - 1])
        if now in ready:
            gather.s_whole(ready[now]).wait_recv()
            fetch(ready[now]).start()
    gather.finish(main)
    for p in main[-2:]:
        store(p).wait()
    for i in range(3):
        put(i).wait()


def prologue(tokens, small, gain, members, narrow, groups, parts):
    bits = groups.bit_length() - 1
    rows = members[0].shape[0]
    wide = sum(w.shape[1] for w in members)
    padded = -(-narrow[0].shape[0] // WIDE) * WIDE
    blocks, token_rows, width = tokens.shape
    pieces = [(1, 0, small.shape[1], small.shape[1])]
    pieces += [(0, at, at + WIDE // 2, at + WIDE) for at in range(0, wide, WIDE)]
    length = blocks * token_rows
    any_spec = pl.BlockSpec(memory_space=pl.ANY)
    vmem_spec = pl.BlockSpec(memory_space=pltpu.VMEM)
    dma = lambda *shape: pltpu.SemaphoreType.DMA(shape)
    return pl.pallas_call(
        partial(prologue_kernel, bits, parts, pieces),
        out_shape=(
            jax.ShapeDtypeStruct(tokens.shape, BF16),
            jax.ShapeDtypeStruct((parts, groups, rows, wide), BF16),
            jax.ShapeDtypeStruct((parts, groups) + small.shape, BF16),
            jax.ShapeDtypeStruct((parts, length, wide), F32),
            jax.ShapeDtypeStruct(tokens.shape, BF16),
            jax.ShapeDtypeStruct((width, length), BF16),
            *[jax.ShapeDtypeStruct((rows, padded), BF16)] * 3,
        ),
        in_specs=[any_spec] * 2 + [vmem_spec] + [any_spec] * 7,
        out_specs=(any_spec,) * 4 + (vmem_spec,) * 2 + (any_spec,) * 3,
        scratch_shapes=[
            *[pltpu.VMEM(w.shape, BF16) for w in (*members, *narrow)],
            *[pltpu.VMEM((rows, padded), BF16)] * 3,
            dma(7), dma(3),
            pltpu.VMEM((rows, wide), BF16),
            pltpu.VMEM(tokens.shape, BF16),
            pltpu.VMEM((2, parts, groups, rows, WIDE), BF16),
            pltpu.VMEM((2, parts, length, WIDE), F32),
            dma(1), dma(2), dma(2),
            *Gather.scratch(bits, len(pieces)),
            dma(1), dma(1), dma(1),
        ],
        compiler_params=pltpu.CompilerParams(
            collective_id=3, has_side_effects=True, vmem_limit_bytes=62 * 2**20
        ),
        cost_estimate=pl.CostEstimate(
            flops=2 * length * width * wide * parts, bytes_accessed=40 * 2**20, transcendentals=0
        ),
        name="prologue",
    )(tokens, small, gain, *members, *narrow)


def forward_kernel(
    heads, parts, bits, pieces,
    raw_ref, gate_ref, raw_any, convw_ref, ab_ref, gain_ref, *refs,
):
    weights = len({item[0] for item in pieces})
    swap_in, sources, refs = refs[0], refs[1 : 1 + weights], refs[1 + weights :]
    head_ref, o_ref, s_ref, t_ref, qe_ref, phi_ref, phil_ref, halo_ref = refs[:8]
    swap_out, targets, refs = refs[8], refs[9 : 9 + weights], refs[9 + weights :]
    (qe_s, o0_s, phi_s, b_s, phil_s, bl_s, send_s, recv_s, halo_s, ext_s,
     send_sem, recv_sem, halo_send_sem, halo_recv_sem) = refs[:14]
    swap = Swap(2**bits, swap_in, swap_out, *[s.at[0] for s in refs[14:17]])
    gather = Gather(bits, parts, sources, targets, pieces, refs[17:])
    step = pl.program_id(0)
    early = pl.program_id(1) == 0
    z = lax.axis_index("mp")
    lag = parts - 1
    slots = lag + 1
    length = gate_ref.shape[1]
    size = min(CHUNK, length)
    chunks = length // size
    per = heads // parts

    @pl.when((step == 0) & early)
    def _():
        greet_all(bits, parts, True)
        swap.start()

    last = 2 * (heads + lag) - 1
    for spot in range(last + 1):
        moves = [m for m in range(gather.moves()) if m * last // (gather.moves() - 1) == spot]
        if moves:
            @pl.when(step * 2 + pl.program_id(1) == spot)
            def _():
                for m in moves:
                    gather.move(m)

    def hop(h):
        return pltpu.make_async_remote_copy(
            src_ref=send_s.at[h], dst_ref=recv_s.at[h], send_sem=send_sem.at[h],
            recv_sem=recv_sem.at[h], device_id={"mp": lax.rem(z + 1, parts)},
            device_id_type=pl.DeviceIdType.MESH,
        )

    def halo_hop(g):
        return pltpu.make_async_remote_copy(
            src_ref=raw_any.at[g, length - HALO :], dst_ref=halo_s.at[g], send_sem=halo_send_sem.at[g],
            recv_sem=halo_recv_sem.at[g], device_id={"mp": lax.rem(z + 1, parts)},
            device_id_type=pl.DeviceIdType.MESH,
        )

    @pl.when((step == 0) & early & (z == 0))
    def _():
        recv_s[...] = jnp.zeros_like(recv_s)
        halo_s[...] = jnp.zeros_like(halo_s)

    @pl.when((step == 0) & early & (z < parts - 1))
    def _():
        for g in range(parts):
            halo_hop(g).start()

    @pl.when((step < heads) & early)
    def _():
        slot = lax.rem(step, slots)
        part, sub = lax.div(step, per), lax.rem(step, per)

        @pl.when((sub == 0) & (z > 0))
        def _():
            halo_hop(part).wait_recv()

        for k in range(per):
            @pl.when(sub == k)
            def _():
                ext_s[0:HALO] = halo_s[part, :, k * (HEADW + DV) : k * (HEADW + DV) + HEADW]

        ext_s[HALO:] = raw_ref[0, 0:size, 0:HEADW]
        rows, cols = masks(size)
        upper = (rows <= cols).astype(F32)
        convw = convw_ref[0]
        kept = [None] * chunks
        lowers = [None] * chunks

        def open_chunk(c):
            conv = conv_of(windows(raw_ref, ext_s, c, size), convw)
            _, q_silu, k_silu, value, q_scale, k_scale = unit_parts(conv)
            query = q_silu * (q_scale * DK ** (-0.5))
            keyed = k_silu * k_scale
            yield
            gamma_row, gamma_col, beta = decays(ab_ref, c * size, size, upper)
            inclusive, strict = fades(gamma_row, gamma_col, rows, cols)
            gram = mm(jnp.concatenate([keyed, query], axis=0), keyed, 1, 1)
            yield
            lowers[c] = beta * gram[:size] * strict
            scores = gram[size:] * inclusive
            growth = jnp.exp(gamma_col)
            last = gamma_row[:, size - 1 :]
            rhs = jnp.concatenate([(beta * growth) * keyed, beta * value], axis=1)
            kept[c] = (scores, rhs, query * growth, keyed * jnp.exp(last - gamma_col), last)

        in_step([open_chunk(c) for c in range(chunks)])
        inverses = invert_many(lowers, rows, cols)
        eye = (masks(DK)[0] == masks(DK)[1]).astype(F32)
        flows = [None] * chunks

        def close_chunk(c):
            scores, rhs, query_g, keyed_g, last = kept[c]
            t_ref[0, c] = inverses[c]
            solved = mm(inverses[c], rhs)
            yield
            mixed = mm(scores, solved)
            yield
            moved = mm(keyed_g, solved, 0, 0)
            yield
            query_e = query_g - mixed[:, :DK]
            phi = jnp.exp(last) * eye - moved[:, :DK]
            qe_ref[0, c * size : (c + 1) * size] = query_e
            qe_s[slot, c * size : (c + 1) * size] = query_e
            o0_s[slot, c * size : (c + 1) * size] = mixed[:, DK:]
            phi_ref[0, c] = phi.T
            phi_s[slot, c] = phi
            b_s[slot, c] = moved[:, DK:]
            flows[c] = phi

        in_step([close_chunk(c) for c in range(chunks)])
        phi_all, b_all = flows[0], b_s[slot, 0]
        for c in range(1, chunks):
            moved_all = mm(flows[c], jnp.concatenate([phi_all, b_all], axis=1))
            phi_all = moved_all[:, :DK]
            b_all = moved_all[:, DK:] + b_s[slot, c]
        phil_ref[0] = phi_all.T
        phil_s[slot] = phi_all
        bl_s[slot] = b_all

    relay = step - z

    @pl.when((relay >= 0) & (relay < heads) & ~early)
    def _():
        slot = lax.rem(relay, slots)

        @pl.when(z > 0)
        def _():
            hop(relay).wait_recv()

        @pl.when(z < parts - 1)
        def _():
            send_s[relay] = mm(phil_s[slot], recv_s[relay]) + bl_s[slot]
            hop(relay).start()

    @pl.when((step >= lag) & ~early)
    def _():
        head = step - lag
        slot = lax.rem(head, slots)
        state = recv_s[head]
        for c in range(chunks):
            at = slice(c * size, (c + 1) * size)
            s_ref[0, c] = state
            result = mm(qe_s[slot, at], state) + o0_s[slot, at]
            if c + 1 < chunks:
                state = mm(phi_s[slot, c], state) + b_s[slot, c]
            o_ref[0, at] = result
            scale = lax.rsqrt(jnp.mean(result * result, axis=-1, keepdims=True) + 1e-05)
            gate = gate_ref[0, c * size : (c + 1) * size]
            gated = result * scale * gain_ref[...] * (gate * jax.nn.sigmoid(gate))
            head_ref[0, at] = gated.astype(BF16)

    @pl.when((step == pl.num_programs(0) - 1) & ~early & (z < parts - 1))
    def _():
        @pl.loop(0, heads)
        def _(h):
            hop(h).wait_send()

        for g in range(parts):
            halo_hop(g).wait_send()

    @pl.when((step == pl.num_programs(0) - 1) & ~early)
    def _():
        halo_ref[...] = halo_s[...]
        gather.finish()
        swap.finish()


class Scatter:
    def __init__(self, bits, parts, plan, rows, lhs_refs, rhs_refs, out_ref, scratch, stride):
        self.stride = stride
        self.bits, self.parts, self.plan, self.rows = bits, parts, plan, rows
        self.lhs_refs, self.rhs_refs, self.out_ref = lhs_refs, rhs_refs, out_ref
        self.count = len(plan)
        self.planes = planes = bits - 1
        self.half = 2 ** (bits - 1)
        self.lhs_s, self.rhs_s, self.grad_s, self.r1, *rest = scratch
        self.ra, self.rb = rest[:planes], rest[planes : 2 * planes]
        (self.r4, self.load_sem, self.send1, self.recv1, self.send_a, self.recv_a, self.send_b,
         self.recv_b, self.send4, self.recv4) = rest[2 * planes :]
        self.d, self.z = lax.axis_index("dp"), lax.axis_index("mp")
        self.ticks = self.count + 1 + self.stride * (planes + 1)

    @staticmethod
    def scratch(bits, parts, count, rows, length, width):
        planes, half = bits - 1, 2 ** (bits - 1)
        vmem = lambda *shape: pltpu.VMEM(shape, BF16)
        dma = lambda *shape: pltpu.SemaphoreType.DMA(shape)
        strips = [vmem(count, parts, half >> (k + 1), rows, WIDE // 2) for k in range(planes)]
        return [
            vmem(2, width, length),
            vmem(2, parts, length, WIDE),
            vmem(2, parts, half, 2, rows, WIDE),
            vmem(count, parts, half, rows, WIDE),
            *strips, *strips,
            vmem(count, parts - 1, rows, WIDE),
            dma(2, 2),
            dma(count), dma(count),
            dma(planes, count), dma(planes, count),
            dma(planes, count), dma(planes, count),
            dma(count), dma(count),
        ]

    def bit(self, b):
        return lax.rem(lax.div(self.d, 2**b), 2)

    def partner(self, b):
        return self.d + (1 - 2 * self.bit(b)) * 2**b

    def remote(self, src, dst, send, recv, to):
        return pltpu.make_async_remote_copy(
            src_ref=src, dst_ref=dst, send_sem=send, recv_sem=recv, device_id=to,
            device_id_type=pl.DeviceIdType.MESH,
        )

    def load(self, t):
        slot = lax.rem(t, 2)
        for seg in range(len(self.rhs_refs)):
            at = [k for k, item in enumerate(self.plan) if item[0] == seg]

            @pl.when((t >= at[0]) & (t <= at[-1]))
            def _():
                start = pl.multiple_of((t - at[0]) * WIDE, WIDE)
                pltpu.make_async_copy(
                    self.rhs_refs[seg].at[:, :, pl.ds(start, WIDE)], self.rhs_s.at[slot],
                    self.load_sem.at[0, slot],
                ).start()
                pltpu.make_async_copy(
                    self.lhs_refs[self.plan[at[0]][1]], self.lhs_s.at[slot], self.load_sem.at[1, slot]
                ).start()

    def load_wait(self, t):
        slot = lax.rem(t, 2)
        pltpu.make_async_copy(
            self.rhs_refs[0].at[:, :, pl.ds(0, WIDE)], self.rhs_s.at[slot], self.load_sem.at[0, slot]
        ).wait()
        pltpu.make_async_copy(
            self.lhs_refs[0], self.lhs_s.at[slot], self.load_sem.at[1, slot]
        ).wait()

    def first_hop(self, t):
        return self.remote(
            self.grad_s.at[lax.rem(t, 2), :, :, 1 - self.bit(0)], self.r1.at[t], self.send1.at[t],
            self.recv1.at[t], {"dp": self.partner(0)},
        )

    def a_hop(self, k, t):
        b = self.bits - 1 - k
        keep = self.half >> (k + 1)
        away = pl.ds((1 - self.bit(b)) * keep, keep)
        src = self.r1.at[t, :, away, :, 0 : WIDE // 2] if k == 0 else self.ra[k - 1].at[t, :, away]
        return self.remote(
            src, self.ra[k].at[t], self.send_a.at[k, t], self.recv_a.at[k, t], {"dp": self.partner(b)}
        )

    def b_hops(self, k, t):
        b = 1 + k
        copies = []
        for hi in range(self.half >> (k + 1)):
            away = 2 * hi + 1 - self.bit(b)
            src = self.r1.at[t, :, away, :, WIDE // 2 :] if k == 0 else self.rb[k - 1].at[t, :, away]
            copies.append(
                self.remote(
                    src, self.rb[k].at[t, :, hi], self.send_b.at[k, t], self.recv_b.at[k, t],
                    {"dp": self.partner(b)},
                )
            )
        return copies

    def b_whole(self, k, t):
        return self.remote(
            self.rb[k].at[t], self.rb[k].at[t], self.send_b.at[k, t], self.recv_b.at[k, t],
            {"dp": self.partner(1 + k)},
        )

    def z_hops(self, t):
        copies = []
        side = WIDE // 2
        for delta in range(1, self.parts):
            to = lax.rem(self.z + delta, self.parts)
            for i, buf in enumerate((self.ra[self.planes - 1], self.rb[self.planes - 1])):
                copies.append(
                    self.remote(
                        buf.at[t, to, 0],
                        self.r4.at[t, self.parts - 1 - delta, :, i * side : (i + 1) * side],
                        self.send4.at[t], self.recv4.at[t], {"mp": to},
                    )
                )
        return copies

    def z_whole(self, t):
        return self.remote(
            self.r4.at[t], self.r4.at[t], self.send4.at[t], self.recv4.at[t],
            {"mp": lax.rem(self.z + 1, self.parts)},
        )

    def tick(self, tick):
        count, planes, half, parts = self.count, self.planes, self.half, self.parts
        side = WIDE // 2

        @pl.when(tick == 0)
        def _():
            self.load(tick)

        t = tick - 1 - self.stride * (planes + 1)

        @pl.when((t >= 0) & (t < count))
        def _():
            self.z_whole(t).wait_recv()
            left = self.ra[planes - 1][t, self.z, 0].astype(F32)
            right = self.rb[planes - 1][t, self.z, 0].astype(F32)
            for s in range(parts - 1):
                left = left + self.r4[t, s, :, 0:side].astype(F32)
                right = right + self.r4[t, s, :, side:].astype(F32)
            self.out_ref[t, :, 0:side] = left
            self.out_ref[t, :, side:] = right

        for k in range(planes - 1, -1, -1):
            t_k = tick - 1 - self.stride * (k + 1)

            @pl.when((t_k >= 0) & (t_k < count))
            def _():
                self.a_hop(k, t_k).wait_recv()
                self.b_whole(k, t_k).wait_recv()
                keep = half >> (k + 1)
                bit_a, bit_b = self.bit(self.bits - 1 - k), self.bit(1 + k)
                for m in range(keep):
                    own_a, own_b = bit_a * keep + m, 2 * m + bit_b
                    for j in range(parts):
                        if k == 0:
                            mine_a = self.r1[t_k, j, own_a, :, 0:side]
                            mine_b = self.r1[t_k, j, own_b, :, side:]
                        else:
                            mine_a = self.ra[k - 1][t_k, j, own_a]
                            mine_b = self.rb[k - 1][t_k, j, own_b]
                        for buf, mine in ((self.ra[k], mine_a), (self.rb[k], mine_b)):
                            buf[t_k, j, m] = buf[t_k, j, m] + mine
                if k + 1 < planes:
                    self.a_hop(k + 1, t_k).start()
                    for copy in self.b_hops(k + 1, t_k):
                        copy.start()
                else:
                    for copy in self.z_hops(t_k):
                        copy.start()

        t_1 = tick - 1

        @pl.when((t_1 >= 0) & (t_1 < count))
        def _():
            self.first_hop(t_1).wait_recv()
            slot = lax.rem(t_1, 2)
            color = self.bit(0)

            @pl.loop(0, parts)
            def _(j):
                for m in range(half):
                    self.r1[t_1, j, m] = self.r1[t_1, j, m] + self.grad_s[slot, j, m, color]

            self.a_hop(0, t_1).start()
            for copy in self.b_hops(0, t_1):
                copy.start()

        @pl.when(tick < count)
        def _():
            slot = lax.rem(tick, 2)

            @pl.when(tick + 1 < count)
            def _():
                self.load(tick + 1)

            self.load_wait(tick)

            @pl.when(tick >= 2)
            def _():
                self.first_hop(tick - 2).wait_send()

            @pl.loop(0, parts)
            def _(j):
                full = jnp.dot(self.lhs_s[slot], self.rhs_s[slot, j], preferred_element_type=F32)
                self.grad_s[slot, j] = full.astype(BF16).reshape(half, 2, self.rows, WIDE)

            self.first_hop(tick).start()

    def finish(self):
        for t in range(max(self.count - 2, 0), self.count):
            self.first_hop(t).wait_send()

        @pl.loop(0, self.count)
        def _(t):
            for k in range(self.planes):
                self.a_hop(k, t).wait_send()
                self.b_whole(k, t).wait_send()
            self.z_whole(t).wait_send()


def plan_of(pairs):
    plan = []
    for seg, (kind, right) in enumerate(pairs):
        plan += [(seg, kind)] * (right.shape[2] // WIDE)
    return plan


def small_rows(heads, width, smalls):
    starts = [0]
    for count in (width // 128, width // 128, DV // 128, heads * TAPS * HEADW // 128, 1, smalls * width // 128):
        starts.append(starts[-1] + count)
    return starts, -(-starts[-1] // 8) * 8


def scatter_kernel(bits, parts, plan, rows, lhs_ref, *refs):
    sources = len({item[0] for item in plan})
    rhs_refs, refs = refs[:sources], refs[sources:]
    (ffn_ref, hgain_ref, conv_ref, line_ref, w_ref, d_small, w_small, x_ref, dx1_ref, gain_ref, out_ref, vec_out,
     g_out) = refs[:13]
    refs = refs[3:]
    v_own, v_acc, v_in, v_z, v_send, v_recv, v_z_send, v_z_recv = refs[10:18]
    swap_own, swap_send, swap_recv = refs[18:21]
    dp_s, w_s, acc_s, dx_s, in_sem = refs[21:26]
    scatter = Scatter(bits, parts, plan, rows, [lhs_ref], rhs_refs, out_ref, refs[26:], STRIDE)
    z = lax.axis_index("mp")
    mesh_id = pl.DeviceIdType.MESH
    greet_all(bits, parts, True)
    swap = Swap(2**bits, dx_s, g_out, swap_own.at[0], swap_send.at[0], swap_recv.at[0])

    def v_hop(b):
        return pltpu.make_async_remote_copy(
            src_ref=v_own if b == 0 else v_acc.at[b - 1], dst_ref=v_in.at[b], send_sem=v_send.at[b],
            recv_sem=v_recv.at[b], device_id={"dp": scatter.partner(b)}, device_id_type=mesh_id,
        )

    def v_z_hop(src, dst, delta):
        return pltpu.make_async_remote_copy(
            src_ref=src, dst_ref=dst, send_sem=v_z_send.at[0], recv_sem=v_z_recv.at[0],
            device_id={"mp": lax.rem(z + delta, parts)}, device_id_type=mesh_id,
        )

    def small_sum(stage):
        if stage == 0:
            v_hop(0).start()
        elif stage <= bits:
            b = stage - 1
            v_hop(b).wait_recv()
            total = (v_own[...] if b == 0 else v_acc[b - 1]) + v_in[b]
            if stage < bits:
                v_acc[b] = total
                v_hop(stage).start()
            else:
                v_z[z] = total
                for delta in range(1, parts):
                    v_z_hop(v_z.at[z], v_z.at[z], delta).start()
        else:
            whole = v_z.at[pl.ds(0, parts - 1)]
            v_z_hop(whole, whole, 1).wait_recv()
            total = v_z[0]
            for s in range(1, parts):
                total = total + v_z[s]
            vec_out[...] = total
            for b in range(bits):
                v_hop(b).wait_send()
            v_z_hop(whole, whole, 1).wait_send()

    def fetch(g, slot):
        return (
            pltpu.make_async_copy(rhs_refs[0].at[g], dp_s.at[slot], in_sem.at[0, slot]),
            pltpu.make_async_copy(w_ref.at[g], w_s.at[slot], in_sem.at[1, slot]),
        )

    def input_grad():
        acc_s[...] += lax.dot_general(
            d_small[...], w_small[...], (((0,), (0,)), ((), ())), preferred_element_type=F32
        )
        blocks, token_rows, width = x_ref.shape

        def body(i, gain_sum):
            x = x_ref[i].astype(F32)
            scale = lax.rsqrt(jnp.mean(x * x, axis=-1, keepdims=True) + 1e-05)
            unit = x * scale
            at = pl.ds(pl.multiple_of(i * token_rows, token_rows), token_rows)
            d_h1 = acc_s[at]
            e = d_h1 * gain_ref[...]
            d_x = dx1_ref[at] + scale * (e - unit * jnp.mean(e * unit, axis=-1, keepdims=True))
            dx_s[i] = d_x.astype(BF16)
            return gain_sum + jnp.sum(d_h1 * unit, axis=0, keepdims=True)

        gain_sum = lax.fori_loop(0, blocks, body, jnp.zeros((1, width), F32))
        starts, _ = small_rows(conv_ref.shape[0], width, d_small.shape[0])

        def put(start, row):
            for i in range(row.shape[1] // 128):
                v_own[start + i : start + i + 1] = row[:, i * 128 : (i + 1) * 128]

        put(starts[0], gain_sum)
        put(starts[1], ffn_ref[...])
        put(starts[2], hgain_ref[...])
        for h in range(conv_ref.shape[0]):
            for tap in range(TAPS):
                put(starts[3] + (h * TAPS + tap) * HEADW // 128, conv_ref[h, tap : tap + 1])
        put(starts[4], line_ref[...])
        small_grad = lax.dot_general(
            d_small[...], scatter.lhs_s[0], (((1,), (1,)), ((), ())), preferred_element_type=F32
        )
        for i in range(d_small.shape[0]):
            put(starts[5] + i * width // 128, small_grad[i : i + 1])
        if starts[6] < v_own.shape[0]:
            v_own[starts[6] :] = jnp.zeros((v_own.shape[0] - starts[6], 128), F32)

    for copy in fetch(0, 0):
        copy.start()

    @pl.loop(0, max(scatter.ticks, 1 + parts + bits + 2))
    def _(now):
        scatter.tick(now)
        tick = now - 1

        @pl.when((tick >= 0) & (tick < parts))
        def _():
            slot = lax.rem(tick, 2)

            @pl.when(tick + 1 < parts)
            def _():
                for copy in fetch(tick + 1, 1 - slot):
                    copy.start()

            for copy in fetch(tick, slot):
                copy.wait()
            part = lax.dot_general(
                dp_s[slot], w_s[slot], (((1,), (1,)), ((), ())), preferred_element_type=F32
            )

            @pl.when(tick == 0)
            def _():
                acc_s[...] = part

            @pl.when(tick > 0)
            def _():
                acc_s[...] += part

        @pl.when(tick == parts)
        def _():
            input_grad()
            swap.start()

        for stage in range(bits + 2):
            @pl.when(tick == parts + stage)
            def _():
                small_sum(stage)

    swap.finish()
    scatter.finish()


def scatter_sum(left, pairs, smalls, weight, d_small, w_small, x, d_x1, gain, groups, parts, collective):
    width, length = left.shape
    vector = jax.ShapeDtypeStruct((small_rows(smalls[2].shape[0], width, d_small.shape[0])[1], 128), F32)
    bits = groups.bit_length() - 1
    rows = width // groups
    plan = plan_of(pairs)
    count = len(plan)
    vmem_spec = pl.BlockSpec(memory_space=pltpu.VMEM)
    any_spec = pl.BlockSpec(memory_space=pl.ANY)
    dma = lambda *shape: pltpu.SemaphoreType.DMA(shape)
    return pl.pallas_call(
        partial(scatter_kernel, bits, parts, plan, rows),
        out_shape=(
            jax.ShapeDtypeStruct((count, rows, WIDE), F32),
            jax.ShapeDtypeStruct(vector.shape, F32),
            jax.ShapeDtypeStruct(x.shape, BF16),
        ),
        in_specs=[any_spec] * (1 + len(pairs)) + [vmem_spec] * 4 + [any_spec] + [vmem_spec] * 5,
        out_specs=(vmem_spec, vmem_spec, any_spec),
        scratch_shapes=[
            pltpu.VMEM(vector.shape, F32),
            pltpu.VMEM((bits - 1,) + vector.shape, F32),
            pltpu.VMEM((bits,) + vector.shape, F32),
            pltpu.VMEM((parts,) + vector.shape, F32),
            dma(bits), dma(bits), dma(1), dma(1),
            dma(1), dma(1), dma(1),
            pltpu.VMEM((2,) + pairs[0][1].shape[1:], BF16),
            pltpu.VMEM((2,) + weight.shape[1:], BF16),
            pltpu.VMEM((length, width), F32),
            pltpu.VMEM(x.shape, BF16),
            dma(2, 2),
            *Scatter.scratch(bits, parts, count, rows, length, width),
        ],
        compiler_params=pltpu.CompilerParams(
            collective_id=collective, has_side_effects=True, vmem_limit_bytes=60 * 2**20
        ),
        cost_estimate=pl.CostEstimate(
            flops=4 * count * WIDE * parts * length * width, bytes_accessed=count * parts * length * WIDE * 4,
            transcendentals=0,
        ),
        name="scatter_sum",
    )(left, *[right for _, right in pairs], *smalls, weight, d_small, w_small, x, d_x1, gain)


def backward_kernel(
    heads, parts, bits, plan, rows_held,
    dhead_ref, o_ref, gate_ref, qe_ref, phi_ref, phil_ref,
    raw_ref, halo_ref, convw_ref, ab_ref, gain_ref, s_ref, t_ref, phi_late_ref, *refs,
):
    sources = len({item[0] for item in plan})
    kinds = len({item[1] for item in plan})
    lhs_refs, refs = refs[:kinds], refs[kinds:]
    rhs_refs, swap_in, refs = refs[:sources], refs[sources], refs[sources + 1 :]
    dproj_ref, dab_ref, dconv_ref, dgain_ref, sums_ref, swap_out = refs[:6]
    (do_s, d_s, dgate_s, dl_s, phil_s, g_s, dext_s, ext_s, send_s, recv_s, halo_send, halo_recv,
     send_sem, recv_sem, halo_send_sem, halo_recv_sem) = refs[6:22]
    scatter = Scatter(bits, parts, plan, rows_held, lhs_refs, rhs_refs, sums_ref, refs[25:], 3)
    swap = Swap(2**bits, swap_in, swap_out, *[s.at[0] for s in refs[22:25]])
    step = pl.program_id(0)
    early = pl.program_id(1) == 0
    z = lax.axis_index("mp")
    back = parts - 1 - z
    lag = parts - 1
    slots = lag + 1
    length = o_ref.shape[1]
    size = min(CHUNK, length)
    chunks = length // size

    @pl.when((step == 0) & early)
    def _():
        greet_all(bits, parts, True)
        swap.start()

    sub = pl.program_id(1)
    now = jnp.where(step < lag, step, lag + 2 * (step - lag) + sub)
    last = lag + 2 * (heads + 1) - 1
    stop = jnp.where(now == last, max(scatter.ticks, last + 1), now + 1)
    stop = jnp.where((step < lag) & early, now, stop)

    @pl.loop(now, stop)
    def _(tick):
        scatter.tick(tick)


    def hop(h):
        return pltpu.make_async_remote_copy(
            src_ref=send_s.at[h], dst_ref=recv_s.at[h], send_sem=send_sem.at[h],
            recv_sem=recv_sem.at[h], device_id={"mp": lax.rem(z + parts - 1, parts)},
            device_id_type=pl.DeviceIdType.MESH,
        )

    def halo_hop(h):
        return pltpu.make_async_remote_copy(
            src_ref=halo_send.at[h], dst_ref=halo_recv.at[h], send_sem=halo_send_sem.at[h],
            recv_sem=halo_recv_sem.at[h], device_id={"mp": lax.rem(z + parts - 1, parts)},
            device_id_type=pl.DeviceIdType.MESH,
        )

    @pl.when((step == 0) & early)
    def _():
        dgain_ref[...] = jnp.zeros_like(dgain_ref)
        g_s[...] = jnp.zeros_like(g_s)

    @pl.when((step == 0) & early & (back == 0))
    def _():
        recv_s[...] = jnp.zeros_like(recv_s)
        halo_recv[...] = jnp.zeros_like(halo_recv)

    @pl.when((step < heads) & early)
    def _():
        slot = lax.rem(step, slots)
        gslot = lax.rem(step, slots + 1)
        gain = gain_ref[...]
        d_gain = jnp.zeros((1, DV), F32)
        for c in range(chunks):
            at = slice(c * size, (c + 1) * size)
            out = o_ref[0, at]
            d_head = dhead_ref[0, at]
            gate = gate_ref[0, c * size : (c + 1) * size]
            scale = lax.rsqrt(jnp.mean(out * out, axis=-1, keepdims=True) + 1e-05)
            unit = out * scale
            sig = jax.nn.sigmoid(gate)
            gated = gate * sig
            both = d_head * unit
            d_gain = d_gain + jnp.sum(both * gated, axis=0, keepdims=True)
            e = d_head * gated * gain
            d_out = scale * (e - unit * jnp.mean(e * unit, axis=-1, keepdims=True))
            dgate_s[gslot, at] = (both * gain * sig * (1.0 + gate * (1.0 - sig))).astype(BF16)
            do_s[slot, at] = d_out
            d_s[slot, c] = mm(qe_ref[0, at], d_out, 0, 0)
        dgain_ref[...] += d_gain
        total = d_s[slot, chunks - 1]
        for c in range(chunks - 2, -1, -1):
            total = mm(phi_ref[0, c], total) + d_s[slot, c]
        dl_s[slot] = total
        phil_s[slot] = phil_ref[0]

    relay = step - back

    @pl.when((relay >= 0) & (relay < heads) & early)
    def _():
        slot = lax.rem(relay, slots)

        @pl.when(back > 0)
        def _():
            hop(relay).wait_recv()

        @pl.when(z > 0)
        def _():
            send_s[relay] = mm(phil_s[slot], recv_s[relay]) + dl_s[slot]
            hop(relay).start()

    @pl.when((step >= lag) & (step < lag + heads) & ~early)
    def _():
        head = step - lag
        slot = lax.rem(head, slots)
        eslot = lax.rem(head, 2)
        rows, cols = masks(size)
        upper = (rows <= cols).astype(F32)
        convw = convw_ref[0]
        d_state = recv_s[head]
        ext_s[0:HALO] = halo_ref[0, :, 0:HEADW]
        ext_s[HALO:] = raw_ref[0, 0:size, 0:HEADW]
        d_states = [None] * chunks
        d_states[chunks - 1] = d_state
        for c in range(chunks - 1, 0, -1):
            d_states[c - 1] = mm(phi_late_ref[0, c], d_states[c]) + d_s[slot, c]
        taps_grad = [None] * chunks

        def work(c):
            at = slice(c * size, (c + 1) * size)
            shifted = windows(raw_ref, ext_s, c, size)
            conv = conv_of(shifted, convw)
            sig, q_silu, k_silu, value, q_scale, k_scale = unit_parts(conv)
            query = q_silu * (q_scale * DK ** (-0.5))
            keyed = k_silu * k_scale
            yield
            gamma_row, gamma_col, beta = decays(ab_ref, c * size, size, upper)
            inclusive, strict = fades(gamma_row, gamma_col, rows, cols)
            gram = mm(jnp.concatenate([keyed, query], axis=0), keyed, 1, 1)
            yield
            gram_f = gram[:size] * strict
            lower = beta * gram_f
            scores = gram[size:] * inclusive
            growth = jnp.exp(gamma_col)
            last = gamma_row[:, size - 1 :]
            tail = jnp.exp(last - gamma_col)
            query_g = query * growth
            grown = keyed * growth
            keyed_b = beta * grown
            keyed_g = keyed * tail
            state = s_ref[0, c]
            d_state = d_states[c]
            inverse = t_ref[0, c]
            d_out = do_s[slot, at]
            held = mm(keyed_b, state)
            yield
            fresh = mm(inverse, beta * value - held)
            yield
            d_fresh = mm(scores, d_out, 0, 0) + mm(keyed_g, d_state)
            yield
            d_rhs = mm(inverse, d_fresh, 0, 0)
            yield
            stacked = jnp.concatenate([d_out, d_rhs], axis=0)
            by_fresh = mm(stacked, fresh, 1, 1)
            yield
            by_state = mm(stacked, state, 1, 1)
            yield
            d_scores = by_fresh[:size] * inclusive
            d_lower = -by_fresh[size:]
            d_query_g = by_state[:size]
            d_keyed_b = -by_state[size:]
            d_keyed_g = mm(fresh, d_state, 1, 1)
            yield
            d_gram = d_lower * (beta * strict)
            by_keyed = mm(jnp.concatenate([d_scores, d_gram], axis=0), keyed)
            yield
            d_query = by_keyed[:size] + growth * d_query_g
            d_keyed = (
                by_keyed[size:]
                + mm(jnp.concatenate([d_scores, d_gram], axis=0),
                     jnp.concatenate([query, keyed], axis=0), 0, 0)
                + (beta * growth) * d_keyed_b
                + tail * d_keyed_g
            )
            yield
            d_value = beta * d_rhs
            d_beta = (
                jnp.sum(d_rhs * value, axis=-1, keepdims=True)
                + jnp.sum(d_lower * gram_f, axis=-1, keepdims=True)
                + jnp.sum(d_keyed_b * grown, axis=-1, keepdims=True)
            )
            moved = by_fresh[:size] * scores + d_lower * lower
            tail_part = jnp.sum(d_keyed_g * keyed_g, axis=-1, keepdims=True)
            d_gamma = (
                jnp.sum(moved, axis=-1, keepdims=True)
                + jnp.sum(d_query_g * query_g, axis=-1, keepdims=True)
                + jnp.sum(d_keyed_b * keyed_b, axis=-1, keepdims=True)
                - tail_part
            )
            at_end = jnp.sum(tail_part, axis=0, keepdims=True) + jnp.exp(last) * jnp.sum(
                jnp.sum(state * d_state, axis=-1, keepdims=True), axis=0, keepdims=True
            )
            lanes = lax.broadcasted_iota(jnp.int32, (size, DK), 1)
            packed = jnp.where(lanes == 0, d_gamma, jnp.where(lanes == 1, d_beta, 0.0)).T[:8]
            row_id = lax.broadcasted_iota(jnp.int32, packed.shape, 0)
            packed = packed - jnp.where(row_id == 0, jnp.sum(moved, axis=0, keepdims=True), 0.0)
            yield
            summed = mm(packed, upper, 1, 1) + at_end
            dab_ref[0, :, at] = jnp.where(row_id == 0, summed, packed)
            d_q_silu = (DK ** (-0.5) * q_scale) * (
                d_query
                - q_silu * (q_scale * q_scale) * jnp.sum(q_silu * d_query, axis=-1, keepdims=True)
            )
            d_k_silu = k_scale * (
                d_keyed
                - k_silu * (k_scale * k_scale) * jnp.sum(k_silu * d_keyed, axis=-1, keepdims=True)
            )
            d_silu = jnp.concatenate([d_q_silu, d_k_silu, d_value], axis=1)
            d_conv = d_silu * sig * (1.0 + conv * (1.0 - sig))
            g_s[HALO + c * size : HALO + (c + 1) * size] = d_conv
            taps_grad[c] = [jnp.sum(shifted[i] * d_conv, axis=0, keepdims=True) for i in range(TAPS)]

        for first in range(0, chunks, 2):
            in_step([work(c) for c in range(first, min(first + 2, chunks))])
        d_conv_rows = [sum(row[i] for row in taps_grad[1:]) + taps_grad[0][i] for i in range(TAPS)]
        for i in range(TAPS):
            dconv_ref[0, i : i + 1] = d_conv_rows[i]
        for base, count in [(0, HALO)] + [(HALO + c * size, size) for c in range(chunks)]:
            d_raw = None
            for i in range(TAPS):
                part = g_s[pl.ds(base + TAPS - 1 - i, count)] * convw[i : i + 1]
                d_raw = part if d_raw is None else d_raw + part
            if base == 0:
                halo_send[head] = d_raw
            else:
                dext_s[eslot, base - HALO : base - HALO + count] = d_raw

        @pl.when(z > 0)
        def _():
            halo_hop(head).start()

    @pl.when((step > lag) & ~early)
    def _():
        head = step - lag - 1
        eslot = lax.rem(head, 2)
        gslot = lax.rem(head, slots + 1)

        @pl.when(back > 0)
        def _():
            halo_hop(head).wait_recv()

        dext_s[eslot, length - HALO : length] += halo_recv[head]
        dproj_ref[0, :, 0:HEADW] = dext_s[eslot].astype(BF16)
        dproj_ref[0, :, HEADW:] = dgate_s[gslot]

    @pl.when((step == pl.num_programs(0) - 1) & ~early)
    def _():
        scatter.finish()
        swap.finish()

    @pl.when((step == pl.num_programs(0) - 1) & ~early & (z > 0))
    def _():
        @pl.loop(0, heads)
        def _(h):
            hop(h).wait_send()
            halo_hop(h).wait_send()


def assemble_kernel(
    per, starts, ffn_ref, proj_ref, vec_ref, y_ref, g_ref,
    query_ref, key_ref, value_ref, outgate_ref, out_ref, gate_ref, up_ref, down_ref, conv_ref, y_out, g_out,
    mix_ref, gain_ref, hgain_ref, small_ref,
):
    y_out[...] = y_ref[...]
    g_out[...] = g_ref[...]
    for h in range(per):
        query_ref[:, h * DK : (h + 1) * DK] = proj_ref[3 * h, :, 0:DK]
        key_ref[:, h * DK : (h + 1) * DK] = proj_ref[3 * h, :, DK:]
        value_ref[:, h * DV : (h + 1) * DV] = proj_ref[3 * h + 1]
        outgate_ref[:, h * DV : (h + 1) * DV] = proj_ref[3 * h + 2]
    piece = 0
    for target in (down_ref, gate_ref, up_ref):
        total = target.shape[0]
        for start in range(0, total, WIDE):
            size = min(WIDE, total - start)
            target[start : start + size] = ffn_ref[piece].T[0:size]
            piece += 1
    for start in range(0, out_ref.shape[1], WIDE):
        out_ref[:, start : start + WIDE] = ffn_ref[piece]
        piece += 1
    width = conv_ref.shape[1]
    heads = width // HEADW
    for h in range(heads):
        for tap in range(TAPS):
            row = starts[3] + (h * TAPS + tap) * HEADW // 128
            spots = [h * DK, (heads + h) * DK, 2 * heads * DK + h * DV, 2 * heads * DK + h * DV + 128]
            for i, spot in enumerate(spots):
                conv_ref[tap : tap + 1, spot : spot + 128] = vec_ref[row + i : row + i + 1]
    mix_ref[...] = vec_ref[starts[0] : starts[1]]
    gain_ref[...] = vec_ref[starts[1] : starts[2]]
    hgain_ref[...] = vec_ref[starts[2] : starts[3]]
    smalls, rows = small_ref.shape
    lines = starts[1] - starts[0]
    first = lax.axis_index("dp") * rows
    share = lax.axis_index("mp")
    shift = lax.rem(first, 128)
    pick = lax.broadcasted_iota(jnp.int32, (128, rows), 0) == lax.broadcasted_iota(jnp.int32, (128, rows), 1) + shift
    for c in range(smalls):
        row = vec_ref[pl.ds(starts[5] + (share * smalls + c) * lines + lax.div(first, 128), 1)]
        if rows != 128:
            row = jnp.sum(jnp.where(pick, row.T, 0.0), axis=0, keepdims=True)
        small_ref[c : c + 1] = row


def assemble(ffn, proj, vec, y, g, per, hidden, starts, conv_shape):
    rows = ffn.shape[1]
    f32 = lambda *shape: jax.ShapeDtypeStruct(shape, F32)
    vmem_spec = pl.BlockSpec(memory_space=pltpu.VMEM)
    return pl.pallas_call(
        partial(assemble_kernel, per, starts),
        out_shape=(
            f32(rows, per * DK), f32(rows, per * DK), f32(rows, per * DV), f32(rows, per * DV), f32(rows, per * DV),
            f32(hidden, rows), f32(hidden, rows), f32(hidden, rows), f32(*conv_shape),
            jax.ShapeDtypeStruct(y.shape, BF16), jax.ShapeDtypeStruct(g.shape, BF16),
            *[f32(starts[i + 1] - starts[i], 128) for i in range(3)], f32(2 * per, rows),
        ),
        in_specs=[vmem_spec] * 5,
        out_specs=(vmem_spec,) * 15,
        compiler_params=pltpu.CompilerParams(vmem_limit_bytes=40 * 2**20),
        cost_estimate=pl.CostEstimate(flops=0, bytes_accessed=10 * 2**20, transcendentals=0),
        name="assemble",
    )(ffn, proj, vec, y, g)


def forward_core(raw, convw, ab, gain, swapped, weights, heads, parts, groups):
    bits = groups.bit_length() - 1
    pieces = []
    for w, weight in enumerate(weights):
        wide = weight.shape[1]
        pieces += [(w, at, at + WIDE // 2, at + WIDE) for at in range(0, wide, WIDE)]
    rows = weights[0].shape[0]
    any_spec = pl.BlockSpec(memory_space=pl.ANY)
    length = raw.shape[1]
    size = min(CHUNK, length)
    chunks = length // size
    per = heads // raw.shape[0]
    lag = parts - 1
    slots = lag + 1
    now = lambda s: jnp.minimum(s, heads - 1)
    late = lambda s: jnp.maximum(s - lag, 0)
    return pl.pallas_call(
        partial(forward_kernel, heads, parts, bits, pieces),
        grid=(heads + lag, 2),
        out_shape=(
            jax.ShapeDtypeStruct((raw.shape[0], length, per * DV), BF16),
            jax.ShapeDtypeStruct((heads, length, DV), F32),
            jax.ShapeDtypeStruct((heads, chunks, DK, DV), F32),
            jax.ShapeDtypeStruct((heads, chunks, size, size), F32),
            jax.ShapeDtypeStruct((heads, length, DK), F32),
            jax.ShapeDtypeStruct((heads, chunks, DK, DK), F32),
            jax.ShapeDtypeStruct((heads, DK, DK), F32),
            jax.ShapeDtypeStruct((parts, HALO, per * (HEADW + DV)), F32),
            jax.ShapeDtypeStruct(swapped.shape, BF16),
            *[jax.ShapeDtypeStruct((parts, groups) + w.shape, BF16) for w in weights],
        ),
        in_specs=[
            pl.BlockSpec((1, length, HEADW + DV), lambda s, _: (now(s) // per, 0, now(s) % per)),
            pl.BlockSpec((1, length, DV), lambda s, _: (late(s) // per, 0, (late(s) % per) * 3 + 2)),
            any_spec,
            pl.BlockSpec((1, TAPS, HEADW), lambda s, _: (now(s), 0, 0)),
            pl.BlockSpec((1, 8, length), lambda s, _: (now(s), 0, 0)),
            pl.BlockSpec((1, DV), lambda s, _: (0, 0)),
            *[any_spec] * (1 + len(weights)),
        ],
        out_specs=(
            pl.BlockSpec((1, length, DV), lambda s, _: (late(s) // per, 0, late(s) % per)),
            pl.BlockSpec((1, length, DV), lambda s, _: (late(s), 0, 0)),
            pl.BlockSpec((1, chunks, DK, DV), lambda s, _: (late(s), 0, 0, 0)),
            pl.BlockSpec((1, chunks, size, size), lambda s, _: (now(s), 0, 0, 0)),
            pl.BlockSpec((1, length, DK), lambda s, _: (now(s), 0, 0)),
            pl.BlockSpec((1, chunks, DK, DK), lambda s, _: (now(s), 0, 0, 0)),
            pl.BlockSpec((1, DK, DK), lambda s, _: (now(s), 0, 0)),
            pl.BlockSpec((parts, HALO, per * (HEADW + DV)), lambda s, _: (0, 0, 0)),
            *[any_spec] * (1 + len(weights)),
        ),
        scratch_shapes=[
            pltpu.VMEM((slots, length, DK), F32),
            pltpu.VMEM((slots, length, DV), F32),
            pltpu.VMEM((slots, chunks, DK, DK), F32),
            pltpu.VMEM((slots, chunks, DK, DV), F32),
            pltpu.VMEM((slots, DK, DK), F32),
            pltpu.VMEM((slots, DK, DV), F32),
            pltpu.VMEM((heads, DK, DV), F32),
            pltpu.VMEM((heads, DK, DV), F32),
            pltpu.VMEM((parts, HALO, per * (HEADW + DV)), F32),
            pltpu.VMEM((HALO + size, HEADW), F32),
            pltpu.SemaphoreType.DMA((heads,)),
            pltpu.SemaphoreType.DMA((heads,)),
            pltpu.SemaphoreType.DMA((parts,)),
            pltpu.SemaphoreType.DMA((parts,)),
            *[pltpu.SemaphoreType.DMA((1,))] * 3,
            *Gather.scratch(bits, len(pieces)),
        ],
        compiler_params=pltpu.CompilerParams(
            collective_id=0, has_side_effects=True, vmem_limit_bytes=56 * 2**20
        ),
        cost_estimate=pl.CostEstimate(flops=20 * 10**9, bytes_accessed=40 * 2**20, transcendentals=0),
        name="delta_forward",
    )(raw, raw, raw, convw, ab, gain, swapped, *weights)


def backward_core(d_head, out, raw, halo, query_e, phi, phi_all, convw, ab, gain, states, inverses, lefts, pairs, swapped,
                  heads, parts, groups):
    length = raw.shape[1]
    size = min(CHUNK, length)
    chunks = length // size
    per = heads // raw.shape[0]
    lag = parts - 1
    slots = lag + 1
    bits = groups.bit_length() - 1
    plan = plan_of(pairs)
    rows = lefts[0].shape[0] // groups
    any_spec = pl.BlockSpec(memory_space=pl.ANY)
    now = lambda s: jnp.minimum(s, heads - 1)
    late = lambda s: jnp.clip(s - lag, 0, heads - 1)
    later = lambda s: jnp.maximum(s - lag - 1, 0)
    return pl.pallas_call(
        partial(backward_kernel, heads, parts, bits, plan, rows),
        grid=(heads + lag + 1, 2),
        out_shape=(
            jax.ShapeDtypeStruct((raw.shape[0], length, per * (HEADW + DV)), BF16),
            jax.ShapeDtypeStruct((heads, 8, length), F32),
            jax.ShapeDtypeStruct((heads, TAPS, HEADW), F32),
            jax.ShapeDtypeStruct((1, DV), F32),
            jax.ShapeDtypeStruct((len(plan), rows, WIDE), F32),
            jax.ShapeDtypeStruct(swapped.shape, BF16),
        ),
        in_specs=[
            pl.BlockSpec((1, length, DV), lambda s, _: (now(s) // per, 0, now(s) % per)),
            pl.BlockSpec((1, length, DV), lambda s, _: (now(s), 0, 0)),
            pl.BlockSpec((1, length, DV), lambda s, _: (now(s) // per, 0, (now(s) % per) * 3 + 2)),
            pl.BlockSpec((1, length, DK), lambda s, _: (now(s), 0, 0)),
            pl.BlockSpec((1, chunks, DK, DK), lambda s, _: (now(s), 0, 0, 0)),
            pl.BlockSpec((1, DK, DK), lambda s, _: (now(s), 0, 0)),
            pl.BlockSpec((1, length, HEADW + DV), lambda s, _: (late(s) // per, 0, late(s) % per)),
            pl.BlockSpec((1, HALO, HEADW + DV), lambda s, _: (late(s) // per, 0, late(s) % per)),
            pl.BlockSpec((1, TAPS, HEADW), lambda s, _: (late(s), 0, 0)),
            pl.BlockSpec((1, 8, length), lambda s, _: (late(s), 0, 0)),
            pl.BlockSpec((1, DV), lambda s, _: (0, 0)),
            pl.BlockSpec((1, chunks, DK, DV), lambda s, _: (late(s), 0, 0, 0)),
            pl.BlockSpec((1, chunks, size, size), lambda s, _: (late(s), 0, 0, 0)),
            pl.BlockSpec((1, chunks, DK, DK), lambda s, _: (late(s), 0, 0, 0)),
            *[any_spec] * (1 + len(lefts) + len(pairs)),
        ],
        out_specs=(
            pl.BlockSpec((1, length, HEADW + DV), lambda s, _: (later(s) // per, 0, later(s) % per)),
            pl.BlockSpec((1, 8, length), lambda s, _: (late(s), 0, 0)),
            pl.BlockSpec((1, TAPS, HEADW), lambda s, _: (late(s), 0, 0)),
            pl.BlockSpec((1, DV), lambda s, _: (0, 0)),
            pl.BlockSpec((len(plan), rows, WIDE), lambda s, _: (0, 0, 0)),
            any_spec,
        ),
        scratch_shapes=[
            pltpu.VMEM((slots, length, DV), F32),
            pltpu.VMEM((slots, chunks, DK, DV), F32),
            pltpu.VMEM((slots + 1, length, DV), BF16),
            pltpu.VMEM((slots, DK, DV), F32),
            pltpu.VMEM((slots, DK, DK), F32),
            pltpu.VMEM((length + 2 * HALO, HEADW), F32),
            pltpu.VMEM((2, length, HEADW), F32),
            pltpu.VMEM((HALO + size, HEADW), F32),
            pltpu.VMEM((heads, DK, DV), F32),
            pltpu.VMEM((heads, DK, DV), F32),
            pltpu.VMEM((heads, HALO, HEADW), F32),
            pltpu.VMEM((heads, HALO, HEADW), F32),
            pltpu.SemaphoreType.DMA((heads,)),
            pltpu.SemaphoreType.DMA((heads,)),
            pltpu.SemaphoreType.DMA((heads,)),
            pltpu.SemaphoreType.DMA((heads,)),
            *[pltpu.SemaphoreType.DMA((1,))] * 3,
            *Scatter.scratch(bits, parts, len(plan), rows, length, lefts[0].shape[0]),
        ],
        compiler_params=pltpu.CompilerParams(
            collective_id=1, has_side_effects=True, vmem_limit_bytes=62 * 2**20
        ),
        cost_estimate=pl.CostEstimate(flops=40 * 10**9, bytes_accessed=60 * 2**20, transcendentals=0),
        name="delta_backward",
    )(d_head, out, raw, query_e, phi, phi_all, raw, halo, convw, ab, gain, states, inverses, phi,
      *lefts, *[right for _, right in pairs], swapped)


def dot(spec, a, b):
    return jnp.einsum(spec, a, b, preferred_element_type=F32)


def unit_rms(v):
    return lax.rsqrt(jnp.mean(v * v, axis=-1, keepdims=True) + 1e-05)


def per_device(
    tokens, out_grad, seq_lengths, mix_gain, w_query, w_key, w_value, w_outgate, w_decay, w_beta,
    conv_weight, rate_log, step_bias, head_gain, w_out, ffn_gain, w_ffn_gate, w_ffn_up, w_ffn_down,
):
    groups = lax.axis_size("dp")
    parts = lax.axis_size("mp")
    group = lax.axis_index("dp")
    share = lax.axis_index("mp")
    heads = rate_log.shape[0]
    per = heads // parts
    width = tokens.shape[2]
    local_rows = w_query.shape[0]

    hidden = w_ffn_gate.shape[1]
    wide = -(-hidden // WIDE) * WIDE
    small_w = jnp.concatenate([w_decay, w_beta], axis=1).T
    small_w = jnp.pad(small_w, ((0, -small_w.shape[0] % 16), (0, 0)))
    x_bf, g_proj, g_small, raw, h1, h1_t, *padded = prologue(
        tokens, small_w, mix_gain[None], (w_query, w_key, w_value, w_outgate),
        (w_ffn_gate.T, w_ffn_up.T, w_ffn_down.T), groups, parts,
    )
    h1 = h1.reshape(-1, width)
    whole = lambda g: g.reshape(parts, width, g.shape[3])
    g_proj = whole(g_proj)
    g_small = g_small[:, :, : 2 * per].transpose(0, 2, 1, 3).reshape(parts, 2 * per, width)
    x_swapped = x_bf
    x_bf = x_bf.reshape(-1, width)
    length = x_bf.shape[0]

    my_length = lax.dynamic_slice_in_dim(seq_lengths, group, 1)
    positions = share * length + jnp.arange(length, dtype=jnp.int32)
    live = (positions < my_length).astype(F32)[:, None]

    x = x_bf.astype(F32)
    small = dot("td,gcd->gct", h1, g_small)
    decay_raw = small[:, :per].reshape(heads, length)
    beta_raw = small[:, per:].reshape(heads, length)
    rate = -jnp.exp(rate_log)[:, None]
    shifted = decay_raw + step_bias[:, None]
    decay = rate * jax.nn.softplus(shifted)
    beta = jax.nn.sigmoid(beta_raw)
    ab = jnp.concatenate(
        [decay[:, None], beta[:, None], jnp.zeros((heads, 6, length), F32)], axis=1
    )
    taps = conv_weight.shape[0]
    key_cols = heads * DK
    convw = jnp.concatenate(
        [
            conv_weight[:, :key_cols].reshape(taps, heads, DK),
            conv_weight[:, key_cols : 2 * key_cols].reshape(taps, heads, DK),
            conv_weight[:, 2 * key_cols :].reshape(taps, heads, DV),
        ],
        axis=2,
    ).transpose(1, 0, 2)
    gain_row = head_gain[None]
    head_out, mixed, states, inverses, query_e, phi, phi_all, halo, dy_bf, *rest = forward_core(
        raw, convw, ab, gain_row, out_grad,
        [w_out] + padded,
        heads, parts, groups,
    )
    g_out, g_gate, g_up, g_down = [whole(w) for w in rest]

    dy = live * dy_bf.reshape(-1, width).astype(F32)
    d_ffo = dy.astype(BF16)
    x1 = x + dot("gtc,gmc->tm", head_out, g_out)
    scale2 = unit_rms(x1)
    n2 = x1 * scale2
    h2 = (n2 * ffn_gain).astype(BF16)
    gate = dot("td,gdf->gtf", h2, g_gate)
    up = dot("td,gdf->gtf", h2, g_up)
    sig = jax.nn.sigmoid(gate)
    act = (gate * sig * up).astype(BF16)
    block_out = (live * (x1 + dot("gtf,gdf->td", act, g_down))).astype(BF16)
    d_act = dot("td,gdf->gtf", d_ffo, g_down)
    d_gate = (d_act * up * sig * (1.0 + gate * (1.0 - sig))).astype(BF16)
    d_up = (d_act * gate * sig).astype(BF16)
    d_h2 = dot("gtf,gdf->td", d_gate, g_gate) + dot("gtf,gdf->td", d_up, g_up)
    e2 = d_h2 * ffn_gain
    d_x1 = dy + scale2 * (e2 - n2 * jnp.mean(e2 * n2, axis=-1, keepdims=True))
    ffn_gain_grad = jnp.sum(d_h2 * n2, axis=0)
    d_mix = d_x1.astype(BF16)
    d_head = dot("tm,gmc->gtc", d_mix, g_out)

    d_proj, d_ab, d_convw, d_head_gain, sums_ffn, final_out = backward_core(
        d_head, mixed, raw, halo, query_e, phi, phi_all, convw, ab, gain_row, states, inverses,
        [d_mix.T, h2.T, d_ffo.T], [(2, act), (1, d_gate), (1, d_up), (0, head_out)],
        block_out.reshape(tokens.shape), heads, parts, groups,
    )
    d_decay = d_ab[:, 0]
    d_beta_raw = d_ab[:, 1] * beta * (1.0 - beta)
    d_decay_raw = d_decay * rate * jax.nn.sigmoid(shifted)
    rate_grad = jnp.sum(d_decay * decay, axis=1)
    bias_grad = jnp.sum(d_decay_raw, axis=1)
    d_small = jnp.concatenate(
        [d_decay_raw.reshape(parts, per, length), d_beta_raw.reshape(parts, per, length)], axis=1
    ).astype(BF16)
    line = jnp.pad(jnp.concatenate([rate_grad, bias_grad])[None], ((0, 0), (0, 128 - 2 * heads)))
    sums_proj, sums, final_grad = scatter_sum(
        h1_t, [(0, d_proj)],
        (ffn_gain_grad[None], d_head_gain, d_convw, line), g_proj, d_small.reshape(-1, length),
        g_small.reshape(-1, width), x_swapped, d_x1, mix_gain[None], groups, parts, 2,
    )
    starts, _ = small_rows(heads, width, 2 * heads)
    part = lambda i: sums[starts[i] : starts[i + 1]].reshape(-1)
    (s_query, s_key, s_value, s_outgate, s_out, s_gate, s_up, s_down, s_conv, final_out, final_grad,
     s_mix, s_gain, s_hgain, s_small) = assemble(
        sums_ffn, sums_proj, sums, final_out, final_grad, per, hidden, starts, conv_weight.shape
    )
    return (
        final_out,
        final_grad,
        s_mix.reshape(-1),
        s_query,
        s_key,
        s_value,
        s_outgate,
        s_small[:per].T,
        s_small[per:].T,
        s_conv,
        part(4)[:heads],
        part(4)[heads : 2 * heads],
        s_hgain.reshape(-1),
        s_out,
        s_gain.reshape(-1),
        s_gate.T,
        s_up.T,
        s_down.T,
    )


def solution(mesh):
    seq = P(None, ("mp", "dp"), None)
    shard = P("dp", "mp")
    rep = P()
    return jax.shard_map(
        per_device,
        mesh=mesh,
        in_specs=(
            seq, seq, rep, rep, shard, shard, shard, shard, shard, shard,
            rep, rep, rep, rep, shard, rep, shard, shard, shard,
        ),
        out_specs=(
            seq, seq, rep, shard, shard, shard, shard, shard, shard,
            rep, rep, rep, rep, shard, rep, shard, shard, shard,
        ),
        check_vma=False,
    )
```
